32 devices in a mesh: frames: 8 (over z, y), atoms: 4 (over x, core).
Axes of the slice: x: 2, y: 2, z: 4, core: 2. Of those that a mesh axis runs over, the one named last changes fastest.
Arguments:
- frames: float32 [512, 3, 4096], P('frames', None, 'atoms'), may hold values from -40 to 40
- mean_structure: float32 [3, 4096], P(None, 'atoms'), may hold values from -8 to 8
- eigvecs: bfloat16 [3, 4096, 256], P(None, 'atoms'), may hold values from -0.0546875 to 0.0546875
Outputs:
- covariance: float32 [3, 4096, 3, 4096], P(None, 'atoms', None, 'frames')
- projections: float32 [512, 256], P('frames', 'atoms')
The draws below stay inside these ranges and needn't reach their ends.
All inputs are finite; a program needn't handle non-finite values.
Results may differ from the reference program's by a relative error of at most 0.0039.
Values may be sent and summed in bfloat16 or wider, within the bound.
No kernel may reach another device: no remote copies, remote signals or barrier semaphores. Data moves between devices by JAX's collectives and lax.ppermute only.
A program may use at most 128 MiB of HBM per device.

```python
import jax
import jax.numpy as jnp
from jax import lax

ATOMS = 4096
K = 256
POLAR = 6
FRAMES = 512


def anchor_shape(key, blend, scale_x, scale_y, scale_z):
    key = jax.random.fold_in(key, 101)
    first, second = jax.random.split(key)
    plain = jax.random.normal(first, (3, ATOMS), jnp.float32)
    flat = jax.random.uniform(second, (3, ATOMS), jnp.float32, -1.732, 1.732)
    mixed = (1.0 - blend) * plain + blend * flat
    scales = jnp.array([scale_x, scale_y, scale_z], jnp.float32)[:, None]
    return jnp.clip(mixed * scales, -8.0, 8.0)


def draw_mean_structure(key, part):
    shape_ref = anchor_shape(key, 0.0, 1.6, 1.2, 0.9)
    return shape_ref


def draw_frames(key, part):
    shape_ref = anchor_shape(key, 0.0, 1.6, 1.2, 0.9)
    blend = 0.0
    common_weight = 0.0
    key = jax.random.fold_in(key, 7)
    keys = jax.random.split(key, 10)
    alpha = jax.random.uniform(keys[0], (FRAMES,), jnp.float32, -3.14159, 3.14159)
    beta = jax.random.uniform(keys[1], (FRAMES,), jnp.float32, -3.14159, 3.14159)
    gamma = jax.random.uniform(keys[2], (FRAMES,), jnp.float32, -3.14159, 3.14159)
    cos_a, sin_a = (jnp.cos(alpha), jnp.sin(alpha))
    cos_b, sin_b = (jnp.cos(beta), jnp.sin(beta))
    cos_c, sin_c = (jnp.cos(gamma), jnp.sin(gamma))
    matrix_rows = [[cos_a * cos_b * cos_c - sin_a * sin_c, -cos_a * cos_b * sin_c - sin_a * cos_c, cos_a * sin_b], [sin_a * cos_b * cos_c + cos_a * sin_c, -sin_a * cos_b * sin_c + cos_a * cos_c, sin_a * sin_b], [-sin_b * cos_c, sin_b * sin_c, cos_b]]
    rotated = jnp.stack([sum((matrix_rows[row][col][:, None] * shape_ref[col][None, :] for col in range(3))) for row in range(3)], axis=1)
    shift = jnp.clip(2.0 * jax.random.normal(keys[3], (FRAMES, 3), jnp.float32), -6.0, 6.0)
    frame_scale = jnp.exp(jax.random.uniform(keys[4], (FRAMES,), jnp.float32, jnp.log(0.5), jnp.log(2.0)))
    atom_scale = jnp.exp(jax.random.uniform(keys[5], (ATOMS,), jnp.float32, jnp.log(0.3), jnp.log(3.0)))
    plain = jnp.clip(jax.random.normal(keys[6], (FRAMES, 3, ATOMS), jnp.float32), -4.0, 4.0)
    flat = jax.random.uniform(keys[7], (FRAMES, 3, ATOMS), jnp.float32, -1.732, 1.732)
    noise = (1.0 - blend) * plain + blend * flat
    noise = 0.35 * noise * frame_scale[:, None, None] * atom_scale[None, None, :]
    pattern = jnp.clip(jax.random.normal(keys[8], (3, ATOMS), jnp.float32), -3.0, 3.0)
    weights = jnp.clip(jax.random.normal(keys[9], (FRAMES,), jnp.float32), -3.0, 3.0)
    common = common_weight * weights[:, None, None] * pattern[None]
    return rotated + shift[:, :, None] + noise + common


def block_levels(key, shape, pieces, smallest, largest):
    gain, own = 1.0, jax.random.fold_in(key, 6)
    for axis_at, shards_of in pieces:
        heights = jnp.exp(jax.random.uniform(jax.random.fold_in(own, axis_at), (shards_of,), jnp.float32, smallest / len(pieces), largest / len(pieces)))
        gain = gain * jnp.repeat(heights, shape[axis_at] // shards_of).reshape([-1 if axis == axis_at else 1 for axis in range(len(shape))])
    return gain


def normal_values(stream_key, extent, scale, limit, pieces=(), kind=jnp.bfloat16):
    values = scale * jax.random.normal(stream_key, extent, jnp.float32)
    if pieces:
        values = values * block_levels(stream_key, extent, pieces, -0.22, 0.18)
    return jnp.clip(values, -limit, limit).astype(kind)


def setup_inputs(seed: int = 0) -> dict:
    key_of = jax.random.split(jax.random.key(seed), 4)
    frames = draw_frames(jax.random.fold_in(key_of[3], 71), 0)
    mean_structure = draw_mean_structure(jax.random.fold_in(key_of[3], 71), 0)
    eigvecs = normal_values(key_of[2], (3, ATOMS, K), (3 * ATOMS) ** -0.5, 0.0546875, ((1, 4),))
    return dict(frames=frames, mean_structure=mean_structure, eigvecs=eigvecs)


def polar_factor(start):
    eye = jnp.eye(3, dtype=jnp.float32)
    current = start
    for step in range(POLAR):
        gram = jnp.einsum('fki,fkj->fij', current, current, precision=lax.Precision.HIGHEST)
        current = 0.5 * jnp.einsum('fik,fkj->fij', current, 3.0 * eye - gram, precision=lax.Precision.HIGHEST)
    return current

def reference(frames, mean_structure, eigvecs):
    ref_centre = lax.optimization_barrier(jnp.sum(mean_structure, axis=1)) / ATOMS
    centred_ref = mean_structure - ref_centre[:, None]
    ref_spread = jnp.sum(centred_ref * centred_ref)
    centre = lax.optimization_barrier(jnp.sum(frames, axis=2)) / ATOMS
    centred = frames - centre[:, :, None]
    spread = lax.optimization_barrier(jnp.sum(centred * centred, axis=(1, 2)))
    corr = jnp.einsum('fia,ja->fij', centred, centred_ref, precision=lax.Precision.HIGHEST)
    start = corr / jnp.sqrt(spread * ref_spread + 1e-06)[:, None, None]
    rotation = polar_factor(start)
    aligned = jnp.einsum('fji,fja->fia', rotation, centred, precision=lax.Precision.HIGHEST)
    displaced = (aligned - centred_ref[None]).astype(jnp.bfloat16)
    flat = displaced.reshape(FRAMES, 3 * ATOMS).astype(jnp.float32)
    projections = jnp.dot(flat, eigvecs.reshape(3 * ATOMS, K).astype(jnp.float32), precision=lax.Precision.HIGHEST)
    covariance = jnp.dot(flat.T, flat, precision=lax.Precision.HIGHEST) / FRAMES
    return (covariance.reshape(3, ATOMS, 3, ATOMS), projections)
```

```python
import functools

import jax
import jax.numpy as jnp
from jax import lax
from jax.experimental import pallas as pl
from jax.experimental.pallas import tpu as pltpu
from jax.sharding import PartitionSpec as P

POLAR = 6
LANES = 128
VMEM = pl.BlockSpec(memory_space=pltpu.VMEM)
SMEM = pl.BlockSpec(memory_space=pltpu.SMEM)
ANY = pl.BlockSpec(memory_space=pl.ANY)
BIG = pltpu.CompilerParams(vmem_limit_bytes=48 * 1024 * 1024)


def lane_mean(value):
    return jnp.sum(value, axis=1, keepdims=True) * (1.0 / value.shape[1])


def stats_kernel(x_ref, ref_ref, out_ref):
    values = []
    centred = []
    for i in range(3):
        x = x_ref[i]
        mean = lane_mean(x)
        values.append(mean)
        centred.append(x - mean)
    spread = sum(jnp.sum(c * c, axis=1, keepdims=True) for c in centred)
    values.append(spread)
    ref_mean = [lane_mean(ref_ref[j : j + 1, :]) for j in range(3)]
    ref_centred = [ref_ref[j : j + 1, :] - ref_mean[j] for j in range(3)]
    for i in range(3):
        for j in range(3):
            values.append(jnp.sum(centred[i] * ref_centred[j], axis=1, keepdims=True))
    values += ref_mean
    values.append(sum(jnp.sum(c * c, axis=1, keepdims=True) for c in ref_centred))
    lane = lax.broadcasted_iota(jnp.int32, out_ref.shape, 1)
    out = jnp.zeros(out_ref.shape, jnp.float32)
    for k, value in enumerate(values):
        out = jnp.where(lane == k, jnp.broadcast_to(value, out.shape), out)
    out_ref[...] = out


def align_kernel(parts, atoms, half_ref, *refs):
    stats = refs[:parts]
    x_ref, ref_ref, first_ref, second_ref, cols_ref = refs[parts:]
    local = x_ref.shape[2]
    rows = x_ref.shape[1]

    def columns(at):
        return [s[:, at : at + 1] for s in stats]

    means = [columns(i) for i in range(3)]
    ref_means = [columns(13 + j) for j in range(3)]
    centre = [sum(m) * (1.0 / parts) for m in means]
    ref_centre = [sum(r) * (1.0 / parts) for r in ref_means]
    off = [[m - centre[i] for m in means[i]] for i in range(3)]
    ref_off = [[r - ref_centre[j] for r in ref_means[j]] for j in range(3)]
    spread = sum(columns(3)) + local * sum(o * o for i in range(3) for o in off[i])
    ref_spread = sum(columns(16)) + local * sum(o * o for j in range(3) for o in ref_off[j])
    scale = 1.0 / jnp.sqrt(spread * ref_spread + 1e-06)
    now = [
        [
            (sum(columns(4 + 3 * i + j)) + local * sum(o * r for o, r in zip(off[i], ref_off[j]))) * scale
            for j in range(3)
        ]
        for i in range(3)
    ]
    for _ in range(POLAR):
        gram = {}
        for i in range(3):
            for j in range(i, 3):
                gram[i, j] = sum(now[k][i] * now[k][j] for k in range(3))
                gram[j, i] = gram[i, j]
        left = [
            [(3.0 if k == j else 0.0) - gram[k, j] for j in range(3)] for k in range(3)
        ]
        now = [
            [0.5 * sum(now[i][k] * left[k][j] for k in range(3)) for j in range(3)]
            for i in range(3)
        ]
    centred = [x_ref[j] - centre[j] for j in range(3)]
    block = cols_ref.shape[2]
    for i in range(3):
        target = ref_ref[i : i + 1, :] - ref_centre[i][0:1, :]
        moved = sum(now[j][i] * centred[j] for j in range(3)) - target
        moved = moved.astype(jnp.bfloat16)
        first_ref[i] = moved[: rows // 2]
        second_ref[i] = moved[rows // 2 :]
    start = pl.multiple_of(half_ref[0] * block, LANES)
    for i in range(3):
        cols_ref[i, : rows // 2, :] = first_ref[i, :, pl.ds(start, block)]
        cols_ref[i, rows // 2 :, :] = second_ref[i, :, pl.ds(start, block)]


def pick_kernel(half_ref, first_ref, second_ref, cols_ref):
    block = cols_ref.shape[2]
    rows = first_ref.shape[1]
    start = pl.multiple_of(half_ref[0] * block, LANES)
    for i in range(3):
        cols_ref[i, :rows, :] = first_ref[i, :, pl.ds(start, block)]
        cols_ref[i, rows:, :] = second_ref[i, :, pl.ds(start, block)]


def covariance_kernel(steps, parts, scale, role_ref, *refs):
    rows = refs[: 2 * steps]
    choices = [
        refs[2 * steps + p * steps : 2 * steps + (p + 1) * steps] for p in range(parts)
    ]
    out_ref, cols, sem = refs[2 * steps + parts * steps :]
    depth = choices[0][0].shape[1]

    @pl.when((pl.program_id(0) == 0) & (pl.program_id(1) == 0))
    def _():
        for p in range(parts):

            @pl.when(role_ref[0] == p)
            def _(p=p):
                copies = [
                    pltpu.make_async_copy(
                        choices[p][s], cols.at[:, pl.ds(s * depth, depth), :], sem.at[s]
                    )
                    for s in range(steps)
                ]
                for copy in copies:
                    copy.start()
                for copy in copies:
                    copy.wait()

    tile = out_ref.shape[2]
    at = pl.multiple_of(pl.program_id(1) * tile, LANES)
    left = jnp.concatenate([r[0, :, pl.ds(at, tile)] for r in rows], axis=0)
    for d in range(3):
        out_ref[0, d] = scale * lax.dot_general(
            left, cols[d], (((0,), (0,)), ((), ())), preferred_element_type=jnp.float32
        )


def ring_order(count):
    return list(range(0, count, 2)) + list(range(1, count, 2))[::-1]


def project(first, second, eigvecs, me_a, atom_axis):
    flat = jnp.concatenate([first, second], axis=1)
    proj = jnp.einsum("cfa,cak->fk", flat, eigvecs, preferred_element_type=jnp.float32)
    width = proj.shape[1] // atom_axis
    total = lax.dynamic_slice_in_dim(proj, me_a * width, width, axis=1)
    for d in range(1, atom_axis):
        share = lax.dynamic_slice_in_dim(
            proj, lax.bitwise_xor(me_a, jnp.int32(d)) * width, width, axis=1
        )
        total = total + lax.ppermute(
            share, "atoms", [(a, a ^ d) for a in range(atom_axis)]
        )
    return total


def long_axis_covariance(first, second, half, role, block, spread_pairs, scale):
    flat = jnp.concatenate([first, second], axis=1)
    rows = lax.all_gather(flat, "frames", axis=1, tiled=True)
    cut = lax.dynamic_slice_in_dim(rows, half * block, block, axis=2)
    cols = jnp.where(role == 0, cut, jnp.zeros_like(cut))
    for d, pairs in enumerate(spread_pairs):
        sent = lax.ppermute(cut, ("frames", "atoms"), pairs)
        cols = jnp.where(role == d + 1, sent, cols)
    return scale * jnp.einsum(
        "cfp,dfq->cpdq", rows, cols, preferred_element_type=jnp.float32
    )


def per_device(frames, mean_structure, eigvecs):
    local_frames, _, local_atoms = frames.shape
    frame_axis = lax.axis_size("frames")
    atom_axis = lax.axis_size("atoms")
    total_frames = local_frames * frame_axis
    block = local_atoms * atom_axis // frame_axis
    blocks = frame_axis // atom_axis
    me_f = lax.axis_index("frames")
    me_a = lax.axis_index("atoms")
    half = lax.rem(me_f, blocks).astype(jnp.int32).reshape(1)
    owner = lax.div(me_f, blocks)
    role = lax.bitwise_xor(me_a, owner).astype(jnp.int32).reshape(1)
    x = jnp.transpose(frames, (1, 0, 2))

    stats = pl.pallas_call(
        stats_kernel,
        out_shape=jax.ShapeDtypeStruct((local_frames, LANES), jnp.float32),
        in_specs=[VMEM, VMEM],
        out_specs=VMEM,
        compiler_params=BIG,
        name="local_moments",
    )(x, mean_structure)
    others = [
        lax.ppermute(stats, "atoms", [(a, a ^ d) for a in range(atom_axis)])
        for d in range(1, atom_axis)
    ]
    piece = jax.ShapeDtypeStruct((3, local_frames // 2, local_atoms), jnp.bfloat16)
    col_piece = jax.ShapeDtypeStruct((3, local_frames, block), jnp.bfloat16)
    first, second, cols = pl.pallas_call(
        functools.partial(align_kernel, atom_axis, local_atoms * atom_axis),
        out_shape=(piece, piece, col_piece),
        in_specs=[SMEM] + [VMEM] * (atom_axis + 2),
        out_specs=(VMEM, VMEM, VMEM),
        compiler_params=BIG,
        name="polar_align",
    )(half, stats, *others, x, mean_structure)

    order = ring_order(frame_axis)
    forward = [(order[i], order[(i + 1) % frame_axis]) for i in range(frame_axis)]
    backward = [(b, a) for a, b in forward]
    spread_pairs = [
        [
            (f * atom_axis + f // blocks, f * atom_axis + ((f // blocks) ^ d))
            for f in range(frame_axis)
        ]
        for d in range(1, atom_axis)
    ]

    projections = project(first, second, eigvecs, me_a, atom_axis)
    if block % LANES or frame_axis > 16:
        covariance = long_axis_covariance(
            first, second, half[0], role[0], block, spread_pairs, 1.0 / total_frames
        )
        return covariance, projections

    rows = [first, second]
    choices = [[] for _ in range(atom_axis)]

    def spread(value):
        choices[0].append(value)
        for d, pairs in enumerate(spread_pairs):
            choices[d + 1].append(lax.ppermute(value, ("frames", "atoms"), pairs))

    spread(cols)
    up, down = first, second
    for step in range(1, frame_axis):
        up = lax.ppermute(up, "frames", forward)
        down = lax.ppermute(down, "frames", backward)
        rows += [up, down]
        spread(
            pl.pallas_call(
                pick_kernel,
                out_shape=col_piece,
                in_specs=[SMEM, VMEM, VMEM],
                out_specs=VMEM,
                compiler_params=BIG,
                name="pick_columns",
            )(half, up, down)
        )

    tile = 256
    steps = frame_axis
    covariance = pl.pallas_call(
        functools.partial(covariance_kernel, steps, atom_axis, 1.0 / total_frames),
        grid=(3, local_atoms // tile),
        out_shape=jax.ShapeDtypeStruct((3, 3, local_atoms, block), jnp.float32),
        in_specs=[SMEM]
        + [pl.BlockSpec((1, local_frames // 2, local_atoms), lambda c, t: (c, 0, 0))] * (2 * steps)
        + [ANY] * (atom_axis * steps),
        out_specs=pl.BlockSpec((1, 3, tile, block), lambda c, t: (c, 0, t, 0)),
        scratch_shapes=[
            pltpu.VMEM((3, total_frames, block), jnp.bfloat16),
            pltpu.SemaphoreType.DMA((steps,)),
        ],
        compiler_params=BIG,
        name="covariance_tile",
    )(role, *rows, *[c for per_role in choices for c in per_role])
    return jnp.transpose(covariance, (0, 2, 1, 3)), projections


def solution(mesh):
    placed = (P("frames", None, "atoms"), P(None, "atoms"), P(None, "atoms", None))
    return jax.shard_map(
        per_device,
        mesh=mesh,
        in_specs=placed,
        out_specs=(P(None, "atoms", None, "frames"), P("frames", "atoms")),
        check_vma=False,
    )
```

```python
import functools

import jax
import jax.numpy as jnp
from jax import lax
from jax.experimental import pallas as pl
from jax.experimental.pallas import tpu as pltpu
from jax.sharding import PartitionSpec as P

POLAR = 6
LANES = 128
STATS = 24
TILE = 256
VMEM = pl.BlockSpec(memory_space=pltpu.VMEM)
SMEM = pl.BlockSpec(memory_space=pltpu.SMEM)
ANY = pl.BlockSpec(memory_space=pl.ANY)
MIB = 1024 * 1024


def params(mib):
    return pltpu.CompilerParams(vmem_limit_bytes=mib * MIB)


def lane_mean(value):
    return jnp.sum(value, axis=1, keepdims=True) * (1.0 / value.shape[1])


def run_copies(copies):
    for copy in copies:
        copy.start()
    for copy in copies:
        copy.wait()


def stats_kernel(x_hbm, ref_hbm, out_ref, x_ref, ref_ref, sem):
    run_copies(
        [
            pltpu.make_async_copy(ref_hbm, ref_ref, sem.at[0]),
            pltpu.make_async_copy(x_hbm, x_ref, sem.at[1]),
        ]
    )
    values = []
    centred = []
    for i in range(3):
        x = x_ref[i]
        mean = lane_mean(x)
        values.append(mean)
        centred.append(x - mean)
    values.append(sum(jnp.sum(c * c, axis=1, keepdims=True) for c in centred))
    ref_mean = [lane_mean(ref_ref[j : j + 1, :]) for j in range(3)]
    ref_centred = [ref_ref[j : j + 1, :] - ref_mean[j] for j in range(3)]
    for i in range(3):
        for j in range(3):
            values.append(jnp.sum(centred[i] * ref_centred[j], axis=1, keepdims=True))
    values += ref_mean
    values.append(sum(jnp.sum(c * c, axis=1, keepdims=True) for c in ref_centred))
    shape = (x_ref.shape[1], LANES)
    lane = lax.broadcasted_iota(jnp.int32, shape, 1)
    out = jnp.zeros(shape, jnp.float32)
    for k, value in enumerate(values):
        out = jnp.where(lane == k, jnp.broadcast_to(value, shape), out)
    out_ref[...] = out.T[:STATS]


def align_kernel(parts, atoms, *refs):
    stats = refs[:parts]
    x_hbm, ref_hbm, first_ref, second_ref, x_ref, ref_ref, turn, sem = refs[parts:]
    copies = [
        pltpu.make_async_copy(ref_hbm, ref_ref, sem.at[0]),
        pltpu.make_async_copy(x_hbm, x_ref, sem.at[1]),
    ]
    for copy in copies:
        copy.start()
    local = x_ref.shape[2]
    rows = x_ref.shape[1]

    def row(at):
        return [s[at : at + 1, :] for s in stats]

    means = [row(i) for i in range(3)]
    ref_means = [row(13 + j) for j in range(3)]
    centre = [sum(m) * (1.0 / parts) for m in means]
    ref_centre = [sum(r) * (1.0 / parts) for r in ref_means]
    off = [[m - centre[i] for m in means[i]] for i in range(3)]
    ref_off = [[r - ref_centre[j] for r in ref_means[j]] for j in range(3)]
    spread = sum(row(3)) + local * sum(o * o for i in range(3) for o in off[i])
    ref_spread = sum(row(16)) + local * sum(o * o for j in range(3) for o in ref_off[j])
    scale = 1.0 / jnp.sqrt(spread * ref_spread + 1e-06)
    now = [
        [
            (sum(row(4 + 3 * i + j)) + local * sum(o * r for o, r in zip(off[i], ref_off[j])))
            * scale
            for j in range(3)
        ]
        for i in range(3)
    ]
    for _ in range(POLAR):
        gram = {}
        for i in range(3):
            for j in range(i, 3):
                gram[i, j] = sum(now[k][i] * now[k][j] for k in range(3))
                gram[j, i] = gram[i, j]
        left = [
            [(1.5 if k == j else 0.0) - 0.5 * gram[k, j] for j in range(3)] for k in range(3)
        ]
        now = [
            [sum(now[i][k] * left[k][j] for k in range(3)) for j in range(3)]
            for i in range(3)
        ]
    for k, value in enumerate(sum(now, []) + centre + ref_centre):
        turn[k : k + 1, :rows] = value
    turned = turn[...].T
    column = [turned[:rows, k : k + 1] for k in range(12)]
    for copy in copies:
        copy.wait()
    centred = [x_ref[j] - column[9 + j] for j in range(3)]
    for i in range(3):
        target = ref_ref[i : i + 1, :] - turned[0:1, 12 + i : 13 + i]
        moved = sum(column[3 * j + i] * centred[j] for j in range(3)) - target
        moved = moved.astype(jnp.bfloat16)
        first_ref[i] = moved[: rows // 2]
        second_ref[i] = moved[rows // 2 :]


def cut_kernel(pieces, half_ref, *refs):
    sources, cols_ref, sem = refs[:pieces], refs[pieces], refs[pieces + 1]
    block = cols_ref.shape[2]
    rows = sources[0].shape[1]
    start = pl.multiple_of(half_ref[0] * block, LANES)
    run_copies(
        [
            pltpu.make_async_copy(
                source.at[:, :, pl.ds(start, block)],
                cols_ref.at[:, pl.ds(k * rows, rows), :],
                sem.at[k],
            )
            for k, source in enumerate(sources)
        ]
    )


def fetch(role_ref, rows_in, groups, rows, cols, sem):
    height = rows_in[0].shape[1]
    copies = [
        pltpu.make_async_copy(piece, rows.at[:, pl.ds(k * height, height), :], sem.at[k])
        for k, piece in enumerate(rows_in)
    ]
    for copy in copies:
        copy.start()
    used = len(rows_in)
    for role in range(len(groups[0][0])):

        @pl.when(role_ref[0] == role)
        def _(role=role):
            run_copies(
                [
                    pltpu.make_async_copy(
                        arrays[role].at[:, pl.ds(at, count), :],
                        cols.at[:, pl.ds(to, count), :],
                        sem.at[used + k],
                    )
                    for k, (arrays, at, count, to) in enumerate(groups)
                ]
            )

    for copy in copies:
        copy.wait()


def unpack(refs, pieces, roles, spans):
    role_ref, rows_in = refs[0], refs[1 : 1 + pieces]
    at = 1 + pieces
    groups = []
    for span in spans:
        groups.append((refs[at : at + roles],) + span)
        at += roles
    return role_ref, rows_in, groups, refs[at:]


def product(rows, cols, c, start, d):
    left = rows[c, :, pl.ds(start, TILE)]
    return lax.dot_general(
        left, cols[d], (((0,), (0,)), ((), ())), preferred_element_type=jnp.float32
    )


def first_kernel(pieces, roles, spans, *refs):
    role_ref, rows_in, groups, (acc, rows, cols, sem) = unpack(refs, pieces, roles, spans)
    fetch(role_ref, rows_in, groups, rows, cols, sem)
    tiles = acc.shape[2] // TILE

    @pl.loop(0, 3 * tiles)
    def _(i):
        c = lax.div(i, tiles)
        start = pl.multiple_of(lax.rem(i, tiles) * TILE, TILE)
        for d in range(3):
            acc[c, d, pl.ds(start, TILE), :] = product(rows, cols, c, start, d)


def second_kernel(pieces, roles, spans, scale, *refs):
    role_ref, rows_in, groups, rest = unpack(refs, pieces, roles, spans)
    acc, out_ref, rows, cols, done, sem, out_sem = rest
    fetch(role_ref, rows_in, groups, rows, cols, sem)
    tiles = acc.shape[2] // TILE

    def write(i):
        c = lax.div(i, tiles)
        start = pl.multiple_of(lax.rem(i, tiles) * TILE, TILE)
        slot = lax.rem(i, 2)
        return pltpu.make_async_copy(
            done.at[slot], out_ref.at[c, :, pl.ds(start, TILE), :], out_sem.at[slot]
        )

    @pl.loop(0, 3 * tiles)
    def _(i):
        c = lax.div(i, tiles)
        start = pl.multiple_of(lax.rem(i, tiles) * TILE, TILE)
        slot = lax.rem(i, 2)

        @pl.when(i >= 2)
        def _():
            write(i - 2).wait()

        for d in range(3):
            done[slot, d] = scale * (
                acc[c, d, pl.ds(start, TILE), :] + product(rows, cols, c, start, d)
            )
        write(i).start()

    write(3 * tiles - 2).wait()
    write(3 * tiles - 1).wait()


def ring_order(count):
    return list(range(0, count, 2)) + list(range(1, count, 2))[::-1]


def long_axis_covariance(first, second, half, role, block, spread_pairs, scale):
    flat = jnp.concatenate([first, second], axis=1)
    rows = lax.all_gather(flat, "frames", axis=1, tiled=True)
    cut = lax.dynamic_slice_in_dim(rows, half * block, block, axis=2)
    cols = jnp.where(role == 0, cut, jnp.zeros_like(cut))
    for d, pairs in enumerate(spread_pairs):
        sent = lax.ppermute(cut, ("frames", "atoms"), pairs)
        cols = jnp.where(role == d + 1, sent, cols)
    return scale * jnp.einsum(
        "cfp,dfq->cpdq", rows, cols, preferred_element_type=jnp.float32
    )


def per_device(frames, mean_structure, eigvecs):
    local_frames, _, local_atoms = frames.shape
    frame_axis = lax.axis_size("frames")
    atom_axis = lax.axis_size("atoms")
    total_frames = local_frames * frame_axis
    block = local_atoms * atom_axis // frame_axis
    blocks = frame_axis // atom_axis
    me_f = lax.axis_index("frames")
    me_a = lax.axis_index("atoms")
    half = lax.rem(me_f, blocks).astype(jnp.int32).reshape(1)
    owner = lax.div(me_f, blocks)
    role = lax.bitwise_xor(me_a, owner).astype(jnp.int32).reshape(1)
    x = jnp.transpose(frames, (1, 0, 2))
    x_copy = [
        pltpu.VMEM(x.shape, jnp.float32),
        pltpu.VMEM(mean_structure.shape, jnp.float32),
    ]

    stats = pl.pallas_call(
        stats_kernel,
        out_shape=jax.ShapeDtypeStruct((STATS, local_frames), jnp.float32),
        in_specs=[ANY, ANY],
        out_specs=VMEM,
        scratch_shapes=x_copy + [pltpu.SemaphoreType.DMA((2,))],
        compiler_params=params(8),
        name="local_moments",
    )(x, mean_structure)
    others = [
        lax.ppermute(stats, "atoms", [(a, a ^ d) for a in range(atom_axis)])
        for d in range(1, atom_axis)
    ]
    height = local_frames // 2
    piece = jax.ShapeDtypeStruct((3, height, local_atoms), jnp.bfloat16)
    first, second = pl.pallas_call(
        functools.partial(align_kernel, atom_axis, local_atoms * atom_axis),
        out_shape=(piece, piece),
        in_specs=[VMEM] * atom_axis + [ANY, ANY],
        out_specs=(VMEM, VMEM),
        scratch_shapes=x_copy
        + [pltpu.VMEM((LANES, LANES), jnp.float32), pltpu.SemaphoreType.DMA((2,))],
        compiler_params=params(8),
        name="polar_align",
    )(stats, *others, x, mean_structure)

    proj = jnp.einsum(
        "cfa,cak->fk",
        jnp.concatenate([first, second], axis=1),
        eigvecs,
        preferred_element_type=jnp.float32,
    )
    projections = lax.psum_scatter(proj, "atoms", scatter_dimension=1, tiled=True)

    def pairs(source, target):
        return [
            (
                f * atom_axis + ((f // blocks) ^ source),
                f * atom_axis + ((f // blocks) ^ target),
            )
            for f in range(frame_axis)
        ]

    if block % LANES or frame_axis != 8 or atom_axis != 4:
        spread_pairs = [pairs(0, d) for d in range(1, atom_axis)]
        covariance = long_axis_covariance(
            first, second, half[0], role[0], block, spread_pairs, 1.0 / total_frames
        )
        return covariance, projections

    def spread(pieces):
        frames_in = len(pieces) * height
        cut = pl.pallas_call(
            functools.partial(cut_kernel, len(pieces)),
            out_shape=jax.ShapeDtypeStruct((3, frames_in, block), jnp.bfloat16),
            in_specs=[SMEM] + [ANY] * len(pieces),
            out_specs=ANY,
            scratch_shapes=[pltpu.SemaphoreType.DMA((len(pieces),))],
            compiler_params=params(8),
            name="cut_columns",
        )(half, *pieces)
        axes = ("frames", "atoms")
        across = lax.ppermute(cut, axes, pairs(0, 2))
        beside = lax.ppermute(cut, axes, pairs(0, 1))
        last = lax.ppermute(across, axes, pairs(2, 3))
        return [cut, beside, across, last]

    order = ring_order(frame_axis)
    forward = [(order[i], order[(i + 1) % frame_axis]) for i in range(frame_axis)]
    backward = [(b, a) for a, b in forward]

    def hop(arrays, way):
        return [lax.ppermute(a, "frames", way) for a in arrays]

    own = [first, second]
    up, down = own, own
    ups, downs = [], []
    for _ in range(1, frame_axis // 2):
        up, down = hop(up, forward), hop(down, backward)
        ups.append(up)
        downs.append(down)
    far = hop(up[:1], forward) + hop(down[1:], backward)
    lots = [own + ups[0] + downs[0], ups[1] + downs[1], ups[2] + downs[2], far]
    cuts = [spread(lot) for lot in lots]

    early = lots[0] + ups[1]
    late = downs[1] + lots[2] + far
    early_spans = [(0, 6 * height, 0), (0, 2 * height, 6 * height)]
    early_cuts = cuts[0] + cuts[1]
    late_spans = [
        (2 * height, 2 * height, 0),
        (0, 4 * height, 2 * height),
        (0, 2 * height, 6 * height),
    ]
    late_cuts = cuts[1] + cuts[2] + cuts[3]
    depth = 8 * height
    operand_scratch = [
        pltpu.VMEM((3, depth, local_atoms), jnp.bfloat16),
        pltpu.VMEM((3, depth, block), jnp.bfloat16),
    ]
    shape = (3, 3, local_atoms, block)
    flops = 2 * 9 * local_atoms * block * depth
    acc = pl.pallas_call(
        functools.partial(first_kernel, len(early), atom_axis, early_spans),
        out_shape=pltpu.VMEM(shape, jnp.float32),
        in_specs=[SMEM] + [ANY] * (len(early) + len(early_cuts)),
        out_specs=VMEM,
        scratch_shapes=operand_scratch + [pltpu.SemaphoreType.DMA((len(early) + 2,))],
        compiler_params=params(40),
        cost_estimate=pl.CostEstimate(flops=flops, bytes_accessed=4 * MIB, transcendentals=0),
        name="covariance_first",
    )(role, *early, *early_cuts)
    covariance = pl.pallas_call(
        functools.partial(
            second_kernel, len(late), atom_axis, late_spans, 1.0 / total_frames
        ),
        out_shape=jax.ShapeDtypeStruct(shape, jnp.float32),
        in_specs=[SMEM] + [ANY] * (len(late) + len(late_cuts)) + [VMEM],
        out_specs=ANY,
        scratch_shapes=operand_scratch
        + [
            pltpu.VMEM((2, 3, TILE, block), jnp.float32),
            pltpu.SemaphoreType.DMA((len(late) + 3,)),
            pltpu.SemaphoreType.DMA((2,)),
        ],
        compiler_params=params(40),
        cost_estimate=pl.CostEstimate(flops=flops, bytes_accessed=20 * MIB, transcendentals=0),
        name="covariance_second",
    )(role, *late, *late_cuts, acc)
    return jnp.transpose(covariance, (0, 2, 1, 3)), projections


def solution(mesh):
    placed = (P("frames", None, "atoms"), P(None, "atoms"), P(None, "atoms", None))
    return jax.shard_map(
        per_device,
        mesh=mesh,
        in_specs=placed,
        out_specs=(P(None, "atoms", None, "frames"), P("frames", "atoms")),
        check_vma=False,
    )
```

```python
import functools

import jax
import jax.numpy as jnp
from jax import lax
from jax.experimental import pallas as pl
from jax.experimental.pallas import tpu as pltpu
from jax.sharding import PartitionSpec as P

POLAR = 6
LANES = 128
STATS = 24
VMEM = pl.BlockSpec(memory_space=pltpu.VMEM)
SMEM = pl.BlockSpec(memory_space=pltpu.SMEM)
HBM = pl.BlockSpec(memory_space=pltpu.HBM)
ANY = pl.BlockSpec(memory_space=pl.ANY)
MIB = 1024 * 1024


def params(mib):
    return pltpu.CompilerParams(vmem_limit_bytes=mib * MIB)


def lane_mean(value):
    return jnp.sum(value, axis=1, keepdims=True) * (1.0 / value.shape[1])


def run_copies(copies):
    for copy in copies:
        copy.start()
    for copy in copies:
        copy.wait()


def stats_kernel(x_hbm, ref_hbm, out_ref, x_ref, ref_ref, sem):
    run_copies(
        [
            pltpu.make_async_copy(ref_hbm, ref_ref, sem.at[0]),
            pltpu.make_async_copy(x_hbm, x_ref, sem.at[1]),
        ]
    )
    values = []
    centred = []
    for i in range(3):
        x = x_ref[i]
        mean = lane_mean(x)
        values.append(mean)
        centred.append(x - mean)
    values.append(sum(jnp.sum(c * c, axis=1, keepdims=True) for c in centred))
    ref_mean = [lane_mean(ref_ref[j : j + 1, :]) for j in range(3)]
    ref_centred = [ref_ref[j : j + 1, :] - ref_mean[j] for j in range(3)]
    for i in range(3):
        for j in range(3):
            values.append(jnp.sum(centred[i] * ref_centred[j], axis=1, keepdims=True))
    values += ref_mean
    values.append(sum(jnp.sum(c * c, axis=1, keepdims=True) for c in ref_centred))
    shape = (x_ref.shape[1], LANES)
    lane = lax.broadcasted_iota(jnp.int32, shape, 1)
    out = jnp.zeros(shape, jnp.float32)
    for k, value in enumerate(values):
        out = jnp.where(lane == k, jnp.broadcast_to(value, shape), out)
    out_ref[...] = out.T[:STATS]


def align_kernel(parts, atoms, *refs):
    stats = refs[:parts]
    x_hbm, ref_hbm, first_ref, second_ref, flat_ref, x_ref, ref_ref, turn, sem = refs[parts:]
    copies = [
        pltpu.make_async_copy(ref_hbm, ref_ref, sem.at[0]),
        pltpu.make_async_copy(x_hbm, x_ref, sem.at[1]),
    ]
    for copy in copies:
        copy.start()
    local = x_ref.shape[2]
    rows = x_ref.shape[1]

    def row(at):
        return [s[at : at + 1, :] for s in stats]

    means = [row(i) for i in range(3)]
    ref_means = [row(13 + j) for j in range(3)]
    centre = [sum(m) * (1.0 / parts) for m in means]
    ref_centre = [sum(r) * (1.0 / parts) for r in ref_means]
    off = [[m - centre[i] for m in means[i]] for i in range(3)]
    ref_off = [[r - ref_centre[j] for r in ref_means[j]] for j in range(3)]
    spread = sum(row(3)) + local * sum(o * o for i in range(3) for o in off[i])
    ref_spread = sum(row(16)) + local * sum(o * o for j in range(3) for o in ref_off[j])
    scale = 1.0 / jnp.sqrt(spread * ref_spread + 1e-06)
    now = [
        [
            (sum(row(4 + 3 * i + j)) + local * sum(o * r for o, r in zip(off[i], ref_off[j])))
            * scale
            for j in range(3)
        ]
        for i in range(3)
    ]
    for _ in range(POLAR):
        gram = {}
        for i in range(3):
            for j in range(i, 3):
                gram[i, j] = sum(now[k][i] * now[k][j] for k in range(3))
                gram[j, i] = gram[i, j]
        left = [
            [(1.5 if k == j else 0.0) - 0.5 * gram[k, j] for j in range(3)] for k in range(3)
        ]
        now = [
            [sum(now[i][k] * left[k][j] for k in range(3)) for j in range(3)]
            for i in range(3)
        ]
    for k, value in enumerate(sum(now, []) + centre + ref_centre):
        turn[k : k + 1, :rows] = value
    turned = turn[...].T
    column = [turned[:rows, k : k + 1] for k in range(12)]
    for copy in copies:
        copy.wait()
    centred = [x_ref[j] - column[9 + j] for j in range(3)]
    for i in range(3):
        target = ref_ref[i : i + 1, :] - turned[0:1, 12 + i : 13 + i]
        moved = sum(column[3 * j + i] * centred[j] for j in range(3)) - target
        flat_ref[i] = moved.astype(jnp.bfloat16)
        run = first_ref.shape[1]
        for at, piece in enumerate((first_ref, second_ref)):
            pair = [moved[:, (2 * at + k) * run : (2 * at + k + 1) * run] for k in range(2)]
            piece[i] = jnp.concatenate(pair, axis=0).T.astype(jnp.bfloat16)


def cut_kernel(pieces, half_ref, *refs):
    sources, cols_ref, sem = refs[:pieces], refs[pieces], refs[pieces + 1]
    for half in range(2):

        @pl.when(half_ref[0] == half)
        def _(half=half):
            run_copies(
                [
                    pltpu.make_async_copy(source, cols_ref.at[k], sem.at[k])
                    for k, source in enumerate(sources[half::2])
                ]
            )


def side_by_side(first, second):
    middle = first.shape[1] // 2
    left = jnp.concatenate([first[:, :middle], second[:, :middle]], axis=1)
    right = jnp.concatenate([first[:, middle:], second[:, middle:]], axis=1)
    return left, right


def covariance_kernel(slots, roles, lots, scale, *refs):
    role_ref, pieces = refs[0], refs[1 : 1 + 2 * slots]
    at = 1 + 2 * slots
    groups = [refs[at + k * roles : at + (k + 1) * roles] for k in range(len(lots))]
    at += len(lots) * roles
    out_ref, rows_in, cols_in, left, right, done, sem, out_sem = refs[at:]
    copies = [
        pltpu.make_async_copy(piece, rows_in.at[k % 2, k // 2], sem.at[k])
        for k, piece in enumerate(pieces)
    ]
    for copy in copies:
        copy.start()
    for role in range(roles):

        @pl.when(role_ref[0] == role)
        def _(role=role):
            to = 0
            wanted = []
            for k, count in enumerate(lots):
                wanted.append(
                    pltpu.make_async_copy(
                        groups[k][role], cols_in.at[pl.ds(to, count)], sem.at[2 * slots + k]
                    )
                )
                to += count
            run_copies(wanted)

    run = rows_in.shape[3]
    for d in range(3):
        for q in range(slots // 2):
            low, high = side_by_side(cols_in[2 * q, d], cols_in[2 * q + 1, d])
            right[d, :run, q * LANES : (q + 1) * LANES] = low
            right[d, run:, q * LANES : (q + 1) * LANES] = high
    for copy in copies:
        copy.wait()

    def assemble(i, slot):
        c = lax.div(i, 2)
        at = lax.rem(i, 2)
        for q in range(slots // 2):
            low, high = side_by_side(rows_in[at, 2 * q, c], rows_in[at, 2 * q + 1, c])
            left[slot, :run, q * LANES : (q + 1) * LANES] = low
            left[slot, run:, q * LANES : (q + 1) * LANES] = high

    def write(i):
        start = pl.multiple_of(lax.rem(i, 2) * 2 * run, 2 * run)
        slot = lax.rem(i, 2)
        return pltpu.make_async_copy(
            done.at[slot],
            out_ref.at[lax.div(i, 2), :, pl.ds(start, 2 * run), :],
            out_sem.at[slot],
        )

    assemble(0, 0)

    @pl.loop(0, 6)
    def _(i):
        slot = lax.rem(i, 2)

        @pl.when(i >= 2)
        def _():
            write(i - 2).wait()

        assemble(jnp.minimum(i + 1, 5), 1 - slot)
        for d in range(3):
            done[slot, d] = scale * lax.dot_general(
                left[slot],
                right[d],
                (((1,), (1,)), ((), ())),
                preferred_element_type=jnp.float32,
            )
        write(i).start()

    write(4).wait()
    write(5).wait()


def project(flat, eigvecs, me_a, atom_axis):
    proj = jnp.einsum("cfa,cak->fk", flat, eigvecs, preferred_element_type=jnp.float32)
    width = proj.shape[1] // atom_axis

    def share(to):
        return lax.dynamic_slice_in_dim(proj, to * width, width, axis=1)

    total = share(me_a)
    for d in range(1, atom_axis):
        total = total + lax.ppermute(
            share(lax.bitwise_xor(me_a, jnp.int32(d))),
            "atoms",
            [(a, a ^ d) for a in range(atom_axis)],
        )
    return total


def ring_order(count):
    return list(range(0, count, 2)) + list(range(1, count, 2))[::-1]


def long_axis_covariance(flat, half, role, block, spread_pairs, scale):
    rows = lax.all_gather(flat, "frames", axis=1, tiled=True)
    cut = lax.dynamic_slice_in_dim(rows, half * block, block, axis=2)
    cols = jnp.where(role == 0, cut, jnp.zeros_like(cut))
    for d, pairs in enumerate(spread_pairs):
        sent = lax.ppermute(cut, ("frames", "atoms"), pairs)
        cols = jnp.where(role == d + 1, sent, cols)
    return scale * jnp.einsum(
        "cfp,dfq->cpdq", rows, cols, preferred_element_type=jnp.float32
    )


def per_device(frames, mean_structure, eigvecs):
    local_frames, _, local_atoms = frames.shape
    frame_axis = lax.axis_size("frames")
    atom_axis = lax.axis_size("atoms")
    total_frames = local_frames * frame_axis
    block = local_atoms * atom_axis // frame_axis
    blocks = frame_axis // atom_axis
    me_f = lax.axis_index("frames")
    me_a = lax.axis_index("atoms")
    half = lax.rem(me_f, blocks).astype(jnp.int32).reshape(1)
    owner = lax.div(me_f, blocks)
    role = lax.bitwise_xor(me_a, owner).astype(jnp.int32).reshape(1)
    x = jnp.transpose(frames, (1, 0, 2))
    x_copy = [
        pltpu.VMEM(x.shape, jnp.float32),
        pltpu.VMEM(mean_structure.shape, jnp.float32),
    ]

    stats = pl.pallas_call(
        stats_kernel,
        out_shape=jax.ShapeDtypeStruct((STATS, local_frames), jnp.float32),
        in_specs=[HBM, HBM],
        out_specs=VMEM,
        scratch_shapes=x_copy + [pltpu.SemaphoreType.DMA((2,))],
        compiler_params=params(8),
        name="local_moments",
    )(x, mean_structure)
    others = [
        lax.ppermute(stats, "atoms", [(a, a ^ d) for a in range(atom_axis)])
        for d in range(1, atom_axis)
    ]
    run = local_atoms // 4
    piece = jax.ShapeDtypeStruct((3, run, 2 * local_frames), jnp.bfloat16)
    first, second, flat = pl.pallas_call(
        functools.partial(align_kernel, atom_axis, local_atoms * atom_axis),
        out_shape=(piece, piece, jax.ShapeDtypeStruct(x.shape, jnp.bfloat16)),
        in_specs=[VMEM] * atom_axis + [HBM, HBM],
        out_specs=(VMEM, VMEM, VMEM),
        scratch_shapes=x_copy
        + [pltpu.VMEM((LANES, LANES), jnp.float32), pltpu.SemaphoreType.DMA((2,))],
        compiler_params=params(8),
        name="polar_align",
    )(stats, *others, x, mean_structure)
    projections = project(flat, eigvecs, me_a, atom_axis)

    def pairs(source, target):
        return [
            (
                f * atom_axis + ((f // blocks) ^ source),
                f * atom_axis + ((f // blocks) ^ target),
            )
            for f in range(frame_axis)
        ]

    if blocks != 2 or frame_axis != 8:
        spread_pairs = [pairs(0, d) for d in range(1, atom_axis)]
        covariance = long_axis_covariance(
            flat, half[0], role[0], block, spread_pairs, 1.0 / total_frames
        )
        return covariance, projections

    def spread(pieces):
        cut = pl.pallas_call(
            functools.partial(cut_kernel, len(pieces)),
            out_shape=jax.ShapeDtypeStruct((len(pieces) // 2,) + piece.shape, jnp.bfloat16),
            in_specs=[SMEM] + [ANY] * len(pieces),
            out_specs=ANY,
            scratch_shapes=[pltpu.SemaphoreType.DMA((len(pieces) // 2,))],
            compiler_params=params(8),
            name="cut_columns",
        )(half, *pieces)
        axes = ("frames", "atoms")
        across = lax.ppermute(cut, axes, pairs(0, 2))
        beside = lax.ppermute(cut, axes, pairs(0, 1))
        last = lax.ppermute(across, axes, pairs(2, 3))
        return [cut, beside, across, last]

    order = ring_order(frame_axis)
    forward = [(order[i], order[(i + 1) % frame_axis]) for i in range(frame_axis)]
    backward = [(b, a) for a, b in forward]

    def hop(arrays, way):
        return [lax.ppermute(a, "frames", way) for a in arrays]

    own = [first, second]
    up, down = own, own
    ups, downs = [], []
    for _ in range(1, frame_axis // 2):
        up, down = hop(up, forward), hop(down, backward)
        ups.append(up)
        downs.append(down)
    far = hop(up[:1], forward) + hop(down[1:], backward)
    lots = [own + ups[0] + downs[0] + ups[1] + downs[1], ups[2] + downs[2], far]
    cuts = sum([spread(lot) for lot in lots], [])
    pieces = sum(lots, [])
    counts = [len(lot) // 2 for lot in lots]
    covariance = pl.pallas_call(
        functools.partial(
            covariance_kernel, frame_axis, atom_axis, counts, 1.0 / total_frames
        ),
        out_shape=jax.ShapeDtypeStruct((3, 3, local_atoms, block), jnp.float32),
        in_specs=[SMEM] + [ANY] * (len(pieces) + len(cuts)),
        out_specs=ANY,
        scratch_shapes=[
            pltpu.VMEM((2, frame_axis) + piece.shape, jnp.bfloat16),
            pltpu.VMEM((frame_axis,) + piece.shape, jnp.bfloat16),
            pltpu.VMEM((2, 2 * run, total_frames), jnp.bfloat16),
            pltpu.VMEM((3, block, total_frames), jnp.bfloat16),
            pltpu.VMEM((2, 3, 2 * run, block), jnp.float32),
            pltpu.SemaphoreType.DMA((len(pieces) + len(lots),)),
            pltpu.SemaphoreType.DMA((2,)),
        ],
        compiler_params=params(24),
        cost_estimate=pl.CostEstimate(
            flops=18 * local_atoms * block * total_frames,
            bytes_accessed=24 * MIB,
            transcendentals=0,
        ),
        name="covariance_tile",
    )(role, *pieces, *cuts)
    return jnp.transpose(covariance, (0, 2, 1, 3)), projections


def solution(mesh):
    placed = (P("frames", None, "atoms"), P(None, "atoms"), P(None, "atoms", None))
    return jax.shard_map(
        per_device,
        mesh=mesh,
        in_specs=placed,
        out_specs=(P(None, "atoms", None, "frames"), P("frames", "atoms")),
        check_vma=False,
    )
```

```python
import functools

import jax
import jax.numpy as jnp
from jax import lax
from jax.experimental import pallas as pl
from jax.experimental.pallas import tpu as pltpu
from jax.sharding import PartitionSpec as P

POLAR = 6
LANES = 128
STATS = 24
VMEM = pl.BlockSpec(memory_space=pltpu.VMEM)
SMEM = pl.BlockSpec(memory_space=pltpu.SMEM)
HBM = pl.BlockSpec(memory_space=pltpu.HBM)
ANY = pl.BlockSpec(memory_space=pl.ANY)
MIB = 1024 * 1024


def params(mib):
    return pltpu.CompilerParams(vmem_limit_bytes=mib * MIB)


def lane_mean(value):
    return jnp.sum(value, axis=1, keepdims=True) * (1.0 / value.shape[1])


def run_copies(copies):
    for copy in copies:
        copy.start()
    for copy in copies:
        copy.wait()


def stats_kernel(x_hbm, ref_hbm, out_ref, x_ref, ref_ref, sem):
    run_copies(
        [
            pltpu.make_async_copy(ref_hbm, ref_ref, sem.at[0]),
            pltpu.make_async_copy(x_hbm, x_ref, sem.at[1]),
        ]
    )
    values = []
    centred = []
    for i in range(3):
        x = x_ref[i]
        mean = lane_mean(x)
        values.append(mean)
        centred.append(x - mean)
    values.append(sum(jnp.sum(c * c, axis=1, keepdims=True) for c in centred))
    ref_mean = [lane_mean(ref_ref[j : j + 1, :]) for j in range(3)]
    ref_centred = [ref_ref[j : j + 1, :] - ref_mean[j] for j in range(3)]
    for i in range(3):
        for j in range(3):
            values.append(jnp.sum(centred[i] * ref_centred[j], axis=1, keepdims=True))
    values += ref_mean
    values.append(sum(jnp.sum(c * c, axis=1, keepdims=True) for c in ref_centred))
    shape = (x_ref.shape[1], LANES)
    lane = lax.broadcasted_iota(jnp.int32, shape, 1)
    out = jnp.zeros(shape, jnp.float32)
    for k, value in enumerate(values):
        out = jnp.where(lane == k, jnp.broadcast_to(value, shape), out)
    out_ref[...] = out.T[:STATS]


def align_kernel(parts, atoms, *refs):
    stats = refs[:parts]
    x_hbm, ref_hbm, first_ref, second_ref, flat_ref, x_ref, ref_ref, turn, sem = refs[parts:]
    copies = [
        pltpu.make_async_copy(ref_hbm, ref_ref, sem.at[0]),
        pltpu.make_async_copy(x_hbm, x_ref, sem.at[1]),
    ]
    for copy in copies:
        copy.start()
    local = x_ref.shape[2]
    rows = x_ref.shape[1]

    def row(at):
        return [s[at : at + 1, :] for s in stats]

    means = [row(i) for i in range(3)]
    ref_means = [row(13 + j) for j in range(3)]
    centre = [sum(m) * (1.0 / parts) for m in means]
    ref_centre = [sum(r) * (1.0 / parts) for r in ref_means]
    off = [[m - centre[i] for m in means[i]] for i in range(3)]
    ref_off = [[r - ref_centre[j] for r in ref_means[j]] for j in range(3)]
    spread = sum(row(3)) + local * sum(o * o for i in range(3) for o in off[i])
    ref_spread = sum(row(16)) + local * sum(o * o for j in range(3) for o in ref_off[j])
    scale = 1.0 / jnp.sqrt(spread * ref_spread + 1e-06)
    now = [
        [
            (sum(row(4 + 3 * i + j)) + local * sum(o * r for o, r in zip(off[i], ref_off[j])))
            * scale
            for j in range(3)
        ]
        for i in range(3)
    ]
    for _ in range(POLAR):
        gram = {}
        for i in range(3):
            for j in range(i, 3):
                gram[i, j] = sum(now[k][i] * now[k][j] for k in range(3))
                gram[j, i] = gram[i, j]
        left = [
            [(1.5 if k == j else 0.0) - 0.5 * gram[k, j] for j in range(3)] for k in range(3)
        ]
        now = [
            [sum(now[i][k] * left[k][j] for k in range(3)) for j in range(3)]
            for i in range(3)
        ]
    for k, value in enumerate(sum(now, []) + centre + ref_centre):
        turn[k : k + 1, :rows] = value
    turned = turn[...].T
    column = [turned[:rows, k : k + 1] for k in range(12)]
    for copy in copies:
        copy.wait()
    centred = [x_ref[j] - column[9 + j] for j in range(3)]
    for i in range(3):
        target = ref_ref[i : i + 1, :] - turned[0:1, 12 + i : 13 + i]
        moved = sum(column[3 * j + i] * centred[j] for j in range(3)) - target
        flat_ref[i] = moved.astype(jnp.bfloat16)
        run = first_ref.shape[1]
        for at, piece in enumerate((first_ref, second_ref)):
            pair = [moved[:, (2 * at + k) * run : (2 * at + k + 1) * run] for k in range(2)]
            piece[i] = jnp.concatenate(pair, axis=0).T.astype(jnp.bfloat16)


def project_kernel(me_ref, flat_ref, eig_ref, *refs):
    shares, cut = refs[:-1], refs[-1]
    total = sum(
        jnp.dot(flat_ref[c], eig_ref[c], preferred_element_type=jnp.float32) for c in range(3)
    )
    width = cut.shape[2]
    for k in range(len(shares)):
        cut[k] = total[:, k * width : (k + 1) * width]
    for k, share in enumerate(shares):
        share[...] = cut[lax.bitwise_xor(me_ref[0], k)]


def cut_kernel(slots, half_ref, *refs):
    sources, (cols_ref, held, sem) = refs[: 2 * slots], refs[2 * slots :]
    for half in range(2):

        @pl.when(half_ref[0] == half)
        def _(half=half):
            run_copies(
                [
                    pltpu.make_async_copy(source, held.at[k], sem.at[k])
                    for k, source in enumerate(sources[half::2])
                ]
            )

    run, lanes = held.shape[2:]
    for k in range(slots):
        for c in range(3):
            turned = held[k, c].astype(jnp.float32).T.astype(jnp.bfloat16)
            cols_ref[k, c, :, :run] = turned[: lanes // 2]
            cols_ref[k, c, :, run:] = turned[lanes // 2 :]


def side_by_side(first, second):
    middle = first.shape[1] // 2
    left = jnp.concatenate([first[:, :middle], second[:, :middle]], axis=1)
    right = jnp.concatenate([first[:, middle:], second[:, middle:]], axis=1)
    return left, right


def covariance_kernel(slots, roles, lots, scale, *refs):
    role_ref, pieces = refs[0], refs[1 : 1 + 2 * slots]
    at = 1 + 2 * slots
    groups = [refs[at + k * roles : at + (k + 1) * roles] for k in range(len(lots))]
    at += len(lots) * roles
    out_ref, rows_in, left, right, done, sem, out_sem = refs[at:]
    copies = [
        pltpu.make_async_copy(piece, rows_in.at[k % 2, k // 2], sem.at[k])
        for k, piece in enumerate(pieces)
    ]
    depth = right.shape[1] // slots
    for role in range(roles):

        @pl.when(role_ref[0] == role)
        def _(role=role):
            to = 0
            for k, count in enumerate(lots):
                for n in range(count):
                    pltpu.make_async_copy(
                        groups[k][role].at[n],
                        right.at[:, pl.ds(to * depth, depth), :],
                        sem.at[2 * slots + to],
                    ).start()
                    to += 1

    for copy in copies:
        copy.start()
    for k in range(slots):
        part = right.at[:, pl.ds(k * depth, depth), :]
        pltpu.make_async_copy(part, part, sem.at[2 * slots + k]).wait()
    for copy in copies:
        copy.wait()
    run = rows_in.shape[3]

    def assemble(i, slot):
        c = lax.div(i, 2)
        at = lax.rem(i, 2)
        for q in range(slots // 2):
            low, high = side_by_side(rows_in[at, 2 * q, c], rows_in[at, 2 * q + 1, c])
            left[slot, :run, q * LANES : (q + 1) * LANES] = low
            left[slot, run:, q * LANES : (q + 1) * LANES] = high

    def write(i, d):
        start = pl.multiple_of(lax.rem(i, 2) * 2 * run, 2 * run)
        slot = lax.rem(i, 2)
        return pltpu.make_async_copy(
            done.at[slot, d],
            out_ref.at[lax.div(i, 2), d, pl.ds(start, 2 * run), :],
            out_sem.at[slot, d],
        )

    assemble(0, 0)

    @pl.loop(0, 6)
    def _(i):
        slot = lax.rem(i, 2)

        @pl.when(i >= 2)
        def _():
            for d in range(3):
                write(i - 2, d).wait()

        assemble(jnp.minimum(i + 1, 5), 1 - slot)
        for d in range(3):
            done[slot, d] = scale * jnp.dot(
                left[slot], right[d], preferred_element_type=jnp.float32
            )
            write(i, d).start()

    for d in range(3):
        write(4, d).wait()
        write(5, d).wait()


def after(value, *others):
    return lax.optimization_barrier((value,) + others)[0]


def ring_order(count):
    return list(range(0, count, 2)) + list(range(1, count, 2))[::-1]


def long_axis_covariance(flat, half, role, block, spread_pairs, scale):
    rows = lax.all_gather(flat, "frames", axis=1, tiled=True)
    cut = lax.dynamic_slice_in_dim(rows, half * block, block, axis=2)
    cols = jnp.where(role == 0, cut, jnp.zeros_like(cut))
    for d, pairs in enumerate(spread_pairs):
        sent = lax.ppermute(cut, ("frames", "atoms"), pairs)
        cols = jnp.where(role == d + 1, sent, cols)
    return scale * jnp.einsum(
        "cfp,dfq->cpdq", rows, cols, preferred_element_type=jnp.float32
    )


def per_device(frames, mean_structure, eigvecs):
    local_frames, _, local_atoms = frames.shape
    frame_axis = lax.axis_size("frames")
    atom_axis = lax.axis_size("atoms")
    total_frames = local_frames * frame_axis
    block = local_atoms * atom_axis // frame_axis
    blocks = frame_axis // atom_axis
    me_f = lax.axis_index("frames")
    me_a = lax.axis_index("atoms")
    half = lax.rem(me_f, blocks).astype(jnp.int32).reshape(1)
    owner = lax.div(me_f, blocks)
    role = lax.bitwise_xor(me_a, owner).astype(jnp.int32).reshape(1)
    x = jnp.transpose(frames, (1, 0, 2))
    x_copy = [
        pltpu.VMEM(x.shape, jnp.float32),
        pltpu.VMEM(mean_structure.shape, jnp.float32),
    ]

    stats = pl.pallas_call(
        stats_kernel,
        out_shape=jax.ShapeDtypeStruct((STATS, local_frames), jnp.float32),
        in_specs=[HBM, HBM],
        out_specs=VMEM,
        scratch_shapes=x_copy + [pltpu.SemaphoreType.DMA((2,))],
        compiler_params=params(8),
        name="local_moments",
    )(x, mean_structure)
    others = [
        lax.ppermute(stats, "atoms", [(a, a ^ d) for a in range(atom_axis)])
        for d in range(1, atom_axis)
    ]
    run = local_atoms // 4
    piece = jax.ShapeDtypeStruct((3, run, 2 * local_frames), jnp.bfloat16)
    first, second, flat = pl.pallas_call(
        functools.partial(align_kernel, atom_axis, local_atoms * atom_axis),
        out_shape=(piece, piece, jax.ShapeDtypeStruct(x.shape, jnp.bfloat16)),
        in_specs=[VMEM] * atom_axis + [HBM, HBM],
        out_specs=(VMEM, VMEM, VMEM),
        scratch_shapes=x_copy
        + [pltpu.VMEM((LANES, LANES), jnp.float32), pltpu.SemaphoreType.DMA((2,))],
        compiler_params=params(8),
        name="polar_align",
    )(stats, *others, x, mean_structure)
    share = jax.ShapeDtypeStruct((local_frames, eigvecs.shape[2] // atom_axis), jnp.float32)
    shares = pl.pallas_call(
        project_kernel,
        out_shape=(share,) * atom_axis,
        in_specs=[SMEM, VMEM, VMEM],
        out_specs=(VMEM,) * atom_axis,
        scratch_shapes=[pltpu.VMEM((atom_axis,) + share.shape, jnp.float32)],
        compiler_params=params(8),
        name="project",
    )(me_a.astype(jnp.int32).reshape(1), flat, eigvecs)
    parts = [shares[0]] + [
        lax.ppermute(shares[d], "atoms", [(a, a ^ d) for a in range(atom_axis)])
        for d in range(1, atom_axis)
    ]
    projections = sum(parts)

    def pairs(source, target):
        return [
            (
                f * atom_axis + ((f // blocks) ^ source),
                f * atom_axis + ((f // blocks) ^ target),
            )
            for f in range(frame_axis)
        ]

    if blocks != 2 or frame_axis != 8:
        spread_pairs = [pairs(0, d) for d in range(1, atom_axis)]
        covariance = long_axis_covariance(
            flat, half[0], role[0], block, spread_pairs, 1.0 / total_frames
        )
        return covariance, projections

    def spread(pieces):
        slots = len(pieces) // 2
        cut = pl.pallas_call(
            functools.partial(cut_kernel, slots),
            out_shape=jax.ShapeDtypeStruct((slots, 3, local_frames, block), jnp.bfloat16),
            in_specs=[SMEM] + [ANY] * len(pieces),
            out_specs=VMEM,
            scratch_shapes=[
                pltpu.VMEM((slots,) + piece.shape, jnp.bfloat16),
                pltpu.SemaphoreType.DMA((slots,)),
            ],
            compiler_params=params(8),
            name="cut_columns",
        )(half, *pieces)
        axes = ("frames", "atoms")
        across = lax.ppermute(cut, axes, pairs(0, 2))
        beside = lax.ppermute(cut, axes, pairs(0, 1))
        last = lax.ppermute(across, axes, pairs(2, 3))
        return [cut, beside, across, last]

    order = ring_order(frame_axis)
    forward = [(order[i], order[(i + 1) % frame_axis]) for i in range(frame_axis)]
    backward = [(b, a) for a, b in forward]

    def hop(up, down):
        up_a = lax.ppermute(up[0], "frames", forward)
        down_a = lax.ppermute(down[0], "frames", backward)
        up_b = lax.ppermute(up[1], "frames", forward)
        down_b = lax.ppermute(down[1], "frames", backward)
        return [up_a, up_b], [down_a, down_b]

    own = [first, second]
    up1, down1 = hop(own, own)
    up1[0] = after(up1[0], *shares)
    up2, down2 = hop(up1, down1)
    up2[1] = after(up2[1], *parts)
    up3, down3 = hop(up2, down2)
    lots = [own + up1 + down1 + up2 + down2, up3 + down3]
    cuts = [spread(lots[0])]
    down3[1] = after(down3[1], cuts[0][0])
    far = [
        lax.ppermute(up3[0], "frames", forward),
        lax.ppermute(down3[1], "frames", backward),
    ]
    cuts.append(spread(lots[1]))
    far[0] = after(far[0], cuts[1][0], cuts[0][2])
    lots.append(far)
    cuts.append(spread(far))
    cuts = sum(cuts, [])
    pieces = sum(lots, [])
    counts = [len(lot) // 2 for lot in lots]
    covariance = pl.pallas_call(
        functools.partial(
            covariance_kernel, frame_axis, atom_axis, counts, 1.0 / total_frames
        ),
        out_shape=jax.ShapeDtypeStruct((3, 3, local_atoms, block), jnp.float32),
        in_specs=[SMEM] + [ANY] * (len(pieces) + len(cuts)),
        out_specs=ANY,
        scratch_shapes=[
            pltpu.VMEM((2, frame_axis) + piece.shape, jnp.bfloat16),
            pltpu.VMEM((2, 2 * run, total_frames), jnp.bfloat16),
            pltpu.VMEM((3, total_frames, block), jnp.bfloat16),
            pltpu.VMEM((2, 3, 2 * run, block), jnp.float32),
            pltpu.SemaphoreType.DMA((len(pieces) + frame_axis,)),
            pltpu.SemaphoreType.DMA((2, 3)),
        ],
        compiler_params=params(24),
        cost_estimate=pl.CostEstimate(
            flops=18 * local_atoms * block * total_frames,
            bytes_accessed=24 * MIB,
            transcendentals=0,
        ),
        name="covariance_tile",
    )(role, *pieces, *cuts)
    return jnp.transpose(covariance, (0, 2, 1, 3)), projections


def solution(mesh):
    placed = (P("frames", None, "atoms"), P(None, "atoms"), P(None, "atoms", None))
    return jax.shard_map(
        per_device,
        mesh=mesh,
        in_specs=placed,
        out_specs=(P(None, "atoms", None, "frames"), P("frames", "atoms")),
        check_vma=False,
    )
```

```python
import functools

import jax
import jax.numpy as jnp
from jax import lax
from jax.experimental import pallas as pl
from jax.experimental.pallas import tpu as pltpu
from jax.sharding import PartitionSpec as P

POLAR = 6
LANES = 128
STATS = 24
VMEM = pl.BlockSpec(memory_space=pltpu.VMEM)
SMEM = pl.BlockSpec(memory_space=pltpu.SMEM)
HBM = pl.BlockSpec(memory_space=pltpu.HBM)
ANY = pl.BlockSpec(memory_space=pl.ANY)
MIB = 1024 * 1024


def params(mib):
    return pltpu.CompilerParams(vmem_limit_bytes=mib * MIB)


def lane_mean(value):
    return jnp.sum(value, axis=1, keepdims=True) * (1.0 / value.shape[1])


def run_copies(copies):
    for copy in copies:
        copy.start()
    for copy in copies:
        copy.wait()


def stats_kernel(x_hbm, ref_hbm, out_ref, x_ref, ref_ref, sem):
    run_copies(
        [
            pltpu.make_async_copy(ref_hbm, ref_ref, sem.at[0]),
            pltpu.make_async_copy(x_hbm, x_ref, sem.at[1]),
        ]
    )
    values = []
    centred = []
    for i in range(3):
        x = x_ref[i]
        mean = lane_mean(x)
        values.append(mean)
        centred.append(x - mean)
    values.append(sum(jnp.sum(c * c, axis=1, keepdims=True) for c in centred))
    ref_mean = [lane_mean(ref_ref[j : j + 1, :]) for j in range(3)]
    ref_centred = [ref_ref[j : j + 1, :] - ref_mean[j] for j in range(3)]
    for i in range(3):
        for j in range(3):
            values.append(jnp.sum(centred[i] * ref_centred[j], axis=1, keepdims=True))
    values += ref_mean
    values.append(sum(jnp.sum(c * c, axis=1, keepdims=True) for c in ref_centred))
    shape = (x_ref.shape[1], LANES)
    lane = lax.broadcasted_iota(jnp.int32, shape, 1)
    out = jnp.zeros(shape, jnp.float32)
    for k, value in enumerate(values):
        out = jnp.where(lane == k, jnp.broadcast_to(value, shape), out)
    out_ref[...] = out.T[:STATS]


def align_kernel(parts, atoms, *refs):
    stats = refs[:parts]
    x_hbm, ref_hbm, first_ref, second_ref, flat_ref, x_ref, ref_ref, turn, sem = refs[parts:]
    copies = [
        pltpu.make_async_copy(ref_hbm, ref_ref, sem.at[0]),
        pltpu.make_async_copy(x_hbm, x_ref, sem.at[1]),
    ]
    for copy in copies:
        copy.start()
    local = x_ref.shape[2]
    rows = x_ref.shape[1]

    def row(at):
        return [s[at : at + 1, :] for s in stats]

    means = [row(i) for i in range(3)]
    ref_means = [row(13 + j) for j in range(3)]
    centre = [sum(m) * (1.0 / parts) for m in means]
    ref_centre = [sum(r) * (1.0 / parts) for r in ref_means]
    off = [[m - centre[i] for m in means[i]] for i in range(3)]
    ref_off = [[r - ref_centre[j] for r in ref_means[j]] for j in range(3)]
    spread = sum(row(3)) + local * sum(o * o for i in range(3) for o in off[i])
    ref_spread = sum(row(16)) + local * sum(o * o for j in range(3) for o in ref_off[j])
    scale = 1.0 / jnp.sqrt(spread * ref_spread + 1e-06)
    now = [
        [
            (sum(row(4 + 3 * i + j)) + local * sum(o * r for o, r in zip(off[i], ref_off[j])))
            * scale
            for j in range(3)
        ]
        for i in range(3)
    ]
    for _ in range(POLAR):
        gram = {}
        for i in range(3):
            for j in range(i, 3):
                gram[i, j] = sum(now[k][i] * now[k][j] for k in range(3))
                gram[j, i] = gram[i, j]
        left = [
            [(1.5 if k == j else 0.0) - 0.5 * gram[k, j] for j in range(3)] for k in range(3)
        ]
        now = [
            [sum(now[i][k] * left[k][j] for k in range(3)) for j in range(3)]
            for i in range(3)
        ]
    for k, value in enumerate(sum(now, []) + centre + ref_centre):
        turn[k : k + 1, :rows] = value
    turned = turn[...].T
    column = [turned[:rows, k : k + 1] for k in range(12)]
    for copy in copies:
        copy.wait()
    centred = [x_ref[j] - column[9 + j] for j in range(3)]
    for i in range(3):
        target = ref_ref[i : i + 1, :] - turned[0:1, 12 + i : 13 + i]
        moved = sum(column[3 * j + i] * centred[j] for j in range(3)) - target
        flat_ref[i] = moved.astype(jnp.bfloat16)
        run = first_ref.shape[1]
        for at, piece in enumerate((first_ref, second_ref)):
            pair = [moved[:, (2 * at + k) * run : (2 * at + k + 1) * run] for k in range(2)]
            piece[i] = jnp.concatenate(pair, axis=0).T.astype(jnp.bfloat16)


def project_kernel(me_ref, flat_ref, eig_ref, *refs):
    shares, cut = refs[:-1], refs[-1]
    total = sum(
        jnp.dot(flat_ref[c], eig_ref[c], preferred_element_type=jnp.float32) for c in range(3)
    )
    width = cut.shape[2]
    for k in range(len(shares)):
        cut[k] = total[:, k * width : (k + 1) * width]
    for k, share in enumerate(shares):
        share[...] = cut[lax.bitwise_xor(me_ref[0], k)]


def cut_kernel(slots, half_ref, *refs):
    sources, cols_ref = refs[: 2 * slots], refs[2 * slots]
    run, lanes = sources[0].shape[1:]
    for half in range(2):

        @pl.when(half_ref[0] == half)
        def _(half=half):
            for k, source in enumerate(sources[half::2]):
                for c in range(3):
                    turned = source[c].astype(jnp.float32).T.astype(jnp.bfloat16)
                    cols_ref[k, c, :, :run] = turned[: lanes // 2]
                    cols_ref[k, c, :, run:] = turned[lanes // 2 :]


def side_by_side(first, second):
    middle = first.shape[1] // 2
    left = jnp.concatenate([first[:, :middle], second[:, :middle]], axis=1)
    right = jnp.concatenate([first[:, middle:], second[:, middle:]], axis=1)
    return left, right


def covariance_kernel(slots, roles, lots, scale, *refs):
    role_ref, pieces = refs[0], refs[1 : 1 + 2 * slots]
    at = 1 + 2 * slots
    groups = [refs[at + k * roles : at + (k + 1) * roles] for k in range(len(lots))]
    at += len(lots) * roles
    out_ref, left, right, done, out_sem = refs[at:]
    depth = right.shape[1] // slots
    run = pieces[0].shape[1]
    for role in range(roles):

        @pl.when(role_ref[0] == role)
        def _(role=role):
            to = 0
            for k, count in enumerate(lots):
                for n in range(count):
                    for d in range(3):
                        right[d, to : to + depth, :] = groups[k][role][n, d]
                    to += depth

    def assemble(c, at):
        for q in range(slots // 2):
            low, high = side_by_side(pieces[4 * q + at][c], pieces[4 * q + 2 + at][c])
            left[at, :run, q * LANES : (q + 1) * LANES] = low
            left[at, run:, q * LANES : (q + 1) * LANES] = high

    def write(c, at, d):
        return pltpu.make_async_copy(
            done.at[at, d],
            out_ref.at[c, d, pl.ds(at * 2 * run, 2 * run), :],
            out_sem.at[at, d],
        )

    assemble(0, 0)

    @pl.loop(0, 3)
    def _(c):
        for at in range(2):

            @pl.when(c > 0)
            def _():
                for d in range(3):
                    write(c - 1, at, d).wait()

            assemble(jnp.minimum(c + at, 2), 1 - at)
            for d in range(3):
                done[at, d] = scale * jnp.dot(
                    left[at], right[d], preferred_element_type=jnp.float32
                )
                write(c, at, d).start()

    for at in range(2):
        for d in range(3):
            write(2, at, d).wait()


pinned = pltpu.with_memory_space_constraint


def after(value, *others):
    return lax.optimization_barrier((value,) + others)[0] if others else value


def ring_order(count):
    return list(range(0, count, 2)) + list(range(1, count, 2))[::-1]


def long_axis_covariance(flat, half, role, block, spread_pairs, scale):
    rows = lax.all_gather(flat, "frames", axis=1, tiled=True)
    cut = lax.dynamic_slice_in_dim(rows, half * block, block, axis=2)
    cols = jnp.where(role == 0, cut, jnp.zeros_like(cut))
    for d, pairs in enumerate(spread_pairs):
        sent = lax.ppermute(cut, ("frames", "atoms"), pairs)
        cols = jnp.where(role == d + 1, sent, cols)
    return scale * jnp.einsum(
        "cfp,dfq->cpdq", rows, cols, preferred_element_type=jnp.float32
    )


def per_device(frames, mean_structure, eigvecs):
    local_frames, _, local_atoms = frames.shape
    frame_axis = lax.axis_size("frames")
    atom_axis = lax.axis_size("atoms")
    total_frames = local_frames * frame_axis
    block = local_atoms * atom_axis // frame_axis
    blocks = frame_axis // atom_axis
    me_f = lax.axis_index("frames")
    me_a = lax.axis_index("atoms")
    half = lax.rem(me_f, blocks).astype(jnp.int32).reshape(1)
    owner = lax.div(me_f, blocks)
    role = lax.bitwise_xor(me_a, owner).astype(jnp.int32).reshape(1)
    x = pinned(jnp.transpose(frames, (1, 0, 2)), pltpu.HBM)
    mean_structure = pinned(mean_structure, pltpu.HBM)
    x_copy = [
        pltpu.VMEM(x.shape, jnp.float32),
        pltpu.VMEM(mean_structure.shape, jnp.float32),
    ]

    stats = pl.pallas_call(
        stats_kernel,
        out_shape=jax.ShapeDtypeStruct((STATS, local_frames), jnp.float32),
        in_specs=[HBM, HBM],
        out_specs=VMEM,
        scratch_shapes=x_copy + [pltpu.SemaphoreType.DMA((2,))],
        compiler_params=params(8),
        name="local_moments",
    )(x, mean_structure)
    others = [
        lax.ppermute(stats, "atoms", [(a, a ^ d) for a in range(atom_axis)])
        for d in range(1, atom_axis)
    ]
    run = local_atoms // 4
    piece = jax.ShapeDtypeStruct((3, run, 2 * local_frames), jnp.bfloat16)
    first, second, flat = pl.pallas_call(
        functools.partial(align_kernel, atom_axis, local_atoms * atom_axis),
        out_shape=(piece, piece, jax.ShapeDtypeStruct(x.shape, jnp.bfloat16)),
        in_specs=[VMEM] * atom_axis + [HBM, HBM],
        out_specs=(VMEM, VMEM, VMEM),
        scratch_shapes=x_copy
        + [pltpu.VMEM((LANES, LANES), jnp.float32), pltpu.SemaphoreType.DMA((2,))],
        compiler_params=params(8),
        name="polar_align",
    )(stats, *others, x, mean_structure)
    share = jax.ShapeDtypeStruct((local_frames, eigvecs.shape[2] // atom_axis), jnp.float32)
    shares = pl.pallas_call(
        project_kernel,
        out_shape=(share,) * atom_axis,
        in_specs=[SMEM, VMEM, VMEM],
        out_specs=(VMEM,) * atom_axis,
        scratch_shapes=[pltpu.VMEM((atom_axis,) + share.shape, jnp.float32)],
        compiler_params=params(8),
        name="project",
    )(me_a.astype(jnp.int32).reshape(1), flat, eigvecs)
    def exchange(values):
        return values[0] + sum(
            lax.ppermute(values[d], "atoms", [(a, a ^ d) for a in range(atom_axis)])
            for d in range(1, atom_axis)
        )

    def pairs(source, target):
        return [
            (
                f * atom_axis + ((f // blocks) ^ source),
                f * atom_axis + ((f // blocks) ^ target),
            )
            for f in range(frame_axis)
        ]

    if blocks != 2 or frame_axis != 8:
        spread_pairs = [pairs(0, d) for d in range(1, atom_axis)]
        projections = exchange(shares)
        covariance = long_axis_covariance(
            flat, half[0], role[0], block, spread_pairs, 1.0 / total_frames
        )
        return covariance, projections

    def spread(pieces, earlier, before_last=()):
        slots = len(pieces) // 2
        cut = pl.pallas_call(
            functools.partial(cut_kernel, slots),
            out_shape=pltpu.VMEM((slots, 3, local_frames, block), jnp.bfloat16),
            in_specs=[SMEM] + [VMEM] * len(pieces),
            out_specs=VMEM,
            compiler_params=params(4),
            name="cut_columns",
        )(after(half, *earlier), *[pinned(piece, pltpu.VMEM) for piece in pieces])
        axes = ("frames", "atoms")
        across = lax.ppermute(cut, axes, pairs(0, 2))
        beside = lax.ppermute(cut, axes, pairs(0, 1))
        last = lax.ppermute(after(across, *before_last), axes, pairs(2, 3))
        return [cut, beside, across, last]

    order = ring_order(frame_axis)
    forward = [(order[i], order[(i + 1) % frame_axis]) for i in range(frame_axis)]
    backward = [(b, a) for a, b in forward]

    def hop(up, down):
        up_a = lax.ppermute(up[0], "frames", forward)
        down_a = lax.ppermute(down[0], "frames", backward)
        up_b = lax.ppermute(up[1], "frames", forward)
        down_b = lax.ppermute(down[1], "frames", backward)
        return [up_a, up_b], [down_a, down_b]

    own = [first, second]
    up1, down1 = hop(own, own)
    up2, down2 = hop(up1, down1)
    up3, down3 = hop(up2, down2)
    far = [
        lax.ppermute(up3[0], "frames", forward),
        lax.ppermute(down3[1], "frames", backward),
    ]
    lots = [own + up1 + down1, up2 + down2, up3 + down3, far]
    cuts = [spread(lots[0], shares), spread(lots[1], []), spread(lots[2], [])]
    cuts.append(spread(far, [], cuts[0][1:]))
    cuts = sum(cuts, [])
    projections = exchange([after(value, cuts[-4]) for value in shares])
    pieces = sum(lots, [])
    counts = [len(lot) // 2 for lot in lots]
    covariance = pl.pallas_call(
        functools.partial(
            covariance_kernel, frame_axis, atom_axis, counts, 1.0 / total_frames
        ),
        out_shape=jax.ShapeDtypeStruct((3, 3, local_atoms, block), jnp.float32),
        in_specs=[SMEM] + [VMEM] * (len(pieces) + len(cuts)),
        out_specs=ANY,
        scratch_shapes=[
            pltpu.VMEM((2, 2 * run, total_frames), jnp.bfloat16),
            pltpu.VMEM((3, total_frames, block), jnp.bfloat16),
            pltpu.VMEM((2, 3, 2 * run, block), jnp.float32),
            pltpu.SemaphoreType.DMA((2, 3)),
        ],
        compiler_params=params(24),
        cost_estimate=pl.CostEstimate(
            flops=18 * local_atoms * block * total_frames,
            bytes_accessed=24 * MIB,
            transcendentals=0,
        ),
        name="covariance_tile",
    )(role, *[pinned(value, pltpu.VMEM) for value in pieces + cuts])
    return jnp.transpose(covariance, (0, 2, 1, 3)), projections


def solution(mesh):
    placed = (P("frames", None, "atoms"), P(None, "atoms"), P(None, "atoms", None))
    return jax.shard_map(
        per_device,
        mesh=mesh,
        in_specs=placed,
        out_specs=(P(None, "atoms", None, "frames"), P("frames", "atoms")),
        check_vma=False,
    )
```

```python
import functools

import jax
import jax.numpy as jnp
from jax import lax
from jax.experimental import pallas as pl
from jax.experimental.pallas import tpu as pltpu
from jax.sharding import PartitionSpec as P

POLAR = 6
LANES = 128
STATS = 24
VMEM = pl.BlockSpec(memory_space=pltpu.VMEM)
SMEM = pl.BlockSpec(memory_space=pltpu.SMEM)
HBM = pl.BlockSpec(memory_space=pltpu.HBM)
ANY = pl.BlockSpec(memory_space=pl.ANY)
MIB = 1024 * 1024


def params(mib):
    return pltpu.CompilerParams(vmem_limit_bytes=mib * MIB)


def lane_mean(value):
    return jnp.sum(value, axis=1, keepdims=True) * (1.0 / value.shape[1])


def run_copies(copies):
    for copy in copies:
        copy.start()
    for copy in copies:
        copy.wait()


def stats_kernel(x_hbm, ref_hbm, out_ref, x_ref, ref_ref, sem):
    run_copies(
        [
            pltpu.make_async_copy(ref_hbm, ref_ref, sem.at[0]),
            pltpu.make_async_copy(x_hbm, x_ref, sem.at[1]),
        ]
    )
    values = []
    centred = []
    for i in range(3):
        x = x_ref[i]
        mean = lane_mean(x)
        values.append(mean)
        centred.append(x - mean)
    values.append(sum(jnp.sum(c * c, axis=1, keepdims=True) for c in centred))
    ref_mean = [lane_mean(ref_ref[j : j + 1, :]) for j in range(3)]
    ref_centred = [ref_ref[j : j + 1, :] - ref_mean[j] for j in range(3)]
    for i in range(3):
        for j in range(3):
            values.append(jnp.sum(centred[i] * ref_centred[j], axis=1, keepdims=True))
    values += ref_mean
    values.append(sum(jnp.sum(c * c, axis=1, keepdims=True) for c in ref_centred))
    shape = (x_ref.shape[1], LANES)
    lane = lax.broadcasted_iota(jnp.int32, shape, 1)
    out = jnp.zeros(shape, jnp.float32)
    for k, value in enumerate(values):
        out = jnp.where(lane == k, jnp.broadcast_to(value, shape), out)
    turned = out.T[:STATS]
    for k in range(out_ref.shape[0]):
        out_ref[k] = jnp.concatenate([turned, jnp.zeros_like(turned)], axis=1)


def align_kernel(parts, *refs):
    stats, x_ref, ref_ref, first_ref, second_ref, flat_ref, turn = refs
    local = x_ref.shape[2]
    rows = x_ref.shape[1]

    def row(at):
        return [stats[p, at : at + 1, :] for p in range(parts)]

    means = [row(i) for i in range(3)]
    ref_means = [row(13 + j) for j in range(3)]
    centre = [sum(m) * (1.0 / parts) for m in means]
    ref_centre = [sum(r) * (1.0 / parts) for r in ref_means]
    off = [[m - centre[i] for m in means[i]] for i in range(3)]
    ref_off = [[r - ref_centre[j] for r in ref_means[j]] for j in range(3)]
    spread = sum(row(3)) + local * sum(o * o for i in range(3) for o in off[i])
    ref_spread = sum(row(16)) + local * sum(o * o for j in range(3) for o in ref_off[j])
    scale = 1.0 / jnp.sqrt(spread * ref_spread + 1e-06)
    now = [
        [
            (sum(row(4 + 3 * i + j)) + local * sum(o * r for o, r in zip(off[i], ref_off[j])))
            * scale
            for j in range(3)
        ]
        for i in range(3)
    ]
    for _ in range(POLAR):
        gram = {}
        for i in range(3):
            for j in range(i, 3):
                gram[i, j] = sum(now[k][i] * now[k][j] for k in range(3))
                gram[j, i] = gram[i, j]
        left = [
            [(1.5 if k == j else 0.0) - 0.5 * gram[k, j] for j in range(3)] for k in range(3)
        ]
        now = [
            [sum(now[i][k] * left[k][j] for k in range(3)) for j in range(3)]
            for i in range(3)
        ]
    for k, value in enumerate(sum(now, []) + centre + ref_centre):
        turn[k : k + 1, :] = value
    turned = turn[...].T
    column = [turned[:rows, k : k + 1] for k in range(12)]
    centred = [x_ref[j] - column[9 + j] for j in range(3)]
    for i in range(3):
        target = ref_ref[i : i + 1, :] - turned[0:1, 12 + i : 13 + i]
        moved = sum(column[3 * j + i] * centred[j] for j in range(3)) - target
        flat_ref[i] = moved.astype(jnp.bfloat16)
        run = first_ref.shape[1]
        for at, piece in enumerate((first_ref, second_ref)):
            pair = [moved[:, (2 * at + k) * run : (2 * at + k + 1) * run] for k in range(2)]
            piece[i] = jnp.concatenate(pair, axis=0).T.astype(jnp.bfloat16)


def project_kernel(flat_ref, eig_ref, out_ref):
    total = sum(
        jnp.dot(flat_ref[c], eig_ref[c], preferred_element_type=jnp.float32) for c in range(3)
    )
    middle, width = out_ref.shape[1], out_ref.shape[2] // 2
    for k in range(out_ref.shape[0]):
        part = total[:, k * width : (k + 1) * width]
        out_ref[k] = jnp.concatenate([part[:middle], part[middle:]], axis=1)


def sum_kernel(parts_ref, out_ref):
    middle, width = parts_ref.shape[1], parts_ref.shape[2] // 2
    total = sum(parts_ref[k] for k in range(parts_ref.shape[0]))
    out_ref[:middle] = total[:, :width]
    out_ref[middle:] = total[:, width:]


def cut_kernel(slots, half_ref, *refs):
    sources, cols_ref = refs[: 2 * slots], refs[2 * slots]
    run, lanes = sources[0].shape[1:]
    for half in range(2):

        @pl.when(half_ref[0] == half)
        def _(half=half):
            for k, source in enumerate(sources[half::2]):
                for c in range(3):
                    turned = source[c].astype(jnp.float32).T.astype(jnp.bfloat16)
                    cols_ref[k, c, :, :run] = turned[: lanes // 2]
                    cols_ref[k, c, :, run:] = turned[lanes // 2 :]


def side_by_side(first, second):
    middle = first.shape[1] // 2
    left = jnp.concatenate([first[:, :middle], second[:, :middle]], axis=1)
    right = jnp.concatenate([first[:, middle:], second[:, middle:]], axis=1)
    return left, right


def covariance_kernel(slots, roles, lots, scale, *refs):
    role_ref, pieces = refs[0], refs[1 : 1 + 2 * slots]
    at = 1 + 2 * slots
    groups = [refs[at + k * roles : at + (k + 1) * roles] for k in range(len(lots))]
    at += len(lots) * roles
    out_ref, left, right, done, out_sem = refs[at:]
    depth = right.shape[1] // slots
    run = pieces[0].shape[1]
    for role in range(roles):

        @pl.when(role_ref[0] == role)
        def _(role=role):
            to = 0
            for k, count in enumerate(lots):
                for n in range(count):
                    for d in range(3):
                        right[d, to : to + depth, :] = groups[k][role][n, d]
                    to += depth

    def assemble(c, at):
        for q in range(slots // 2):
            low, high = side_by_side(pieces[4 * q + at][c], pieces[4 * q + 2 + at][c])
            left[at, :run, q * LANES : (q + 1) * LANES] = low
            left[at, run:, q * LANES : (q + 1) * LANES] = high

    def write(c, at, d):
        return pltpu.make_async_copy(
            done.at[at, d],
            out_ref.at[c, d, pl.ds(at * 2 * run, 2 * run), :],
            out_sem.at[at, d],
        )

    assemble(0, 0)

    @pl.loop(0, 3)
    def _(c):
        for at in range(2):

            @pl.when(c > 0)
            def _():
                for d in range(3):
                    write(c - 1, at, d).wait()

            assemble(jnp.minimum(c + at, 2), 1 - at)
            for d in range(3):
                done[at, d] = scale * jnp.dot(
                    left[at], right[d], preferred_element_type=jnp.float32
                )
                write(c, at, d).start()

    for at in range(2):
        for d in range(3):
            write(2, at, d).wait()


pinned = pltpu.with_memory_space_constraint


def after(value, *others):
    return lax.optimization_barrier((value,) + others)[0] if others else value


def ring_order(count):
    return list(range(0, count, 2)) + list(range(1, count, 2))[::-1]


def long_axis_covariance(flat, half, role, block, spread_pairs, scale):
    rows = lax.all_gather(flat, "frames", axis=1, tiled=True)
    cut = lax.dynamic_slice_in_dim(rows, half * block, block, axis=2)
    cols = jnp.where(role == 0, cut, jnp.zeros_like(cut))
    for d, pairs in enumerate(spread_pairs):
        sent = lax.ppermute(cut, ("frames", "atoms"), pairs)
        cols = jnp.where(role == d + 1, sent, cols)
    return scale * jnp.einsum(
        "cfp,dfq->cpdq", rows, cols, preferred_element_type=jnp.float32
    )


def per_device(frames, mean_structure, eigvecs):
    local_frames, _, local_atoms = frames.shape
    frame_axis = lax.axis_size("frames")
    atom_axis = lax.axis_size("atoms")
    total_frames = local_frames * frame_axis
    block = local_atoms * atom_axis // frame_axis
    blocks = frame_axis // atom_axis
    me_f = lax.axis_index("frames")
    me_a = lax.axis_index("atoms")
    half = lax.rem(me_f, blocks).astype(jnp.int32).reshape(1)
    owner = lax.div(me_f, blocks)
    role = lax.bitwise_xor(me_a, owner).astype(jnp.int32).reshape(1)
    x = pinned(jnp.transpose(frames, (1, 0, 2)), pltpu.HBM)
    mean_structure = pinned(mean_structure, pltpu.HBM)
    stats, x, mean_structure = pl.pallas_call(
        stats_kernel,
        out_shape=(
            pltpu.VMEM((atom_axis, STATS, LANES), jnp.float32),
            pltpu.VMEM(x.shape, jnp.float32),
            pltpu.VMEM(mean_structure.shape, jnp.float32),
        ),
        in_specs=[HBM, HBM],
        out_specs=(VMEM, VMEM, VMEM),
        scratch_shapes=[pltpu.SemaphoreType.DMA((2,))],
        compiler_params=params(8),
        name="local_moments",
    )(x, mean_structure)
    stats = lax.all_to_all(stats, "atoms", split_axis=0, concat_axis=0, tiled=True)
    run = local_atoms // 4
    piece = jax.ShapeDtypeStruct((3, run, 2 * local_frames), jnp.bfloat16)
    first, second, flat = pl.pallas_call(
        functools.partial(align_kernel, atom_axis),
        out_shape=(piece, piece, jax.ShapeDtypeStruct(x.shape, jnp.bfloat16)),
        in_specs=[VMEM, VMEM, VMEM],
        out_specs=(VMEM, VMEM, VMEM),
        scratch_shapes=[pltpu.VMEM((LANES, LANES), jnp.float32)],
        compiler_params=params(8),
        name="polar_align",
    )(stats, x, mean_structure)
    share = (local_frames, eigvecs.shape[2] // atom_axis)
    shares = pl.pallas_call(
        project_kernel,
        out_shape=jax.ShapeDtypeStruct(
            (atom_axis, local_frames // 2, 2 * share[1]), jnp.float32
        ),
        in_specs=[VMEM, VMEM],
        out_specs=VMEM,
        compiler_params=params(8),
        name="project",
    )(flat, eigvecs)
    projections = pl.pallas_call(
        sum_kernel,
        out_shape=jax.ShapeDtypeStruct(share, jnp.float32),
        in_specs=[VMEM],
        out_specs=VMEM,
        compiler_params=params(4),
        name="sum_shares",
    )(lax.all_to_all(shares, "atoms", split_axis=0, concat_axis=0, tiled=True))

    def pairs(source, target):
        return [
            (
                f * atom_axis + ((f // blocks) ^ source),
                f * atom_axis + ((f // blocks) ^ target),
            )
            for f in range(frame_axis)
        ]

    if blocks != 2 or frame_axis != 8:
        spread_pairs = [pairs(0, d) for d in range(1, atom_axis)]
        covariance = long_axis_covariance(
            flat, half[0], role[0], block, spread_pairs, 1.0 / total_frames
        )
        return covariance, projections

    def spread(pieces, earlier, before_last=()):
        slots = len(pieces) // 2
        cut = pl.pallas_call(
            functools.partial(cut_kernel, slots),
            out_shape=pltpu.VMEM((slots, 3, local_frames, block), jnp.bfloat16),
            in_specs=[SMEM] + [VMEM] * len(pieces),
            out_specs=VMEM,
            compiler_params=params(4),
            name="cut_columns",
        )(after(half, *earlier), *[pinned(piece, pltpu.VMEM) for piece in pieces])
        axes = ("frames", "atoms")
        across = lax.ppermute(cut, axes, pairs(0, 2))
        beside = lax.ppermute(cut, axes, pairs(0, 1))
        last = lax.ppermute(after(across, *before_last), axes, pairs(2, 3))
        return [cut, beside, across, last]

    order = ring_order(frame_axis)
    forward = [(order[i], order[(i + 1) % frame_axis]) for i in range(frame_axis)]
    backward = [(b, a) for a, b in forward]

    def hop(up, down):
        up_a = lax.ppermute(up[0], "frames", forward)
        down_a = lax.ppermute(down[0], "frames", backward)
        up_b = lax.ppermute(up[1], "frames", forward)
        down_b = lax.ppermute(down[1], "frames", backward)
        return [up_a, up_b], [down_a, down_b]

    own = [first, second]
    up1, down1 = hop(own, own)
    up2, down2 = hop(up1, down1)
    up3, down3 = hop(up2, down2)
    far = [
        lax.ppermute(up3[0], "frames", forward),
        lax.ppermute(down3[1], "frames", backward),
    ]
    lots = [own + up1 + down1, up2 + down2, up3 + down3, far]
    cuts = [spread(lots[0], [shares]), spread(lots[1], []), spread(lots[2], [])]
    cuts.append(spread(far, [], cuts[0][1:]))
    cuts = sum(cuts, [])
    pieces = sum(lots, [])
    counts = [len(lot) // 2 for lot in lots]
    covariance = pl.pallas_call(
        functools.partial(
            covariance_kernel, frame_axis, atom_axis, counts, 1.0 / total_frames
        ),
        out_shape=jax.ShapeDtypeStruct((3, 3, local_atoms, block), jnp.float32),
        in_specs=[SMEM] + [VMEM] * (len(pieces) + len(cuts)),
        out_specs=ANY,
        scratch_shapes=[
            pltpu.VMEM((2, 2 * run, total_frames), jnp.bfloat16),
            pltpu.VMEM((3, total_frames, block), jnp.bfloat16),
            pltpu.VMEM((2, 3, 2 * run, block), jnp.float32),
            pltpu.SemaphoreType.DMA((2, 3)),
        ],
        compiler_params=params(24),
        cost_estimate=pl.CostEstimate(
            flops=18 * local_atoms * block * total_frames,
            bytes_accessed=24 * MIB,
            transcendentals=0,
        ),
        name="covariance_tile",
    )(role, *[pinned(value, pltpu.VMEM) for value in pieces + cuts])
    return jnp.transpose(covariance, (0, 2, 1, 3)), projections


def solution(mesh):
    placed = (P("frames", None, "atoms"), P(None, "atoms"), P(None, "atoms", None))
    return jax.shard_map(
        per_device,
        mesh=mesh,
        in_specs=placed,
        out_specs=(P(None, "atoms", None, "frames"), P("frames", "atoms")),
        check_vma=False,
    )
```

```python
import functools

import jax
import jax.numpy as jnp
from jax import lax
from jax.experimental import pallas as pl
from jax.experimental.pallas import tpu as pltpu
from jax.sharding import PartitionSpec as P

POLAR = 6
LANES = 128
STATS = 24
VMEM = pl.BlockSpec(memory_space=pltpu.VMEM)
SMEM = pl.BlockSpec(memory_space=pltpu.SMEM)
HBM = pl.BlockSpec(memory_space=pltpu.HBM)
ANY = pl.BlockSpec(memory_space=pl.ANY)
MIB = 1024 * 1024


def params(mib):
    return pltpu.CompilerParams(vmem_limit_bytes=mib * MIB)


def lane_mean(value):
    return jnp.sum(value, axis=1, keepdims=True) * (1.0 / value.shape[1])


def run_copies(copies):
    for copy in copies:
        copy.start()
    for copy in copies:
        copy.wait()


def stats_kernel(x_hbm, ref_hbm, out_ref, x_ref, ref_ref, sem):
    run_copies(
        [
            pltpu.make_async_copy(ref_hbm, ref_ref, sem.at[0]),
            pltpu.make_async_copy(x_hbm, x_ref, sem.at[1]),
        ]
    )
    values = []
    centred = []
    for i in range(3):
        x = x_ref[i]
        mean = lane_mean(x)
        values.append(mean)
        centred.append(x - mean)
    values.append(sum(jnp.sum(c * c, axis=1, keepdims=True) for c in centred))
    ref_mean = [lane_mean(ref_ref[j : j + 1, :]) for j in range(3)]
    ref_centred = [ref_ref[j : j + 1, :] - ref_mean[j] for j in range(3)]
    for i in range(3):
        for j in range(3):
            values.append(jnp.sum(centred[i] * ref_centred[j], axis=1, keepdims=True))
    values += ref_mean
    values.append(sum(jnp.sum(c * c, axis=1, keepdims=True) for c in ref_centred))
    shape = (x_ref.shape[1], LANES)
    lane = lax.broadcasted_iota(jnp.int32, shape, 1)
    out = jnp.zeros(shape, jnp.float32)
    for k, value in enumerate(values):
        out = jnp.where(lane == k, jnp.broadcast_to(value, shape), out)
    out_ref[...] = out.T[:STATS]


def align_kernel(parts, *refs):
    stats = refs[:parts]
    x_ref, ref_ref, piece_ref, flat_ref, turn = refs[parts:]
    local = x_ref.shape[2]
    rows = x_ref.shape[1]

    def row(at):
        return [s[at : at + 1, :] for s in stats]

    means = [row(i) for i in range(3)]
    ref_means = [row(13 + j) for j in range(3)]
    centre = [sum(m) * (1.0 / parts) for m in means]
    ref_centre = [sum(r) * (1.0 / parts) for r in ref_means]
    off = [[m - centre[i] for m in means[i]] for i in range(3)]
    ref_off = [[r - ref_centre[j] for r in ref_means[j]] for j in range(3)]
    spread = sum(row(3)) + local * sum(o * o for i in range(3) for o in off[i])
    ref_spread = sum(row(16)) + local * sum(o * o for j in range(3) for o in ref_off[j])
    scale = 1.0 / jnp.sqrt(spread * ref_spread + 1e-06)
    now = [
        [
            (sum(row(4 + 3 * i + j)) + local * sum(o * r for o, r in zip(off[i], ref_off[j])))
            * scale
            for j in range(3)
        ]
        for i in range(3)
    ]
    for _ in range(POLAR):
        gram = {}
        for i in range(3):
            for j in range(i, 3):
                gram[i, j] = sum(now[k][i] * now[k][j] for k in range(3))
                gram[j, i] = gram[i, j]
        left = [
            [(1.5 if k == j else 0.0) - 0.5 * gram[k, j] for j in range(3)] for k in range(3)
        ]
        now = [
            [sum(now[i][k] * left[k][j] for k in range(3)) for j in range(3)]
            for i in range(3)
        ]
    for k, value in enumerate(sum(now, []) + centre + ref_centre):
        turn[k : k + 1, :rows] = value
    turned = turn[...].T
    column = [turned[:rows, k : k + 1] for k in range(12)]
    centred = [x_ref[j] - column[9 + j] for j in range(3)]
    for i in range(3):
        target = ref_ref[i : i + 1, :] - turned[0:1, 12 + i : 13 + i]
        moved = sum(column[3 * j + i] * centred[j] for j in range(3)) - target
        flat_ref[i] = moved.astype(jnp.bfloat16)
        run = piece_ref.shape[2]
        for at in range(2):
            pair = [moved[:, (2 * at + k) * run : (2 * at + k + 1) * run] for k in range(2)]
            piece_ref[at, i] = jnp.concatenate(pair, axis=0).T.astype(jnp.bfloat16)


def project_kernel(me_ref, flat_ref, eig_ref, *refs):
    shares, cut = refs[:-1], refs[-1]
    total = sum(
        jnp.dot(flat_ref[c], eig_ref[c], preferred_element_type=jnp.float32) for c in range(3)
    )
    width = cut.shape[2]
    for k in range(len(shares)):
        cut[k] = total[:, k * width : (k + 1) * width]
    for k, share in enumerate(shares):
        share[...] = cut[lax.bitwise_xor(me_ref[0], k)]


def sum_kernel(*refs):
    refs[-1][...] = sum(ref[...] for ref in refs[:-1])


def cut_columns(half_ref, halves, cols_ref):
    for half in range(2):

        @pl.when(half_ref[0] == half)
        def _(half=half):
            for k, pair in enumerate(halves):
                run, lanes = pair[half].shape[1:]
                for c in range(3):
                    turned = pair[half][c].astype(jnp.float32).T.astype(jnp.bfloat16)
                    cols_ref[k, c, :, :run] = turned[: lanes // 2]
                    cols_ref[k, c, :, run:] = turned[lanes // 2 :]


def cut_kernel(half_ref, *refs):
    cut_columns(half_ref, [(r.at[0], r.at[1]) for r in refs[:-1]], refs[-1])


def cut_last_kernel(half_ref, up_ref, down_ref, cols_ref, up_half, down_half):
    up_half[...] = up_ref[0]
    down_half[...] = down_ref[1]
    cut_columns(half_ref, [(r.at[0], r.at[1]) for r in (up_ref, down_ref)], cols_ref)


def cut_far_kernel(half_ref, up_half, down_half, cols_ref):
    cut_columns(half_ref, [(up_half, down_half)], cols_ref)


def pass_on_kernel(role_ref, cut_ref, across_ref, out_ref):
    @pl.when(role_ref[0] == 0)
    def _():
        out_ref[...] = cut_ref[...]

    @pl.when(role_ref[0] != 0)
    def _():
        out_ref[...] = across_ref[...]


def side_by_side(first, second):
    middle = first.shape[1] // 2
    left = jnp.concatenate([first[:, :middle], second[:, :middle]], axis=1)
    right = jnp.concatenate([first[:, middle:], second[:, middle:]], axis=1)
    return left, right


def covariance_kernel(slots, roles, groups, scale, role_ref, *refs):
    shards, up_half, down_half = refs[: slots - 1], refs[slots - 1], refs[slots]
    refs = refs[slots + 1 :]
    arrays = []
    for _, _, holder in groups:
        count = max(holder) + 1
        arrays.append(refs[:count])
        refs = refs[count:]
    out_ref, left, right, done, col_sem, out_sem = refs
    depth = right.shape[1] // slots
    run = up_half.shape[1]

    def fetches(k, role, to):
        source = arrays[k][groups[k][2][role]]
        return [
            pltpu.make_async_copy(
                source.at[n],
                right.at[:, pl.ds(to + n * depth, depth), :],
                col_sem.at[to // depth + n],
            )
            for n in range(groups[k][0])
        ]

    def for_each_group(from_hbm, act):
        for role in range(roles):

            @pl.when(role_ref[0] == role)
            def _(role=role):
                to = 0
                for k, (count, in_hbm, _) in enumerate(groups):
                    if in_hbm == from_hbm:
                        act(k, role, to)
                    to += count * depth

    def start(k, role, to):
        for copy in fetches(k, role, to):
            copy.start()

    def wait(k, role, to):
        for copy in fetches(k, role, to):
            copy.wait()

    def load(k, role, to):
        source = arrays[k][groups[k][2][role]]
        for n in range(groups[k][0]):
            for d in range(3):
                right[d, to + n * depth : to + (n + 1) * depth, :] = source[n, d]

    def piece(slot, at, c):
        if slot < slots - 1:
            return shards[slot][at, c]
        return (up_half, down_half)[at][c]

    def assemble(c, at):
        for q in range(slots // 2):
            low, high = side_by_side(piece(2 * q, at, c), piece(2 * q + 1, at, c))
            left[at, :run, q * LANES : (q + 1) * LANES] = low
            left[at, run:, q * LANES : (q + 1) * LANES] = high

    for_each_group(True, start)
    for_each_group(False, load)
    assemble(0, 0)
    for_each_group(True, wait)

    def write(c, at, d):
        return pltpu.make_async_copy(
            done.at[at, d],
            out_ref.at[c, d, pl.ds(at * 2 * run, 2 * run), :],
            out_sem.at[at, d],
        )

    @pl.loop(0, 3)
    def _(c):
        for at in range(2):

            @pl.when(c > 0)
            def _():
                for d in range(3):
                    write(c - 1, at, d).wait()

            assemble(jnp.minimum(c + at, 2), 1 - at)
            for d in range(3):
                done[at, d] = scale * jnp.dot(
                    left[at], right[d], preferred_element_type=jnp.float32
                )
                write(c, at, d).start()

    for at in range(2):
        for d in range(3):
            write(2, at, d).wait()


pinned = pltpu.with_memory_space_constraint


def after(value, *others):
    return lax.optimization_barrier((value,) + others)[0] if others else value


def ring_order(count):
    return list(range(0, count, 2)) + list(range(1, count, 2))[::-1]


def long_axis_covariance(flat, half, role, block, spread_pairs, scale):
    rows = lax.all_gather(flat, "frames", axis=1, tiled=True)
    cut = lax.dynamic_slice_in_dim(rows, half * block, block, axis=2)
    cols = jnp.where(role == 0, cut, jnp.zeros_like(cut))
    for d, pairs in enumerate(spread_pairs):
        sent = lax.ppermute(cut, ("frames", "atoms"), pairs)
        cols = jnp.where(role == d + 1, sent, cols)
    return scale * jnp.einsum(
        "cfp,dfq->cpdq", rows, cols, preferred_element_type=jnp.float32
    )


def per_device(frames, mean_structure, eigvecs):
    local_frames, _, local_atoms = frames.shape
    frame_axis = lax.axis_size("frames")
    atom_axis = lax.axis_size("atoms")
    total_frames = local_frames * frame_axis
    block = local_atoms * atom_axis // frame_axis
    blocks = frame_axis // atom_axis
    me_f = lax.axis_index("frames")
    me_a = lax.axis_index("atoms")
    half = lax.rem(me_f, blocks).astype(jnp.int32).reshape(1)
    owner = lax.div(me_f, blocks)
    role = lax.bitwise_xor(me_a, owner).astype(jnp.int32).reshape(1)
    x = pinned(jnp.transpose(frames, (1, 0, 2)), pltpu.HBM)
    mean_structure = pinned(mean_structure, pltpu.HBM)
    stats, x, mean_structure = pl.pallas_call(
        stats_kernel,
        out_shape=(
            pltpu.VMEM((STATS, local_frames), jnp.float32),
            pltpu.VMEM(x.shape, jnp.float32),
            pltpu.VMEM(mean_structure.shape, jnp.float32),
        ),
        in_specs=[HBM, HBM],
        out_specs=(VMEM, VMEM, VMEM),
        scratch_shapes=[pltpu.SemaphoreType.DMA((2,))],
        compiler_params=params(8),
        name="local_moments",
    )(x, mean_structure)
    def swap(value, distance):
        return lax.ppermute(value, "atoms", [(a, a ^ distance) for a in range(atom_axis)])

    others = [swap(stats, d) for d in range(1, atom_axis)]
    run = local_atoms // 4
    piece = (3, run, 2 * local_frames)
    own, flat = pl.pallas_call(
        functools.partial(align_kernel, atom_axis),
        out_shape=(
            jax.ShapeDtypeStruct((2,) + piece, jnp.bfloat16),
            jax.ShapeDtypeStruct(x.shape, jnp.bfloat16),
        ),
        in_specs=[VMEM] * (atom_axis + 2),
        out_specs=(VMEM, VMEM),
        scratch_shapes=[pltpu.VMEM((LANES, LANES), jnp.float32)],
        compiler_params=params(8),
        name="polar_align",
    )(stats, *others, x, mean_structure)
    share = jax.ShapeDtypeStruct((local_frames, eigvecs.shape[2] // atom_axis), jnp.float32)
    shares = pl.pallas_call(
        project_kernel,
        out_shape=(share,) * atom_axis,
        in_specs=[SMEM, VMEM, VMEM],
        out_specs=(VMEM,) * atom_axis,
        scratch_shapes=[pltpu.VMEM((atom_axis,) + share.shape, jnp.float32)],
        compiler_params=params(8),
        name="project",
    )(me_a.astype(jnp.int32).reshape(1), flat, eigvecs)
    parts = [shares[0]] + [swap(shares[d], d) for d in range(1, atom_axis)]
    projections = pl.pallas_call(
        sum_kernel,
        out_shape=share,
        in_specs=[VMEM] * atom_axis,
        out_specs=VMEM,
        compiler_params=params(4),
        name="sum_shares",
    )(*parts)

    def pairs(source, target):
        return [
            (
                f * atom_axis + ((f // blocks) ^ source),
                f * atom_axis + ((f // blocks) ^ target),
            )
            for f in range(frame_axis)
        ]

    if blocks != 2 or frame_axis != 8:
        spread_pairs = [pairs(0, d) for d in range(1, atom_axis)]
        covariance = long_axis_covariance(
            flat, half[0], role[0], block, spread_pairs, 1.0 / total_frames
        )
        return covariance, projections

    axes = ("frames", "atoms")

    def columns(slots):
        return pltpu.VMEM((slots, 3, local_frames, block), jnp.bfloat16)

    def kernel(body, out_shape, scalar, values, name):
        single = not isinstance(out_shape, tuple)
        return pl.pallas_call(
            body,
            out_shape=out_shape,
            in_specs=[SMEM] + [VMEM] * len(values),
            out_specs=VMEM if single else (VMEM,) * len(out_shape),
            compiler_params=params(4),
            name=name,
        )(scalar, *[pinned(value, pltpu.VMEM) for value in values])

    def spread_paired(cut):
        across = lax.ppermute(cut, axes, pairs(0, 2))
        held = kernel(pass_on_kernel, columns(cut.shape[0]), role, [cut, across], "pass_on")
        return [held, lax.ppermute(held, axes, pairs(0, 1) + pairs(2, 3))]

    order = ring_order(frame_axis)
    forward = [(order[i], order[(i + 1) % frame_axis]) for i in range(frame_axis)]
    backward = [(b, a) for a, b in forward]

    def hop(up, down):
        return lax.ppermute(up, "frames", forward), lax.ppermute(down, "frames", backward)

    one = hop(own, own)
    cut_one = kernel(cut_kernel, columns(3), after(half, *shares), [own, *one], "cut_columns")
    in_hbm = spread_paired(cut_one)
    two = hop(*one)
    cut_two = kernel(cut_kernel, columns(2), after(half, *parts), list(two), "cut_columns")
    three = hop(*two)
    half_shard = pltpu.VMEM(piece, jnp.bfloat16)
    cut_three, *halves = kernel(
        cut_last_kernel,
        (columns(2), half_shard, half_shard),
        after(half, projections, in_hbm[0]),
        list(three),
        "cut_columns",
    )
    far = hop(*halves)
    cut_four = kernel(cut_far_kernel, columns(1), half, list(far), "cut_columns")

    direct = [cut_three] + [lax.ppermute(cut_three, axes, pairs(0, d)) for d in (1, 2, 3)]
    across = lax.ppermute(cut_four, axes, pairs(0, 2))
    beside = lax.ppermute(cut_four, axes, pairs(0, 1))
    last = lax.ppermute(across, axes, pairs(2, 3))

    groups = (
        (3, True, (0, 1, 0, 1)),
        (2, True, (0, 1, 0, 1)),
        (2, False, (0, 1, 2, 3)),
        (1, False, (0, 1, 2, 3)),
    )
    in_hbm += spread_paired(cut_two)
    in_vmem = direct + [cut_four, beside, across, last]
    rows = [own, *one, *two, *three, *far]
    covariance = pl.pallas_call(
        functools.partial(
            covariance_kernel, frame_axis, atom_axis, groups, 1.0 / total_frames
        ),
        out_shape=jax.ShapeDtypeStruct((3, 3, local_atoms, block), jnp.float32),
        in_specs=[SMEM]
        + [VMEM] * len(rows)
        + [HBM] * len(in_hbm)
        + [VMEM] * len(in_vmem),
        out_specs=ANY,
        scratch_shapes=[
            pltpu.VMEM((2, 2 * run, total_frames), jnp.bfloat16),
            pltpu.VMEM((3, total_frames, block), jnp.bfloat16),
            pltpu.VMEM((2, 3, 2 * run, block), jnp.float32),
            pltpu.SemaphoreType.DMA((frame_axis,)),
            pltpu.SemaphoreType.DMA((2, 3)),
        ],
        compiler_params=params(16),
        cost_estimate=pl.CostEstimate(
            flops=18 * local_atoms * block * total_frames,
            bytes_accessed=24 * MIB,
            transcendentals=0,
        ),
        name="covariance_tile",
    )(
        role,
        *[pinned(value, pltpu.VMEM) for value in rows],
        *[pinned(value, pltpu.HBM) for value in in_hbm],
        *[pinned(value, pltpu.VMEM) for value in in_vmem],
    )
    return jnp.transpose(covariance, (0, 2, 1, 3)), projections


def solution(mesh):
    placed = (P("frames", None, "atoms"), P(None, "atoms"), P(None, "atoms", None))
    return jax.shard_map(
        per_device,
        mesh=mesh,
        in_specs=placed,
        out_specs=(P(None, "atoms", None, "frames"), P("frames", "atoms")),
        check_vma=False,
    )
```

```python
import functools

import jax
import jax.numpy as jnp
from jax import lax
from jax.experimental import pallas as pl
from jax.experimental.pallas import tpu as pltpu
from jax.sharding import PartitionSpec as P

POLAR = 6
LANES = 128
STATS = 24
VMEM = pl.BlockSpec(memory_space=pltpu.VMEM)
SMEM = pl.BlockSpec(memory_space=pltpu.SMEM)
HBM = pl.BlockSpec(memory_space=pltpu.HBM)
ANY = pl.BlockSpec(memory_space=pl.ANY)
MIB = 1024 * 1024


def params(mib):
    return pltpu.CompilerParams(vmem_limit_bytes=mib * MIB)


def lane_mean(value):
    return jnp.sum(value, axis=1, keepdims=True) * (1.0 / value.shape[1])


def run_copies(copies):
    for copy in copies:
        copy.start()
    for copy in copies:
        copy.wait()


def stats_kernel(x_hbm, ref_hbm, out_ref, x_ref, ref_ref, sem):
    run_copies(
        [
            pltpu.make_async_copy(ref_hbm, ref_ref, sem.at[0]),
            pltpu.make_async_copy(x_hbm, x_ref, sem.at[1]),
        ]
    )
    values = []
    centred = []
    for i in range(3):
        x = x_ref[i]
        mean = lane_mean(x)
        values.append(mean)
        centred.append(x - mean)
    values.append(sum(jnp.sum(c * c, axis=1, keepdims=True) for c in centred))
    ref_mean = [lane_mean(ref_ref[j : j + 1, :]) for j in range(3)]
    ref_centred = [ref_ref[j : j + 1, :] - ref_mean[j] for j in range(3)]
    for i in range(3):
        for j in range(3):
            values.append(jnp.sum(centred[i] * ref_centred[j], axis=1, keepdims=True))
    values += ref_mean
    values.append(sum(jnp.sum(c * c, axis=1, keepdims=True) for c in ref_centred))
    shape = (x_ref.shape[1], LANES)
    lane = lax.broadcasted_iota(jnp.int32, shape, 1)
    out = jnp.zeros(shape, jnp.float32)
    for k, value in enumerate(values):
        out = jnp.where(lane == k, jnp.broadcast_to(value, shape), out)
    out_ref[...] = out.T[:STATS]


def align_kernel(parts, *refs):
    stats = refs[:parts]
    x_ref, ref_ref, piece_ref, flat_ref, turn = refs[parts:]
    local = x_ref.shape[2]
    rows = x_ref.shape[1]

    def row(at):
        return [s[at : at + 1, :] for s in stats]

    means = [row(i) for i in range(3)]
    ref_means = [row(13 + j) for j in range(3)]
    centre = [sum(m) * (1.0 / parts) for m in means]
    ref_centre = [sum(r) * (1.0 / parts) for r in ref_means]
    off = [[m - centre[i] for m in means[i]] for i in range(3)]
    ref_off = [[r - ref_centre[j] for r in ref_means[j]] for j in range(3)]
    spread = sum(row(3)) + local * sum(o * o for i in range(3) for o in off[i])
    ref_spread = sum(row(16)) + local * sum(o * o for j in range(3) for o in ref_off[j])
    scale = 1.0 / jnp.sqrt(spread * ref_spread + 1e-06)
    now = [
        [
            (sum(row(4 + 3 * i + j)) + local * sum(o * r for o, r in zip(off[i], ref_off[j])))
            * scale
            for j in range(3)
        ]
        for i in range(3)
    ]
    for _ in range(POLAR):
        gram = {}
        for i in range(3):
            for j in range(i, 3):
                gram[i, j] = sum(now[k][i] * now[k][j] for k in range(3))
                gram[j, i] = gram[i, j]
        left = [
            [(1.5 if k == j else 0.0) - 0.5 * gram[k, j] for j in range(3)] for k in range(3)
        ]
        now = [
            [sum(now[i][k] * left[k][j] for k in range(3)) for j in range(3)]
            for i in range(3)
        ]
    for k, value in enumerate(sum(now, []) + centre + ref_centre):
        turn[k : k + 1, :rows] = value
    turned = turn[...].T
    column = [turned[:rows, k : k + 1] for k in range(12)]
    centred = [x_ref[j] - column[9 + j] for j in range(3)]
    for i in range(3):
        target = ref_ref[i : i + 1, :] - turned[0:1, 12 + i : 13 + i]
        moved = sum(column[3 * j + i] * centred[j] for j in range(3)) - target
        flat_ref[i] = moved.astype(jnp.bfloat16)
        run = piece_ref.shape[2]
        for at in range(2):
            pair = [moved[:, (2 * at + k) * run : (2 * at + k + 1) * run] for k in range(2)]
            piece_ref[at, i] = jnp.concatenate(pair, axis=0).T.astype(jnp.bfloat16)


def project_kernel(me_ref, flat_ref, eig_ref, *refs):
    shares, cut = refs[:-1], refs[-1]
    total = sum(
        jnp.dot(flat_ref[c], eig_ref[c], preferred_element_type=jnp.float32) for c in range(3)
    )
    width = cut.shape[2]
    for k in range(len(shares)):
        cut[k] = total[:, k * width : (k + 1) * width]
    for k, share in enumerate(shares):
        share[...] = cut[lax.bitwise_xor(me_ref[0], k)]


def sum_kernel(*refs):
    refs[-1][...] = sum(ref[...] for ref in refs[:-1])


def cut_columns(half_ref, halves, cols_ref):
    for half in range(2):

        @pl.when(half_ref[0] == half)
        def _(half=half):
            for k, pair in enumerate(halves):
                run, lanes = pair[half].shape[1:]
                for c in range(3):
                    turned = pair[half][c].astype(jnp.float32).T.astype(jnp.bfloat16)
                    cols_ref[k, c, :, :run] = turned[: lanes // 2]
                    cols_ref[k, c, :, run:] = turned[lanes // 2 :]


def cut_kernel(half_ref, *refs):
    cut_columns(half_ref, [(r.at[0], r.at[1]) for r in refs[:-1]], refs[-1])


def cut_last_kernel(half_ref, up_ref, down_ref, cols_ref, up_half, down_half):
    up_half[...] = up_ref[0]
    down_half[...] = down_ref[1]
    cut_columns(half_ref, [(r.at[0], r.at[1]) for r in (up_ref, down_ref)], cols_ref)


def cut_far_kernel(half_ref, up_half, down_half, cols_ref):
    cut_columns(half_ref, [(up_half, down_half)], cols_ref)


def pass_on_kernel(role_ref, *refs):
    sources, out_ref = refs[:-1], refs[-1]
    for role in range(2):

        @pl.when((role_ref[0] != 0) == bool(role))
        def _(role=role):
            to = 0
            for source in sources[role::2]:
                out_ref[to : to + source.shape[0]] = source[...]
                to += source.shape[0]


def side_by_side(first, second):
    middle = first.shape[1] // 2
    left = jnp.concatenate([first[:, :middle], second[:, :middle]], axis=1)
    right = jnp.concatenate([first[:, middle:], second[:, middle:]], axis=1)
    return left, right


def covariance_kernel(slots, roles, groups, scale, role_ref, *refs):
    shards, up_half, down_half = refs[: slots - 1], refs[slots - 1], refs[slots]
    refs = refs[slots + 1 :]
    arrays = []
    for _, _, holder in groups:
        count = max(holder) + 1
        arrays.append(refs[:count])
        refs = refs[count:]
    out_ref, left, right, done, col_sem, out_sem = refs
    depth = right.shape[1] // slots
    run = up_half.shape[1]

    def fetches(k, role, to):
        source = arrays[k][groups[k][2][role]]
        return [
            pltpu.make_async_copy(
                source.at[n],
                right.at[:, pl.ds(to + n * depth, depth), :],
                col_sem.at[to // depth + n],
            )
            for n in range(groups[k][0])
        ]

    def for_each_group(from_hbm, act):
        for role in range(roles):

            @pl.when(role_ref[0] == role)
            def _(role=role):
                to = 0
                for k, (count, in_hbm, _) in enumerate(groups):
                    if in_hbm == from_hbm:
                        act(k, role, to)
                    to += count * depth

    def start(k, role, to):
        for copy in fetches(k, role, to):
            copy.start()

    def wait(k, role, to):
        for copy in fetches(k, role, to):
            copy.wait()

    def load(k, role, to):
        source = arrays[k][groups[k][2][role]]
        for n in range(groups[k][0]):
            for d in range(3):
                right[d, to + n * depth : to + (n + 1) * depth, :] = source[n, d]

    def piece(slot, at, c):
        if slot < slots - 1:
            return shards[slot][at, c]
        return (up_half, down_half)[at][c]

    def assemble(c, at):
        for q in range(slots // 2):
            low, high = side_by_side(piece(2 * q, at, c), piece(2 * q + 1, at, c))
            left[at, :run, q * LANES : (q + 1) * LANES] = low
            left[at, run:, q * LANES : (q + 1) * LANES] = high

    for_each_group(True, start)
    for_each_group(False, load)
    assemble(0, 0)
    for_each_group(True, wait)

    def write(c, at, d):
        return pltpu.make_async_copy(
            done.at[at, d],
            out_ref.at[c, d, pl.ds(at * 2 * run, 2 * run), :],
            out_sem.at[at, d],
        )

    @pl.loop(0, 3)
    def _(c):
        for at in range(2):

            @pl.when(c > 0)
            def _():
                for d in range(3):
                    write(c - 1, at, d).wait()

            assemble(jnp.minimum(c + at, 2), 1 - at)
            for d in range(3):
                done[at, d] = scale * jnp.dot(
                    left[at], right[d], preferred_element_type=jnp.float32
                )
                write(c, at, d).start()

    for at in range(2):
        for d in range(3):
            write(2, at, d).wait()


pinned = pltpu.with_memory_space_constraint


def after(value, *others):
    return lax.optimization_barrier((value,) + others)[0] if others else value


def ring_order(count):
    return list(range(0, count, 2)) + list(range(1, count, 2))[::-1]


def long_axis_covariance(flat, half, role, block, spread_pairs, scale):
    rows = lax.all_gather(flat, "frames", axis=1, tiled=True)
    cut = lax.dynamic_slice_in_dim(rows, half * block, block, axis=2)
    cols = jnp.where(role == 0, cut, jnp.zeros_like(cut))
    for d, pairs in enumerate(spread_pairs):
        sent = lax.ppermute(cut, ("frames", "atoms"), pairs)
        cols = jnp.where(role == d + 1, sent, cols)
    return scale * jnp.einsum(
        "cfp,dfq->cpdq", rows, cols, preferred_element_type=jnp.float32
    )


def per_device(frames, mean_structure, eigvecs):
    local_frames, _, local_atoms = frames.shape
    frame_axis = lax.axis_size("frames")
    atom_axis = lax.axis_size("atoms")
    total_frames = local_frames * frame_axis
    block = local_atoms * atom_axis // frame_axis
    blocks = frame_axis // atom_axis
    me_f = lax.axis_index("frames")
    me_a = lax.axis_index("atoms")
    half = lax.rem(me_f, blocks).astype(jnp.int32).reshape(1)
    owner = lax.div(me_f, blocks)
    role = lax.bitwise_xor(me_a, owner).astype(jnp.int32).reshape(1)
    x = pinned(jnp.transpose(frames, (1, 0, 2)), pltpu.HBM)
    mean_structure = pinned(mean_structure, pltpu.HBM)
    stats, x, mean_structure = pl.pallas_call(
        stats_kernel,
        out_shape=(
            pltpu.VMEM((STATS, local_frames), jnp.float32),
            pltpu.VMEM(x.shape, jnp.float32),
            pltpu.VMEM(mean_structure.shape, jnp.float32),
        ),
        in_specs=[HBM, HBM],
        out_specs=(VMEM, VMEM, VMEM),
        scratch_shapes=[pltpu.SemaphoreType.DMA((2,))],
        compiler_params=params(8),
        name="local_moments",
    )(x, mean_structure)
    def swap(value, distance):
        return lax.ppermute(value, "atoms", [(a, a ^ distance) for a in range(atom_axis)])

    others = [swap(stats, d) for d in range(1, atom_axis)]
    run = local_atoms // 4
    piece = (3, run, 2 * local_frames)
    own, flat = pl.pallas_call(
        functools.partial(align_kernel, atom_axis),
        out_shape=(
            jax.ShapeDtypeStruct((2,) + piece, jnp.bfloat16),
            jax.ShapeDtypeStruct(x.shape, jnp.bfloat16),
        ),
        in_specs=[VMEM] * (atom_axis + 2),
        out_specs=(VMEM, VMEM),
        scratch_shapes=[pltpu.VMEM((LANES, LANES), jnp.float32)],
        compiler_params=params(8),
        name="polar_align",
    )(stats, *others, x, mean_structure)
    share = jax.ShapeDtypeStruct((local_frames, eigvecs.shape[2] // atom_axis), jnp.float32)
    shares = pl.pallas_call(
        project_kernel,
        out_shape=(share,) * atom_axis,
        in_specs=[SMEM, VMEM, VMEM],
        out_specs=(VMEM,) * atom_axis,
        scratch_shapes=[pltpu.VMEM((atom_axis,) + share.shape, jnp.float32)],
        compiler_params=params(8),
        name="project",
    )(me_a.astype(jnp.int32).reshape(1), flat, eigvecs)
    parts = [shares[0]] + [swap(shares[d], d) for d in range(1, atom_axis)]
    projections = pl.pallas_call(
        sum_kernel,
        out_shape=share,
        in_specs=[VMEM] * atom_axis,
        out_specs=VMEM,
        compiler_params=params(4),
        name="sum_shares",
    )(*parts)

    def pairs(source, target):
        return [
            (
                f * atom_axis + ((f // blocks) ^ source),
                f * atom_axis + ((f // blocks) ^ target),
            )
            for f in range(frame_axis)
        ]

    if blocks != 2 or frame_axis != 8:
        spread_pairs = [pairs(0, d) for d in range(1, atom_axis)]
        covariance = long_axis_covariance(
            flat, half[0], role[0], block, spread_pairs, 1.0 / total_frames
        )
        return covariance, projections

    axes = ("frames", "atoms")

    def columns(slots):
        return pltpu.VMEM((slots, 3, local_frames, block), jnp.bfloat16)

    def kernel(body, out_shape, scalar, values, name):
        single = not isinstance(out_shape, tuple)
        return pl.pallas_call(
            body,
            out_shape=out_shape,
            in_specs=[SMEM] + [VMEM] * len(values),
            out_specs=VMEM if single else (VMEM,) * len(out_shape),
            compiler_params=params(4),
            name=name,
        )(scalar, *[pinned(value, pltpu.VMEM) for value in values])

    def cross(cut):
        return [cut, lax.ppermute(cut, axes, pairs(0, 2))]

    def pass_on(values, role):
        slots = sum(value.shape[0] for value in values[::2])
        held = kernel(pass_on_kernel, columns(slots), role, values, "pass_on")
        return [held, lax.ppermute(held, axes, pairs(0, 1) + pairs(2, 3))]

    order = ring_order(frame_axis)
    forward = [(order[i], order[(i + 1) % frame_axis]) for i in range(frame_axis)]
    backward = [(b, a) for a, b in forward]

    def hop(up, down):
        return lax.ppermute(up, "frames", forward), lax.ppermute(down, "frames", backward)

    one = hop(own, own)
    crossed = cross(kernel(cut_kernel, columns(1), half, [own], "cut_columns"))
    cut_one = kernel(cut_kernel, columns(2), half, list(one), "cut_columns")
    two = hop(after(one[0], crossed[1], *parts), one[1])
    in_hbm = pass_on(crossed + cross(cut_one), role)
    cut_two = kernel(cut_kernel, columns(2), half, list(two), "cut_columns")
    three = hop(*two)
    crossed = cross(cut_two)
    half_shard = pltpu.VMEM(piece, jnp.bfloat16)
    cut_three, *halves = kernel(
        cut_last_kernel,
        (columns(2), half_shard, half_shard),
        after(half, projections, in_hbm[0]),
        list(three),
        "cut_columns",
    )
    far = hop(*halves)
    cut_four = kernel(
        cut_far_kernel, columns(1), after(half, crossed[1]), list(far), "cut_columns"
    )
    in_vmem = pass_on(
        crossed + cross(cut_three) + cross(cut_four), after(role, in_hbm[1])
    )
    groups = ((3, True, (0, 1, 0, 1)), (5, False, (0, 1, 0, 1)))
    rows = [own, *one, *two, *three, *far]
    covariance = pl.pallas_call(
        functools.partial(
            covariance_kernel, frame_axis, atom_axis, groups, 1.0 / total_frames
        ),
        out_shape=jax.ShapeDtypeStruct((3, 3, local_atoms, block), jnp.float32),
        in_specs=[SMEM]
        + [VMEM] * len(rows)
        + [HBM] * len(in_hbm)
        + [VMEM] * len(in_vmem),
        out_specs=ANY,
        scratch_shapes=[
            pltpu.VMEM((2, 2 * run, total_frames), jnp.bfloat16),
            pltpu.VMEM((3, total_frames, block), jnp.bfloat16),
            pltpu.VMEM((2, 3, 2 * run, block), jnp.float32),
            pltpu.SemaphoreType.DMA((frame_axis,)),
            pltpu.SemaphoreType.DMA((2, 3)),
        ],
        compiler_params=params(16),
        cost_estimate=pl.CostEstimate(
            flops=18 * local_atoms * block * total_frames,
            bytes_accessed=24 * MIB,
            transcendentals=0,
        ),
        name="covariance_tile",
    )(
        role,
        *[pinned(value, pltpu.VMEM) for value in rows],
        *[pinned(value, pltpu.HBM) for value in in_hbm],
        *[pinned(value, pltpu.VMEM) for value in in_vmem],
    )
    return jnp.transpose(covariance, (0, 2, 1, 3)), projections


def solution(mesh):
    placed = (P("frames", None, "atoms"), P(None, "atoms"), P(None, "atoms", None))
    return jax.shard_map(
        per_device,
        mesh=mesh,
        in_specs=placed,
        out_specs=(P(None, "atoms", None, "frames"), P("frames", "atoms")),
        check_vma=False,
    )
```

```python
import functools

import jax
import jax.numpy as jnp
from jax import lax
from jax.experimental import pallas as pl
from jax.experimental.pallas import tpu as pltpu
from jax.sharding import PartitionSpec as P

POLAR = 6
LANES = 128
STATS = 24
VMEM = pl.BlockSpec(memory_space=pltpu.VMEM)
SMEM = pl.BlockSpec(memory_space=pltpu.SMEM)
HBM = pl.BlockSpec(memory_space=pltpu.HBM)
ANY = pl.BlockSpec(memory_space=pl.ANY)
MIB = 1024 * 1024
LONG = 40 * 10**9


def params(mib):
    return pltpu.CompilerParams(vmem_limit_bytes=mib * MIB)


def lane_mean(value):
    return jnp.sum(value, axis=1, keepdims=True) * (1.0 / value.shape[1])


def run_copies(copies):
    for copy in copies:
        copy.start()
    for copy in copies:
        copy.wait()


def stats_kernel(x_hbm, ref_hbm, out_ref, x_ref, ref_ref, sem):
    run_copies(
        [
            pltpu.make_async_copy(ref_hbm, ref_ref, sem.at[0]),
            pltpu.make_async_copy(x_hbm, x_ref, sem.at[1]),
        ]
    )
    values = []
    centred = []
    for i in range(3):
        x = x_ref[i]
        mean = lane_mean(x)
        values.append(mean)
        centred.append(x - mean)
    values.append(sum(jnp.sum(c * c, axis=1, keepdims=True) for c in centred))
    ref_mean = [lane_mean(ref_ref[j : j + 1, :]) for j in range(3)]
    ref_centred = [ref_ref[j : j + 1, :] - ref_mean[j] for j in range(3)]
    for i in range(3):
        for j in range(3):
            values.append(jnp.sum(centred[i] * ref_centred[j], axis=1, keepdims=True))
    values += ref_mean
    values.append(sum(jnp.sum(c * c, axis=1, keepdims=True) for c in ref_centred))
    shape = (x_ref.shape[1], LANES)
    lane = lax.broadcasted_iota(jnp.int32, shape, 1)
    out = jnp.zeros(shape, jnp.float32)
    for k, value in enumerate(values):
        out = jnp.where(lane == k, jnp.broadcast_to(value, shape), out)
    out_ref[...] = out.T[:STATS]


def align_kernel(parts, *refs):
    stats = refs[:parts]
    x_ref, ref_ref, first_ref, second_ref, flat_ref, turn = refs[parts:]
    local = x_ref.shape[2]
    rows = x_ref.shape[1]

    def row(at):
        return [s[at : at + 1, :] for s in stats]

    means = [row(i) for i in range(3)]
    ref_means = [row(13 + j) for j in range(3)]
    centre = [sum(m) * (1.0 / parts) for m in means]
    ref_centre = [sum(r) * (1.0 / parts) for r in ref_means]
    off = [[m - centre[i] for m in means[i]] for i in range(3)]
    ref_off = [[r - ref_centre[j] for r in ref_means[j]] for j in range(3)]
    spread = sum(row(3)) + local * sum(o * o for i in range(3) for o in off[i])
    ref_spread = sum(row(16)) + local * sum(o * o for j in range(3) for o in ref_off[j])
    scale = 1.0 / jnp.sqrt(spread * ref_spread + 1e-06)
    now = [
        [
            (sum(row(4 + 3 * i + j)) + local * sum(o * r for o, r in zip(off[i], ref_off[j])))
            * scale
            for j in range(3)
        ]
        for i in range(3)
    ]
    for _ in range(POLAR):
        gram = {}
        for i in range(3):
            for j in range(i, 3):
                gram[i, j] = sum(now[k][i] * now[k][j] for k in range(3))
                gram[j, i] = gram[i, j]
        left = [
            [(1.5 if k == j else 0.0) - 0.5 * gram[k, j] for j in range(3)] for k in range(3)
        ]
        now = [
            [sum(now[i][k] * left[k][j] for k in range(3)) for j in range(3)]
            for i in range(3)
        ]
    for k, value in enumerate(sum(now, []) + centre + ref_centre):
        turn[k : k + 1, :rows] = value
    turned = turn[...].T
    column = [turned[:rows, k : k + 1] for k in range(12)]
    centred = [x_ref[j] - column[9 + j] for j in range(3)]
    for i in range(3):
        target = ref_ref[i : i + 1, :] - turned[0:1, 12 + i : 13 + i]
        moved = sum(column[3 * j + i] * centred[j] for j in range(3)) - target
        flat_ref[i] = moved.astype(jnp.bfloat16)
        run = first_ref.shape[1]
        for at, piece in enumerate((first_ref, second_ref)):
            pair = [moved[:, (2 * at + k) * run : (2 * at + k + 1) * run] for k in range(2)]
            piece[i] = jnp.concatenate(pair, axis=0).T.astype(jnp.bfloat16)


def project_kernel(me_ref, flat_ref, eig_ref, *refs):
    shares, cut = refs[:-1], refs[-1]
    total = sum(
        jnp.dot(flat_ref[c], eig_ref[c], preferred_element_type=jnp.float32) for c in range(3)
    )
    width = cut.shape[2]
    for k in range(len(shares)):
        cut[k] = total[:, k * width : (k + 1) * width]
    for k, share in enumerate(shares):
        share[...] = cut[lax.bitwise_xor(me_ref[0], k)]


def sum_kernel(*refs):
    refs[-1][...] = sum(ref[...] for ref in refs[:-1])


def cut_kernel(half_ref, *refs):
    pieces, cols_ref = refs[:-1], refs[-1]
    for half in range(2):

        @pl.when(half_ref[0] == half)
        def _(half=half):
            for k, piece in enumerate(pieces[half::2]):
                run, lanes = piece.shape[1:]
                for c in range(3):
                    turned = piece[c].astype(jnp.float32).T.astype(jnp.bfloat16)
                    cols_ref[k, c, :, :run] = turned[: lanes // 2]
                    cols_ref[k, c, :, run:] = turned[lanes // 2 :]


def pass_on_kernel(role_ref, *refs):
    sources, out_ref = refs[:-1], refs[-1]
    for role in range(2):

        @pl.when((role_ref[0] != 0) == bool(role))
        def _(role=role):
            to = 0
            for source in sources[role::2]:
                out_ref[to : to + source.shape[0]] = source[...]
                to += source.shape[0]


def side_by_side(first, second):
    middle = first.shape[1] // 2
    left = jnp.concatenate([first[:, :middle], second[:, :middle]], axis=1)
    right = jnp.concatenate([first[:, middle:], second[:, middle:]], axis=1)
    return left, right


def covariance_kernel(slots, roles, groups, scale, role_ref, *refs):
    pieces, refs = refs[: 2 * slots], refs[2 * slots :]
    arrays = []
    for _, _, holder in groups:
        count = max(holder) + 1
        arrays.append(refs[:count])
        refs = refs[count:]
    out_ref, left, right, done, col_sem, out_sem = refs
    depth = right.shape[1] // slots
    run = pieces[0].shape[1]

    def fetches(k, role, to):
        source = arrays[k][groups[k][2][role]]
        return [
            pltpu.make_async_copy(
                source.at[n],
                right.at[:, pl.ds(to + n * depth, depth), :],
                col_sem.at[to // depth + n],
            )
            for n in range(groups[k][0])
        ]

    def for_each_group(from_hbm, act):
        for role in range(roles):

            @pl.when(role_ref[0] == role)
            def _(role=role):
                to = 0
                for k, (count, in_hbm, _) in enumerate(groups):
                    if in_hbm == from_hbm:
                        act(k, role, to)
                    to += count * depth

    def start(k, role, to):
        for copy in fetches(k, role, to):
            copy.start()

    def wait(k, role, to):
        for copy in fetches(k, role, to):
            copy.wait()

    def load(k, role, to):
        source = arrays[k][groups[k][2][role]]
        for n in range(groups[k][0]):
            for d in range(3):
                right[d, to + n * depth : to + (n + 1) * depth, :] = source[n, d]

    def assemble(c, at):
        for q in range(slots // 2):
            low, high = side_by_side(pieces[4 * q + at][c], pieces[4 * q + 2 + at][c])
            left[at, :run, q * LANES : (q + 1) * LANES] = low
            left[at, run:, q * LANES : (q + 1) * LANES] = high

    for_each_group(True, start)
    for_each_group(False, load)
    assemble(0, 0)
    for_each_group(True, wait)

    def write(c, at, d):
        return pltpu.make_async_copy(
            done.at[at, d],
            out_ref.at[c, d, pl.ds(at * 2 * run, 2 * run), :],
            out_sem.at[at, d],
        )

    @pl.loop(0, 3)
    def _(c):
        for at in range(2):

            @pl.when(c > 0)
            def _():
                for d in range(3):
                    write(c - 1, at, d).wait()

            assemble(jnp.minimum(c + at, 2), 1 - at)
            for d in range(3):
                done[at, d] = scale * jnp.dot(
                    left[at], right[d], preferred_element_type=jnp.float32
                )
                write(c, at, d).start()

    for at in range(2):
        for d in range(3):
            write(2, at, d).wait()


pinned = pltpu.with_memory_space_constraint


def after(value, *others):
    return lax.optimization_barrier((value,) + others)[0] if others else value


def ring_order(count):
    return list(range(0, count, 2)) + list(range(1, count, 2))[::-1]


def long_axis_covariance(flat, half, role, block, spread_pairs, scale):
    rows = lax.all_gather(flat, "frames", axis=1, tiled=True)
    cut = lax.dynamic_slice_in_dim(rows, half * block, block, axis=2)
    cols = jnp.where(role == 0, cut, jnp.zeros_like(cut))
    for d, pairs in enumerate(spread_pairs):
        sent = lax.ppermute(cut, ("frames", "atoms"), pairs)
        cols = jnp.where(role == d + 1, sent, cols)
    return scale * jnp.einsum(
        "cfp,dfq->cpdq", rows, cols, preferred_element_type=jnp.float32
    )


def per_device(frames, mean_structure, eigvecs):
    local_frames, _, local_atoms = frames.shape
    frame_axis = lax.axis_size("frames")
    atom_axis = lax.axis_size("atoms")
    total_frames = local_frames * frame_axis
    block = local_atoms * atom_axis // frame_axis
    blocks = frame_axis // atom_axis
    me_f = lax.axis_index("frames")
    me_a = lax.axis_index("atoms")
    half = lax.rem(me_f, blocks).astype(jnp.int32).reshape(1)
    owner = lax.div(me_f, blocks)
    role = lax.bitwise_xor(me_a, owner).astype(jnp.int32).reshape(1)
    x = pinned(jnp.transpose(frames, (1, 0, 2)), pltpu.HBM)
    mean_structure = pinned(mean_structure, pltpu.HBM)
    stats, x, mean_structure = pl.pallas_call(
        stats_kernel,
        out_shape=(
            pltpu.VMEM((STATS, local_frames), jnp.float32),
            pltpu.VMEM(x.shape, jnp.float32),
            pltpu.VMEM(mean_structure.shape, jnp.float32),
        ),
        in_specs=[HBM, HBM],
        out_specs=(VMEM, VMEM, VMEM),
        scratch_shapes=[pltpu.SemaphoreType.DMA((2,))],
        compiler_params=params(8),
        name="local_moments",
    )(x, mean_structure)
    def swap(value, distance):
        return lax.ppermute(value, "atoms", [(a, a ^ distance) for a in range(atom_axis)])

    others = [swap(stats, d) for d in range(1, atom_axis)]
    run = local_atoms // 4
    piece = jax.ShapeDtypeStruct((3, run, 2 * local_frames), jnp.bfloat16)
    *own, flat = pl.pallas_call(
        functools.partial(align_kernel, atom_axis),
        out_shape=(piece, piece, jax.ShapeDtypeStruct(x.shape, jnp.bfloat16)),
        in_specs=[VMEM] * (atom_axis + 2),
        out_specs=(VMEM, VMEM, VMEM),
        scratch_shapes=[pltpu.VMEM((LANES, LANES), jnp.float32)],
        compiler_params=params(8),
        name="polar_align",
    )(stats, *others, x, mean_structure)
    share = jax.ShapeDtypeStruct((local_frames, eigvecs.shape[2] // atom_axis), jnp.float32)
    shares = pl.pallas_call(
        project_kernel,
        out_shape=(share,) * atom_axis,
        in_specs=[SMEM, VMEM, VMEM],
        out_specs=(VMEM,) * atom_axis,
        scratch_shapes=[pltpu.VMEM((atom_axis,) + share.shape, jnp.float32)],
        compiler_params=params(8),
        name="project",
    )(me_a.astype(jnp.int32).reshape(1), flat, eigvecs)
    def sum_shares(shares):
        return pl.pallas_call(
            sum_kernel,
            out_shape=share,
            in_specs=[VMEM] * atom_axis,
            out_specs=VMEM,
            compiler_params=params(4),
            name="sum_shares",
        )(shares[0], *[swap(shares[d], d) for d in range(1, atom_axis)])

    def pairs(source, target):
        return [
            (
                f * atom_axis + ((f // blocks) ^ source),
                f * atom_axis + ((f // blocks) ^ target),
            )
            for f in range(frame_axis)
        ]

    if blocks != 2 or frame_axis != 8:
        projections = sum_shares(shares)
        spread_pairs = [pairs(0, d) for d in range(1, atom_axis)]
        covariance = long_axis_covariance(
            flat, half[0], role[0], block, spread_pairs, 1.0 / total_frames
        )
        return covariance, projections

    axes = ("frames", "atoms")

    def columns(slots):
        return pltpu.VMEM((slots, 3, local_frames, block), jnp.bfloat16)

    def kernel(body, out_shape, scalar, values, name, cost=None):
        single = not isinstance(out_shape, tuple)
        return pl.pallas_call(
            body,
            out_shape=out_shape,
            in_specs=[SMEM] + [VMEM] * len(values),
            out_specs=VMEM if single else (VMEM,) * len(out_shape),
            compiler_params=params(4),
            cost_estimate=cost,
            name=name,
        )(scalar, *[pinned(value, pltpu.VMEM) for value in values])

    def cross(cut):
        return [cut, lax.ppermute(cut, axes, pairs(0, 2))]

    def pass_on(values, role):
        slots = sum(value.shape[0] for value in values[::2])
        held = kernel(pass_on_kernel, columns(slots), role, values, "pass_on")
        return [held, lax.ppermute(held, axes, pairs(0, 1) + pairs(2, 3))]

    order = ring_order(frame_axis)
    forward = [(order[i], order[(i + 1) % frame_axis]) for i in range(frame_axis)]
    backward = [(b, a) for a, b in forward]

    def hop(up, down):
        up_a = lax.ppermute(up[0], "frames", forward)
        down_a = lax.ppermute(down[0], "frames", backward)
        up_b = lax.ppermute(up[1], "frames", forward)
        down_b = lax.ppermute(down[1], "frames", backward)
        return [up_a, up_b], [down_a, down_b]

    def cut(slots, *earlier, cost=None):
        pieces = sum(slots, [])
        return kernel(
            cut_kernel, columns(len(slots)), after(half, *earlier), pieces, "cut_columns", cost
        )

    long = pl.CostEstimate(flops=LONG, bytes_accessed=0, transcendentals=0)
    one = hop(own, own)
    two = hop(*one)
    in_hbm = pass_on(cross(cut([own] + list(one))), role)
    three = hop(*two)
    crossed = cross(cut(two, *shares))
    far = [
        lax.ppermute(three[0][0], "frames", forward),
        lax.ppermute(three[1][1], "frames", backward),
    ]
    crossed += cross(cut(three))
    crossed += cross(cut([far], crossed[1], cost=long))
    projections = sum_shares([after(value, crossed[-2]) for value in shares])
    in_vmem = pass_on(crossed, after(role, in_hbm[1]))
    groups = ((3, True, (0, 1, 0, 1)), (5, False, (0, 1, 0, 1)))
    rows = sum([own, *one, *two, *three, far], [])
    covariance = pl.pallas_call(
        functools.partial(
            covariance_kernel, frame_axis, atom_axis, groups, 1.0 / total_frames
        ),
        out_shape=jax.ShapeDtypeStruct((3, 3, local_atoms, block), jnp.float32),
        in_specs=[SMEM]
        + [VMEM] * len(rows)
        + [HBM] * len(in_hbm)
        + [VMEM] * len(in_vmem),
        out_specs=ANY,
        scratch_shapes=[
            pltpu.VMEM((2, 2 * run, total_frames), jnp.bfloat16),
            pltpu.VMEM((3, total_frames, block), jnp.bfloat16),
            pltpu.VMEM((2, 3, 2 * run, block), jnp.float32),
            pltpu.SemaphoreType.DMA((frame_axis,)),
            pltpu.SemaphoreType.DMA((2, 3)),
        ],
        compiler_params=params(16),
        cost_estimate=pl.CostEstimate(
            flops=18 * local_atoms * block * total_frames,
            bytes_accessed=24 * MIB,
            transcendentals=0,
        ),
        name="covariance_tile",
    )(
        role,
        *[pinned(value, pltpu.VMEM) for value in rows],
        *[pinned(value, pltpu.HBM) for value in in_hbm],
        *[pinned(value, pltpu.VMEM) for value in in_vmem],
    )
    return jnp.transpose(covariance, (0, 2, 1, 3)), projections


def solution(mesh):
    placed = (P("frames", None, "atoms"), P(None, "atoms"), P(None, "atoms", None))
    return jax.shard_map(
        per_device,
        mesh=mesh,
        in_specs=placed,
        out_specs=(P(None, "atoms", None, "frames"), P("frames", "atoms")),
        check_vma=False,
    )
```

```python
import functools

import jax
import jax.numpy as jnp
from jax import lax
from jax.experimental import pallas as pl
from jax.experimental.pallas import tpu as pltpu
from jax.sharding import PartitionSpec as P

POLAR = 6
LANES = 128
STATS = 24
VMEM = pl.BlockSpec(memory_space=pltpu.VMEM)
SMEM = pl.BlockSpec(memory_space=pltpu.SMEM)
HBM = pl.BlockSpec(memory_space=pltpu.HBM)
ANY = pl.BlockSpec(memory_space=pl.ANY)
MIB = 1024 * 1024
LONG = 4 * 10**9


def params(mib):
    return pltpu.CompilerParams(vmem_limit_bytes=mib * MIB)


def lane_mean(value):
    return jnp.sum(value, axis=1, keepdims=True) * (1.0 / value.shape[1])


def run_copies(copies):
    for copy in copies:
        copy.start()
    for copy in copies:
        copy.wait()


def stats_kernel(x_hbm, ref_hbm, out_ref, x_ref, ref_ref, sem):
    run_copies(
        [
            pltpu.make_async_copy(ref_hbm, ref_ref, sem.at[0]),
            pltpu.make_async_copy(x_hbm, x_ref, sem.at[1]),
        ]
    )
    values = []
    centred = []
    for i in range(3):
        x = x_ref[i]
        mean = lane_mean(x)
        values.append(mean)
        centred.append(x - mean)
    values.append(sum(jnp.sum(c * c, axis=1, keepdims=True) for c in centred))
    ref_mean = [lane_mean(ref_ref[j : j + 1, :]) for j in range(3)]
    ref_centred = [ref_ref[j : j + 1, :] - ref_mean[j] for j in range(3)]
    for i in range(3):
        for j in range(3):
            values.append(jnp.sum(centred[i] * ref_centred[j], axis=1, keepdims=True))
    values += ref_mean
    values.append(sum(jnp.sum(c * c, axis=1, keepdims=True) for c in ref_centred))
    shape = (x_ref.shape[1], LANES)
    lane = lax.broadcasted_iota(jnp.int32, shape, 1)
    out = jnp.zeros(shape, jnp.float32)
    for k, value in enumerate(values):
        out = jnp.where(lane == k, jnp.broadcast_to(value, shape), out)
    out_ref[...] = out.T[:STATS]


def align_kernel(parts, *refs):
    stats = refs[:parts]
    x_ref, ref_ref, piece_ref, flat_ref, turn = refs[parts:]
    local = x_ref.shape[2]
    rows = x_ref.shape[1]

    def row(at):
        return [s[at : at + 1, :] for s in stats]

    means = [row(i) for i in range(3)]
    ref_means = [row(13 + j) for j in range(3)]
    centre = [sum(m) * (1.0 / parts) for m in means]
    ref_centre = [sum(r) * (1.0 / parts) for r in ref_means]
    off = [[m - centre[i] for m in means[i]] for i in range(3)]
    ref_off = [[r - ref_centre[j] for r in ref_means[j]] for j in range(3)]
    spread = sum(row(3)) + local * sum(o * o for i in range(3) for o in off[i])
    ref_spread = sum(row(16)) + local * sum(o * o for j in range(3) for o in ref_off[j])
    scale = 1.0 / jnp.sqrt(spread * ref_spread + 1e-06)
    now = [
        [
            (sum(row(4 + 3 * i + j)) + local * sum(o * r for o, r in zip(off[i], ref_off[j])))
            * scale
            for j in range(3)
        ]
        for i in range(3)
    ]
    for _ in range(POLAR):
        gram = {}
        for i in range(3):
            for j in range(i, 3):
                gram[i, j] = sum(now[k][i] * now[k][j] for k in range(3))
                gram[j, i] = gram[i, j]
        left = [
            [(1.5 if k == j else 0.0) - 0.5 * gram[k, j] for j in range(3)] for k in range(3)
        ]
        now = [
            [sum(now[i][k] * left[k][j] for k in range(3)) for j in range(3)]
            for i in range(3)
        ]
    for k, value in enumerate(sum(now, []) + centre + ref_centre):
        turn[k : k + 1, :rows] = value
    turned = turn[...].T
    column = [turned[:rows, k : k + 1] for k in range(12)]
    centred = [x_ref[j] - column[9 + j] for j in range(3)]
    for i in range(3):
        target = ref_ref[i : i + 1, :] - turned[0:1, 12 + i : 13 + i]
        moved = sum(column[3 * j + i] * centred[j] for j in range(3)) - target
        flat_ref[i] = moved.astype(jnp.bfloat16)
        run = piece_ref.shape[2]
        for at in range(2):
            pair = [moved[:, (2 * at + k) * run : (2 * at + k + 1) * run] for k in range(2)]
            piece_ref[at, i] = jnp.concatenate(pair, axis=0).T.astype(jnp.bfloat16)


def project_kernel(me_ref, flat_ref, eig_ref, *refs):
    shares, cut = refs[:-1], refs[-1]
    total = sum(
        jnp.dot(flat_ref[c], eig_ref[c], preferred_element_type=jnp.float32) for c in range(3)
    )
    width = cut.shape[2]
    for k in range(len(shares)):
        cut[k] = total[:, k * width : (k + 1) * width]
    for k, share in enumerate(shares):
        share[...] = cut[lax.bitwise_xor(me_ref[0], k)]


def sum_kernel(*refs):
    refs[-1][...] = sum(ref[...] for ref in refs[:-1])


def cut_columns(half_ref, halves, cols_ref):
    for half in range(2):

        @pl.when(half_ref[0] == half)
        def _(half=half):
            for k, pair in enumerate(halves):
                run, lanes = pair[half].shape[1:]
                for c in range(3):
                    turned = pair[half][c].astype(jnp.float32).T.astype(jnp.bfloat16)
                    cols_ref[k, c, :, :run] = turned[: lanes // 2]
                    cols_ref[k, c, :, run:] = turned[lanes // 2 :]


def cut_kernel(half_ref, *refs):
    cut_columns(half_ref, [(r.at[0], r.at[1]) for r in refs[:-1]], refs[-1])


def cut_split_kernel(half_ref, up_ref, down_ref, cols_ref, *refs):
    for k, shard in enumerate((up_ref, down_ref)):
        for at in range(2):
            refs[2 * k + at][...] = shard[at]
    cut_columns(half_ref, [(r.at[0], r.at[1]) for r in (up_ref, down_ref)], cols_ref)


def cut_pieces_kernel(half_ref, *refs):
    cut_columns(half_ref, list(zip(refs[:-1:2], refs[1:-1:2])), refs[-1])


def pass_on_kernel(role_ref, *refs):
    sources, out_ref = refs[:-1], refs[-1]
    for role in range(2):

        @pl.when((role_ref[0] != 0) == bool(role))
        def _(role=role):
            to = 0
            for source in sources[role::2]:
                out_ref[to : to + source.shape[0]] = source[...]
                to += source.shape[0]


def side_by_side(first, second):
    middle = first.shape[1] // 2
    left = jnp.concatenate([first[:, :middle], second[:, :middle]], axis=1)
    right = jnp.concatenate([first[:, middle:], second[:, middle:]], axis=1)
    return left, right


def covariance_kernel(slots, whole, roles, groups, scale, role_ref, *refs):
    shards, pieces, refs = refs[:whole], refs[whole : 2 * slots - whole], refs[2 * slots - whole :]
    arrays = []
    for _, _, holder in groups:
        count = max(holder) + 1
        arrays.append(refs[:count])
        refs = refs[count:]
    out_ref, left, right, done, col_sem, out_sem = refs
    depth = right.shape[1] // slots
    run = pieces[0].shape[1]

    def fetches(k, role, to):
        source = arrays[k][groups[k][2][role]]
        return [
            pltpu.make_async_copy(
                source.at[n],
                right.at[:, pl.ds(to + n * depth, depth), :],
                col_sem.at[to // depth + n],
            )
            for n in range(groups[k][0])
        ]

    def for_each_group(from_hbm, act):
        for role in range(roles):

            @pl.when(role_ref[0] == role)
            def _(role=role):
                to = 0
                for k, (count, in_hbm, _) in enumerate(groups):
                    if in_hbm == from_hbm:
                        act(k, role, to)
                    to += count * depth

    def start(k, role, to):
        for copy in fetches(k, role, to):
            copy.start()

    def wait(k, role, to):
        for copy in fetches(k, role, to):
            copy.wait()

    def load(k, role, to):
        source = arrays[k][groups[k][2][role]]
        for n in range(groups[k][0]):
            for d in range(3):
                right[d, to + n * depth : to + (n + 1) * depth, :] = source[n, d]

    def piece(slot, at, c):
        if slot < whole:
            return shards[slot][at, c]
        return pieces[2 * (slot - whole) + at][c]

    def assemble(c, at):
        for q in range(slots // 2):
            low, high = side_by_side(piece(2 * q, at, c), piece(2 * q + 1, at, c))
            left[at, :run, q * LANES : (q + 1) * LANES] = low
            left[at, run:, q * LANES : (q + 1) * LANES] = high

    for_each_group(True, start)
    for_each_group(False, load)
    assemble(0, 0)
    for_each_group(True, wait)

    def write(c, at, d):
        return pltpu.make_async_copy(
            done.at[at, d],
            out_ref.at[c, d, pl.ds(at * 2 * run, 2 * run), :],
            out_sem.at[at, d],
        )

    @pl.loop(0, 3)
    def _(c):
        for at in range(2):

            @pl.when(c > 0)
            def _():
                for d in range(3):
                    write(c - 1, at, d).wait()

            assemble(jnp.minimum(c + at, 2), 1 - at)
            for d in range(3):
                done[at, d] = scale * jnp.dot(
                    left[at], right[d], preferred_element_type=jnp.float32
                )
                write(c, at, d).start()

    for at in range(2):
        for d in range(3):
            write(2, at, d).wait()


pinned = pltpu.with_memory_space_constraint


def after(value, *others):
    return lax.optimization_barrier((value,) + others)[0] if others else value


def ring_order(count):
    return list(range(0, count, 2)) + list(range(1, count, 2))[::-1]


def long_axis_covariance(flat, half, role, block, spread_pairs, scale):
    rows = lax.all_gather(flat, "frames", axis=1, tiled=True)
    cut = lax.dynamic_slice_in_dim(rows, half * block, block, axis=2)
    cols = jnp.where(role == 0, cut, jnp.zeros_like(cut))
    for d, pairs in enumerate(spread_pairs):
        sent = lax.ppermute(cut, ("frames", "atoms"), pairs)
        cols = jnp.where(role == d + 1, sent, cols)
    return scale * jnp.einsum(
        "cfp,dfq->cpdq", rows, cols, preferred_element_type=jnp.float32
    )


def per_device(frames, mean_structure, eigvecs):
    local_frames, _, local_atoms = frames.shape
    frame_axis = lax.axis_size("frames")
    atom_axis = lax.axis_size("atoms")
    total_frames = local_frames * frame_axis
    block = local_atoms * atom_axis // frame_axis
    blocks = frame_axis // atom_axis
    me_f = lax.axis_index("frames")
    me_a = lax.axis_index("atoms")
    half = lax.rem(me_f, blocks).astype(jnp.int32).reshape(1)
    owner = lax.div(me_f, blocks)
    role = lax.bitwise_xor(me_a, owner).astype(jnp.int32).reshape(1)
    x = pinned(jnp.transpose(frames, (1, 0, 2)), pltpu.HBM)
    mean_structure = pinned(mean_structure, pltpu.HBM)
    stats, x, mean_structure = pl.pallas_call(
        stats_kernel,
        out_shape=(
            pltpu.VMEM((STATS, local_frames), jnp.float32),
            pltpu.VMEM(x.shape, jnp.float32),
            pltpu.VMEM(mean_structure.shape, jnp.float32),
        ),
        in_specs=[HBM, HBM],
        out_specs=(VMEM, VMEM, VMEM),
        scratch_shapes=[pltpu.SemaphoreType.DMA((2,))],
        compiler_params=params(8),
        name="local_moments",
    )(x, mean_structure)
    def swap(value, distance):
        return lax.ppermute(value, "atoms", [(a, a ^ distance) for a in range(atom_axis)])

    others = [swap(stats, d) for d in range(1, atom_axis)]
    run = local_atoms // 4
    piece = (3, run, 2 * local_frames)
    own, flat = pl.pallas_call(
        functools.partial(align_kernel, atom_axis),
        out_shape=(
            jax.ShapeDtypeStruct((2,) + piece, jnp.bfloat16),
            jax.ShapeDtypeStruct(x.shape, jnp.bfloat16),
        ),
        in_specs=[VMEM] * (atom_axis + 2),
        out_specs=(VMEM, VMEM),
        scratch_shapes=[pltpu.VMEM((LANES, LANES), jnp.float32)],
        compiler_params=params(8),
        name="polar_align",
    )(stats, *others, x, mean_structure)
    share = jax.ShapeDtypeStruct((local_frames, eigvecs.shape[2] // atom_axis), jnp.float32)
    shares = pl.pallas_call(
        project_kernel,
        out_shape=(share,) * atom_axis,
        in_specs=[SMEM, VMEM, VMEM],
        out_specs=(VMEM,) * atom_axis,
        scratch_shapes=[pltpu.VMEM((atom_axis,) + share.shape, jnp.float32)],
        compiler_params=params(8),
        name="project",
    )(me_a.astype(jnp.int32).reshape(1), flat, eigvecs)
    parts = [shares[0]] + [swap(shares[d], d) for d in range(1, atom_axis)]
    projections = pl.pallas_call(
        sum_kernel,
        out_shape=share,
        in_specs=[VMEM] * atom_axis,
        out_specs=VMEM,
        compiler_params=params(4),
        name="sum_shares",
    )(*parts)

    def pairs(source, target):
        return [
            (
                f * atom_axis + ((f // blocks) ^ source),
                f * atom_axis + ((f // blocks) ^ target),
            )
            for f in range(frame_axis)
        ]

    if blocks != 2 or frame_axis != 8:
        spread_pairs = [pairs(0, d) for d in range(1, atom_axis)]
        covariance = long_axis_covariance(
            flat, half[0], role[0], block, spread_pairs, 1.0 / total_frames
        )
        return covariance, projections

    axes = ("frames", "atoms")

    def columns(slots):
        return pltpu.VMEM((slots, 3, local_frames, block), jnp.bfloat16)

    def kernel(body, out_shape, scalar, values, name, cost=None):
        single = not isinstance(out_shape, tuple)
        return pl.pallas_call(
            body,
            out_shape=out_shape,
            in_specs=[SMEM] + [VMEM] * len(values),
            out_specs=VMEM if single else (VMEM,) * len(out_shape),
            compiler_params=params(4),
            cost_estimate=cost,
            name=name,
        )(scalar, *[pinned(value, pltpu.VMEM) for value in values])

    def cross(cut):
        return [cut, lax.ppermute(cut, axes, pairs(0, 2))]

    def pass_on(values, role):
        slots = sum(value.shape[0] for value in values[::2])
        held = kernel(pass_on_kernel, columns(slots), role, values, "pass_on")
        return [held, lax.ppermute(held, axes, pairs(0, 1) + pairs(2, 3))]

    order = ring_order(frame_axis)
    forward = [(order[i], order[(i + 1) % frame_axis]) for i in range(frame_axis)]
    backward = [(b, a) for a, b in forward]

    def hop(up, down):
        return lax.ppermute(up, "frames", forward), lax.ppermute(down, "frames", backward)

    one = hop(own, own)
    crossed = cross(kernel(cut_kernel, columns(1), half, [own], "cut_columns"))
    cut_one = kernel(cut_kernel, columns(2), half, list(one), "cut_columns")
    two = hop(after(one[0], crossed[1]), one[1])
    in_hbm = pass_on(crossed + cross(cut_one), role)
    split = pltpu.VMEM(piece, jnp.bfloat16)
    cut_two, *pieces = kernel(
        cut_split_kernel,
        (columns(2),) + (split,) * 4,
        after(half, *parts),
        list(two),
        "cut_columns",
    )
    crossed = cross(cut_two)
    up_a, down_b = hop(pieces[0], pieces[3])
    up_b, down_a = hop(pieces[1], pieces[2])
    far = hop(up_a, down_b)
    three = [up_a, up_b, down_a, down_b]
    cut_three = kernel(
        cut_pieces_kernel,
        columns(2),
        after(half, projections, in_hbm[0]),
        three,
        "cut_columns",
    )
    long = pl.CostEstimate(flops=LONG, bytes_accessed=0, transcendentals=0)
    cut_four = kernel(
        cut_pieces_kernel, columns(1), after(half, crossed[1]), list(far), "cut_columns", long
    )
    in_vmem = pass_on(
        crossed + cross(cut_three) + cross(cut_four), after(role, in_hbm[1])
    )
    groups = ((3, True, (0, 1, 0, 1)), (5, False, (0, 1, 0, 1)))
    rows = [own, *one, *two, *three, *far]
    whole = 5
    covariance = pl.pallas_call(
        functools.partial(
            covariance_kernel, frame_axis, whole, atom_axis, groups, 1.0 / total_frames
        ),
        out_shape=jax.ShapeDtypeStruct((3, 3, local_atoms, block), jnp.float32),
        in_specs=[SMEM]
        + [VMEM] * len(rows)
        + [HBM] * len(in_hbm)
        + [VMEM] * len(in_vmem),
        out_specs=ANY,
        scratch_shapes=[
            pltpu.VMEM((2, 2 * run, total_frames), jnp.bfloat16),
            pltpu.VMEM((3, total_frames, block), jnp.bfloat16),
            pltpu.VMEM((2, 3, 2 * run, block), jnp.float32),
            pltpu.SemaphoreType.DMA((frame_axis,)),
            pltpu.SemaphoreType.DMA((2, 3)),
        ],
        compiler_params=params(16),
        cost_estimate=pl.CostEstimate(
            flops=18 * local_atoms * block * total_frames,
            bytes_accessed=24 * MIB,
            transcendentals=0,
        ),
        name="covariance_tile",
    )(
        role,
        *[pinned(value, pltpu.VMEM) for value in rows],
        *[pinned(value, pltpu.HBM) for value in in_hbm],
        *[pinned(value, pltpu.VMEM) for value in in_vmem],
    )
    return jnp.transpose(covariance, (0, 2, 1, 3)), projections


def solution(mesh):
    placed = (P("frames", None, "atoms"), P(None, "atoms"), P(None, "atoms", None))
    return jax.shard_map(
        per_device,
        mesh=mesh,
        in_specs=placed,
        out_specs=(P(None, "atoms", None, "frames"), P("frames", "atoms")),
        check_vma=False,
    )
```

```python
import functools

import jax
import jax.numpy as jnp
from jax import lax
from jax.experimental import pallas as pl
from jax.experimental.pallas import tpu as pltpu
from jax.sharding import PartitionSpec as P

POLAR = 6
LANES = 128
STATS = 24
VMEM = pl.BlockSpec(memory_space=pltpu.VMEM)
SMEM = pl.BlockSpec(memory_space=pltpu.SMEM)
HBM = pl.BlockSpec(memory_space=pltpu.HBM)
ANY = pl.BlockSpec(memory_space=pl.ANY)
MIB = 1024 * 1024
LONG = 4 * 10**9


def params(mib):
    return pltpu.CompilerParams(vmem_limit_bytes=mib * MIB)


def lane_mean(value):
    return jnp.sum(value, axis=1, keepdims=True) * (1.0 / value.shape[1])


def run_copies(copies):
    for copy in copies:
        copy.start()
    for copy in copies:
        copy.wait()


def stats_kernel(x_hbm, ref_hbm, out_ref, x_ref, ref_ref, sem):
    run_copies(
        [
            pltpu.make_async_copy(ref_hbm, ref_ref, sem.at[0]),
            pltpu.make_async_copy(x_hbm, x_ref, sem.at[1]),
        ]
    )
    values = []
    centred = []
    for i in range(3):
        x = x_ref[i]
        mean = lane_mean(x)
        values.append(mean)
        centred.append(x - mean)
    values.append(sum(jnp.sum(c * c, axis=1, keepdims=True) for c in centred))
    ref_mean = [lane_mean(ref_ref[j : j + 1, :]) for j in range(3)]
    ref_centred = [ref_ref[j : j + 1, :] - ref_mean[j] for j in range(3)]
    for i in range(3):
        for j in range(3):
            values.append(jnp.sum(centred[i] * ref_centred[j], axis=1, keepdims=True))
    values += ref_mean
    values.append(sum(jnp.sum(c * c, axis=1, keepdims=True) for c in ref_centred))
    shape = (x_ref.shape[1], LANES)
    lane = lax.broadcasted_iota(jnp.int32, shape, 1)
    out = jnp.zeros(shape, jnp.float32)
    for k, value in enumerate(values):
        out = jnp.where(lane == k, jnp.broadcast_to(value, shape), out)
    out_ref[...] = out.T[:STATS]


def align_kernel(parts, *refs):
    stats = refs[:parts]
    x_ref, ref_ref, piece_ref, flat_ref, turn = refs[parts:]
    local = x_ref.shape[2]
    rows = x_ref.shape[1]

    def row(at):
        return [s[at : at + 1, :] for s in stats]

    means = [row(i) for i in range(3)]
    ref_means = [row(13 + j) for j in range(3)]
    centre = [sum(m) * (1.0 / parts) for m in means]
    ref_centre = [sum(r) * (1.0 / parts) for r in ref_means]
    off = [[m - centre[i] for m in means[i]] for i in range(3)]
    ref_off = [[r - ref_centre[j] for r in ref_means[j]] for j in range(3)]
    spread = sum(row(3)) + local * sum(o * o for i in range(3) for o in off[i])
    ref_spread = sum(row(16)) + local * sum(o * o for j in range(3) for o in ref_off[j])
    scale = 1.0 / jnp.sqrt(spread * ref_spread + 1e-06)
    now = [
        [
            (sum(row(4 + 3 * i + j)) + local * sum(o * r for o, r in zip(off[i], ref_off[j])))
            * scale
            for j in range(3)
        ]
        for i in range(3)
    ]
    for _ in range(POLAR):
        gram = {}
        for i in range(3):
            for j in range(i, 3):
                gram[i, j] = sum(now[k][i] * now[k][j] for k in range(3))
                gram[j, i] = gram[i, j]
        left = [
            [(1.5 if k == j else 0.0) - 0.5 * gram[k, j] for j in range(3)] for k in range(3)
        ]
        now = [
            [sum(now[i][k] * left[k][j] for k in range(3)) for j in range(3)]
            for i in range(3)
        ]
    for k, value in enumerate(sum(now, []) + centre + ref_centre):
        turn[k : k + 1, :rows] = value
    turned = turn[...].T
    column = [turned[:rows, k : k + 1] for k in range(12)]
    centred = [x_ref[j] - column[9 + j] for j in range(3)]
    for i in range(3):
        target = ref_ref[i : i + 1, :] - turned[0:1, 12 + i : 13 + i]
        moved = sum(column[3 * j + i] * centred[j] for j in range(3)) - target
        flat_ref[i] = moved.astype(jnp.bfloat16)
        run = piece_ref.shape[2]
        for at in range(2):
            pair = [moved[:, (2 * at + k) * run : (2 * at + k + 1) * run] for k in range(2)]
            piece_ref[at, i] = jnp.concatenate(pair, axis=0).T.astype(jnp.bfloat16)


def project_kernel(me_ref, flat_ref, eig_ref, *refs):
    shares, cut = refs[:-1], refs[-1]
    total = sum(
        jnp.dot(flat_ref[c], eig_ref[c], preferred_element_type=jnp.float32) for c in range(3)
    )
    width = cut.shape[2]
    for k in range(len(shares)):
        cut[k] = total[:, k * width : (k + 1) * width]
    for k, share in enumerate(shares):
        share[...] = cut[lax.bitwise_xor(me_ref[0], k)]


def cut_columns(half_ref, halves, cols_ref):
    for half in range(2):

        @pl.when(half_ref[0] == half)
        def _(half=half):
            for k, pair in enumerate(halves):
                run, lanes = pair[half].shape[1:]
                for c in range(3):
                    turned = pair[half][c].astype(jnp.float32).T.astype(jnp.bfloat16)
                    cols_ref[k, c, :, :run] = turned[: lanes // 2]
                    cols_ref[k, c, :, run:] = turned[lanes // 2 :]


def cut_kernel(half_ref, *refs):
    cut_columns(half_ref, [(r.at[0], r.at[1]) for r in refs[:-1]], refs[-1])


def cut_split_kernel(half_ref, up_ref, down_ref, cols_ref, *refs):
    for k, shard in enumerate((up_ref, down_ref)):
        for at in range(2):
            refs[2 * k + at][...] = shard[at]
    cut_columns(half_ref, [(r.at[0], r.at[1]) for r in (up_ref, down_ref)], cols_ref)


def cut_pieces_kernel(half_ref, *refs):
    cut_columns(half_ref, list(zip(refs[:-1:2], refs[1:-1:2])), refs[-1])


def pass_on_kernel(role_ref, *refs):
    sources, out_ref = refs[:-1], refs[-1]
    for role in range(2):

        @pl.when((role_ref[0] != 0) == bool(role))
        def _(role=role):
            to = 0
            for source in sources[role::2]:
                out_ref[to : to + source.shape[0]] = source[...]
                to += source.shape[0]


def side_by_side(first, second):
    middle = first.shape[1] // 2
    left = jnp.concatenate([first[:, :middle], second[:, :middle]], axis=1)
    right = jnp.concatenate([first[:, middle:], second[:, middle:]], axis=1)
    return left, right


def covariance_kernel(slots, whole, roles, groups, scale, role_ref, *refs):
    shards, pieces, refs = refs[:whole], refs[whole : 2 * slots - whole], refs[2 * slots - whole :]
    arrays = []
    for _, _, holder in groups:
        count = max(holder) + 1
        arrays.append(refs[:count])
        refs = refs[count:]
    shares, refs = refs[:roles], refs[roles:]
    out_ref, proj_ref, left, right, done, held, col_sem, out_sem, share_sem = refs
    sums = [
        pltpu.make_async_copy(part, held.at[k], share_sem.at[k]) for k, part in enumerate(shares)
    ]
    for copy in sums:
        copy.start()
    depth = right.shape[1] // slots
    run = pieces[0].shape[1]

    def fetches(k, role, to):
        source = arrays[k][groups[k][2][role]]
        return [
            pltpu.make_async_copy(
                source.at[n],
                right.at[:, pl.ds(to + n * depth, depth), :],
                col_sem.at[to // depth + n],
            )
            for n in range(groups[k][0])
        ]

    def for_each_group(from_hbm, act):
        for role in range(roles):

            @pl.when(role_ref[0] == role)
            def _(role=role):
                to = 0
                for k, (count, in_hbm, _) in enumerate(groups):
                    if in_hbm == from_hbm:
                        act(k, role, to)
                    to += count * depth

    def start(k, role, to):
        for copy in fetches(k, role, to):
            copy.start()

    def wait(k, role, to):
        for copy in fetches(k, role, to):
            copy.wait()

    def load(k, role, to):
        source = arrays[k][groups[k][2][role]]
        for n in range(groups[k][0]):
            for d in range(3):
                right[d, to + n * depth : to + (n + 1) * depth, :] = source[n, d]

    def piece(slot, at, c):
        if slot < whole:
            return shards[slot][at, c]
        return pieces[2 * (slot - whole) + at][c]

    def assemble(c, at):
        for q in range(slots // 2):
            low, high = side_by_side(piece(2 * q, at, c), piece(2 * q + 1, at, c))
            left[at, :run, q * LANES : (q + 1) * LANES] = low
            left[at, run:, q * LANES : (q + 1) * LANES] = high

    for_each_group(True, start)
    for_each_group(False, load)
    assemble(0, 0)
    for_each_group(True, wait)
    for copy in sums:
        copy.wait()
    proj_ref[...] = sum(held[k] for k in range(roles))

    def write(c, at, d):
        return pltpu.make_async_copy(
            done.at[at, d],
            out_ref.at[c, d, pl.ds(at * 2 * run, 2 * run), :],
            out_sem.at[at, d],
        )

    @pl.loop(0, 3)
    def _(c):
        for at in range(2):

            @pl.when(c > 0)
            def _():
                for d in range(3):
                    write(c - 1, at, d).wait()

            assemble(jnp.minimum(c + at, 2), 1 - at)
            for d in range(3):
                done[at, d] = scale * jnp.dot(
                    left[at], right[d], preferred_element_type=jnp.float32
                )
                write(c, at, d).start()

    for at in range(2):
        for d in range(3):
            write(2, at, d).wait()


pinned = pltpu.with_memory_space_constraint


def after(value, *others):
    return lax.optimization_barrier((value,) + others)[0] if others else value


def ring_order(count):
    return list(range(0, count, 2)) + list(range(1, count, 2))[::-1]


def long_axis_covariance(flat, half, role, block, spread_pairs, scale):
    rows = lax.all_gather(flat, "frames", axis=1, tiled=True)
    cut = lax.dynamic_slice_in_dim(rows, half * block, block, axis=2)
    cols = jnp.where(role == 0, cut, jnp.zeros_like(cut))
    for d, pairs in enumerate(spread_pairs):
        sent = lax.ppermute(cut, ("frames", "atoms"), pairs)
        cols = jnp.where(role == d + 1, sent, cols)
    return scale * jnp.einsum(
        "cfp,dfq->cpdq", rows, cols, preferred_element_type=jnp.float32
    )


def per_device(frames, mean_structure, eigvecs):
    local_frames, _, local_atoms = frames.shape
    frame_axis = lax.axis_size("frames")
    atom_axis = lax.axis_size("atoms")
    total_frames = local_frames * frame_axis
    block = local_atoms * atom_axis // frame_axis
    blocks = frame_axis // atom_axis
    me_f = lax.axis_index("frames")
    me_a = lax.axis_index("atoms")
    half = lax.rem(me_f, blocks).astype(jnp.int32).reshape(1)
    owner = lax.div(me_f, blocks)
    role = lax.bitwise_xor(me_a, owner).astype(jnp.int32).reshape(1)
    x = pinned(jnp.transpose(frames, (1, 0, 2)), pltpu.HBM)
    mean_structure = pinned(mean_structure, pltpu.HBM)
    stats, x, mean_structure = pl.pallas_call(
        stats_kernel,
        out_shape=(
            pltpu.VMEM((STATS, local_frames), jnp.float32),
            pltpu.VMEM(x.shape, jnp.float32),
            pltpu.VMEM(mean_structure.shape, jnp.float32),
        ),
        in_specs=[HBM, HBM],
        out_specs=(VMEM, VMEM, VMEM),
        scratch_shapes=[pltpu.SemaphoreType.DMA((2,))],
        compiler_params=params(8),
        name="local_moments",
    )(x, mean_structure)
    def swap(value, distance):
        return lax.ppermute(value, "atoms", [(a, a ^ distance) for a in range(atom_axis)])

    others = [swap(stats, d) for d in range(1, atom_axis)]
    run = local_atoms // 4
    piece = (3, run, 2 * local_frames)
    own, flat = pl.pallas_call(
        functools.partial(align_kernel, atom_axis),
        out_shape=(
            jax.ShapeDtypeStruct((2,) + piece, jnp.bfloat16),
            jax.ShapeDtypeStruct(x.shape, jnp.bfloat16),
        ),
        in_specs=[VMEM] * (atom_axis + 2),
        out_specs=(VMEM, VMEM),
        scratch_shapes=[pltpu.VMEM((LANES, LANES), jnp.float32)],
        compiler_params=params(8),
        name="polar_align",
    )(stats, *others, x, mean_structure)
    share = jax.ShapeDtypeStruct((local_frames, eigvecs.shape[2] // atom_axis), jnp.float32)
    shares = pl.pallas_call(
        project_kernel,
        out_shape=(share,) * atom_axis,
        in_specs=[SMEM, VMEM, VMEM],
        out_specs=(VMEM,) * atom_axis,
        scratch_shapes=[pltpu.VMEM((atom_axis,) + share.shape, jnp.float32)],
        compiler_params=params(8),
        name="project",
    )(me_a.astype(jnp.int32).reshape(1), flat, eigvecs)
    parts = [shares[0]] + [swap(shares[d], d) for d in range(1, atom_axis)]
    def pairs(source, target):
        return [
            (
                f * atom_axis + ((f // blocks) ^ source),
                f * atom_axis + ((f // blocks) ^ target),
            )
            for f in range(frame_axis)
        ]

    if blocks != 2 or frame_axis != 8:
        projections = sum(parts)
        spread_pairs = [pairs(0, d) for d in range(1, atom_axis)]
        covariance = long_axis_covariance(
            flat, half[0], role[0], block, spread_pairs, 1.0 / total_frames
        )
        return covariance, projections

    axes = ("frames", "atoms")

    def columns(slots):
        return pltpu.VMEM((slots, 3, local_frames, block), jnp.bfloat16)

    def kernel(body, out_shape, scalar, values, name, cost=None):
        single = not isinstance(out_shape, tuple)
        return pl.pallas_call(
            body,
            out_shape=out_shape,
            in_specs=[SMEM] + [VMEM] * len(values),
            out_specs=VMEM if single else (VMEM,) * len(out_shape),
            compiler_params=params(4),
            cost_estimate=cost,
            name=name,
        )(scalar, *[pinned(value, pltpu.VMEM) for value in values])

    def cross(cut):
        return [cut, lax.ppermute(cut, axes, pairs(0, 2))]

    def pass_on(values, role):
        slots = sum(value.shape[0] for value in values[::2])
        held = kernel(pass_on_kernel, columns(slots), role, values, "pass_on")
        return [held, lax.ppermute(held, axes, pairs(0, 1) + pairs(2, 3))]

    order = ring_order(frame_axis)
    forward = [(order[i], order[(i + 1) % frame_axis]) for i in range(frame_axis)]
    backward = [(b, a) for a, b in forward]

    def hop(up, down):
        return lax.ppermute(up, "frames", forward), lax.ppermute(down, "frames", backward)

    one = hop(own, own)
    crossed = cross(kernel(cut_kernel, columns(1), half, [own], "cut_columns"))
    cut_one = kernel(cut_kernel, columns(2), half, list(one), "cut_columns")
    two = hop(after(one[0], crossed[1], *parts), one[1])
    in_hbm = pass_on(crossed + cross(cut_one), role)
    split = pltpu.VMEM(piece, jnp.bfloat16)
    cut_two, *pieces = kernel(
        cut_split_kernel,
        (columns(2),) + (split,) * 4,
        half,
        list(two),
        "cut_columns",
    )
    crossed = cross(cut_two)
    up_a, down_b = hop(pieces[0], pieces[3])
    up_b, down_a = hop(pieces[1], pieces[2])
    far = hop(up_a, down_b)
    three = [up_a, up_b, down_a, down_b]
    cut_three = kernel(
        cut_pieces_kernel,
        columns(2),
        after(half, in_hbm[1]),
        three,
        "cut_columns",
    )
    long = pl.CostEstimate(flops=LONG, bytes_accessed=0, transcendentals=0)
    cut_four = kernel(
        cut_pieces_kernel, columns(1), after(half, crossed[1]), list(far), "cut_columns", long
    )
    in_vmem = pass_on(
        crossed + cross(cut_three) + cross(cut_four), after(role, in_hbm[1])
    )
    groups = ((3, True, (0, 1, 0, 1)), (5, False, (0, 1, 0, 1)))
    rows = [own, *one, *two, *three, *far]
    whole = 5
    covariance, projections = pl.pallas_call(
        functools.partial(
            covariance_kernel, frame_axis, whole, atom_axis, groups, 1.0 / total_frames
        ),
        out_shape=(jax.ShapeDtypeStruct((3, 3, local_atoms, block), jnp.float32), share),
        in_specs=[SMEM]
        + [VMEM] * len(rows)
        + [HBM] * len(in_hbm)
        + [VMEM] * len(in_vmem)
        + [HBM] * len(parts),
        out_specs=(ANY, VMEM),
        scratch_shapes=[
            pltpu.VMEM((2, 2 * run, total_frames), jnp.bfloat16),
            pltpu.VMEM((3, total_frames, block), jnp.bfloat16),
            pltpu.VMEM((2, 3, 2 * run, block), jnp.float32),
            pltpu.VMEM((atom_axis,) + share.shape, jnp.float32),
            pltpu.SemaphoreType.DMA((frame_axis,)),
            pltpu.SemaphoreType.DMA((2, 3)),
            pltpu.SemaphoreType.DMA((atom_axis,)),
        ],
        compiler_params=params(16),
        cost_estimate=pl.CostEstimate(
            flops=18 * local_atoms * block * total_frames,
            bytes_accessed=24 * MIB,
            transcendentals=0,
        ),
        name="covariance_tile",
    )(
        role,
        *[pinned(value, pltpu.VMEM) for value in rows],
        *[pinned(value, pltpu.HBM) for value in in_hbm],
        *[pinned(value, pltpu.VMEM) for value in in_vmem],
        *[pinned(value, pltpu.HBM) for value in parts],
    )
    return jnp.transpose(covariance, (0, 2, 1, 3)), projections


def solution(mesh):
    placed = (P("frames", None, "atoms"), P(None, "atoms"), P(None, "atoms", None))
    return jax.shard_map(
        per_device,
        mesh=mesh,
        in_specs=placed,
        out_specs=(P(None, "atoms", None, "frames"), P("frames", "atoms")),
        check_vma=False,
    )
```

```python
import functools

import jax
import jax.numpy as jnp
from jax import lax
from jax.experimental import pallas as pl
from jax.experimental.pallas import tpu as pltpu
from jax.sharding import PartitionSpec as P

POLAR = 6
LANES = 128
STATS = 24
VMEM = pl.BlockSpec(memory_space=pltpu.VMEM)
SMEM = pl.BlockSpec(memory_space=pltpu.SMEM)
HBM = pl.BlockSpec(memory_space=pltpu.HBM)
ANY = pl.BlockSpec(memory_space=pl.ANY)
MIB = 1024 * 1024
LONG = 4 * 10**9


def params(mib):
    return pltpu.CompilerParams(vmem_limit_bytes=mib * MIB)


def lane_mean(value):
    return jnp.sum(value, axis=1, keepdims=True) * (1.0 / value.shape[1])


def run_copies(copies):
    for copy in copies:
        copy.start()
    for copy in copies:
        copy.wait()


def stats_kernel(x_hbm, ref_hbm, out_ref, x_ref, ref_ref, sem):
    run_copies(
        [
            pltpu.make_async_copy(ref_hbm, ref_ref, sem.at[0]),
            pltpu.make_async_copy(x_hbm, x_ref, sem.at[1]),
        ]
    )
    values = []
    centred = []
    for i in range(3):
        x = x_ref[i]
        mean = lane_mean(x)
        values.append(mean)
        centred.append(x - mean)
    values.append(sum(jnp.sum(c * c, axis=1, keepdims=True) for c in centred))
    ref_mean = [lane_mean(ref_ref[j : j + 1, :]) for j in range(3)]
    ref_centred = [ref_ref[j : j + 1, :] - ref_mean[j] for j in range(3)]
    for i in range(3):
        for j in range(3):
            values.append(jnp.sum(centred[i] * ref_centred[j], axis=1, keepdims=True))
    values += ref_mean
    values.append(sum(jnp.sum(c * c, axis=1, keepdims=True) for c in ref_centred))
    shape = (x_ref.shape[1], LANES)
    lane = lax.broadcasted_iota(jnp.int32, shape, 1)
    out = jnp.zeros(shape, jnp.float32)
    for k, value in enumerate(values):
        out = jnp.where(lane == k, jnp.broadcast_to(value, shape), out)
    out_ref[...] = out.T[:STATS]


def align_kernel(parts, *refs):
    stats = refs[:parts]
    x_ref, ref_ref, piece_ref, flat_ref, turn = refs[parts:]
    local = x_ref.shape[2]
    rows = x_ref.shape[1]

    def row(at):
        return [s[at : at + 1, :] for s in stats]

    means = [row(i) for i in range(3)]
    ref_means = [row(13 + j) for j in range(3)]
    centre = [sum(m) * (1.0 / parts) for m in means]
    ref_centre = [sum(r) * (1.0 / parts) for r in ref_means]
    off = [[m - centre[i] for m in means[i]] for i in range(3)]
    ref_off = [[r - ref_centre[j] for r in ref_means[j]] for j in range(3)]
    spread = sum(row(3)) + local * sum(o * o for i in range(3) for o in off[i])
    ref_spread = sum(row(16)) + local * sum(o * o for j in range(3) for o in ref_off[j])
    scale = 1.0 / jnp.sqrt(spread * ref_spread + 1e-06)
    now = [
        [
            (sum(row(4 + 3 * i + j)) + local * sum(o * r for o, r in zip(off[i], ref_off[j])))
            * scale
            for j in range(3)
        ]
        for i in range(3)
    ]
    for _ in range(POLAR):
        gram = {}
        for i in range(3):
            for j in range(i, 3):
                gram[i, j] = sum(now[k][i] * now[k][j] for k in range(3))
                gram[j, i] = gram[i, j]
        left = [
            [(1.5 if k == j else 0.0) - 0.5 * gram[k, j] for j in range(3)] for k in range(3)
        ]
        now = [
            [sum(now[i][k] * left[k][j] for k in range(3)) for j in range(3)]
            for i in range(3)
        ]
    for k, value in enumerate(sum(now, []) + centre + ref_centre):
        turn[k : k + 1, :rows] = value
    turned = turn[...].T
    column = [turned[:rows, k : k + 1] for k in range(12)]
    centred = [x_ref[j] - column[9 + j] for j in range(3)]
    for i in range(3):
        target = ref_ref[i : i + 1, :] - turned[0:1, 12 + i : 13 + i]
        moved = sum(column[3 * j + i] * centred[j] for j in range(3)) - target
        flat_ref[i] = moved.astype(jnp.bfloat16)
        run = piece_ref.shape[2]
        for at in range(2):
            pair = [moved[:, (2 * at + k) * run : (2 * at + k + 1) * run] for k in range(2)]
            piece_ref[at, i] = jnp.concatenate(pair, axis=0).T.astype(jnp.bfloat16)


def project_kernel(me_ref, flat_ref, eig_ref, *refs):
    shares, cut = refs[:-1], refs[-1]
    total = sum(
        jnp.dot(flat_ref[c], eig_ref[c], preferred_element_type=jnp.float32) for c in range(3)
    )
    width = cut.shape[2]
    for k in range(len(shares)):
        cut[k] = total[:, k * width : (k + 1) * width]
    for k, share in enumerate(shares):
        share[...] = cut[lax.bitwise_xor(me_ref[0], k)]


def cut_columns(half_ref, halves, cols_ref):
    for half in range(2):

        @pl.when(half_ref[0] == half)
        def _(half=half):
            for k, pair in enumerate(halves):
                run, lanes = pair[half].shape[1:]
                for c in range(3):
                    turned = pair[half][c].astype(jnp.float32).T.astype(jnp.bfloat16)
                    cols_ref[k, c, :, :run] = turned[: lanes // 2]
                    cols_ref[k, c, :, run:] = turned[lanes // 2 :]


def cut_kernel(half_ref, *refs):
    cut_columns(half_ref, [(r.at[0], r.at[1]) for r in refs[:-1]], refs[-1])


def cut_split_kernel(half_ref, up_ref, down_ref, cols_ref, *refs):
    for k, shard in enumerate((up_ref, down_ref)):
        for at in range(2):
            refs[2 * k + at][...] = shard[at]
    cut_columns(half_ref, [(r.at[0], r.at[1]) for r in (up_ref, down_ref)], cols_ref)


def cut_pieces_kernel(half_ref, *refs):
    cut_columns(half_ref, list(zip(refs[:-1:2], refs[1:-1:2])), refs[-1])


def pass_on_kernel(role_ref, *refs):
    sources, out_ref = refs[:-1], refs[-1]
    for role in range(2):

        @pl.when((role_ref[0] != 0) == bool(role))
        def _(role=role):
            to = 0
            for source in sources[role::2]:
                out_ref[to : to + source.shape[0]] = source[...]
                to += source.shape[0]


def side_by_side(first, second):
    middle = first.shape[1] // 2
    left = jnp.concatenate([first[:, :middle], second[:, :middle]], axis=1)
    right = jnp.concatenate([first[:, middle:], second[:, middle:]], axis=1)
    return left, right


def covariance_kernel(slots, whole, roles, groups, scale, role_ref, *refs):
    shards, pieces, refs = refs[:whole], refs[whole : 2 * slots - whole], refs[2 * slots - whole :]
    arrays = []
    for _, _, holder in groups:
        count = max(holder) + 1
        arrays.append(refs[:count])
        refs = refs[count:]
    shares, refs = refs[:roles], refs[roles:]
    out_ref, proj_ref, left, right, done, held, col_sem, out_sem, share_sem = refs
    sums = [
        pltpu.make_async_copy(part, held.at[k], share_sem.at[k]) for k, part in enumerate(shares)
    ]
    for copy in sums:
        copy.start()
    depth = right.shape[1] // slots
    run = pieces[0].shape[1]

    def fetches(k, role, to):
        source = arrays[k][groups[k][2][role]]
        return [
            pltpu.make_async_copy(
                source.at[n],
                right.at[:, pl.ds(to + n * depth, depth), :],
                col_sem.at[to // depth + n],
            )
            for n in range(groups[k][0])
        ]

    def for_each_group(from_hbm, act):
        for role in range(roles):

            @pl.when(role_ref[0] == role)
            def _(role=role):
                to = 0
                for k, (count, in_hbm, _) in enumerate(groups):
                    if in_hbm == from_hbm:
                        act(k, role, to)
                    to += count * depth

    def start(k, role, to):
        for copy in fetches(k, role, to):
            copy.start()

    def wait(k, role, to):
        for copy in fetches(k, role, to):
            copy.wait()

    def load(k, role, to):
        source = arrays[k][groups[k][2][role]]
        for n in range(groups[k][0]):
            for d in range(3):
                right[d, to + n * depth : to + (n + 1) * depth, :] = source[n, d]

    def piece(slot, at, c):
        if slot < whole:
            return shards[slot][at, c]
        return pieces[2 * (slot - whole) + at][c]

    def assemble(c, at):
        for q in range(slots // 2):
            low, high = side_by_side(piece(2 * q, at, c), piece(2 * q + 1, at, c))
            left[at, :run, q * LANES : (q + 1) * LANES] = low
            left[at, run:, q * LANES : (q + 1) * LANES] = high

    for_each_group(True, start)
    for_each_group(False, load)
    assemble(0, 0)
    for_each_group(True, wait)
    for copy in sums:
        copy.wait()
    proj_ref[...] = sum(held[k] for k in range(roles))

    def write(c, at, d):
        return pltpu.make_async_copy(
            done.at[at, d],
            out_ref.at[c, d, pl.ds(at * 2 * run, 2 * run), :],
            out_sem.at[at, d],
        )

    @pl.loop(0, 3)
    def _(c):
        for at in range(2):

            @pl.when(c > 0)
            def _():
                for d in range(3):
                    write(c - 1, at, d).wait()

            assemble(jnp.minimum(c + at, 2), 1 - at)
            for d in range(3):
                done[at, d] = scale * jnp.dot(
                    left[at], right[d], preferred_element_type=jnp.float32
                )
                write(c, at, d).start()

    for at in range(2):
        for d in range(3):
            write(2, at, d).wait()


pinned = pltpu.with_memory_space_constraint


def after(value, *others):
    return lax.optimization_barrier((value,) + others)[0] if others else value


def ring_order(count):
    return list(range(0, count, 2)) + list(range(1, count, 2))[::-1]


def long_axis_covariance(flat, half, role, block, spread_pairs, scale):
    rows = lax.all_gather(flat, "frames", axis=1, tiled=True)
    cut = lax.dynamic_slice_in_dim(rows, half * block, block, axis=2)
    cols = jnp.where(role == 0, cut, jnp.zeros_like(cut))
    for d, pairs in enumerate(spread_pairs):
        sent = lax.ppermute(cut, ("frames", "atoms"), pairs)
        cols = jnp.where(role == d + 1, sent, cols)
    return scale * jnp.einsum(
        "cfp,dfq->cpdq", rows, cols, preferred_element_type=jnp.float32
    )


def per_device(frames, mean_structure, eigvecs):
    local_frames, _, local_atoms = frames.shape
    frame_axis = lax.axis_size("frames")
    atom_axis = lax.axis_size("atoms")
    total_frames = local_frames * frame_axis
    block = local_atoms * atom_axis // frame_axis
    blocks = frame_axis // atom_axis
    me_f = lax.axis_index("frames")
    me_a = lax.axis_index("atoms")
    half = lax.rem(me_f, blocks).astype(jnp.int32).reshape(1)
    owner = lax.div(me_f, blocks)
    role = lax.bitwise_xor(me_a, owner).astype(jnp.int32).reshape(1)
    x = pinned(jnp.transpose(frames, (1, 0, 2)), pltpu.HBM)
    mean_structure = pinned(mean_structure, pltpu.HBM)
    stats, x, mean_structure = pl.pallas_call(
        stats_kernel,
        out_shape=(
            pltpu.VMEM((STATS, local_frames), jnp.float32),
            pltpu.VMEM(x.shape, jnp.float32),
            pltpu.VMEM(mean_structure.shape, jnp.float32),
        ),
        in_specs=[HBM, HBM],
        out_specs=(VMEM, VMEM, VMEM),
        scratch_shapes=[pltpu.SemaphoreType.DMA((2,))],
        compiler_params=params(8),
        name="local_moments",
    )(x, mean_structure)
    def swap(value, distance):
        return lax.ppermute(value, "atoms", [(a, a ^ distance) for a in range(atom_axis)])

    others = [swap(stats, d) for d in range(1, atom_axis)]
    run = local_atoms // 4
    piece = (3, run, 2 * local_frames)
    own, flat = pl.pallas_call(
        functools.partial(align_kernel, atom_axis),
        out_shape=(
            jax.ShapeDtypeStruct((2,) + piece, jnp.bfloat16),
            jax.ShapeDtypeStruct(x.shape, jnp.bfloat16),
        ),
        in_specs=[VMEM] * (atom_axis + 2),
        out_specs=(VMEM, VMEM),
        scratch_shapes=[pltpu.VMEM((LANES, LANES), jnp.float32)],
        compiler_params=params(8),
        name="polar_align",
    )(stats, *others, x, mean_structure)
    share = jax.ShapeDtypeStruct((local_frames, eigvecs.shape[2] // atom_axis), jnp.float32)
    shares = pl.pallas_call(
        project_kernel,
        out_shape=(share,) * atom_axis,
        in_specs=[SMEM, VMEM, VMEM],
        out_specs=(VMEM,) * atom_axis,
        scratch_shapes=[pltpu.VMEM((atom_axis,) + share.shape, jnp.float32)],
        compiler_params=params(8),
        name="project",
    )(me_a.astype(jnp.int32).reshape(1), flat, eigvecs)
    parts = [shares[0]] + [swap(shares[d], d) for d in range(1, atom_axis)]
    def pairs(source, target):
        return [
            (
                f * atom_axis + ((f // blocks) ^ source),
                f * atom_axis + ((f // blocks) ^ target),
            )
            for f in range(frame_axis)
        ]

    if blocks != 2 or frame_axis != 8:
        projections = sum(parts)
        spread_pairs = [pairs(0, d) for d in range(1, atom_axis)]
        covariance = long_axis_covariance(
            flat, half[0], role[0], block, spread_pairs, 1.0 / total_frames
        )
        return covariance, projections

    axes = ("frames", "atoms")

    def columns(slots):
        return pltpu.VMEM((slots, 3, local_frames, block), jnp.bfloat16)

    def kernel(body, out_shape, scalar, values, name, cost=None):
        single = not isinstance(out_shape, tuple)
        return pl.pallas_call(
            body,
            out_shape=out_shape,
            in_specs=[SMEM] + [VMEM] * len(values),
            out_specs=VMEM if single else (VMEM,) * len(out_shape),
            compiler_params=params(4),
            cost_estimate=cost,
            name=name,
        )(scalar, *[pinned(value, pltpu.VMEM) for value in values])

    def cross(cut):
        return [cut, lax.ppermute(cut, axes, pairs(0, 2))]

    def pass_on(values, role):
        slots = sum(value.shape[0] for value in values[::2])
        held = kernel(pass_on_kernel, columns(slots), role, values, "pass_on")
        return [held, lax.ppermute(held, axes, pairs(0, 1) + pairs(2, 3))]

    order = ring_order(frame_axis)
    forward = [(order[i], order[(i + 1) % frame_axis]) for i in range(frame_axis)]
    backward = [(b, a) for a, b in forward]

    def hop(up, down):
        return lax.ppermute(up, "frames", forward), lax.ppermute(down, "frames", backward)

    one = hop(own, own)
    crossed = cross(kernel(cut_kernel, columns(1), half, [own], "cut_columns"))
    in_hbm = pass_on(crossed, role)
    cut_one = kernel(cut_kernel, columns(2), half, list(one), "cut_columns")
    two = hop(after(one[0], crossed[1]), one[1])
    crossed = cross(cut_one)
    split = pltpu.VMEM(piece, jnp.bfloat16)
    cut_two, *pieces = kernel(
        cut_split_kernel,
        (columns(2),) + (split,) * 4,
        after(half, in_hbm[1], *parts),
        list(two),
        "cut_columns",
    )
    crossed += cross(cut_two)
    up_a, down_b = hop(pieces[0], pieces[3])
    up_b, down_a = hop(pieces[1], pieces[2])
    far = hop(up_a, down_b)
    three = [up_a, up_b, down_a, down_b]
    cut_three = kernel(cut_pieces_kernel, columns(2), after(half, crossed[1]), three, "cut_columns")
    long = pl.CostEstimate(flops=LONG, bytes_accessed=0, transcendentals=0)
    cut_four = kernel(
        cut_pieces_kernel, columns(1), half, list(far), "cut_columns", long
    )
    in_vmem = pass_on(crossed + cross(cut_three) + cross(cut_four), role)
    groups = ((1, True, (0, 1, 0, 1)), (7, False, (0, 1, 0, 1)))
    rows = [own, *one, *two, *three, *far]
    whole = 5
    covariance, projections = pl.pallas_call(
        functools.partial(
            covariance_kernel, frame_axis, whole, atom_axis, groups, 1.0 / total_frames
        ),
        out_shape=(jax.ShapeDtypeStruct((3, 3, local_atoms, block), jnp.float32), share),
        in_specs=[SMEM]
        + [VMEM] * len(rows)
        + [HBM] * len(in_hbm)
        + [VMEM] * len(in_vmem)
        + [HBM] * len(parts),
        out_specs=(ANY, VMEM),
        scratch_shapes=[
            pltpu.VMEM((2, 2 * run, total_frames), jnp.bfloat16),
            pltpu.VMEM((3, total_frames, block), jnp.bfloat16),
            pltpu.VMEM((2, 3, 2 * run, block), jnp.float32),
            pltpu.VMEM((atom_axis,) + share.shape, jnp.float32),
            pltpu.SemaphoreType.DMA((frame_axis,)),
            pltpu.SemaphoreType.DMA((2, 3)),
            pltpu.SemaphoreType.DMA((atom_axis,)),
        ],
        compiler_params=params(16),
        cost_estimate=pl.CostEstimate(
            flops=18 * local_atoms * block * total_frames,
            bytes_accessed=24 * MIB,
            transcendentals=0,
        ),
        name="covariance_tile",
    )(
        role,
        *[pinned(value, pltpu.VMEM) for value in rows],
        *[pinned(value, pltpu.HBM) for value in in_hbm],
        *[pinned(value, pltpu.VMEM) for value in in_vmem],
        *[pinned(value, pltpu.HBM) for value in parts],
    )
    return jnp.transpose(covariance, (0, 2, 1, 3)), projections


def solution(mesh):
    placed = (P("frames", None, "atoms"), P(None, "atoms"), P(None, "atoms", None))
    return jax.shard_map(
        per_device,
        mesh=mesh,
        in_specs=placed,
        out_specs=(P(None, "atoms", None, "frames"), P("frames", "atoms")),
        check_vma=False,
    )
```

```python
import functools

import jax
import jax.numpy as jnp
from jax import lax
from jax.experimental import pallas as pl
from jax.experimental.pallas import tpu as pltpu
from jax.sharding import PartitionSpec as P

POLAR = 6
LANES = 128
STATS = 24
VMEM = pl.BlockSpec(memory_space=pltpu.VMEM)
SMEM = pl.BlockSpec(memory_space=pltpu.SMEM)
HBM = pl.BlockSpec(memory_space=pltpu.HBM)
ANY = pl.BlockSpec(memory_space=pl.ANY)
MIB = 1024 * 1024


def params(mib):
    return pltpu.CompilerParams(vmem_limit_bytes=mib * MIB)


def lane_mean(value):
    return jnp.sum(value, axis=1, keepdims=True) * (1.0 / value.shape[1])


def run_copies(copies):
    for copy in copies:
        copy.start()
    for copy in copies:
        copy.wait()


def stats_kernel(x_hbm, ref_hbm, out_ref, x_ref, ref_ref, sem):
    run_copies(
        [
            pltpu.make_async_copy(ref_hbm, ref_ref, sem.at[0]),
            pltpu.make_async_copy(x_hbm, x_ref, sem.at[1]),
        ]
    )
    values = []
    centred = []
    for i in range(3):
        x = x_ref[i]
        mean = lane_mean(x)
        values.append(mean)
        centred.append(x - mean)
    values.append(sum(jnp.sum(c * c, axis=1, keepdims=True) for c in centred))
    ref_mean = [lane_mean(ref_ref[j : j + 1, :]) for j in range(3)]
    ref_centred = [ref_ref[j : j + 1, :] - ref_mean[j] for j in range(3)]
    for i in range(3):
        for j in range(3):
            values.append(jnp.sum(centred[i] * ref_centred[j], axis=1, keepdims=True))
    values += ref_mean
    values.append(sum(jnp.sum(c * c, axis=1, keepdims=True) for c in ref_centred))
    shape = (x_ref.shape[1], LANES)
    lane = lax.broadcasted_iota(jnp.int32, shape, 1)
    out = jnp.zeros(shape, jnp.float32)
    for k, value in enumerate(values):
        out = jnp.where(lane == k, jnp.broadcast_to(value, shape), out)
    out_ref[...] = out.T[:STATS]


def align_kernel(parts, *refs):
    stats = refs[:parts]
    x_ref, ref_ref, piece_ref, flat_ref, turn = refs[parts:]
    local = x_ref.shape[2]
    rows = x_ref.shape[1]

    def row(at):
        return [s[at : at + 1, :] for s in stats]

    means = [row(i) for i in range(3)]
    ref_means = [row(13 + j) for j in range(3)]
    centre = [sum(m) * (1.0 / parts) for m in means]
    ref_centre = [sum(r) * (1.0 / parts) for r in ref_means]
    off = [[m - centre[i] for m in means[i]] for i in range(3)]
    ref_off = [[r - ref_centre[j] for r in ref_means[j]] for j in range(3)]
    spread = sum(row(3)) + local * sum(o * o for i in range(3) for o in off[i])
    ref_spread = sum(row(16)) + local * sum(o * o for j in range(3) for o in ref_off[j])
    scale = 1.0 / jnp.sqrt(spread * ref_spread + 1e-06)
    now = [
        [
            (sum(row(4 + 3 * i + j)) + local * sum(o * r for o, r in zip(off[i], ref_off[j])))
            * scale
            for j in range(3)
        ]
        for i in range(3)
    ]
    for _ in range(POLAR):
        gram = {}
        for i in range(3):
            for j in range(i, 3):
                gram[i, j] = sum(now[k][i] * now[k][j] for k in range(3))
                gram[j, i] = gram[i, j]
        left = [
            [(1.5 if k == j else 0.0) - 0.5 * gram[k, j] for j in range(3)] for k in range(3)
        ]
        now = [
            [sum(now[i][k] * left[k][j] for k in range(3)) for j in range(3)]
            for i in range(3)
        ]
    for k, value in enumerate(sum(now, []) + centre + ref_centre):
        turn[k : k + 1, :rows] = value
    turned = turn[...].T
    column = [turned[:rows, k : k + 1] for k in range(12)]
    centred = [x_ref[j] - column[9 + j] for j in range(3)]
    for i in range(3):
        target = ref_ref[i : i + 1, :] - turned[0:1, 12 + i : 13 + i]
        moved = sum(column[3 * j + i] * centred[j] for j in range(3)) - target
        flat_ref[i] = moved.astype(jnp.bfloat16)
        run = piece_ref.shape[2]
        for at in range(2):
            pair = [moved[:, (2 * at + k) * run : (2 * at + k + 1) * run] for k in range(2)]
            piece_ref[at, i] = jnp.concatenate(pair, axis=0).T.astype(jnp.bfloat16)


def project_kernel(me_ref, flat_ref, eig_ref, *refs):
    shares, cut = refs[:-1], refs[-1]
    total = sum(
        jnp.dot(flat_ref[c], eig_ref[c], preferred_element_type=jnp.float32) for c in range(3)
    )
    width = cut.shape[2]
    for k in range(len(shares)):
        cut[k] = total[:, k * width : (k + 1) * width]
    for k, share in enumerate(shares):
        share[...] = cut[lax.bitwise_xor(me_ref[0], k)]


def sum_kernel(*refs):
    refs[-1][...] = sum(ref[...] for ref in refs[:-1])


def cut_columns(half_ref, halves, cols_ref):
    for half in range(2):

        @pl.when(half_ref[0] == half)
        def _(half=half):
            for k, pair in enumerate(halves):
                run, lanes = pair[half].shape[1:]
                for c in range(3):
                    turned = pair[half][c].astype(jnp.float32).T.astype(jnp.bfloat16)
                    cols_ref[k, c, :, :run] = turned[: lanes // 2]
                    cols_ref[k, c, :, run:] = turned[lanes // 2 :]


def cut_kernel(half_ref, *refs):
    cut_columns(half_ref, [(r.at[0], r.at[1]) for r in refs[:-1]], refs[-1])


def cut_last_kernel(half_ref, up_ref, down_ref, cols_ref, up_half, down_half):
    up_half[...] = up_ref[0]
    down_half[...] = down_ref[1]
    cut_columns(half_ref, [(r.at[0], r.at[1]) for r in (up_ref, down_ref)], cols_ref)


def cut_far_kernel(half_ref, up_half, down_half, cols_ref):
    cut_columns(half_ref, [(up_half, down_half)], cols_ref)


def pass_on_kernel(role_ref, *refs):
    sources, out_ref = refs[:-1], refs[-1]
    for role in range(2):

        @pl.when((role_ref[0] != 0) == bool(role))
        def _(role=role):
            to = 0
            for source in sources[role::2]:
                out_ref[to : to + source.shape[0]] = source[...]
                to += source.shape[0]


def side_by_side(first, second):
    middle = first.shape[1] // 2
    left = jnp.concatenate([first[:, :middle], second[:, :middle]], axis=1)
    right = jnp.concatenate([first[:, middle:], second[:, middle:]], axis=1)
    return left, right


def covariance_kernel(slots, roles, groups, scale, role_ref, *refs):
    shards, up_half, down_half = refs[: slots - 1], refs[slots - 1], refs[slots]
    refs = refs[slots + 1 :]
    arrays = []
    for _, _, holder in groups:
        count = max(holder) + 1
        arrays.append(refs[:count])
        refs = refs[count:]
    out_ref, left, right, done, col_sem, out_sem = refs
    depth = right.shape[1] // slots
    run = up_half.shape[1]

    def fetches(k, role, to):
        source = arrays[k][groups[k][2][role]]
        return [
            pltpu.make_async_copy(
                source.at[n],
                right.at[:, pl.ds(to + n * depth, depth), :],
                col_sem.at[to // depth + n],
            )
            for n in range(groups[k][0])
        ]

    def for_each_group(from_hbm, act):
        for role in range(roles):

            @pl.when(role_ref[0] == role)
            def _(role=role):
                to = 0
                for k, (count, in_hbm, _) in enumerate(groups):
                    if in_hbm == from_hbm:
                        act(k, role, to)
                    to += count * depth

    def start(k, role, to):
        for copy in fetches(k, role, to):
            copy.start()

    def wait(k, role, to):
        for copy in fetches(k, role, to):
            copy.wait()

    def load(k, role, to):
        source = arrays[k][groups[k][2][role]]
        for n in range(groups[k][0]):
            for d in range(3):
                right[d, to + n * depth : to + (n + 1) * depth, :] = source[n, d]

    def piece(slot, at, c):
        if slot < slots - 1:
            return shards[slot][at, c]
        return (up_half, down_half)[at][c]

    def assemble(c, at):
        for q in range(slots // 2):
            low, high = side_by_side(piece(2 * q, at, c), piece(2 * q + 1, at, c))
            left[at, :run, q * LANES : (q + 1) * LANES] = low
            left[at, run:, q * LANES : (q + 1) * LANES] = high

    for_each_group(True, start)
    for_each_group(False, load)
    assemble(0, 0)
    for_each_group(True, wait)

    def write(c, at, d):
        return pltpu.make_async_copy(
            done.at[at, d],
            out_ref.at[c, d, pl.ds(at * 2 * run, 2 * run), :],
            out_sem.at[at, d],
        )

    @pl.loop(0, 3)
    def _(c):
        for at in range(2):

            @pl.when(c > 0)
            def _():
                for d in range(3):
                    write(c - 1, at, d).wait()

            assemble(jnp.minimum(c + at, 2), 1 - at)
            for d in range(3):
                done[at, d] = scale * jnp.dot(
                    left[at], right[d], preferred_element_type=jnp.float32
                )
                write(c, at, d).start()

    for at in range(2):
        for d in range(3):
            write(2, at, d).wait()


pinned = pltpu.with_memory_space_constraint


def after(value, *others):
    return lax.optimization_barrier((value,) + others)[0] if others else value


def ring_order(count):
    return list(range(0, count, 2)) + list(range(1, count, 2))[::-1]


def long_axis_covariance(flat, half, role, block, spread_pairs, scale):
    rows = lax.all_gather(flat, "frames", axis=1, tiled=True)
    cut = lax.dynamic_slice_in_dim(rows, half * block, block, axis=2)
    cols = jnp.where(role == 0, cut, jnp.zeros_like(cut))
    for d, pairs in enumerate(spread_pairs):
        sent = lax.ppermute(cut, ("frames", "atoms"), pairs)
        cols = jnp.where(role == d + 1, sent, cols)
    return scale * jnp.einsum(
        "cfp,dfq->cpdq", rows, cols, preferred_element_type=jnp.float32
    )


def per_device(frames, mean_structure, eigvecs):
    local_frames, _, local_atoms = frames.shape
    frame_axis = lax.axis_size("frames")
    atom_axis = lax.axis_size("atoms")
    total_frames = local_frames * frame_axis
    block = local_atoms * atom_axis // frame_axis
    blocks = frame_axis // atom_axis
    me_f = lax.axis_index("frames")
    me_a = lax.axis_index("atoms")
    half = lax.rem(me_f, blocks).astype(jnp.int32).reshape(1)
    owner = lax.div(me_f, blocks)
    role = lax.bitwise_xor(me_a, owner).astype(jnp.int32).reshape(1)
    x = pinned(jnp.transpose(frames, (1, 0, 2)), pltpu.HBM)
    mean_structure = pinned(mean_structure, pltpu.HBM)
    stats, x, mean_structure = pl.pallas_call(
        stats_kernel,
        out_shape=(
            pltpu.VMEM((STATS, local_frames), jnp.float32),
            pltpu.VMEM(x.shape, jnp.float32),
            pltpu.VMEM(mean_structure.shape, jnp.float32),
        ),
        in_specs=[HBM, HBM],
        out_specs=(VMEM, VMEM, VMEM),
        scratch_shapes=[pltpu.SemaphoreType.DMA((2,))],
        compiler_params=params(8),
        name="local_moments",
    )(x, mean_structure)
    def swap(value, distance):
        return lax.ppermute(value, "atoms", [(a, a ^ distance) for a in range(atom_axis)])

    others = [swap(stats, d) for d in range(1, atom_axis)]
    run = local_atoms // 4
    piece = (3, run, 2 * local_frames)
    own, flat = pl.pallas_call(
        functools.partial(align_kernel, atom_axis),
        out_shape=(
            jax.ShapeDtypeStruct((2,) + piece, jnp.bfloat16),
            jax.ShapeDtypeStruct(x.shape, jnp.bfloat16),
        ),
        in_specs=[VMEM] * (atom_axis + 2),
        out_specs=(VMEM, VMEM),
        scratch_shapes=[pltpu.VMEM((LANES, LANES), jnp.float32)],
        compiler_params=params(8),
        name="polar_align",
    )(stats, *others, x, mean_structure)
    share = jax.ShapeDtypeStruct((local_frames, eigvecs.shape[2] // atom_axis), jnp.float32)
    shares = pl.pallas_call(
        project_kernel,
        out_shape=(share,) * atom_axis,
        in_specs=[SMEM, VMEM, VMEM],
        out_specs=(VMEM,) * atom_axis,
        scratch_shapes=[pltpu.VMEM((atom_axis,) + share.shape, jnp.float32)],
        compiler_params=params(8),
        name="project",
    )(me_a.astype(jnp.int32).reshape(1), flat, eigvecs)
    parts = [shares[0]] + [swap(shares[d], d) for d in range(1, atom_axis)]
    projections = pl.pallas_call(
        sum_kernel,
        out_shape=share,
        in_specs=[VMEM] * atom_axis,
        out_specs=VMEM,
        compiler_params=params(4),
        name="sum_shares",
    )(*parts)

    def pairs(source, target):
        return [
            (
                f * atom_axis + ((f // blocks) ^ source),
                f * atom_axis + ((f // blocks) ^ target),
            )
            for f in range(frame_axis)
        ]

    if blocks != 2 or frame_axis != 8:
        spread_pairs = [pairs(0, d) for d in range(1, atom_axis)]
        covariance = long_axis_covariance(
            flat, half[0], role[0], block, spread_pairs, 1.0 / total_frames
        )
        return covariance, projections

    axes = ("frames", "atoms")

    def columns(slots):
        return pltpu.VMEM((slots, 3, local_frames, block), jnp.bfloat16)

    def kernel(body, out_shape, scalar, values, name):
        single = not isinstance(out_shape, tuple)
        return pl.pallas_call(
            body,
            out_shape=out_shape,
            in_specs=[SMEM] + [VMEM] * len(values),
            out_specs=VMEM if single else (VMEM,) * len(out_shape),
            compiler_params=params(4),
            name=name,
        )(scalar, *[pinned(value, pltpu.VMEM) for value in values])

    def cross(cut):
        return [cut, lax.ppermute(cut, axes, pairs(0, 2) + pairs(2, 0))]

    def pass_on(values, role):
        slots = sum(value.shape[0] for value in values[::2])
        held = kernel(pass_on_kernel, columns(slots), role, values, "pass_on")
        return [held, swap(held, 1)]

    order = ring_order(frame_axis)
    forward = [(order[i], order[(i + 1) % frame_axis]) for i in range(frame_axis)]
    backward = [(b, a) for a, b in forward]

    def hop(up, down):
        return lax.ppermute(up, "frames", forward), lax.ppermute(down, "frames", backward)

    one = hop(own, own)
    crossed = cross(kernel(cut_kernel, columns(1), half, [own], "cut_columns"))
    cut_one = kernel(cut_kernel, columns(2), half, list(one), "cut_columns")
    two = hop(after(one[0], crossed[1], *parts), one[1])
    in_hbm = pass_on(crossed + cross(cut_one), role)
    cut_two = kernel(
        cut_kernel, columns(2), after(half, projections), list(two), "cut_columns"
    )
    three = hop(*two)
    crossed = cross(cut_two)
    half_shard = pltpu.VMEM(piece, jnp.bfloat16)
    cut_three, *halves = kernel(
        cut_last_kernel,
        (columns(2), half_shard, half_shard),
        after(half, in_hbm[0]),
        list(three),
        "cut_columns",
    )
    far = hop(*halves)
    cut_four = kernel(
        cut_far_kernel, columns(1), after(half, crossed[1]), list(far), "cut_columns"
    )
    in_vmem = pass_on(
        crossed + cross(cut_three) + cross(cut_four), after(role, in_hbm[1])
    )
    groups = ((3, True, (0, 1, 0, 1)), (5, False, (0, 1, 0, 1)))
    rows = [own, *one, *two, *three, *far]
    covariance = pl.pallas_call(
        functools.partial(
            covariance_kernel, frame_axis, atom_axis, groups, 1.0 / total_frames
        ),
        out_shape=jax.ShapeDtypeStruct((3, 3, local_atoms, block), jnp.float32),
        in_specs=[SMEM]
        + [VMEM] * len(rows)
        + [HBM] * len(in_hbm)
        + [VMEM] * len(in_vmem),
        out_specs=ANY,
        scratch_shapes=[
            pltpu.VMEM((2, 2 * run, total_frames), jnp.bfloat16),
            pltpu.VMEM((3, total_frames, block), jnp.bfloat16),
            pltpu.VMEM((2, 3, 2 * run, block), jnp.float32),
            pltpu.SemaphoreType.DMA((frame_axis,)),
            pltpu.SemaphoreType.DMA((2, 3)),
        ],
        compiler_params=params(16),
        cost_estimate=pl.CostEstimate(
            flops=18 * local_atoms * block * total_frames,
            bytes_accessed=24 * MIB,
            transcendentals=0,
        ),
        name="covariance_tile",
    )(
        role,
        *[pinned(value, pltpu.VMEM) for value in rows],
        *[pinned(value, pltpu.HBM) for value in in_hbm],
        *[pinned(value, pltpu.VMEM) for value in in_vmem],
    )
    return jnp.transpose(covariance, (0, 2, 1, 3)), projections


def solution(mesh):
    placed = (P("frames", None, "atoms"), P(None, "atoms"), P(None, "atoms", None))
    return jax.shard_map(
        per_device,
        mesh=mesh,
        in_specs=placed,
        out_specs=(P(None, "atoms", None, "frames"), P("frames", "atoms")),
        check_vma=False,
    )
```

```python
import functools

import jax
import jax.numpy as jnp
from jax import lax
from jax.experimental import pallas as pl
from jax.experimental.pallas import tpu as pltpu
from jax.sharding import PartitionSpec as P

POLAR = 6
LANES = 128
STATS = 24
VMEM = pl.BlockSpec(memory_space=pltpu.VMEM)
SMEM = pl.BlockSpec(memory_space=pltpu.SMEM)
HBM = pl.BlockSpec(memory_space=pltpu.HBM)
ANY = pl.BlockSpec(memory_space=pl.ANY)
MIB = 1024 * 1024


def params(mib):
    return pltpu.CompilerParams(vmem_limit_bytes=mib * MIB)


def lane_mean(value):
    return jnp.sum(value, axis=1, keepdims=True) * (1.0 / value.shape[1])


def run_copies(copies):
    for copy in copies:
        copy.start()
    for copy in copies:
        copy.wait()


def stats_kernel(x_hbm, ref_hbm, out_ref, x_ref, ref_ref, sem):
    run_copies(
        [
            pltpu.make_async_copy(ref_hbm, ref_ref, sem.at[0]),
            pltpu.make_async_copy(x_hbm, x_ref, sem.at[1]),
        ]
    )
    values = []
    centred = []
    for i in range(3):
        x = x_ref[i]
        mean = lane_mean(x)
        values.append(mean)
        centred.append(x - mean)
    values.append(sum(jnp.sum(c * c, axis=1, keepdims=True) for c in centred))
    ref_mean = [lane_mean(ref_ref[j : j + 1, :]) for j in range(3)]
    ref_centred = [ref_ref[j : j + 1, :] - ref_mean[j] for j in range(3)]
    for i in range(3):
        for j in range(3):
            values.append(jnp.sum(centred[i] * ref_centred[j], axis=1, keepdims=True))
    values += ref_mean
    values.append(sum(jnp.sum(c * c, axis=1, keepdims=True) for c in ref_centred))
    shape = (x_ref.shape[1], LANES)
    lane = lax.broadcasted_iota(jnp.int32, shape, 1)
    out = jnp.zeros(shape, jnp.float32)
    for k, value in enumerate(values):
        out = jnp.where(lane == k, jnp.broadcast_to(value, shape), out)
    out_ref[...] = out.T[:STATS]


def align_kernel(parts, *refs):
    stats = refs[:parts]
    x_ref, ref_ref, piece_ref, flat_ref, turn = refs[parts:]
    local = x_ref.shape[2]
    rows = x_ref.shape[1]

    def row(at):
        return [s[at : at + 1, :] for s in stats]

    means = [row(i) for i in range(3)]
    ref_means = [row(13 + j) for j in range(3)]
    centre = [sum(m) * (1.0 / parts) for m in means]
    ref_centre = [sum(r) * (1.0 / parts) for r in ref_means]
    off = [[m - centre[i] for m in means[i]] for i in range(3)]
    ref_off = [[r - ref_centre[j] for r in ref_means[j]] for j in range(3)]
    spread = sum(row(3)) + local * sum(o * o for i in range(3) for o in off[i])
    ref_spread = sum(row(16)) + local * sum(o * o for j in range(3) for o in ref_off[j])
    scale = 1.0 / jnp.sqrt(spread * ref_spread + 1e-06)
    now = [
        [
            (sum(row(4 + 3 * i + j)) + local * sum(o * r for o, r in zip(off[i], ref_off[j])))
            * scale
            for j in range(3)
        ]
        for i in range(3)
    ]
    for _ in range(POLAR):
        gram = {}
        for i in range(3):
            for j in range(i, 3):
                gram[i, j] = sum(now[k][i] * now[k][j] for k in range(3))
                gram[j, i] = gram[i, j]
        left = [
            [(1.5 if k == j else 0.0) - 0.5 * gram[k, j] for j in range(3)] for k in range(3)
        ]
        now = [
            [sum(now[i][k] * left[k][j] for k in range(3)) for j in range(3)]
            for i in range(3)
        ]
    for k, value in enumerate(sum(now, []) + centre + ref_centre):
        turn[k : k + 1, :rows] = value
    turned = turn[...].T
    column = [turned[:rows, k : k + 1] for k in range(12)]
    centred = [x_ref[j] - column[9 + j] for j in range(3)]
    for i in range(3):
        target = ref_ref[i : i + 1, :] - turned[0:1, 12 + i : 13 + i]
        moved = sum(column[3 * j + i] * centred[j] for j in range(3)) - target
        flat_ref[i] = moved.astype(jnp.bfloat16)
        run = piece_ref.shape[2]
        for at in range(2):
            pair = [moved[:, (2 * at + k) * run : (2 * at + k + 1) * run] for k in range(2)]
            piece_ref[at, i] = jnp.concatenate(pair, axis=0).T.astype(jnp.bfloat16)


def project_kernel(me_ref, flat_ref, eig_ref, *refs):
    shares, cut = refs[:-1], refs[-1]
    total = sum(
        jnp.dot(flat_ref[c], eig_ref[c], preferred_element_type=jnp.float32) for c in range(3)
    )
    width = cut.shape[2]
    for k in range(len(shares)):
        cut[k] = total[:, k * width : (k + 1) * width]
    for k, share in enumerate(shares):
        share[...] = cut[lax.bitwise_xor(me_ref[0], k)]


def sum_kernel(*refs):
    refs[-1][...] = sum(ref[...] for ref in refs[:-1])


def cut_columns(half_ref, halves, cols_ref):
    for half in range(2):

        @pl.when(half_ref[0] == half)
        def _(half=half):
            for k, pair in enumerate(halves):
                run, lanes = pair[half].shape[1:]
                for c in range(3):
                    turned = pair[half][c].astype(jnp.float32).T.astype(jnp.bfloat16)
                    cols_ref[k, c, :, :run] = turned[: lanes // 2]
                    cols_ref[k, c, :, run:] = turned[lanes // 2 :]


def cut_kernel(half_ref, *refs):
    cut_columns(half_ref, [(r.at[0], r.at[1]) for r in refs[:-1]], refs[-1])


def cut_last_kernel(half_ref, up_ref, down_ref, cols_ref, up_half, down_half):
    up_half[...] = up_ref[0]
    down_half[...] = down_ref[1]
    cut_columns(half_ref, [(r.at[0], r.at[1]) for r in (up_ref, down_ref)], cols_ref)


def cut_far_kernel(half_ref, up_half, down_half, cols_ref):
    cut_columns(half_ref, [(up_half, down_half)], cols_ref)


def pass_on_kernel(role_ref, *refs):
    sources, out_ref = refs[:-1], refs[-1]
    for role in range(2):

        @pl.when((role_ref[0] != 0) == bool(role))
        def _(role=role):
            to = 0
            for source in sources[role::2]:
                out_ref[to : to + source.shape[0]] = source[...]
                to += source.shape[0]


def side_by_side(first, second):
    middle = first.shape[1] // 2
    left = jnp.concatenate([first[:, :middle], second[:, :middle]], axis=1)
    right = jnp.concatenate([first[:, middle:], second[:, middle:]], axis=1)
    return left, right


def covariance_kernel(slots, roles, groups, scale, role_ref, *refs):
    shards, up_half, down_half = refs[: slots - 1], refs[slots - 1], refs[slots]
    refs = refs[slots + 1 :]
    arrays = []
    for _, _, holder in groups:
        count = max(holder) + 1
        arrays.append(refs[:count])
        refs = refs[count:]
    out_ref, left, right, done, col_sem, out_sem = refs
    depth = right.shape[1] // slots
    run = up_half.shape[1]

    def fetches(k, role, to):
        source = arrays[k][groups[k][2][role]]
        return [
            pltpu.make_async_copy(
                source.at[n],
                right.at[:, pl.ds(to + n * depth, depth), :],
                col_sem.at[to // depth + n],
            )
            for n in range(groups[k][0])
        ]

    def for_each_group(from_hbm, act):
        for role in range(roles):

            @pl.when(role_ref[0] == role)
            def _(role=role):
                to = 0
                for k, (count, in_hbm, _) in enumerate(groups):
                    if in_hbm == from_hbm:
                        act(k, role, to)
                    to += count * depth

    def start(k, role, to):
        for copy in fetches(k, role, to):
            copy.start()

    def wait(k, role, to):
        for copy in fetches(k, role, to):
            copy.wait()

    def load(k, role, to):
        source = arrays[k][groups[k][2][role]]
        for n in range(groups[k][0]):
            for d in range(3):
                right[d, to + n * depth : to + (n + 1) * depth, :] = source[n, d]

    def piece(slot, at, c):
        if slot < slots - 1:
            return shards[slot][at, c]
        return (up_half, down_half)[at][c]

    def assemble(c, at):
        for q in range(slots // 2):
            low, high = side_by_side(piece(2 * q, at, c), piece(2 * q + 1, at, c))
            left[at, :run, q * LANES : (q + 1) * LANES] = low
            left[at, run:, q * LANES : (q + 1) * LANES] = high

    for_each_group(True, start)
    for_each_group(False, load)
    assemble(0, 0)
    for_each_group(True, wait)

    def write(c, at, d):
        return pltpu.make_async_copy(
            done.at[at, d],
            out_ref.at[c, d, pl.ds(at * 2 * run, 2 * run), :],
            out_sem.at[at, d],
        )

    @pl.loop(0, 3)
    def _(c):
        for at in range(2):

            @pl.when(c > 0)
            def _():
                for d in range(3):
                    write(c - 1, at, d).wait()

            assemble(jnp.minimum(c + at, 2), 1 - at)
            for d in range(3):
                done[at, d] = scale * jnp.dot(
                    left[at], right[d], preferred_element_type=jnp.float32
                )
                write(c, at, d).start()

    for at in range(2):
        for d in range(3):
            write(2, at, d).wait()


pinned = pltpu.with_memory_space_constraint


def after(value, *others):
    return lax.optimization_barrier((value,) + others)[0] if others else value


def ring_order(count):
    return list(range(0, count, 2)) + list(range(1, count, 2))[::-1]


def long_axis_covariance(flat, half, role, block, spread_pairs, scale):
    rows = lax.all_gather(flat, "frames", axis=1, tiled=True)
    cut = lax.dynamic_slice_in_dim(rows, half * block, block, axis=2)
    cols = jnp.where(role == 0, cut, jnp.zeros_like(cut))
    for d, pairs in enumerate(spread_pairs):
        sent = lax.ppermute(cut, ("frames", "atoms"), pairs)
        cols = jnp.where(role == d + 1, sent, cols)
    return scale * jnp.einsum(
        "cfp,dfq->cpdq", rows, cols, preferred_element_type=jnp.float32
    )


def per_device(frames, mean_structure, eigvecs):
    local_frames, _, local_atoms = frames.shape
    frame_axis = lax.axis_size("frames")
    atom_axis = lax.axis_size("atoms")
    total_frames = local_frames * frame_axis
    block = local_atoms * atom_axis // frame_axis
    blocks = frame_axis // atom_axis
    me_f = lax.axis_index("frames")
    me_a = lax.axis_index("atoms")
    half = lax.rem(me_f, blocks).astype(jnp.int32).reshape(1)
    owner = lax.div(me_f, blocks)
    role = lax.bitwise_xor(me_a, owner).astype(jnp.int32).reshape(1)
    x = pinned(jnp.transpose(frames, (1, 0, 2)), pltpu.HBM)
    mean_structure = pinned(mean_structure, pltpu.HBM)
    stats, x, mean_structure = pl.pallas_call(
        stats_kernel,
        out_shape=(
            pltpu.VMEM((STATS, local_frames), jnp.float32),
            pltpu.VMEM(x.shape, jnp.float32),
            pltpu.VMEM(mean_structure.shape, jnp.float32),
        ),
        in_specs=[HBM, HBM],
        out_specs=(VMEM, VMEM, VMEM),
        scratch_shapes=[pltpu.SemaphoreType.DMA((2,))],
        compiler_params=params(8),
        name="local_moments",
    )(x, mean_structure)
    def swap(value, distance):
        return lax.ppermute(value, "atoms", [(a, a ^ distance) for a in range(atom_axis)])

    others = [swap(stats, d) for d in range(1, atom_axis)]
    run = local_atoms // 4
    piece = (3, run, 2 * local_frames)
    own, flat = pl.pallas_call(
        functools.partial(align_kernel, atom_axis),
        out_shape=(
            jax.ShapeDtypeStruct((2,) + piece, jnp.bfloat16),
            jax.ShapeDtypeStruct(x.shape, jnp.bfloat16),
        ),
        in_specs=[VMEM] * (atom_axis + 2),
        out_specs=(VMEM, VMEM),
        scratch_shapes=[pltpu.VMEM((LANES, LANES), jnp.float32)],
        compiler_params=params(8),
        name="polar_align",
    )(stats, *others, x, mean_structure)
    share = jax.ShapeDtypeStruct((local_frames, eigvecs.shape[2] // atom_axis), jnp.float32)
    shares = pl.pallas_call(
        project_kernel,
        out_shape=(share,) * atom_axis,
        in_specs=[SMEM, VMEM, VMEM],
        out_specs=(VMEM,) * atom_axis,
        scratch_shapes=[pltpu.VMEM((atom_axis,) + share.shape, jnp.float32)],
        compiler_params=params(8),
        name="project",
    )(me_a.astype(jnp.int32).reshape(1), flat, eigvecs)
    parts = [shares[0]] + [swap(shares[d], d) for d in range(1, atom_axis)]
    projections = pl.pallas_call(
        sum_kernel,
        out_shape=share,
        in_specs=[VMEM] * atom_axis,
        out_specs=VMEM,
        compiler_params=params(4),
        name="sum_shares",
    )(*parts)

    def pairs(source, target):
        return [
            (
                f * atom_axis + ((f // blocks) ^ source),
                f * atom_axis + ((f // blocks) ^ target),
            )
            for f in range(frame_axis)
        ]

    if blocks != 2 or frame_axis != 8:
        spread_pairs = [pairs(0, d) for d in range(1, atom_axis)]
        covariance = long_axis_covariance(
            flat, half[0], role[0], block, spread_pairs, 1.0 / total_frames
        )
        return covariance, projections

    axes = ("frames", "atoms")

    def columns(slots):
        return pltpu.VMEM((slots, 3, local_frames, block), jnp.bfloat16)

    def kernel(body, out_shape, scalar, values, name):
        single = not isinstance(out_shape, tuple)
        return pl.pallas_call(
            body,
            out_shape=out_shape,
            in_specs=[SMEM] + [VMEM] * len(values),
            out_specs=VMEM if single else (VMEM,) * len(out_shape),
            compiler_params=params(4),
            name=name,
        )(scalar, *[pinned(value, pltpu.VMEM) for value in values])

    def cross(cut):
        whole = pairs(0, 2) + pairs(2, 0) + pairs(1, 1) + pairs(3, 3)
        return [cut, lax.ppermute(cut, axes, whole)]

    def pass_on(values, role):
        slots = sum(value.shape[0] for value in values[::2])
        held = kernel(pass_on_kernel, columns(slots), role, values, "pass_on")
        return [held, swap(held, 1)]

    order = ring_order(frame_axis)
    forward = [(order[i], order[(i + 1) % frame_axis]) for i in range(frame_axis)]
    backward = [(b, a) for a, b in forward]

    def hop(up, down):
        return lax.ppermute(up, "frames", forward), lax.ppermute(down, "frames", backward)

    one = hop(own, own)
    crossed = cross(kernel(cut_kernel, columns(1), half, [own], "cut_columns"))
    cut_one = kernel(cut_kernel, columns(2), half, list(one), "cut_columns")
    two = hop(after(one[0], crossed[1], *parts), one[1])
    in_hbm = pass_on(crossed + cross(cut_one), role)
    cut_two = kernel(
        cut_kernel, columns(2), after(half, projections), list(two), "cut_columns"
    )
    three = hop(*two)
    crossed = cross(cut_two)
    half_shard = pltpu.VMEM(piece, jnp.bfloat16)
    cut_three, *halves = kernel(
        cut_last_kernel,
        (columns(2), half_shard, half_shard),
        after(half, in_hbm[0]),
        list(three),
        "cut_columns",
    )
    far = hop(*halves)
    cut_four = kernel(
        cut_far_kernel, columns(1), after(half, crossed[1]), list(far), "cut_columns"
    )
    in_vmem = pass_on(
        crossed + cross(cut_three) + cross(cut_four), after(role, in_hbm[1])
    )
    groups = ((3, True, (0, 1, 0, 1)), (5, False, (0, 1, 0, 1)))
    rows = [own, *one, *two, *three, *far]
    covariance = pl.pallas_call(
        functools.partial(
            covariance_kernel, frame_axis, atom_axis, groups, 1.0 / total_frames
        ),
        out_shape=jax.ShapeDtypeStruct((3, 3, local_atoms, block), jnp.float32),
        in_specs=[SMEM]
        + [VMEM] * len(rows)
        + [HBM] * len(in_hbm)
        + [VMEM] * len(in_vmem),
        out_specs=ANY,
        scratch_shapes=[
            pltpu.VMEM((2, 2 * run, total_frames), jnp.bfloat16),
            pltpu.VMEM((3, total_frames, block), jnp.bfloat16),
            pltpu.VMEM((2, 3, 2 * run, block), jnp.float32),
            pltpu.SemaphoreType.DMA((frame_axis,)),
            pltpu.SemaphoreType.DMA((2, 3)),
        ],
        compiler_params=params(16),
        cost_estimate=pl.CostEstimate(
            flops=18 * local_atoms * block * total_frames,
            bytes_accessed=24 * MIB,
            transcendentals=0,
        ),
        name="covariance_tile",
    )(
        role,
        *[pinned(value, pltpu.VMEM) for value in rows],
        *[pinned(value, pltpu.HBM) for value in in_hbm],
        *[pinned(value, pltpu.VMEM) for value in in_vmem],
    )
    return jnp.transpose(covariance, (0, 2, 1, 3)), projections


def solution(mesh):
    placed = (P("frames", None, "atoms"), P(None, "atoms"), P(None, "atoms", None))
    return jax.shard_map(
        per_device,
        mesh=mesh,
        in_specs=placed,
        out_specs=(P(None, "atoms", None, "frames"), P("frames", "atoms")),
        check_vma=False,
    )
```

```python
import functools

import jax
import jax.numpy as jnp
from jax import lax
from jax.experimental import pallas as pl
from jax.experimental.pallas import tpu as pltpu
from jax.sharding import PartitionSpec as P

POLAR = 6
LANES = 128
STATS = 24
VMEM = pl.BlockSpec(memory_space=pltpu.VMEM)
SMEM = pl.BlockSpec(memory_space=pltpu.SMEM)
HBM = pl.BlockSpec(memory_space=pltpu.HBM)
ANY = pl.BlockSpec(memory_space=pl.ANY)
MIB = 1024 * 1024


def params(mib):
    return pltpu.CompilerParams(vmem_limit_bytes=mib * MIB)


def lane_mean(value):
    return jnp.sum(value, axis=1, keepdims=True) * (1.0 / value.shape[1])


def run_copies(copies):
    for copy in copies:
        copy.start()
    for copy in copies:
        copy.wait()


def stats_kernel(x_hbm, ref_hbm, out_ref, x_ref, ref_ref, sem):
    run_copies(
        [
            pltpu.make_async_copy(ref_hbm, ref_ref, sem.at[0]),
            pltpu.make_async_copy(x_hbm, x_ref, sem.at[1]),
        ]
    )
    values = []
    centred = []
    for i in range(3):
        x = x_ref[i]
        mean = lane_mean(x)
        values.append(mean)
        centred.append(x - mean)
    values.append(sum(jnp.sum(c * c, axis=1, keepdims=True) for c in centred))
    ref_mean = [lane_mean(ref_ref[j : j + 1, :]) for j in range(3)]
    ref_centred = [ref_ref[j : j + 1, :] - ref_mean[j] for j in range(3)]
    for i in range(3):
        for j in range(3):
            values.append(jnp.sum(centred[i] * ref_centred[j], axis=1, keepdims=True))
    values += ref_mean
    values.append(sum(jnp.sum(c * c, axis=1, keepdims=True) for c in ref_centred))
    shape = (x_ref.shape[1], LANES)
    lane = lax.broadcasted_iota(jnp.int32, shape, 1)
    out = jnp.zeros(shape, jnp.float32)
    for k, value in enumerate(values):
        out = jnp.where(lane == k, jnp.broadcast_to(value, shape), out)
    out_ref[...] = out.T[:STATS]


def align_kernel(parts, *refs):
    stats = refs[:parts]
    x_ref, ref_ref, piece_ref, flat_ref, turn = refs[parts:]
    local = x_ref.shape[2]
    rows = x_ref.shape[1]

    def row(at):
        return [s[at : at + 1, :] for s in stats]

    means = [row(i) for i in range(3)]
    ref_means = [row(13 + j) for j in range(3)]
    centre = [sum(m) * (1.0 / parts) for m in means]
    ref_centre = [sum(r) * (1.0 / parts) for r in ref_means]
    off = [[m - centre[i] for m in means[i]] for i in range(3)]
    ref_off = [[r - ref_centre[j] for r in ref_means[j]] for j in range(3)]
    spread = sum(row(3)) + local * sum(o * o for i in range(3) for o in off[i])
    ref_spread = sum(row(16)) + local * sum(o * o for j in range(3) for o in ref_off[j])
    scale = 1.0 / jnp.sqrt(spread * ref_spread + 1e-06)
    now = [
        [
            (sum(row(4 + 3 * i + j)) + local * sum(o * r for o, r in zip(off[i], ref_off[j])))
            * scale
            for j in range(3)
        ]
        for i in range(3)
    ]
    for _ in range(POLAR):
        gram = {}
        for i in range(3):
            for j in range(i, 3):
                gram[i, j] = sum(now[k][i] * now[k][j] for k in range(3))
                gram[j, i] = gram[i, j]
        left = [
            [(1.5 if k == j else 0.0) - 0.5 * gram[k, j] for j in range(3)] for k in range(3)
        ]
        now = [
            [sum(now[i][k] * left[k][j] for k in range(3)) for j in range(3)]
            for i in range(3)
        ]
    for k, value in enumerate(sum(now, []) + centre + ref_centre):
        turn[k : k + 1, :rows] = value
    turned = turn[...].T
    column = [turned[:rows, k : k + 1] for k in range(12)]
    centred = [x_ref[j] - column[9 + j] for j in range(3)]
    for i in range(3):
        target = ref_ref[i : i + 1, :] - turned[0:1, 12 + i : 13 + i]
        moved = sum(column[3 * j + i] * centred[j] for j in range(3)) - target
        flat_ref[i] = moved.astype(jnp.bfloat16)
        run = piece_ref.shape[2]
        for at in range(2):
            pair = [moved[:, (2 * at + k) * run : (2 * at + k + 1) * run] for k in range(2)]
            piece_ref[at, i] = jnp.concatenate(pair, axis=0).T.astype(jnp.bfloat16)


def project_kernel(me_ref, flat_ref, eig_ref, *refs):
    shares, cut = refs[:-1], refs[-1]
    total = sum(
        jnp.dot(flat_ref[c], eig_ref[c], preferred_element_type=jnp.float32) for c in range(3)
    )
    width = cut.shape[2]
    for k in range(len(shares)):
        cut[k] = total[:, k * width : (k + 1) * width]
    for k, share in enumerate(shares):
        share[...] = cut[lax.bitwise_xor(me_ref[0], k)]


def sum_kernel(*refs):
    refs[-1][...] = sum(ref[...] for ref in refs[:-1])


def cut_columns(half_ref, halves, cols_ref):
    for half in range(2):

        @pl.when(half_ref[0] == half)
        def _(half=half):
            for k, pair in enumerate(halves):
                run, lanes = pair[half].shape[1:]
                for c in range(3):
                    turned = pair[half][c].astype(jnp.float32).T.astype(jnp.bfloat16)
                    cols_ref[k, c, :, :run] = turned[: lanes // 2]
                    cols_ref[k, c, :, run:] = turned[lanes // 2 :]


def cut_kernel(half_ref, *refs):
    cut_columns(half_ref, [(r.at[0], r.at[1]) for r in refs[:-1]], refs[-1])


def cut_last_kernel(half_ref, up_ref, down_ref, cols_ref, up_half, down_half):
    up_half[...] = up_ref[0]
    down_half[...] = down_ref[1]
    cut_columns(half_ref, [(r.at[0], r.at[1]) for r in (up_ref, down_ref)], cols_ref)


def cut_far_kernel(half_ref, up_half, down_half, cols_ref):
    cut_columns(half_ref, [(up_half, down_half)], cols_ref)


def pass_on_kernel(role_ref, *refs):
    sources, out_ref = refs[:-1], refs[-1]
    for role in range(2):

        @pl.when((role_ref[0] != 0) == bool(role))
        def _(role=role):
            to = 0
            for source in sources[role::2]:
                out_ref[to : to + source.shape[0]] = source[...]
                to += source.shape[0]


def pick_half_kernel(role_ref, own_ref, beside_ref, out_ref):
    width = out_ref.shape[3]

    @pl.when(role_ref[0] == 0)
    def _():
        out_ref[...] = own_ref[:, :, :, :width]

    @pl.when(role_ref[0] != 0)
    def _():
        out_ref[...] = beside_ref[:, :, :, width:]


def side_by_side(first, second):
    middle = first.shape[1] // 2
    left = jnp.concatenate([first[:, :middle], second[:, :middle]], axis=1)
    right = jnp.concatenate([first[:, middle:], second[:, middle:]], axis=1)
    return left, right


def covariance_kernel(slots, roles, groups, scale, role_ref, *refs):
    shards, up_half, down_half = refs[: slots - 1], refs[slots - 1], refs[slots]
    refs = refs[slots + 1 :]
    arrays = []
    for _, _, count in groups:
        arrays.append(refs[:count])
        refs = refs[count:]
    out_ref, left, right, done, col_sem, out_sem = refs
    depth = right.shape[1] // slots
    run = up_half.shape[1]

    def parts_of(k, role):
        if len(arrays[k]) == 2:
            return [(arrays[k][role % 2], 0)]
        own, beside, across, halves = arrays[k]
        width = across.shape[3]
        return {
            0: [(own, 0)],
            1: [(beside, 0)],
            2: [(across, 0), (halves, width)],
            3: [(halves, 0), (across, width)],
        }[role]

    def fetches(k, role, to):
        return [
            pltpu.make_async_copy(
                source.at[n],
                right.at[:, pl.ds(to + n * depth, depth), pl.ds(at, source.shape[3])],
                col_sem.at[2 * (to // depth + n) + p],
            )
            for p, (source, at) in enumerate(parts_of(k, role))
            for n in range(groups[k][0])
        ]

    def for_each_group(from_hbm, act):
        for role in range(roles):

            @pl.when(role_ref[0] == role)
            def _(role=role):
                to = 0
                for k, (count, in_hbm, _) in enumerate(groups):
                    if in_hbm == from_hbm:
                        act(k, role, to)
                    to += count * depth

    def start(k, role, to):
        for copy in fetches(k, role, to):
            copy.start()

    def wait(k, role, to):
        for copy in fetches(k, role, to):
            copy.wait()

    def load(k, role, to):
        for source, at in parts_of(k, role):
            for n in range(groups[k][0]):
                for d in range(3):
                    right[
                        d, to + n * depth : to + (n + 1) * depth, at : at + source.shape[3]
                    ] = source[n, d]

    def piece(slot, at, c):
        if slot < slots - 1:
            return shards[slot][at, c]
        return (up_half, down_half)[at][c]

    def assemble(c, at):
        for q in range(slots // 2):
            low, high = side_by_side(piece(2 * q, at, c), piece(2 * q + 1, at, c))
            left[at, :run, q * LANES : (q + 1) * LANES] = low
            left[at, run:, q * LANES : (q + 1) * LANES] = high

    for_each_group(True, start)
    for_each_group(False, load)
    assemble(0, 0)
    for_each_group(True, wait)

    def write(c, at, d):
        return pltpu.make_async_copy(
            done.at[at, d],
            out_ref.at[c, d, pl.ds(at * 2 * run, 2 * run), :],
            out_sem.at[at, d],
        )

    @pl.loop(0, 3)
    def _(c):
        for at in range(2):

            @pl.when(c > 0)
            def _():
                for d in range(3):
                    write(c - 1, at, d).wait()

            assemble(jnp.minimum(c + at, 2), 1 - at)
            for d in range(3):
                done[at, d] = scale * jnp.dot(
                    left[at], right[d], preferred_element_type=jnp.float32
                )
                write(c, at, d).start()

    for at in range(2):
        for d in range(3):
            write(2, at, d).wait()


pinned = pltpu.with_memory_space_constraint


def after(value, *others):
    return lax.optimization_barrier((value,) + others)[0] if others else value


def ring_order(count):
    return list(range(0, count, 2)) + list(range(1, count, 2))[::-1]


def long_axis_covariance(flat, half, role, block, spread_pairs, scale):
    rows = lax.all_gather(flat, "frames", axis=1, tiled=True)
    cut = lax.dynamic_slice_in_dim(rows, half * block, block, axis=2)
    cols = jnp.where(role == 0, cut, jnp.zeros_like(cut))
    for d, pairs in enumerate(spread_pairs):
        sent = lax.ppermute(cut, ("frames", "atoms"), pairs)
        cols = jnp.where(role == d + 1, sent, cols)
    return scale * jnp.einsum(
        "cfp,dfq->cpdq", rows, cols, preferred_element_type=jnp.float32
    )


def per_device(frames, mean_structure, eigvecs):
    local_frames, _, local_atoms = frames.shape
    frame_axis = lax.axis_size("frames")
    atom_axis = lax.axis_size("atoms")
    total_frames = local_frames * frame_axis
    block = local_atoms * atom_axis // frame_axis
    blocks = frame_axis // atom_axis
    me_f = lax.axis_index("frames")
    me_a = lax.axis_index("atoms")
    half = lax.rem(me_f, blocks).astype(jnp.int32).reshape(1)
    owner = lax.div(me_f, blocks)
    role = lax.bitwise_xor(me_a, owner).astype(jnp.int32).reshape(1)
    x = pinned(jnp.transpose(frames, (1, 0, 2)), pltpu.HBM)
    mean_structure = pinned(mean_structure, pltpu.HBM)
    stats, x, mean_structure = pl.pallas_call(
        stats_kernel,
        out_shape=(
            pltpu.VMEM((STATS, local_frames), jnp.float32),
            pltpu.VMEM(x.shape, jnp.float32),
            pltpu.VMEM(mean_structure.shape, jnp.float32),
        ),
        in_specs=[HBM, HBM],
        out_specs=(VMEM, VMEM, VMEM),
        scratch_shapes=[pltpu.SemaphoreType.DMA((2,))],
        compiler_params=params(8),
        name="local_moments",
    )(x, mean_structure)
    def swap(value, distance):
        return lax.ppermute(value, "atoms", [(a, a ^ distance) for a in range(atom_axis)])

    others = [swap(stats, d) for d in range(1, atom_axis)]
    run = local_atoms // 4
    piece = (3, run, 2 * local_frames)
    own, flat = pl.pallas_call(
        functools.partial(align_kernel, atom_axis),
        out_shape=(
            jax.ShapeDtypeStruct((2,) + piece, jnp.bfloat16),
            jax.ShapeDtypeStruct(x.shape, jnp.bfloat16),
        ),
        in_specs=[VMEM] * (atom_axis + 2),
        out_specs=(VMEM, VMEM),
        scratch_shapes=[pltpu.VMEM((LANES, LANES), jnp.float32)],
        compiler_params=params(8),
        name="polar_align",
    )(stats, *others, x, mean_structure)
    share = jax.ShapeDtypeStruct((local_frames, eigvecs.shape[2] // atom_axis), jnp.float32)
    shares = pl.pallas_call(
        project_kernel,
        out_shape=(share,) * atom_axis,
        in_specs=[SMEM, VMEM, VMEM],
        out_specs=(VMEM,) * atom_axis,
        scratch_shapes=[pltpu.VMEM((atom_axis,) + share.shape, jnp.float32)],
        compiler_params=params(8),
        name="project",
    )(me_a.astype(jnp.int32).reshape(1), flat, eigvecs)
    parts = [shares[0]] + [swap(shares[d], d) for d in range(1, atom_axis)]
    projections = pl.pallas_call(
        sum_kernel,
        out_shape=share,
        in_specs=[VMEM] * atom_axis,
        out_specs=VMEM,
        compiler_params=params(4),
        name="sum_shares",
    )(*parts)

    def pairs(source, target):
        return [
            (
                f * atom_axis + ((f // blocks) ^ source),
                f * atom_axis + ((f // blocks) ^ target),
            )
            for f in range(frame_axis)
        ]

    if blocks != 2 or frame_axis != 8:
        spread_pairs = [pairs(0, d) for d in range(1, atom_axis)]
        covariance = long_axis_covariance(
            flat, half[0], role[0], block, spread_pairs, 1.0 / total_frames
        )
        return covariance, projections

    axes = ("frames", "atoms")

    def columns(slots):
        return pltpu.VMEM((slots, 3, local_frames, block), jnp.bfloat16)

    def kernel(body, out_shape, scalar, values, name):
        single = not isinstance(out_shape, tuple)
        return pl.pallas_call(
            body,
            out_shape=out_shape,
            in_specs=[SMEM] + [VMEM] * len(values),
            out_specs=VMEM if single else (VMEM,) * len(out_shape),
            compiler_params=params(4),
            name=name,
        )(scalar, *[pinned(value, pltpu.VMEM) for value in values])

    def cross(cut):
        return [cut, lax.ppermute(cut, axes, pairs(0, 2))]

    def pass_on(values, role):
        slots = sum(value.shape[0] for value in values[::2])
        held = kernel(pass_on_kernel, columns(slots), role, values, "pass_on")
        return [held, swap(held, 1)]

    def halves_across(cut):
        beside = swap(cut, 1)
        half_shape = pltpu.VMEM(cut.shape[:3] + (block // 2,), jnp.bfloat16)
        picked = kernel(pick_half_kernel, half_shape, role, [cut, beside], "pick_half")
        across = swap(picked, 2)
        return [cut, beside, across, swap(across, 1)], picked

    order = ring_order(frame_axis)
    forward = [(order[i], order[(i + 1) % frame_axis]) for i in range(frame_axis)]
    backward = [(b, a) for a, b in forward]

    def hop(up, down):
        return lax.ppermute(up, "frames", forward), lax.ppermute(down, "frames", backward)

    one = hop(own, own)
    crossed = cross(kernel(cut_kernel, columns(1), half, [own], "cut_columns"))
    cut_one = kernel(cut_kernel, columns(2), half, list(one), "cut_columns")
    two = hop(after(one[0], crossed[1], *parts), one[1])
    in_hbm = pass_on(crossed + cross(cut_one), role)
    cut_two = kernel(
        cut_kernel, columns(2), after(half, projections), list(two), "cut_columns"
    )
    three = hop(*two)
    crossed = cross(cut_two)
    half_shard = pltpu.VMEM(piece, jnp.bfloat16)
    cut_three, *halves = kernel(
        cut_last_kernel,
        (columns(2), half_shard, half_shard),
        after(half, in_hbm[0]),
        list(three),
        "cut_columns",
    )
    far = hop(*halves)
    cut_four = kernel(
        cut_far_kernel, columns(1), after(half, crossed[1]), list(far), "cut_columns"
    )
    last, picked = halves_across(cut_four)
    in_vmem = pass_on(crossed + cross(cut_three), after(role, in_hbm[1], picked)) + last
    groups = ((3, True, 2), (4, False, 2), (1, False, 4))
    rows = [own, *one, *two, *three, *far]
    covariance = pl.pallas_call(
        functools.partial(
            covariance_kernel, frame_axis, atom_axis, groups, 1.0 / total_frames
        ),
        out_shape=jax.ShapeDtypeStruct((3, 3, local_atoms, block), jnp.float32),
        in_specs=[SMEM]
        + [VMEM] * len(rows)
        + [HBM] * len(in_hbm)
        + [VMEM] * len(in_vmem),
        out_specs=ANY,
        scratch_shapes=[
            pltpu.VMEM((2, 2 * run, total_frames), jnp.bfloat16),
            pltpu.VMEM((3, total_frames, block), jnp.bfloat16),
            pltpu.VMEM((2, 3, 2 * run, block), jnp.float32),
            pltpu.SemaphoreType.DMA((2 * frame_axis,)),
            pltpu.SemaphoreType.DMA((2, 3)),
        ],
        compiler_params=params(16),
        cost_estimate=pl.CostEstimate(
            flops=18 * local_atoms * block * total_frames,
            bytes_accessed=24 * MIB,
            transcendentals=0,
        ),
        name="covariance_tile",
    )(
        role,
        *[pinned(value, pltpu.VMEM) for value in rows],
        *[pinned(value, pltpu.HBM) for value in in_hbm],
        *[pinned(value, pltpu.VMEM) for value in in_vmem],
    )
    return jnp.transpose(covariance, (0, 2, 1, 3)), projections


def solution(mesh):
    placed = (P("frames", None, "atoms"), P(None, "atoms"), P(None, "atoms", None))
    return jax.shard_map(
        per_device,
        mesh=mesh,
        in_specs=placed,
        out_specs=(P(None, "atoms", None, "frames"), P("frames", "atoms")),
        check_vma=False,
    )
```

```python
import functools

import jax
import jax.numpy as jnp
from jax import lax
from jax.experimental import pallas as pl
from jax.experimental.pallas import tpu as pltpu
from jax.sharding import PartitionSpec as P

POLAR = 6
LANES = 128
STATS = 24
VMEM = pl.BlockSpec(memory_space=pltpu.VMEM)
SMEM = pl.BlockSpec(memory_space=pltpu.SMEM)
HBM = pl.BlockSpec(memory_space=pltpu.HBM)
ANY = pl.BlockSpec(memory_space=pl.ANY)
MIB = 1024 * 1024


def params(mib):
    return pltpu.CompilerParams(vmem_limit_bytes=mib * MIB)


def lane_mean(value):
    return jnp.sum(value, axis=1, keepdims=True) * (1.0 / value.shape[1])


def run_copies(copies):
    for copy in copies:
        copy.start()
    for copy in copies:
        copy.wait()


def stats_kernel(x_hbm, ref_hbm, out_ref, x_ref, ref_ref, sem):
    run_copies(
        [
            pltpu.make_async_copy(ref_hbm, ref_ref, sem.at[0]),
            pltpu.make_async_copy(x_hbm, x_ref, sem.at[1]),
        ]
    )
    values = []
    centred = []
    for i in range(3):
        x = x_ref[i]
        mean = lane_mean(x)
        values.append(mean)
        centred.append(x - mean)
    values.append(sum(jnp.sum(c * c, axis=1, keepdims=True) for c in centred))
    ref_mean = [lane_mean(ref_ref[j : j + 1, :]) for j in range(3)]
    ref_centred = [ref_ref[j : j + 1, :] - ref_mean[j] for j in range(3)]
    for i in range(3):
        for j in range(3):
            values.append(jnp.sum(centred[i] * ref_centred[j], axis=1, keepdims=True))
    values += ref_mean
    values.append(sum(jnp.sum(c * c, axis=1, keepdims=True) for c in ref_centred))
    shape = (x_ref.shape[1], LANES)
    lane = lax.broadcasted_iota(jnp.int32, shape, 1)
    out = jnp.zeros(shape, jnp.float32)
    for k, value in enumerate(values):
        out = jnp.where(lane == k, jnp.broadcast_to(value, shape), out)
    out_ref[...] = out.T[:STATS]


def align_kernel(parts, *refs):
    stats = refs[:parts]
    x_ref, ref_ref, piece_ref, flat_ref, turn = refs[parts:]
    local = x_ref.shape[2]
    rows = x_ref.shape[1]

    def row(at):
        return [s[at : at + 1, :] for s in stats]

    means = [row(i) for i in range(3)]
    ref_means = [row(13 + j) for j in range(3)]
    centre = [sum(m) * (1.0 / parts) for m in means]
    ref_centre = [sum(r) * (1.0 / parts) for r in ref_means]
    off = [[m - centre[i] for m in means[i]] for i in range(3)]
    ref_off = [[r - ref_centre[j] for r in ref_means[j]] for j in range(3)]
    spread = sum(row(3)) + local * sum(o * o for i in range(3) for o in off[i])
    ref_spread = sum(row(16)) + local * sum(o * o for j in range(3) for o in ref_off[j])
    scale = 1.0 / jnp.sqrt(spread * ref_spread + 1e-06)
    now = [
        [
            (sum(row(4 + 3 * i + j)) + local * sum(o * r for o, r in zip(off[i], ref_off[j])))
            * scale
            for j in range(3)
        ]
        for i in range(3)
    ]
    for _ in range(POLAR):
        gram = {}
        for i in range(3):
            for j in range(i, 3):
                gram[i, j] = sum(now[k][i] * now[k][j] for k in range(3))
                gram[j, i] = gram[i, j]
        left = [
            [(1.5 if k == j else 0.0) - 0.5 * gram[k, j] for j in range(3)] for k in range(3)
        ]
        now = [
            [sum(now[i][k] * left[k][j] for k in range(3)) for j in range(3)]
            for i in range(3)
        ]
    for k, value in enumerate(sum(now, []) + centre + ref_centre):
        turn[k : k + 1, :rows] = value
    turned = turn[...].T
    column = [turned[:rows, k : k + 1] for k in range(12)]
    centred = [x_ref[j] - column[9 + j] for j in range(3)]
    for i in range(3):
        target = ref_ref[i : i + 1, :] - turned[0:1, 12 + i : 13 + i]
        moved = sum(column[3 * j + i] * centred[j] for j in range(3)) - target
        flat_ref[i] = moved.astype(jnp.bfloat16)
        run = piece_ref.shape[2]
        for at in range(2):
            pair = [moved[:, (2 * at + k) * run : (2 * at + k + 1) * run] for k in range(2)]
            piece_ref[at, i] = jnp.concatenate(pair, axis=0).T.astype(jnp.bfloat16)


def project_kernel(me_ref, flat_ref, eig_ref, *refs):
    shares, cut = refs[:-1], refs[-1]
    total = sum(
        jnp.dot(flat_ref[c], eig_ref[c], preferred_element_type=jnp.float32) for c in range(3)
    )
    width = cut.shape[2]
    for k in range(len(shares)):
        cut[k] = total[:, k * width : (k + 1) * width]
    for k, share in enumerate(shares):
        share[...] = cut[lax.bitwise_xor(me_ref[0], k)]


def sum_kernel(*refs):
    refs[-1][...] = sum(ref[...] for ref in refs[:-1])


def cut_columns(half_ref, halves, cols_ref):
    for half in range(2):

        @pl.when(half_ref[0] == half)
        def _(half=half):
            for k, pair in enumerate(halves):
                run, lanes = pair[half].shape[1:]
                for c in range(3):
                    turned = pair[half][c].astype(jnp.float32).T.astype(jnp.bfloat16)
                    cols_ref[k, c, :, :run] = turned[: lanes // 2]
                    cols_ref[k, c, :, run:] = turned[lanes // 2 :]


def cut_kernel(half_ref, *refs):
    cut_columns(half_ref, [(r.at[0], r.at[1]) for r in refs[:-1]], refs[-1])


def cut_last_kernel(half_ref, up_ref, down_ref, cols_ref, up_half, down_half):
    up_half[...] = up_ref[0]
    down_half[...] = down_ref[1]
    cut_columns(half_ref, [(r.at[0], r.at[1]) for r in (up_ref, down_ref)], cols_ref)


def cut_far_kernel(half_ref, up_half, down_half, cols_ref):
    cut_columns(half_ref, [(up_half, down_half)], cols_ref)


def pass_on_kernel(role_ref, *refs):
    sources, out_ref = refs[:-1], refs[-1]
    for role in range(2):

        @pl.when((role_ref[0] != 0) == bool(role))
        def _(role=role):
            to = 0
            for source in sources[role::2]:
                out_ref[to : to + source.shape[0]] = source[...]
                to += source.shape[0]


def pick_half_kernel(role_ref, own_ref, beside_ref, out_ref):
    width = out_ref.shape[3]

    @pl.when(role_ref[0] == 0)
    def _():
        out_ref[...] = own_ref[:, :, :, :width]

    @pl.when(role_ref[0] != 0)
    def _():
        out_ref[...] = beside_ref[:, :, :, width:]


def side_by_side(first, second):
    middle = first.shape[1] // 2
    left = jnp.concatenate([first[:, :middle], second[:, :middle]], axis=1)
    right = jnp.concatenate([first[:, middle:], second[:, middle:]], axis=1)
    return left, right


def covariance_kernel(slots, roles, groups, scale, role_ref, *refs):
    shards, up_half, down_half = refs[: slots - 1], refs[slots - 1], refs[slots]
    refs = refs[slots + 1 :]
    arrays = []
    for _, _, count in groups:
        arrays.append(refs[:count])
        refs = refs[count:]
    out_ref, left, right, done, col_sem, out_sem = refs
    depth = right.shape[1] // slots
    run = up_half.shape[1]

    def parts_of(k, role):
        if len(arrays[k]) == 2:
            return [(arrays[k][role % 2], 0)]
        own, beside, across, halves = arrays[k]
        width = across.shape[3]
        return {
            0: [(own, 0)],
            1: [(beside, 0)],
            2: [(across, 0), (halves, width)],
            3: [(halves, 0), (across, width)],
        }[role]

    def fetches(k, role, to):
        return [
            pltpu.make_async_copy(
                source.at[n],
                right.at[:, pl.ds(to + n * depth, depth), pl.ds(at, source.shape[3])],
                col_sem.at[2 * (to // depth + n) + p],
            )
            for p, (source, at) in enumerate(parts_of(k, role))
            for n in range(groups[k][0])
        ]

    def for_each_group(from_hbm, act):
        for role in range(roles):

            @pl.when(role_ref[0] == role)
            def _(role=role):
                to = 0
                for k, (count, in_hbm, _) in enumerate(groups):
                    if in_hbm == from_hbm:
                        act(k, role, to)
                    to += count * depth

    def start(k, role, to):
        for copy in fetches(k, role, to):
            copy.start()

    def wait(k, role, to):
        for copy in fetches(k, role, to):
            copy.wait()

    def load(k, role, to):
        for source, at in parts_of(k, role):
            for n in range(groups[k][0]):
                for d in range(3):
                    right[
                        d, to + n * depth : to + (n + 1) * depth, at : at + source.shape[3]
                    ] = source[n, d]

    def piece(slot, at, c):
        if slot < slots - 1:
            return shards[slot][at, c]
        return (up_half, down_half)[at][c]

    def assemble(c, at):
        for q in range(slots // 2):
            low, high = side_by_side(piece(2 * q, at, c), piece(2 * q + 1, at, c))
            left[at, :run, q * LANES : (q + 1) * LANES] = low
            left[at, run:, q * LANES : (q + 1) * LANES] = high

    for_each_group(True, start)
    for_each_group(False, load)
    assemble(0, 0)
    for_each_group(True, wait)

    def write(c, at, d):
        return pltpu.make_async_copy(
            done.at[at, d],
            out_ref.at[c, d, pl.ds(at * 2 * run, 2 * run), :],
            out_sem.at[at, d],
        )

    @pl.loop(0, 3)
    def _(c):
        for at in range(2):

            @pl.when(c > 0)
            def _():
                for d in range(3):
                    write(c - 1, at, d).wait()

            assemble(jnp.minimum(c + at, 2), 1 - at)
            for d in range(3):
                done[at, d] = scale * jnp.dot(
                    left[at], right[d], preferred_element_type=jnp.float32
                )
                write(c, at, d).start()

    for at in range(2):
        for d in range(3):
            write(2, at, d).wait()


pinned = pltpu.with_memory_space_constraint


def after(value, *others):
    return lax.optimization_barrier((value,) + others)[0] if others else value


def ring_order(count):
    return list(range(0, count, 2)) + list(range(1, count, 2))[::-1]


def long_axis_covariance(flat, half, role, block, spread_pairs, scale):
    rows = lax.all_gather(flat, "frames", axis=1, tiled=True)
    cut = lax.dynamic_slice_in_dim(rows, half * block, block, axis=2)
    cols = jnp.where(role == 0, cut, jnp.zeros_like(cut))
    for d, pairs in enumerate(spread_pairs):
        sent = lax.ppermute(cut, ("frames", "atoms"), pairs)
        cols = jnp.where(role == d + 1, sent, cols)
    return scale * jnp.einsum(
        "cfp,dfq->cpdq", rows, cols, preferred_element_type=jnp.float32
    )


def per_device(frames, mean_structure, eigvecs):
    local_frames, _, local_atoms = frames.shape
    frame_axis = lax.axis_size("frames")
    atom_axis = lax.axis_size("atoms")
    total_frames = local_frames * frame_axis
    block = local_atoms * atom_axis // frame_axis
    blocks = frame_axis // atom_axis
    me_f = lax.axis_index("frames")
    me_a = lax.axis_index("atoms")
    half = lax.rem(me_f, blocks).astype(jnp.int32).reshape(1)
    owner = lax.div(me_f, blocks)
    role = lax.bitwise_xor(me_a, owner).astype(jnp.int32).reshape(1)
    x = pinned(jnp.transpose(frames, (1, 0, 2)), pltpu.HBM)
    mean_structure = pinned(mean_structure, pltpu.HBM)
    stats, x, mean_structure = pl.pallas_call(
        stats_kernel,
        out_shape=(
            pltpu.VMEM((STATS, local_frames), jnp.float32),
            pltpu.VMEM(x.shape, jnp.float32),
            pltpu.VMEM(mean_structure.shape, jnp.float32),
        ),
        in_specs=[HBM, HBM],
        out_specs=(VMEM, VMEM, VMEM),
        scratch_shapes=[pltpu.SemaphoreType.DMA((2,))],
        compiler_params=params(8),
        name="local_moments",
    )(x, mean_structure)
    def swap(value, distance):
        return lax.ppermute(value, "atoms", [(a, a ^ distance) for a in range(atom_axis)])

    others = [swap(stats, d) for d in range(1, atom_axis)]
    run = local_atoms // 4
    piece = (3, run, 2 * local_frames)
    own, flat = pl.pallas_call(
        functools.partial(align_kernel, atom_axis),
        out_shape=(
            jax.ShapeDtypeStruct((2,) + piece, jnp.bfloat16),
            jax.ShapeDtypeStruct(x.shape, jnp.bfloat16),
        ),
        in_specs=[VMEM] * (atom_axis + 2),
        out_specs=(VMEM, VMEM),
        scratch_shapes=[pltpu.VMEM((LANES, LANES), jnp.float32)],
        compiler_params=params(8),
        name="polar_align",
    )(stats, *others, x, mean_structure)
    share = jax.ShapeDtypeStruct((local_frames, eigvecs.shape[2] // atom_axis), jnp.float32)
    shares = pl.pallas_call(
        project_kernel,
        out_shape=(share,) * atom_axis,
        in_specs=[SMEM, VMEM, VMEM],
        out_specs=(VMEM,) * atom_axis,
        scratch_shapes=[pltpu.VMEM((atom_axis,) + share.shape, jnp.float32)],
        compiler_params=params(8),
        name="project",
    )(me_a.astype(jnp.int32).reshape(1), flat, eigvecs)
    parts = [shares[0]] + [swap(shares[d], d) for d in range(1, atom_axis)]
    projections = pl.pallas_call(
        sum_kernel,
        out_shape=share,
        in_specs=[VMEM] * atom_axis,
        out_specs=VMEM,
        compiler_params=params(4),
        name="sum_shares",
    )(*parts)

    def pairs(source, target):
        return [
            (
                f * atom_axis + ((f // blocks) ^ source),
                f * atom_axis + ((f // blocks) ^ target),
            )
            for f in range(frame_axis)
        ]

    if blocks != 2 or frame_axis != 8:
        spread_pairs = [pairs(0, d) for d in range(1, atom_axis)]
        covariance = long_axis_covariance(
            flat, half[0], role[0], block, spread_pairs, 1.0 / total_frames
        )
        return covariance, projections

    axes = ("frames", "atoms")

    def columns(slots):
        return pltpu.VMEM((slots, 3, local_frames, block), jnp.bfloat16)

    def kernel(body, out_shape, scalar, values, name):
        single = not isinstance(out_shape, tuple)
        return pl.pallas_call(
            body,
            out_shape=out_shape,
            in_specs=[SMEM] + [VMEM] * len(values),
            out_specs=VMEM if single else (VMEM,) * len(out_shape),
            compiler_params=params(4),
            name=name,
        )(scalar, *[pinned(value, pltpu.VMEM) for value in values])

    def cross(cut):
        return [cut, lax.ppermute(cut, axes, pairs(0, 2))]

    def pass_on(values, role):
        slots = sum(value.shape[0] for value in values[::2])
        held = kernel(pass_on_kernel, columns(slots), role, values, "pass_on")
        return [held, swap(held, 1)]

    def halves_across(cut, *earlier):
        beside = swap(cut, 1)
        half_shape = pltpu.VMEM(cut.shape[:3] + (block // 2,), jnp.bfloat16)
        picked = kernel(
            pick_half_kernel, half_shape, after(role, *earlier), [cut, beside], "pick_half"
        )
        across = swap(picked, 2)
        return [cut, beside, across, swap(across, 1)], picked

    order = ring_order(frame_axis)
    forward = [(order[i], order[(i + 1) % frame_axis]) for i in range(frame_axis)]
    backward = [(b, a) for a, b in forward]

    def hop(up, down):
        return lax.ppermute(up, "frames", forward), lax.ppermute(down, "frames", backward)

    one = hop(own, own)
    crossed = cross(kernel(cut_kernel, columns(1), half, [own], "cut_columns"))
    cut_one = kernel(cut_kernel, columns(2), half, list(one), "cut_columns")
    two = hop(after(one[0], crossed[1], *parts), one[1])
    in_hbm = pass_on(crossed + cross(cut_one), role)
    cut_two = kernel(
        cut_kernel, columns(2), after(half, projections), list(two), "cut_columns"
    )
    three = hop(*two)
    in_hbm += pass_on(cross(cut_two), role)
    half_shard = pltpu.VMEM(piece, jnp.bfloat16)
    cut_three, *halves = kernel(
        cut_last_kernel,
        (columns(2), half_shard, half_shard),
        after(half, in_hbm[0]),
        list(three),
        "cut_columns",
    )
    far = hop(*halves)
    in_vmem, picked = halves_across(cut_three)
    cut_four = kernel(
        cut_far_kernel, columns(1), after(half, in_hbm[0], in_hbm[2], picked), list(far), "cut_columns"
    )
    in_vmem += halves_across(cut_four, in_vmem[2], in_hbm[1])[0]
    groups = ((3, True, 2), (2, True, 2), (2, False, 4), (1, False, 4))
    rows = [own, *one, *two, *three, *far]
    covariance = pl.pallas_call(
        functools.partial(
            covariance_kernel, frame_axis, atom_axis, groups, 1.0 / total_frames
        ),
        out_shape=jax.ShapeDtypeStruct((3, 3, local_atoms, block), jnp.float32),
        in_specs=[SMEM]
        + [VMEM] * len(rows)
        + [HBM] * len(in_hbm)
        + [VMEM] * len(in_vmem),
        out_specs=ANY,
        scratch_shapes=[
            pltpu.VMEM((2, 2 * run, total_frames), jnp.bfloat16),
            pltpu.VMEM((3, total_frames, block), jnp.bfloat16),
            pltpu.VMEM((2, 3, 2 * run, block), jnp.float32),
            pltpu.SemaphoreType.DMA((2 * frame_axis,)),
            pltpu.SemaphoreType.DMA((2, 3)),
        ],
        compiler_params=params(16),
        cost_estimate=pl.CostEstimate(
            flops=18 * local_atoms * block * total_frames,
            bytes_accessed=24 * MIB,
            transcendentals=0,
        ),
        name="covariance_tile",
    )(
        role,
        *[pinned(value, pltpu.VMEM) for value in rows],
        *[pinned(value, pltpu.HBM) for value in in_hbm],
        *[pinned(value, pltpu.VMEM) for value in in_vmem],
    )
    return jnp.transpose(covariance, (0, 2, 1, 3)), projections


def solution(mesh):
    placed = (P("frames", None, "atoms"), P(None, "atoms"), P(None, "atoms", None))
    return jax.shard_map(
        per_device,
        mesh=mesh,
        in_specs=placed,
        out_specs=(P(None, "atoms", None, "frames"), P("frames", "atoms")),
        check_vma=False,
    )
```

```python
import functools

import jax
import jax.numpy as jnp
from jax import lax
from jax.experimental import pallas as pl
from jax.experimental.pallas import tpu as pltpu
from jax.sharding import PartitionSpec as P

POLAR = 6
LANES = 128
STATS = 24
VMEM = pl.BlockSpec(memory_space=pltpu.VMEM)
SMEM = pl.BlockSpec(memory_space=pltpu.SMEM)
HBM = pl.BlockSpec(memory_space=pltpu.HBM)
ANY = pl.BlockSpec(memory_space=pl.ANY)
MIB = 1024 * 1024


def params(mib):
    return pltpu.CompilerParams(vmem_limit_bytes=mib * MIB)


def lane_mean(value):
    return jnp.sum(value, axis=1, keepdims=True) * (1.0 / value.shape[1])


def run_copies(copies):
    for copy in copies:
        copy.start()
    for copy in copies:
        copy.wait()


def stats_kernel(x_hbm, ref_hbm, out_ref, x_ref, ref_ref, sem):
    run_copies(
        [
            pltpu.make_async_copy(ref_hbm, ref_ref, sem.at[0]),
            pltpu.make_async_copy(x_hbm, x_ref, sem.at[1]),
        ]
    )
    values = []
    centred = []
    for i in range(3):
        x = x_ref[i]
        mean = lane_mean(x)
        values.append(mean)
        centred.append(x - mean)
    values.append(sum(jnp.sum(c * c, axis=1, keepdims=True) for c in centred))
    ref_mean = [lane_mean(ref_ref[j : j + 1, :]) for j in range(3)]
    ref_centred = [ref_ref[j : j + 1, :] - ref_mean[j] for j in range(3)]
    for i in range(3):
        for j in range(3):
            values.append(jnp.sum(centred[i] * ref_centred[j], axis=1, keepdims=True))
    values += ref_mean
    values.append(sum(jnp.sum(c * c, axis=1, keepdims=True) for c in ref_centred))
    shape = (x_ref.shape[1], LANES)
    lane = lax.broadcasted_iota(jnp.int32, shape, 1)
    out = jnp.zeros(shape, jnp.float32)
    for k, value in enumerate(values):
        out = jnp.where(lane == k, jnp.broadcast_to(value, shape), out)
    out_ref[...] = out.T[:STATS]


def align_kernel(parts, *refs):
    stats = refs[:parts]
    x_ref, ref_ref, piece_ref, flat_ref, turn = refs[parts:]
    local = x_ref.shape[2]
    rows = x_ref.shape[1]

    def row(at):
        return [s[at : at + 1, :] for s in stats]

    means = [row(i) for i in range(3)]
    ref_means = [row(13 + j) for j in range(3)]
    centre = [sum(m) * (1.0 / parts) for m in means]
    ref_centre = [sum(r) * (1.0 / parts) for r in ref_means]
    off = [[m - centre[i] for m in means[i]] for i in range(3)]
    ref_off = [[r - ref_centre[j] for r in ref_means[j]] for j in range(3)]
    spread = sum(row(3)) + local * sum(o * o for i in range(3) for o in off[i])
    ref_spread = sum(row(16)) + local * sum(o * o for j in range(3) for o in ref_off[j])
    scale = 1.0 / jnp.sqrt(spread * ref_spread + 1e-06)
    now = [
        [
            (sum(row(4 + 3 * i + j)) + local * sum(o * r for o, r in zip(off[i], ref_off[j])))
            * scale
            for j in range(3)
        ]
        for i in range(3)
    ]
    for _ in range(POLAR):
        gram = {}
        for i in range(3):
            for j in range(i, 3):
                gram[i, j] = sum(now[k][i] * now[k][j] for k in range(3))
                gram[j, i] = gram[i, j]
        left = [
            [(1.5 if k == j else 0.0) - 0.5 * gram[k, j] for j in range(3)] for k in range(3)
        ]
        now = [
            [sum(now[i][k] * left[k][j] for k in range(3)) for j in range(3)]
            for i in range(3)
        ]
    for k, value in enumerate(sum(now, []) + centre + ref_centre):
        turn[k : k + 1, :rows] = value
    turned = turn[...].T
    column = [turned[:rows, k : k + 1] for k in range(12)]
    centred = [x_ref[j] - column[9 + j] for j in range(3)]
    for i in range(3):
        target = ref_ref[i : i + 1, :] - turned[0:1, 12 + i : 13 + i]
        moved = sum(column[3 * j + i] * centred[j] for j in range(3)) - target
        flat_ref[i] = moved.astype(jnp.bfloat16)
        run = piece_ref.shape[2]
        for at in range(2):
            pair = [moved[:, (2 * at + k) * run : (2 * at + k + 1) * run] for k in range(2)]
            piece_ref[at, i] = jnp.concatenate(pair, axis=0).T.astype(jnp.bfloat16)


def project_kernel(me_ref, flat_ref, eig_ref, *refs):
    shares, cut = refs[:-1], refs[-1]
    total = sum(
        jnp.dot(flat_ref[c], eig_ref[c], preferred_element_type=jnp.float32) for c in range(3)
    )
    width = cut.shape[2]
    for k in range(len(shares)):
        cut[k] = total[:, k * width : (k + 1) * width]
    for k, share in enumerate(shares):
        share[...] = cut[lax.bitwise_xor(me_ref[0], k)]


def cut_columns(half_ref, halves, cols_ref):
    for half in range(2):

        @pl.when(half_ref[0] == half)
        def _(half=half):
            for k, pair in enumerate(halves):
                run, lanes = pair[half].shape[1:]
                for c in range(3):
                    turned = pair[half][c].astype(jnp.float32).T.astype(jnp.bfloat16)
                    cols_ref[k, c, :, :run] = turned[: lanes // 2]
                    cols_ref[k, c, :, run:] = turned[lanes // 2 :]


def cut_kernel(half_ref, *refs):
    cut_columns(half_ref, [(r.at[0], r.at[1]) for r in refs[:-1]], refs[-1])


def cut_last_kernel(half_ref, up_ref, down_ref, cols_ref, up_half, down_half):
    up_half[...] = up_ref[0]
    down_half[...] = down_ref[1]
    cut_columns(half_ref, [(r.at[0], r.at[1]) for r in (up_ref, down_ref)], cols_ref)


def cut_far_kernel(half_ref, up_half, down_half, cols_ref):
    cut_columns(half_ref, [(up_half, down_half)], cols_ref)


def pass_on_kernel(role_ref, *refs):
    sources, out_ref = refs[:-1], refs[-1]
    for role in range(2):

        @pl.when((role_ref[0] != 0) == bool(role))
        def _(role=role):
            to = 0
            for source in sources[role::2]:
                out_ref[to : to + source.shape[0]] = source[...]
                to += source.shape[0]


def pick_half_kernel(role_ref, own_ref, beside_ref, out_ref):
    width = out_ref.shape[3]

    @pl.when(role_ref[0] == 0)
    def _():
        out_ref[...] = own_ref[:, :, :, :width]

    @pl.when(role_ref[0] != 0)
    def _():
        out_ref[...] = beside_ref[:, :, :, width:]


def side_by_side(first, second):
    middle = first.shape[1] // 2
    left = jnp.concatenate([first[:, :middle], second[:, :middle]], axis=1)
    right = jnp.concatenate([first[:, middle:], second[:, middle:]], axis=1)
    return left, right


def covariance_kernel(slots, roles, groups, scale, role_ref, *refs):
    shards, up_half, down_half = refs[: slots - 1], refs[slots - 1], refs[slots]
    refs = refs[slots + 1 :]
    arrays = []
    for _, _, count in groups:
        arrays.append(refs[:count])
        refs = refs[count:]
    shares, refs = refs[:roles], refs[roles:]
    out_ref, proj_ref, left, right, done, held, col_sem, out_sem, share_sem = refs
    sums = [
        pltpu.make_async_copy(part, held.at[k], share_sem.at[k]) for k, part in enumerate(shares)
    ]
    for copy in sums:
        copy.start()
    depth = right.shape[1] // slots
    run = up_half.shape[1]

    def parts_of(k, role):
        if len(arrays[k]) == 2:
            return [(arrays[k][role % 2], 0)]
        own, beside, across, halves = arrays[k]
        width = across.shape[3]
        return {
            0: [(own, 0)],
            1: [(beside, 0)],
            2: [(across, 0), (halves, width)],
            3: [(halves, 0), (across, width)],
        }[role]

    def fetches(k, role, to):
        return [
            pltpu.make_async_copy(
                source.at[n],
                right.at[:, pl.ds(to + n * depth, depth), pl.ds(at, source.shape[3])],
                col_sem.at[2 * (to // depth + n) + p],
            )
            for p, (source, at) in enumerate(parts_of(k, role))
            for n in range(groups[k][0])
        ]

    def for_each_group(from_hbm, act):
        for role in range(roles):

            @pl.when(role_ref[0] == role)
            def _(role=role):
                to = 0
                for k, (count, in_hbm, _) in enumerate(groups):
                    if in_hbm == from_hbm:
                        act(k, role, to)
                    to += count * depth

    def start(k, role, to):
        for copy in fetches(k, role, to):
            copy.start()

    def wait(k, role, to):
        for copy in fetches(k, role, to):
            copy.wait()

    def load(k, role, to):
        for source, at in parts_of(k, role):
            for n in range(groups[k][0]):
                for d in range(3):
                    right[
                        d, to + n * depth : to + (n + 1) * depth, at : at + source.shape[3]
                    ] = source[n, d]

    def piece(slot, at, c):
        if slot < slots - 1:
            return shards[slot][at, c]
        return (up_half, down_half)[at][c]

    def assemble(c, at):
        for q in range(slots // 2):
            low, high = side_by_side(piece(2 * q, at, c), piece(2 * q + 1, at, c))
            left[at, :run, q * LANES : (q + 1) * LANES] = low
            left[at, run:, q * LANES : (q + 1) * LANES] = high

    for_each_group(True, start)
    for_each_group(False, load)
    assemble(0, 0)
    for_each_group(True, wait)
    for copy in sums:
        copy.wait()
    proj_ref[...] = sum(held[k] for k in range(roles))

    def write(c, at, d):
        return pltpu.make_async_copy(
            done.at[at, d],
            out_ref.at[c, d, pl.ds(at * 2 * run, 2 * run), :],
            out_sem.at[at, d],
        )

    @pl.loop(0, 3)
    def _(c):
        for at in range(2):

            @pl.when(c > 0)
            def _():
                for d in range(3):
                    write(c - 1, at, d).wait()

            assemble(jnp.minimum(c + at, 2), 1 - at)
            for d in range(3):
                done[at, d] = scale * jnp.dot(
                    left[at], right[d], preferred_element_type=jnp.float32
                )
                write(c, at, d).start()

    for at in range(2):
        for d in range(3):
            write(2, at, d).wait()


pinned = pltpu.with_memory_space_constraint


def after(value, *others):
    return lax.optimization_barrier((value,) + others)[0] if others else value


def ring_order(count):
    return list(range(0, count, 2)) + list(range(1, count, 2))[::-1]


def long_axis_covariance(flat, half, role, block, spread_pairs, scale):
    rows = lax.all_gather(flat, "frames", axis=1, tiled=True)
    cut = lax.dynamic_slice_in_dim(rows, half * block, block, axis=2)
    cols = jnp.where(role == 0, cut, jnp.zeros_like(cut))
    for d, pairs in enumerate(spread_pairs):
        sent = lax.ppermute(cut, ("frames", "atoms"), pairs)
        cols = jnp.where(role == d + 1, sent, cols)
    return scale * jnp.einsum(
        "cfp,dfq->cpdq", rows, cols, preferred_element_type=jnp.float32
    )


def per_device(frames, mean_structure, eigvecs):
    local_frames, _, local_atoms = frames.shape
    frame_axis = lax.axis_size("frames")
    atom_axis = lax.axis_size("atoms")
    total_frames = local_frames * frame_axis
    block = local_atoms * atom_axis // frame_axis
    blocks = frame_axis // atom_axis
    me_f = lax.axis_index("frames")
    me_a = lax.axis_index("atoms")
    half = lax.rem(me_f, blocks).astype(jnp.int32).reshape(1)
    owner = lax.div(me_f, blocks)
    role = lax.bitwise_xor(me_a, owner).astype(jnp.int32).reshape(1)
    x = pinned(jnp.transpose(frames, (1, 0, 2)), pltpu.HBM)
    mean_structure = pinned(mean_structure, pltpu.HBM)
    stats, x, mean_structure = pl.pallas_call(
        stats_kernel,
        out_shape=(
            pltpu.VMEM((STATS, local_frames), jnp.float32),
            pltpu.VMEM(x.shape, jnp.float32),
            pltpu.VMEM(mean_structure.shape, jnp.float32),
        ),
        in_specs=[HBM, HBM],
        out_specs=(VMEM, VMEM, VMEM),
        scratch_shapes=[pltpu.SemaphoreType.DMA((2,))],
        compiler_params=params(8),
        name="local_moments",
    )(x, mean_structure)
    def swap(value, distance):
        return lax.ppermute(value, "atoms", [(a, a ^ distance) for a in range(atom_axis)])

    others = [swap(stats, d) for d in range(1, atom_axis)]
    run = local_atoms // 4
    piece = (3, run, 2 * local_frames)
    own, flat = pl.pallas_call(
        functools.partial(align_kernel, atom_axis),
        out_shape=(
            jax.ShapeDtypeStruct((2,) + piece, jnp.bfloat16),
            jax.ShapeDtypeStruct(x.shape, jnp.bfloat16),
        ),
        in_specs=[VMEM] * (atom_axis + 2),
        out_specs=(VMEM, VMEM),
        scratch_shapes=[pltpu.VMEM((LANES, LANES), jnp.float32)],
        compiler_params=params(8),
        name="polar_align",
    )(stats, *others, x, mean_structure)
    share = jax.ShapeDtypeStruct((local_frames, eigvecs.shape[2] // atom_axis), jnp.float32)
    shares = pl.pallas_call(
        project_kernel,
        out_shape=(share,) * atom_axis,
        in_specs=[SMEM, VMEM, VMEM],
        out_specs=(VMEM,) * atom_axis,
        scratch_shapes=[pltpu.VMEM((atom_axis,) + share.shape, jnp.float32)],
        compiler_params=params(8),
        name="project",
    )(me_a.astype(jnp.int32).reshape(1), flat, eigvecs)
    parts = [shares[0]] + [swap(shares[d], d) for d in range(1, atom_axis)]
    def pairs(source, target):
        return [
            (
                f * atom_axis + ((f // blocks) ^ source),
                f * atom_axis + ((f // blocks) ^ target),
            )
            for f in range(frame_axis)
        ]

    if blocks != 2 or frame_axis != 8:
        projections = sum(parts)
        spread_pairs = [pairs(0, d) for d in range(1, atom_axis)]
        covariance = long_axis_covariance(
            flat, half[0], role[0], block, spread_pairs, 1.0 / total_frames
        )
        return covariance, projections

    axes = ("frames", "atoms")

    def columns(slots):
        return pltpu.VMEM((slots, 3, local_frames, block), jnp.bfloat16)

    def kernel(body, out_shape, scalar, values, name):
        single = not isinstance(out_shape, tuple)
        return pl.pallas_call(
            body,
            out_shape=out_shape,
            in_specs=[SMEM] + [VMEM] * len(values),
            out_specs=VMEM if single else (VMEM,) * len(out_shape),
            compiler_params=params(4),
            name=name,
        )(scalar, *[pinned(value, pltpu.VMEM) for value in values])

    def cross(cut):
        return [cut, lax.ppermute(cut, axes, pairs(0, 2))]

    def pass_on(values, role):
        slots = sum(value.shape[0] for value in values[::2])
        held = kernel(pass_on_kernel, columns(slots), role, values, "pass_on")
        return [held, swap(held, 1)]

    def halves_across(cut, *earlier):
        beside = swap(cut, 1)
        half_shape = pltpu.VMEM(cut.shape[:3] + (block // 2,), jnp.bfloat16)
        picked = kernel(
            pick_half_kernel, half_shape, after(role, *earlier), [cut, beside], "pick_half"
        )
        across = swap(picked, 2)
        return [cut, beside, across, swap(across, 1)], picked

    order = ring_order(frame_axis)
    forward = [(order[i], order[(i + 1) % frame_axis]) for i in range(frame_axis)]
    backward = [(b, a) for a, b in forward]

    def hop(up, down):
        return lax.ppermute(up, "frames", forward), lax.ppermute(down, "frames", backward)

    one = hop(own, own)
    crossed = cross(kernel(cut_kernel, columns(1), half, [own], "cut_columns"))
    cut_one = kernel(cut_kernel, columns(2), half, list(one), "cut_columns")
    two = hop(after(one[0], crossed[1], *parts), one[1])
    in_hbm = pass_on(crossed + cross(cut_one), role)
    cut_two = kernel(cut_kernel, columns(2), half, list(two), "cut_columns")
    three = hop(*two)
    in_hbm += pass_on(cross(cut_two), role)
    half_shard = pltpu.VMEM(piece, jnp.bfloat16)
    cut_three, *halves = kernel(
        cut_last_kernel,
        (columns(2), half_shard, half_shard),
        after(half, in_hbm[0]),
        list(three),
        "cut_columns",
    )
    far = hop(*halves)
    in_vmem, picked = halves_across(cut_three)
    cut_four = kernel(
        cut_far_kernel, columns(1), after(half, in_hbm[1], in_hbm[2], picked), list(far), "cut_columns"
    )
    in_vmem += halves_across(cut_four, in_vmem[2])[0]
    groups = ((3, True, 2), (2, True, 2), (2, False, 4), (1, False, 4))
    rows = [own, *one, *two, *three, *far]
    covariance, projections = pl.pallas_call(
        functools.partial(
            covariance_kernel, frame_axis, atom_axis, groups, 1.0 / total_frames
        ),
        out_shape=(jax.ShapeDtypeStruct((3, 3, local_atoms, block), jnp.float32), share),
        in_specs=[SMEM]
        + [VMEM] * len(rows)
        + [HBM] * len(in_hbm)
        + [VMEM] * len(in_vmem)
        + [HBM] * len(parts),
        out_specs=(ANY, VMEM),
        scratch_shapes=[
            pltpu.VMEM((2, 2 * run, total_frames), jnp.bfloat16),
            pltpu.VMEM((3, total_frames, block), jnp.bfloat16),
            pltpu.VMEM((2, 3, 2 * run, block), jnp.float32),
            pltpu.VMEM((atom_axis,) + share.shape, jnp.float32),
            pltpu.SemaphoreType.DMA((2 * frame_axis,)),
            pltpu.SemaphoreType.DMA((2, 3)),
            pltpu.SemaphoreType.DMA((atom_axis,)),
        ],
        compiler_params=params(16),
        cost_estimate=pl.CostEstimate(
            flops=18 * local_atoms * block * total_frames,
            bytes_accessed=24 * MIB,
            transcendentals=0,
        ),
        name="covariance_tile",
    )(
        role,
        *[pinned(value, pltpu.VMEM) for value in rows],
        *[pinned(value, pltpu.HBM) for value in in_hbm],
        *[pinned(value, pltpu.VMEM) for value in in_vmem],
        *[pinned(value, pltpu.HBM) for value in parts],
    )
    return jnp.transpose(covariance, (0, 2, 1, 3)), projections


def solution(mesh):
    placed = (P("frames", None, "atoms"), P(None, "atoms"), P(None, "atoms", None))
    return jax.shard_map(
        per_device,
        mesh=mesh,
        in_specs=placed,
        out_specs=(P(None, "atoms", None, "frames"), P("frames", "atoms")),
        check_vma=False,
    )
```

```python
import functools

import jax
import jax.numpy as jnp
from jax import lax
from jax.experimental import pallas as pl
from jax.experimental.pallas import tpu as pltpu
from jax.sharding import PartitionSpec as P

POLAR = 6
LANES = 128
STATS = 24
VMEM = pl.BlockSpec(memory_space=pltpu.VMEM)
SMEM = pl.BlockSpec(memory_space=pltpu.SMEM)
HBM = pl.BlockSpec(memory_space=pltpu.HBM)
ANY = pl.BlockSpec(memory_space=pl.ANY)
MIB = 1024 * 1024


def params(mib):
    return pltpu.CompilerParams(vmem_limit_bytes=mib * MIB)


def lane_mean(value):
    return jnp.sum(value, axis=1, keepdims=True) * (1.0 / value.shape[1])


def run_copies(copies):
    for copy in copies:
        copy.start()
    for copy in copies:
        copy.wait()


def stats_kernel(x_hbm, ref_hbm, out_ref, x_ref, ref_ref, sem):
    run_copies(
        [
            pltpu.make_async_copy(ref_hbm, ref_ref, sem.at[0]),
            pltpu.make_async_copy(x_hbm, x_ref, sem.at[1]),
        ]
    )
    values = []
    centred = []
    for i in range(3):
        x = x_ref[i]
        mean = lane_mean(x)
        values.append(mean)
        centred.append(x - mean)
    values.append(sum(jnp.sum(c * c, axis=1, keepdims=True) for c in centred))
    ref_mean = [lane_mean(ref_ref[j : j + 1, :]) for j in range(3)]
    ref_centred = [ref_ref[j : j + 1, :] - ref_mean[j] for j in range(3)]
    for i in range(3):
        for j in range(3):
            values.append(jnp.sum(centred[i] * ref_centred[j], axis=1, keepdims=True))
    values += ref_mean
    values.append(sum(jnp.sum(c * c, axis=1, keepdims=True) for c in ref_centred))
    shape = (x_ref.shape[1], LANES)
    lane = lax.broadcasted_iota(jnp.int32, shape, 1)
    out = jnp.zeros(shape, jnp.float32)
    for k, value in enumerate(values):
        out = jnp.where(lane == k, jnp.broadcast_to(value, shape), out)
    out_ref[...] = out.T[:STATS]


def align_kernel(parts, *refs):
    stats = refs[:parts]
    x_ref, ref_ref, piece_ref, flat_ref, turn = refs[parts:]
    local = x_ref.shape[2]
    rows = x_ref.shape[1]

    def row(at):
        return [s[at : at + 1, :] for s in stats]

    means = [row(i) for i in range(3)]
    ref_means = [row(13 + j) for j in range(3)]
    centre = [sum(m) * (1.0 / parts) for m in means]
    ref_centre = [sum(r) * (1.0 / parts) for r in ref_means]
    off = [[m - centre[i] for m in means[i]] for i in range(3)]
    ref_off = [[r - ref_centre[j] for r in ref_means[j]] for j in range(3)]
    spread = sum(row(3)) + local * sum(o * o for i in range(3) for o in off[i])
    ref_spread = sum(row(16)) + local * sum(o * o for j in range(3) for o in ref_off[j])
    scale = 1.0 / jnp.sqrt(spread * ref_spread + 1e-06)
    now = [
        [
            (sum(row(4 + 3 * i + j)) + local * sum(o * r for o, r in zip(off[i], ref_off[j])))
            * scale
            for j in range(3)
        ]
        for i in range(3)
    ]
    for _ in range(POLAR):
        gram = {}
        for i in range(3):
            for j in range(i, 3):
                gram[i, j] = sum(now[k][i] * now[k][j] for k in range(3))
                gram[j, i] = gram[i, j]
        left = [
            [(1.5 if k == j else 0.0) - 0.5 * gram[k, j] for j in range(3)] for k in range(3)
        ]
        now = [
            [sum(now[i][k] * left[k][j] for k in range(3)) for j in range(3)]
            for i in range(3)
        ]
    for k, value in enumerate(sum(now, []) + centre + ref_centre):
        turn[k : k + 1, :rows] = value
    turned = turn[...].T
    column = [turned[:rows, k : k + 1] for k in range(12)]
    centred = [x_ref[j] - column[9 + j] for j in range(3)]
    for i in range(3):
        target = ref_ref[i : i + 1, :] - turned[0:1, 12 + i : 13 + i]
        moved = sum(column[3 * j + i] * centred[j] for j in range(3)) - target
        flat_ref[i] = moved.astype(jnp.bfloat16)
        run = piece_ref.shape[2]
        for at in range(2):
            pair = [moved[:, (2 * at + k) * run : (2 * at + k + 1) * run] for k in range(2)]
            piece_ref[at, i] = jnp.concatenate(pair, axis=0).T.astype(jnp.bfloat16)


def project_kernel(me_ref, flat_ref, eig_ref, *refs):
    shares, cut = refs[:-1], refs[-1]
    total = sum(
        jnp.dot(flat_ref[c], eig_ref[c], preferred_element_type=jnp.float32) for c in range(3)
    )
    width = cut.shape[2]
    for k in range(len(shares)):
        cut[k] = total[:, k * width : (k + 1) * width]
    for k, share in enumerate(shares):
        share[...] = cut[lax.bitwise_xor(me_ref[0], k)]


def cut_columns(half_ref, halves, cols_ref):
    for half in range(2):

        @pl.when(half_ref[0] == half)
        def _(half=half):
            for k, pair in enumerate(halves):
                run, lanes = pair[half].shape[1:]
                for c in range(3):
                    turned = pair[half][c].astype(jnp.float32).T.astype(jnp.bfloat16)
                    cols_ref[k, c, :, :run] = turned[: lanes // 2]
                    cols_ref[k, c, :, run:] = turned[lanes // 2 :]


def cut_kernel(half_ref, *refs):
    cut_columns(half_ref, [(r.at[0], r.at[1]) for r in refs[:-1]], refs[-1])


def cut_last_kernel(half_ref, up_ref, down_ref, cols_ref, up_half, down_half):
    up_half[...] = up_ref[0]
    down_half[...] = down_ref[1]
    cut_columns(half_ref, [(r.at[0], r.at[1]) for r in (up_ref, down_ref)], cols_ref)


def cut_far_kernel(half_ref, up_half, down_half, cols_ref):
    cut_columns(half_ref, [(up_half, down_half)], cols_ref)


def pass_on_kernel(role_ref, *refs):
    sources, out_ref = refs[:-1], refs[-1]
    for role in range(2):

        @pl.when((role_ref[0] != 0) == bool(role))
        def _(role=role):
            to = 0
            for source in sources[role::2]:
                out_ref[to : to + source.shape[0]] = source[...]
                to += source.shape[0]


def pick_half_kernel(role_ref, own_ref, beside_ref, out_ref):
    width = out_ref.shape[3]

    @pl.when(role_ref[0] == 0)
    def _():
        out_ref[...] = own_ref[:, :, :, :width]

    @pl.when(role_ref[0] != 0)
    def _():
        out_ref[...] = beside_ref[:, :, :, width:]


def side_by_side(first, second):
    middle = first.shape[1] // 2
    left = jnp.concatenate([first[:, :middle], second[:, :middle]], axis=1)
    right = jnp.concatenate([first[:, middle:], second[:, middle:]], axis=1)
    return left, right


def covariance_kernel(slots, roles, groups, scale, role_ref, *refs):
    shards, up_half, down_half = refs[: slots - 1], refs[slots - 1], refs[slots]
    refs = refs[slots + 1 :]
    arrays = []
    for _, _, count in groups:
        arrays.append(refs[:count])
        refs = refs[count:]
    shares, refs = refs[:roles], refs[roles:]
    out_ref, proj_ref, left, right, done, held, col_sem, out_sem, share_sem = refs
    sums = [
        pltpu.make_async_copy(part, held.at[k], share_sem.at[k]) for k, part in enumerate(shares)
    ]
    for copy in sums:
        copy.start()
    depth = right.shape[1] // slots
    run = up_half.shape[1]

    def parts_of(k, role):
        if len(arrays[k]) == 2:
            return [(arrays[k][role % 2], 0)]
        own, beside, across, halves = arrays[k]
        width = across.shape[3]
        return {
            0: [(own, 0)],
            1: [(beside, 0)],
            2: [(across, 0), (halves, width)],
            3: [(halves, 0), (across, width)],
        }[role]

    def fetches(k, role, to):
        return [
            pltpu.make_async_copy(
                source.at[n],
                right.at[:, pl.ds(to + n * depth, depth), pl.ds(at, source.shape[3])],
                col_sem.at[2 * (to // depth + n) + p],
            )
            for p, (source, at) in enumerate(parts_of(k, role))
            for n in range(groups[k][0])
        ]

    def for_each_group(from_hbm, act):
        for role in range(roles):

            @pl.when(role_ref[0] == role)
            def _(role=role):
                to = 0
                for k, (count, in_hbm, _) in enumerate(groups):
                    if in_hbm == from_hbm:
                        act(k, role, to)
                    to += count * depth

    def start(k, role, to):
        for copy in fetches(k, role, to):
            copy.start()

    def wait(k, role, to):
        for copy in fetches(k, role, to):
            copy.wait()

    def load(k, role, to):
        for source, at in parts_of(k, role):
            for n in range(groups[k][0]):
                for d in range(3):
                    right[
                        d, to + n * depth : to + (n + 1) * depth, at : at + source.shape[3]
                    ] = source[n, d]

    def piece(slot, at, c):
        if slot < slots - 1:
            return shards[slot][at, c]
        return (up_half, down_half)[at][c]

    def assemble(c, at):
        for q in range(slots // 2):
            low, high = side_by_side(piece(2 * q, at, c), piece(2 * q + 1, at, c))
            left[at, :run, q * LANES : (q + 1) * LANES] = low
            left[at, run:, q * LANES : (q + 1) * LANES] = high

    for_each_group(True, start)
    for_each_group(False, load)
    assemble(0, 0)
    for_each_group(True, wait)
    for copy in sums:
        copy.wait()
    proj_ref[...] = sum(held[k] for k in range(roles))

    def write(c, at, d):
        return pltpu.make_async_copy(
            done.at[at, d],
            out_ref.at[c, d, pl.ds(at * 2 * run, 2 * run), :],
            out_sem.at[at, d],
        )

    @pl.loop(0, 3)
    def _(c):
        for at in range(2):

            @pl.when(c > 0)
            def _():
                for d in range(3):
                    write(c - 1, at, d).wait()

            assemble(jnp.minimum(c + at, 2), 1 - at)
            for d in range(3):
                done[at, d] = scale * jnp.dot(
                    left[at], right[d], preferred_element_type=jnp.float32
                )
                write(c, at, d).start()

    for at in range(2):
        for d in range(3):
            write(2, at, d).wait()


pinned = pltpu.with_memory_space_constraint


def after(value, *others):
    return lax.optimization_barrier((value,) + others)[0] if others else value


def ring_order(count):
    return list(range(0, count, 2)) + list(range(1, count, 2))[::-1]


def long_axis_covariance(flat, half, role, block, spread_pairs, scale):
    rows = lax.all_gather(flat, "frames", axis=1, tiled=True)
    cut = lax.dynamic_slice_in_dim(rows, half * block, block, axis=2)
    cols = jnp.where(role == 0, cut, jnp.zeros_like(cut))
    for d, pairs in enumerate(spread_pairs):
        sent = lax.ppermute(cut, ("frames", "atoms"), pairs)
        cols = jnp.where(role == d + 1, sent, cols)
    return scale * jnp.einsum(
        "cfp,dfq->cpdq", rows, cols, preferred_element_type=jnp.float32
    )


def per_device(frames, mean_structure, eigvecs):
    local_frames, _, local_atoms = frames.shape
    frame_axis = lax.axis_size("frames")
    atom_axis = lax.axis_size("atoms")
    total_frames = local_frames * frame_axis
    block = local_atoms * atom_axis // frame_axis
    blocks = frame_axis // atom_axis
    me_f = lax.axis_index("frames")
    me_a = lax.axis_index("atoms")
    half = lax.rem(me_f, blocks).astype(jnp.int32).reshape(1)
    owner = lax.div(me_f, blocks)
    role = lax.bitwise_xor(me_a, owner).astype(jnp.int32).reshape(1)
    x = pinned(jnp.transpose(frames, (1, 0, 2)), pltpu.HBM)
    mean_structure = pinned(mean_structure, pltpu.HBM)
    stats, x, mean_structure = pl.pallas_call(
        stats_kernel,
        out_shape=(
            pltpu.VMEM((STATS, local_frames), jnp.float32),
            pltpu.VMEM(x.shape, jnp.float32),
            pltpu.VMEM(mean_structure.shape, jnp.float32),
        ),
        in_specs=[HBM, HBM],
        out_specs=(VMEM, VMEM, VMEM),
        scratch_shapes=[pltpu.SemaphoreType.DMA((2,))],
        compiler_params=params(8),
        name="local_moments",
    )(x, mean_structure)
    def swap(value, distance):
        return lax.ppermute(value, "atoms", [(a, a ^ distance) for a in range(atom_axis)])

    others = [swap(stats, d) for d in range(1, atom_axis)]
    run = local_atoms // 4
    piece = (3, run, 2 * local_frames)
    own, flat = pl.pallas_call(
        functools.partial(align_kernel, atom_axis),
        out_shape=(
            jax.ShapeDtypeStruct((2,) + piece, jnp.bfloat16),
            jax.ShapeDtypeStruct(x.shape, jnp.bfloat16),
        ),
        in_specs=[VMEM] * (atom_axis + 2),
        out_specs=(VMEM, VMEM),
        scratch_shapes=[pltpu.VMEM((LANES, LANES), jnp.float32)],
        compiler_params=params(8),
        name="polar_align",
    )(stats, *others, x, mean_structure)
    share = jax.ShapeDtypeStruct((local_frames, eigvecs.shape[2] // atom_axis), jnp.float32)
    shares = pl.pallas_call(
        project_kernel,
        out_shape=(share,) * atom_axis,
        in_specs=[SMEM, VMEM, VMEM],
        out_specs=(VMEM,) * atom_axis,
        scratch_shapes=[pltpu.VMEM((atom_axis,) + share.shape, jnp.float32)],
        compiler_params=params(8),
        name="project",
    )(me_a.astype(jnp.int32).reshape(1), flat, eigvecs)
    parts = [shares[0]] + [swap(shares[d], d) for d in range(1, atom_axis)]
    def pairs(source, target):
        return [
            (
                f * atom_axis + ((f // blocks) ^ source),
                f * atom_axis + ((f // blocks) ^ target),
            )
            for f in range(frame_axis)
        ]

    if blocks != 2 or frame_axis != 8:
        projections = sum(parts)
        spread_pairs = [pairs(0, d) for d in range(1, atom_axis)]
        covariance = long_axis_covariance(
            flat, half[0], role[0], block, spread_pairs, 1.0 / total_frames
        )
        return covariance, projections

    axes = ("frames", "atoms")

    def columns(slots):
        return pltpu.VMEM((slots, 3, local_frames, block), jnp.bfloat16)

    def kernel(body, out_shape, scalar, values, name):
        single = not isinstance(out_shape, tuple)
        return pl.pallas_call(
            body,
            out_shape=out_shape,
            in_specs=[SMEM] + [VMEM] * len(values),
            out_specs=VMEM if single else (VMEM,) * len(out_shape),
            compiler_params=params(4),
            name=name,
        )(scalar, *[pinned(value, pltpu.VMEM) for value in values])

    def cross(cut):
        return [cut, lax.ppermute(cut, axes, pairs(0, 2))]

    def pass_on(values, role):
        slots = sum(value.shape[0] for value in values[::2])
        held = kernel(pass_on_kernel, columns(slots), role, values, "pass_on")
        return [held, swap(held, 1)]

    def halves_across(cut, *earlier):
        beside = swap(cut, 1)
        half_shape = pltpu.VMEM(cut.shape[:3] + (block // 2,), jnp.bfloat16)
        picked = kernel(
            pick_half_kernel, half_shape, after(role, *earlier), [cut, beside], "pick_half"
        )
        across = swap(picked, 2)
        return [cut, beside, across, swap(across, 1)], picked

    order = ring_order(frame_axis)
    forward = [(order[i], order[(i + 1) % frame_axis]) for i in range(frame_axis)]
    backward = [(b, a) for a, b in forward]

    def hop(up, down):
        return lax.ppermute(up, "frames", forward), lax.ppermute(down, "frames", backward)

    one = hop(own, own)
    crossed = cross(kernel(cut_kernel, columns(1), half, [own], "cut_columns"))
    cut_one = kernel(cut_kernel, columns(2), half, list(one), "cut_columns")
    two = hop(after(one[0], crossed[1]), one[1])
    in_hbm = pass_on(crossed + cross(cut_one), role)
    cut_two = kernel(cut_kernel, columns(2), half, list(two), "cut_columns")
    three = hop(after(two[0], *parts), two[1])
    in_vmem = pass_on(cross(cut_two), role)
    half_shard = pltpu.VMEM(piece, jnp.bfloat16)
    cut_three, *halves = kernel(
        cut_last_kernel,
        (columns(2), half_shard, half_shard),
        after(half, in_hbm[0]),
        list(three),
        "cut_columns",
    )
    far = hop(*halves)
    three_halves, picked = halves_across(cut_three)
    in_vmem += three_halves
    cut_four = kernel(
        cut_far_kernel, columns(1), after(half, in_hbm[1], in_vmem[0], picked), list(far), "cut_columns"
    )
    in_vmem += halves_across(cut_four, three_halves[2])[0]
    groups = ((3, True, 2), (2, False, 2), (2, False, 4), (1, False, 4))
    rows = [own, *one, *two, *three, *far]
    covariance, projections = pl.pallas_call(
        functools.partial(
            covariance_kernel, frame_axis, atom_axis, groups, 1.0 / total_frames
        ),
        out_shape=(jax.ShapeDtypeStruct((3, 3, local_atoms, block), jnp.float32), share),
        in_specs=[SMEM]
        + [VMEM] * len(rows)
        + [HBM] * len(in_hbm)
        + [VMEM] * len(in_vmem)
        + [HBM] * len(parts),
        out_specs=(ANY, VMEM),
        scratch_shapes=[
            pltpu.VMEM((2, 2 * run, total_frames), jnp.bfloat16),
            pltpu.VMEM((3, total_frames, block), jnp.bfloat16),
            pltpu.VMEM((2, 3, 2 * run, block), jnp.float32),
            pltpu.VMEM((atom_axis,) + share.shape, jnp.float32),
            pltpu.SemaphoreType.DMA((2 * frame_axis,)),
            pltpu.SemaphoreType.DMA((2, 3)),
            pltpu.SemaphoreType.DMA((atom_axis,)),
        ],
        compiler_params=params(16),
        cost_estimate=pl.CostEstimate(
            flops=18 * local_atoms * block * total_frames,
            bytes_accessed=24 * MIB,
            transcendentals=0,
        ),
        name="covariance_tile",
    )(
        role,
        *[pinned(value, pltpu.VMEM) for value in rows],
        *[pinned(value, pltpu.HBM) for value in in_hbm],
        *[pinned(value, pltpu.VMEM) for value in in_vmem],
        *[pinned(value, pltpu.HBM) for value in parts],
    )
    return jnp.transpose(covariance, (0, 2, 1, 3)), projections


def solution(mesh):
    placed = (P("frames", None, "atoms"), P(None, "atoms"), P(None, "atoms", None))
    return jax.shard_map(
        per_device,
        mesh=mesh,
        in_specs=placed,
        out_specs=(P(None, "atoms", None, "frames"), P("frames", "atoms")),
        check_vma=False,
    )
```

```python
import functools

import jax
import jax.numpy as jnp
from jax import lax
from jax.experimental import pallas as pl
from jax.experimental.pallas import tpu as pltpu
from jax.sharding import PartitionSpec as P

POLAR = 6
LANES = 128
STATS = 24
VMEM = pl.BlockSpec(memory_space=pltpu.VMEM)
SMEM = pl.BlockSpec(memory_space=pltpu.SMEM)
HBM = pl.BlockSpec(memory_space=pltpu.HBM)
ANY = pl.BlockSpec(memory_space=pl.ANY)
MIB = 1024 * 1024


def params(mib):
    return pltpu.CompilerParams(vmem_limit_bytes=mib * MIB)


def lane_mean(value):
    return jnp.sum(value, axis=1, keepdims=True) * (1.0 / value.shape[1])


def run_copies(copies):
    for copy in copies:
        copy.start()
    for copy in copies:
        copy.wait()


def stats_kernel(x_hbm, ref_hbm, out_ref, x_ref, ref_ref, sem):
    run_copies(
        [
            pltpu.make_async_copy(ref_hbm, ref_ref, sem.at[0]),
            pltpu.make_async_copy(x_hbm, x_ref, sem.at[1]),
        ]
    )
    values = []
    centred = []
    for i in range(3):
        x = x_ref[i]
        mean = lane_mean(x)
        values.append(mean)
        centred.append(x - mean)
    values.append(sum(jnp.sum(c * c, axis=1, keepdims=True) for c in centred))
    ref_mean = [lane_mean(ref_ref[j : j + 1, :]) for j in range(3)]
    ref_centred = [ref_ref[j : j + 1, :] - ref_mean[j] for j in range(3)]
    for i in range(3):
        for j in range(3):
            values.append(jnp.sum(centred[i] * ref_centred[j], axis=1, keepdims=True))
    values += ref_mean
    values.append(sum(jnp.sum(c * c, axis=1, keepdims=True) for c in ref_centred))
    shape = (x_ref.shape[1], LANES)
    lane = lax.broadcasted_iota(jnp.int32, shape, 1)
    out = jnp.zeros(shape, jnp.float32)
    for k, value in enumerate(values):
        out = jnp.where(lane == k, jnp.broadcast_to(value, shape), out)
    out_ref[...] = out.T[:STATS]


def align_kernel(parts, *refs):
    stats = refs[:parts]
    x_ref, ref_ref, piece_ref, flat_ref, turn = refs[parts:]
    local = x_ref.shape[2]
    rows = x_ref.shape[1]

    def row(at):
        return [s[at : at + 1, :] for s in stats]

    means = [row(i) for i in range(3)]
    ref_means = [row(13 + j) for j in range(3)]
    centre = [sum(m) * (1.0 / parts) for m in means]
    ref_centre = [sum(r) * (1.0 / parts) for r in ref_means]
    off = [[m - centre[i] for m in means[i]] for i in range(3)]
    ref_off = [[r - ref_centre[j] for r in ref_means[j]] for j in range(3)]
    spread = sum(row(3)) + local * sum(o * o for i in range(3) for o in off[i])
    ref_spread = sum(row(16)) + local * sum(o * o for j in range(3) for o in ref_off[j])
    scale = 1.0 / jnp.sqrt(spread * ref_spread + 1e-06)
    now = [
        [
            (sum(row(4 + 3 * i + j)) + local * sum(o * r for o, r in zip(off[i], ref_off[j])))
            * scale
            for j in range(3)
        ]
        for i in range(3)
    ]
    for _ in range(POLAR):
        gram = {}
        for i in range(3):
            for j in range(i, 3):
                gram[i, j] = sum(now[k][i] * now[k][j] for k in range(3))
                gram[j, i] = gram[i, j]
        left = [
            [(1.5 if k == j else 0.0) - 0.5 * gram[k, j] for j in range(3)] for k in range(3)
        ]
        now = [
            [sum(now[i][k] * left[k][j] for k in range(3)) for j in range(3)]
            for i in range(3)
        ]
    for k, value in enumerate(sum(now, []) + centre + ref_centre):
        turn[k : k + 1, :rows] = value
    turned = turn[...].T
    column = [turned[:rows, k : k + 1] for k in range(12)]
    centred = [x_ref[j] - column[9 + j] for j in range(3)]
    for i in range(3):
        target = ref_ref[i : i + 1, :] - turned[0:1, 12 + i : 13 + i]
        moved = sum(column[3 * j + i] * centred[j] for j in range(3)) - target
        flat_ref[i] = moved.astype(jnp.bfloat16)
        run = piece_ref.shape[2]
        for at in range(2):
            pair = [moved[:, (2 * at + k) * run : (2 * at + k + 1) * run] for k in range(2)]
            piece_ref[at, i] = jnp.concatenate(pair, axis=0).T.astype(jnp.bfloat16)


def project_kernel(me_ref, flat_ref, eig_ref, *refs):
    shares, cut = refs[:-1], refs[-1]
    total = sum(
        jnp.dot(flat_ref[c], eig_ref[c], preferred_element_type=jnp.float32) for c in range(3)
    )
    width = cut.shape[2]
    for k in range(len(shares)):
        cut[k] = total[:, k * width : (k + 1) * width]
    for k, share in enumerate(shares):
        share[...] = cut[lax.bitwise_xor(me_ref[0], k)]


def cut_columns(half_ref, halves, cols_ref):
    for half in range(2):

        @pl.when(half_ref[0] == half)
        def _(half=half):
            for k, pair in enumerate(halves):
                run, lanes = pair[half].shape[1:]
                for c in range(3):
                    turned = pair[half][c].astype(jnp.float32).T.astype(jnp.bfloat16)
                    cols_ref[k, c, :, :run] = turned[: lanes // 2]
                    cols_ref[k, c, :, run:] = turned[lanes // 2 :]


def cut_kernel(half_ref, *refs):
    cut_columns(half_ref, [(r.at[0], r.at[1]) for r in refs[:-1]], refs[-1])


def cut_last_kernel(half_ref, up_ref, down_ref, cols_ref, up_half, down_half):
    up_half[...] = up_ref[0]
    down_half[...] = down_ref[1]
    cut_columns(half_ref, [(r.at[0], r.at[1]) for r in (up_ref, down_ref)], cols_ref)


def cut_far_kernel(half_ref, up_half, down_half, cols_ref):
    cut_columns(half_ref, [(up_half, down_half)], cols_ref)


def pass_on_kernel(role_ref, *refs):
    sources, out_ref = refs[:-1], refs[-1]
    for role in range(2):

        @pl.when((role_ref[0] != 0) == bool(role))
        def _(role=role):
            to = 0
            for source in sources[role::2]:
                out_ref[to : to + source.shape[0]] = source[...]
                to += source.shape[0]


def pick_half_kernel(role_ref, own_ref, beside_ref, out_ref):
    width = out_ref.shape[3]

    @pl.when(role_ref[0] == 0)
    def _():
        out_ref[...] = own_ref[:, :, :, :width]

    @pl.when(role_ref[0] != 0)
    def _():
        out_ref[...] = beside_ref[:, :, :, width:]


def side_by_side(first, second):
    middle = first.shape[1] // 2
    left = jnp.concatenate([first[:, :middle], second[:, :middle]], axis=1)
    right = jnp.concatenate([first[:, middle:], second[:, middle:]], axis=1)
    return left, right


def covariance_kernel(slots, roles, groups, scale, role_ref, *refs):
    shards, up_half, down_half = refs[: slots - 1], refs[slots - 1], refs[slots]
    refs = refs[slots + 1 :]
    arrays = []
    for _, _, count in groups:
        arrays.append(refs[:count])
        refs = refs[count:]
    shares, refs = refs[:roles], refs[roles:]
    out_ref, proj_ref, left, right, done, held, col_sem, out_sem, share_sem = refs
    sums = [
        pltpu.make_async_copy(part, held.at[k], share_sem.at[k]) for k, part in enumerate(shares)
    ]
    for copy in sums:
        copy.start()
    depth = right.shape[1] // slots
    run = up_half.shape[1]

    def parts_of(k, role):
        if len(arrays[k]) == 2:
            return [(arrays[k][role % 2], 0)]
        own, beside, across, halves = arrays[k]
        width = across.shape[3]
        return {
            0: [(own, 0)],
            1: [(beside, 0)],
            2: [(across, 0), (halves, width)],
            3: [(halves, 0), (across, width)],
        }[role]

    def fetches(k, role, to):
        return [
            pltpu.make_async_copy(
                source.at[n],
                right.at[:, pl.ds(to + n * depth, depth), pl.ds(at, source.shape[3])],
                col_sem.at[2 * (to // depth + n) + p],
            )
            for p, (source, at) in enumerate(parts_of(k, role))
            for n in range(groups[k][0])
        ]

    def for_each_group(from_hbm, act):
        for role in range(roles):

            @pl.when(role_ref[0] == role)
            def _(role=role):
                to = 0
                for k, (count, in_hbm, _) in enumerate(groups):
                    if in_hbm == from_hbm:
                        act(k, role, to)
                    to += count * depth

    def start(k, role, to):
        for copy in fetches(k, role, to):
            copy.start()

    def wait(k, role, to):
        for copy in fetches(k, role, to):
            copy.wait()

    def load(k, role, to):
        for source, at in parts_of(k, role):
            for n in range(groups[k][0]):
                for d in range(3):
                    right[
                        d, to + n * depth : to + (n + 1) * depth, at : at + source.shape[3]
                    ] = source[n, d]

    def piece(slot, at, c):
        if slot < slots - 1:
            return shards[slot][at, c]
        return (up_half, down_half)[at][c]

    def assemble(c, at):
        for q in range(slots // 2):
            low, high = side_by_side(piece(2 * q, at, c), piece(2 * q + 1, at, c))
            left[at, :run, q * LANES : (q + 1) * LANES] = low
            left[at, run:, q * LANES : (q + 1) * LANES] = high

    for_each_group(True, start)
    for_each_group(False, load)
    assemble(0, 0)
    for_each_group(True, wait)
    def write(c, at, d):
        return pltpu.make_async_copy(
            done.at[at, d],
            out_ref.at[c, d, pl.ds(at * 2 * run, 2 * run), :],
            out_sem.at[at, d],
        )

    @pl.loop(0, 3)
    def _(c):
        for at in range(2):

            @pl.when(c > 0)
            def _():
                for d in range(3):
                    write(c - 1, at, d).wait()

            assemble(jnp.minimum(c + at, 2), 1 - at)
            for d in range(3):
                done[at, d] = scale * jnp.dot(
                    left[at], right[d], preferred_element_type=jnp.float32
                )
                write(c, at, d).start()

    for copy in sums:
        copy.wait()
    held[0] = sum(held[k] for k in range(roles))
    leave = pltpu.make_async_copy(held.at[0], proj_ref, share_sem.at[0])
    leave.start()
    for at in range(2):
        for d in range(3):
            write(2, at, d).wait()
    leave.wait()


pinned = pltpu.with_memory_space_constraint


def after(value, *others):
    return lax.optimization_barrier((value,) + others)[0] if others else value


def ring_order(count):
    return list(range(0, count, 2)) + list(range(1, count, 2))[::-1]


def long_axis_covariance(flat, half, role, block, spread_pairs, scale):
    rows = lax.all_gather(flat, "frames", axis=1, tiled=True)
    cut = lax.dynamic_slice_in_dim(rows, half * block, block, axis=2)
    cols = jnp.where(role == 0, cut, jnp.zeros_like(cut))
    for d, pairs in enumerate(spread_pairs):
        sent = lax.ppermute(cut, ("frames", "atoms"), pairs)
        cols = jnp.where(role == d + 1, sent, cols)
    return scale * jnp.einsum(
        "cfp,dfq->cpdq", rows, cols, preferred_element_type=jnp.float32
    )


def per_device(frames, mean_structure, eigvecs):
    local_frames, _, local_atoms = frames.shape
    frame_axis = lax.axis_size("frames")
    atom_axis = lax.axis_size("atoms")
    total_frames = local_frames * frame_axis
    block = local_atoms * atom_axis // frame_axis
    blocks = frame_axis // atom_axis
    me_f = lax.axis_index("frames")
    me_a = lax.axis_index("atoms")
    half = lax.rem(me_f, blocks).astype(jnp.int32).reshape(1)
    owner = lax.div(me_f, blocks)
    role = lax.bitwise_xor(me_a, owner).astype(jnp.int32).reshape(1)
    x = pinned(jnp.transpose(frames, (1, 0, 2)), pltpu.HBM)
    mean_structure = pinned(mean_structure, pltpu.HBM)
    stats, x, mean_structure = pl.pallas_call(
        stats_kernel,
        out_shape=(
            pltpu.VMEM((STATS, local_frames), jnp.float32),
            pltpu.VMEM(x.shape, jnp.float32),
            pltpu.VMEM(mean_structure.shape, jnp.float32),
        ),
        in_specs=[HBM, HBM],
        out_specs=(VMEM, VMEM, VMEM),
        scratch_shapes=[pltpu.SemaphoreType.DMA((2,))],
        compiler_params=params(8),
        name="local_moments",
    )(x, mean_structure)
    def swap(value, distance):
        return lax.ppermute(value, "atoms", [(a, a ^ distance) for a in range(atom_axis)])

    others = [swap(stats, d) for d in range(1, atom_axis)]
    run = local_atoms // 4
    piece = (3, run, 2 * local_frames)
    own, flat = pl.pallas_call(
        functools.partial(align_kernel, atom_axis),
        out_shape=(
            jax.ShapeDtypeStruct((2,) + piece, jnp.bfloat16),
            jax.ShapeDtypeStruct(x.shape, jnp.bfloat16),
        ),
        in_specs=[VMEM] * (atom_axis + 2),
        out_specs=(VMEM, VMEM),
        scratch_shapes=[pltpu.VMEM((LANES, LANES), jnp.float32)],
        compiler_params=params(8),
        name="polar_align",
    )(stats, *others, x, mean_structure)
    share = jax.ShapeDtypeStruct((local_frames, eigvecs.shape[2] // atom_axis), jnp.float32)
    shares = pl.pallas_call(
        project_kernel,
        out_shape=(share,) * atom_axis,
        in_specs=[SMEM, VMEM, VMEM],
        out_specs=(VMEM,) * atom_axis,
        scratch_shapes=[pltpu.VMEM((atom_axis,) + share.shape, jnp.float32)],
        compiler_params=params(8),
        name="project",
    )(me_a.astype(jnp.int32).reshape(1), flat, eigvecs)
    parts = [shares[0]] + [swap(shares[d], d) for d in range(1, atom_axis)]
    def pairs(source, target):
        return [
            (
                f * atom_axis + ((f // blocks) ^ source),
                f * atom_axis + ((f // blocks) ^ target),
            )
            for f in range(frame_axis)
        ]

    if blocks != 2 or frame_axis != 8:
        projections = sum(parts)
        spread_pairs = [pairs(0, d) for d in range(1, atom_axis)]
        covariance = long_axis_covariance(
            flat, half[0], role[0], block, spread_pairs, 1.0 / total_frames
        )
        return covariance, projections

    axes = ("frames", "atoms")

    def columns(slots):
        return pltpu.VMEM((slots, 3, local_frames, block), jnp.bfloat16)

    def kernel(body, out_shape, scalar, values, name):
        single = not isinstance(out_shape, tuple)
        return pl.pallas_call(
            body,
            out_shape=out_shape,
            in_specs=[SMEM] + [VMEM] * len(values),
            out_specs=VMEM if single else (VMEM,) * len(out_shape),
            compiler_params=params(4),
            name=name,
        )(scalar, *[pinned(value, pltpu.VMEM) for value in values])

    def cross(cut):
        return [cut, lax.ppermute(cut, axes, pairs(0, 2))]

    def pass_on(values, role):
        slots = sum(value.shape[0] for value in values[::2])
        held = kernel(pass_on_kernel, columns(slots), role, values, "pass_on")
        return [held, swap(held, 1)]

    def halves_across(cut, *earlier):
        beside = swap(cut, 1)
        half_shape = pltpu.VMEM(cut.shape[:3] + (block // 2,), jnp.bfloat16)
        picked = kernel(
            pick_half_kernel, half_shape, after(role, *earlier), [cut, beside], "pick_half"
        )
        across = swap(picked, 2)
        return [cut, beside, across, swap(across, 1)], picked

    order = ring_order(frame_axis)
    forward = [(order[i], order[(i + 1) % frame_axis]) for i in range(frame_axis)]
    backward = [(b, a) for a, b in forward]

    def hop(up, down):
        return lax.ppermute(up, "frames", forward), lax.ppermute(down, "frames", backward)

    one = hop(own, own)
    crossed = cross(kernel(cut_kernel, columns(1), half, [own], "cut_columns"))
    cut_one = kernel(cut_kernel, columns(2), half, list(one), "cut_columns")
    two = hop(after(one[0], crossed[1], *parts), one[1])
    in_hbm = pass_on(crossed + cross(cut_one), role)
    cut_two = kernel(cut_kernel, columns(2), half, list(two), "cut_columns")
    three = hop(*two)
    in_vmem = pass_on(cross(cut_two), role)
    half_shard = pltpu.VMEM(piece, jnp.bfloat16)
    cut_three, *halves = kernel(
        cut_last_kernel,
        (columns(2), half_shard, half_shard),
        after(half, in_hbm[0]),
        list(three),
        "cut_columns",
    )
    far = hop(*halves)
    three_halves, picked = halves_across(cut_three)
    in_vmem += three_halves
    cut_four = kernel(
        cut_far_kernel, columns(1), after(half, in_hbm[1], in_vmem[0], picked), list(far), "cut_columns"
    )
    in_vmem += halves_across(cut_four, three_halves[2])[0]
    groups = ((3, True, 2), (2, False, 2), (2, False, 4), (1, False, 4))
    rows = [own, *one, *two, *three, *far]
    covariance, projections = pl.pallas_call(
        functools.partial(
            covariance_kernel, frame_axis, atom_axis, groups, 1.0 / total_frames
        ),
        out_shape=(jax.ShapeDtypeStruct((3, 3, local_atoms, block), jnp.float32), share),
        in_specs=[SMEM]
        + [VMEM] * len(rows)
        + [HBM] * len(in_hbm)
        + [VMEM] * len(in_vmem)
        + [HBM] * len(parts),
        out_specs=(ANY, ANY),
        scratch_shapes=[
            pltpu.VMEM((2, 2 * run, total_frames), jnp.bfloat16),
            pltpu.VMEM((3, total_frames, block), jnp.bfloat16),
            pltpu.VMEM((2, 3, 2 * run, block), jnp.float32),
            pltpu.VMEM((atom_axis,) + share.shape, jnp.float32),
            pltpu.SemaphoreType.DMA((2 * frame_axis,)),
            pltpu.SemaphoreType.DMA((2, 3)),
            pltpu.SemaphoreType.DMA((atom_axis,)),
        ],
        compiler_params=params(16),
        cost_estimate=pl.CostEstimate(
            flops=18 * local_atoms * block * total_frames,
            bytes_accessed=24 * MIB,
            transcendentals=0,
        ),
        name="covariance_tile",
    )(
        role,
        *[pinned(value, pltpu.VMEM) for value in rows],
        *[pinned(value, pltpu.HBM) for value in in_hbm],
        *[pinned(value, pltpu.VMEM) for value in in_vmem],
        *[pinned(value, pltpu.HBM) for value in parts],
    )
    return jnp.transpose(covariance, (0, 2, 1, 3)), projections


def solution(mesh):
    placed = (P("frames", None, "atoms"), P(None, "atoms"), P(None, "atoms", None))
    return jax.shard_map(
        per_device,
        mesh=mesh,
        in_specs=placed,
        out_specs=(P(None, "atoms", None, "frames"), P("frames", "atoms")),
        check_vma=False,
    )
```

```python
import functools

import jax
import jax.numpy as jnp
from jax import lax
from jax.experimental import pallas as pl
from jax.experimental.pallas import tpu as pltpu
from jax.sharding import PartitionSpec as P

POLAR = 6
LANES = 128
STATS = 24
VMEM = pl.BlockSpec(memory_space=pltpu.VMEM)
SMEM = pl.BlockSpec(memory_space=pltpu.SMEM)
HBM = pl.BlockSpec(memory_space=pltpu.HBM)
ANY = pl.BlockSpec(memory_space=pl.ANY)
MIB = 1024 * 1024


def params(mib):
    return pltpu.CompilerParams(vmem_limit_bytes=mib * MIB)


def lane_mean(value):
    return jnp.sum(value, axis=1, keepdims=True) * (1.0 / value.shape[1])


def run_copies(copies):
    for copy in copies:
        copy.start()
    for copy in copies:
        copy.wait()


def stats_kernel(x_hbm, ref_hbm, out_ref, x_ref, ref_ref, sem):
    run_copies(
        [
            pltpu.make_async_copy(ref_hbm, ref_ref, sem.at[0]),
            pltpu.make_async_copy(x_hbm, x_ref, sem.at[1]),
        ]
    )
    values = []
    centred = []
    for i in range(3):
        x = x_ref[i]
        mean = lane_mean(x)
        values.append(mean)
        centred.append(x - mean)
    values.append(sum(jnp.sum(c * c, axis=1, keepdims=True) for c in centred))
    ref_mean = [lane_mean(ref_ref[j : j + 1, :]) for j in range(3)]
    ref_centred = [ref_ref[j : j + 1, :] - ref_mean[j] for j in range(3)]
    for i in range(3):
        for j in range(3):
            values.append(jnp.sum(centred[i] * ref_centred[j], axis=1, keepdims=True))
    values += ref_mean
    values.append(sum(jnp.sum(c * c, axis=1, keepdims=True) for c in ref_centred))
    shape = (x_ref.shape[1], LANES)
    lane = lax.broadcasted_iota(jnp.int32, shape, 1)
    out = jnp.zeros(shape, jnp.float32)
    for k, value in enumerate(values):
        out = jnp.where(lane == k, jnp.broadcast_to(value, shape), out)
    out_ref[...] = out.T[:STATS]


def align_kernel(parts, *refs):
    stats = refs[:parts]
    x_ref, ref_ref, piece_ref, flat_ref, turn = refs[parts:]
    local = x_ref.shape[2]
    rows = x_ref.shape[1]

    def row(at):
        return [s[at : at + 1, :] for s in stats]

    means = [row(i) for i in range(3)]
    ref_means = [row(13 + j) for j in range(3)]
    centre = [sum(m) * (1.0 / parts) for m in means]
    ref_centre = [sum(r) * (1.0 / parts) for r in ref_means]
    off = [[m - centre[i] for m in means[i]] for i in range(3)]
    ref_off = [[r - ref_centre[j] for r in ref_means[j]] for j in range(3)]
    spread = sum(row(3)) + local * sum(o * o for i in range(3) for o in off[i])
    ref_spread = sum(row(16)) + local * sum(o * o for j in range(3) for o in ref_off[j])
    scale = 1.0 / jnp.sqrt(spread * ref_spread + 1e-06)
    now = [
        [
            (sum(row(4 + 3 * i + j)) + local * sum(o * r for o, r in zip(off[i], ref_off[j])))
            * scale
            for j in range(3)
        ]
        for i in range(3)
    ]
    for _ in range(POLAR):
        gram = {}
        for i in range(3):
            for j in range(i, 3):
                gram[i, j] = sum(now[k][i] * now[k][j] for k in range(3))
                gram[j, i] = gram[i, j]
        left = [
            [(1.5 if k == j else 0.0) - 0.5 * gram[k, j] for j in range(3)] for k in range(3)
        ]
        now = [
            [sum(now[i][k] * left[k][j] for k in range(3)) for j in range(3)]
            for i in range(3)
        ]
    for k, value in enumerate(sum(now, []) + centre + ref_centre):
        turn[k : k + 1, :rows] = value
    turned = turn[...].T
    column = [turned[:rows, k : k + 1] for k in range(12)]
    centred = [x_ref[j] - column[9 + j] for j in range(3)]
    for i in range(3):
        target = ref_ref[i : i + 1, :] - turned[0:1, 12 + i : 13 + i]
        moved = sum(column[3 * j + i] * centred[j] for j in range(3)) - target
        flat_ref[i] = moved.astype(jnp.bfloat16)
        run = piece_ref.shape[2]
        for at in range(2):
            pair = [moved[:, (2 * at + k) * run : (2 * at + k + 1) * run] for k in range(2)]
            piece_ref[at, i] = jnp.concatenate(pair, axis=0).T.astype(jnp.bfloat16)


def project_kernel(me_ref, flat_ref, eig_ref, *refs):
    shares, cut = refs[:-1], refs[-1]
    total = sum(
        jnp.dot(flat_ref[c], eig_ref[c], preferred_element_type=jnp.float32) for c in range(3)
    )
    width = cut.shape[2]
    for k in range(len(shares)):
        cut[k] = total[:, k * width : (k + 1) * width]
    for k, share in enumerate(shares):
        share[...] = cut[lax.bitwise_xor(me_ref[0], k)]


def cut_columns(half_ref, halves, cols_ref):
    for half in range(2):

        @pl.when(half_ref[0] == half)
        def _(half=half):
            for k, pair in enumerate(halves):
                run, lanes = pair[half].shape[1:]
                for c in range(3):
                    turned = pair[half][c].astype(jnp.float32).T.astype(jnp.bfloat16)
                    cols_ref[k, c, :, :run] = turned[: lanes // 2]
                    cols_ref[k, c, :, run:] = turned[lanes // 2 :]


def cut_kernel(half_ref, *refs):
    cut_columns(half_ref, [(r.at[0], r.at[1]) for r in refs[:-1]], refs[-1])


def cut_last_kernel(half_ref, up_ref, down_ref, cols_ref, up_half, down_half):
    up_half[...] = up_ref[0]
    down_half[...] = down_ref[1]
    cut_columns(half_ref, [(r.at[0], r.at[1]) for r in (up_ref, down_ref)], cols_ref)


def cut_far_kernel(half_ref, up_half, down_half, cols_ref):
    cut_columns(half_ref, [(up_half, down_half)], cols_ref)


def pass_on_kernel(role_ref, *refs):
    sources, out_ref = refs[:-1], refs[-1]
    for role in range(2):

        @pl.when((role_ref[0] != 0) == bool(role))
        def _(role=role):
            to = 0
            for source in sources[role::2]:
                out_ref[to : to + source.shape[0]] = source[...]
                to += source.shape[0]


def pick_half_kernel(role_ref, own_ref, beside_ref, out_ref):
    width = out_ref.shape[3]

    @pl.when(role_ref[0] == 0)
    def _():
        out_ref[...] = own_ref[:, :, :, :width]

    @pl.when(role_ref[0] != 0)
    def _():
        out_ref[...] = beside_ref[:, :, :, width:]


def side_by_side(first, second):
    middle = first.shape[1] // 2
    left = jnp.concatenate([first[:, :middle], second[:, :middle]], axis=1)
    right = jnp.concatenate([first[:, middle:], second[:, middle:]], axis=1)
    return left, right


def covariance_kernel(slots, roles, groups, scale, role_ref, *refs):
    shards, up_half, down_half = refs[: slots - 1], refs[slots - 1], refs[slots]
    refs = refs[slots + 1 :]
    arrays = []
    for _, _, count in groups:
        arrays.append(refs[:count])
        refs = refs[count:]
    shares, refs = refs[:roles], refs[roles:]
    out_ref, proj_ref, left, right, done, held, col_sem, out_sem, share_sem = refs
    sums = [
        pltpu.make_async_copy(part, held.at[k], share_sem.at[k]) for k, part in enumerate(shares)
    ]
    for copy in sums:
        copy.start()
    depth = right.shape[1] // slots
    run = up_half.shape[1]

    def parts_of(k, role):
        if len(arrays[k]) == 2:
            return [(arrays[k][role % 2], 0)]
        own, beside, across, halves = arrays[k]
        width = across.shape[3]
        return {
            0: [(own, 0)],
            1: [(beside, 0)],
            2: [(across, 0), (halves, width)],
            3: [(halves, 0), (across, width)],
        }[role]

    def fetches(k, role, to):
        return [
            pltpu.make_async_copy(
                source.at[n],
                right.at[:, pl.ds(to + n * depth, depth), pl.ds(at, source.shape[3])],
                col_sem.at[2 * (to // depth + n) + p],
            )
            for p, (source, at) in enumerate(parts_of(k, role))
            for n in range(groups[k][0])
        ]

    def for_each_group(from_hbm, act):
        for role in range(roles):

            @pl.when(role_ref[0] == role)
            def _(role=role):
                to = 0
                for k, (count, in_hbm, _) in enumerate(groups):
                    if in_hbm == from_hbm:
                        act(k, role, to)
                    to += count * depth

    def start(k, role, to):
        for copy in fetches(k, role, to):
            copy.start()

    def wait(k, role, to):
        for copy in fetches(k, role, to):
            copy.wait()

    def load(k, role, to):
        for source, at in parts_of(k, role):
            for n in range(groups[k][0]):
                for d in range(3):
                    right[
                        d, to + n * depth : to + (n + 1) * depth, at : at + source.shape[3]
                    ] = source[n, d]

    def piece(slot, at, c):
        if slot < slots - 1:
            return shards[slot][at, c]
        return (up_half, down_half)[at][c]

    def assemble(c, at):
        for q in range(slots // 2):
            low, high = side_by_side(piece(2 * q, at, c), piece(2 * q + 1, at, c))
            left[at, :run, q * LANES : (q + 1) * LANES] = low
            left[at, run:, q * LANES : (q + 1) * LANES] = high

    for_each_group(True, start)
    for_each_group(False, load)
    assemble(0, 0)
    for_each_group(True, wait)
    def write(c, at, d):
        return pltpu.make_async_copy(
            done.at[at, d],
            out_ref.at[c, d, pl.ds(at * 2 * run, 2 * run), :],
            out_sem.at[at, d],
        )

    @pl.loop(0, 3)
    def _(c):
        for at in range(2):

            @pl.when(c > 0)
            def _():
                for d in range(3):
                    write(c - 1, at, d).wait()

            assemble(jnp.minimum(c + at, 2), 1 - at)
            for d in range(3):
                done[at, d] = scale * jnp.dot(
                    left[at], right[d], preferred_element_type=jnp.float32
                )
                write(c, at, d).start()

    for copy in sums:
        copy.wait()
    held[0] = sum(held[k] for k in range(roles))
    leave = pltpu.make_async_copy(held.at[0], proj_ref, share_sem.at[0])
    leave.start()
    for at in range(2):
        for d in range(3):
            write(2, at, d).wait()
    leave.wait()


pinned = pltpu.with_memory_space_constraint


def after(value, *others):
    return lax.optimization_barrier((value,) + others)[0] if others else value


def ring_order(count):
    return list(range(0, count, 2)) + list(range(1, count, 2))[::-1]


def long_axis_covariance(flat, half, role, block, spread_pairs, scale):
    rows = lax.all_gather(flat, "frames", axis=1, tiled=True)
    cut = lax.dynamic_slice_in_dim(rows, half * block, block, axis=2)
    cols = jnp.where(role == 0, cut, jnp.zeros_like(cut))
    for d, pairs in enumerate(spread_pairs):
        sent = lax.ppermute(cut, ("frames", "atoms"), pairs)
        cols = jnp.where(role == d + 1, sent, cols)
    return scale * jnp.einsum(
        "cfp,dfq->cpdq", rows, cols, preferred_element_type=jnp.float32
    )


def per_device(frames, mean_structure, eigvecs):
    local_frames, _, local_atoms = frames.shape
    frame_axis = lax.axis_size("frames")
    atom_axis = lax.axis_size("atoms")
    total_frames = local_frames * frame_axis
    block = local_atoms * atom_axis // frame_axis
    blocks = frame_axis // atom_axis
    me_f = lax.axis_index("frames")
    me_a = lax.axis_index("atoms")
    half = lax.rem(me_f, blocks).astype(jnp.int32).reshape(1)
    owner = lax.div(me_f, blocks)
    role = lax.bitwise_xor(me_a, owner).astype(jnp.int32).reshape(1)
    x = pinned(jnp.transpose(frames, (1, 0, 2)), pltpu.HBM)
    mean_structure = pinned(mean_structure, pltpu.HBM)
    stats, x, mean_structure = pl.pallas_call(
        stats_kernel,
        out_shape=(
            pltpu.VMEM((STATS, local_frames), jnp.float32),
            pltpu.VMEM(x.shape, jnp.float32),
            pltpu.VMEM(mean_structure.shape, jnp.float32),
        ),
        in_specs=[HBM, HBM],
        out_specs=(VMEM, VMEM, VMEM),
        scratch_shapes=[pltpu.SemaphoreType.DMA((2,))],
        compiler_params=params(8),
        name="local_moments",
    )(x, mean_structure)
    def swap(value, distance):
        return lax.ppermute(value, "atoms", [(a, a ^ distance) for a in range(atom_axis)])

    others = [swap(stats, d) for d in range(1, atom_axis)]
    run = local_atoms // 4
    piece = (3, run, 2 * local_frames)
    own, flat = pl.pallas_call(
        functools.partial(align_kernel, atom_axis),
        out_shape=(
            jax.ShapeDtypeStruct((2,) + piece, jnp.bfloat16),
            jax.ShapeDtypeStruct(x.shape, jnp.bfloat16),
        ),
        in_specs=[VMEM] * (atom_axis + 2),
        out_specs=(VMEM, VMEM),
        scratch_shapes=[pltpu.VMEM((LANES, LANES), jnp.float32)],
        compiler_params=params(8),
        name="polar_align",
    )(stats, *others, x, mean_structure)
    share = jax.ShapeDtypeStruct((local_frames, eigvecs.shape[2] // atom_axis), jnp.float32)
    shares = pl.pallas_call(
        project_kernel,
        out_shape=(share,) * atom_axis,
        in_specs=[SMEM, VMEM, VMEM],
        out_specs=(VMEM,) * atom_axis,
        scratch_shapes=[pltpu.VMEM((atom_axis,) + share.shape, jnp.float32)],
        compiler_params=params(8),
        name="project",
    )(me_a.astype(jnp.int32).reshape(1), flat, eigvecs)
    parts = [shares[0]] + [swap(shares[d], d) for d in range(1, atom_axis)]
    def pairs(source, target):
        return [
            (
                f * atom_axis + ((f // blocks) ^ source),
                f * atom_axis + ((f // blocks) ^ target),
            )
            for f in range(frame_axis)
        ]

    if blocks != 2 or frame_axis != 8:
        projections = sum(parts)
        spread_pairs = [pairs(0, d) for d in range(1, atom_axis)]
        covariance = long_axis_covariance(
            flat, half[0], role[0], block, spread_pairs, 1.0 / total_frames
        )
        return covariance, projections

    axes = ("frames", "atoms")

    def columns(slots):
        return pltpu.VMEM((slots, 3, local_frames, block), jnp.bfloat16)

    def kernel(body, out_shape, scalar, values, name):
        single = not isinstance(out_shape, tuple)
        return pl.pallas_call(
            body,
            out_shape=out_shape,
            in_specs=[SMEM] + [VMEM] * len(values),
            out_specs=VMEM if single else (VMEM,) * len(out_shape),
            compiler_params=params(4),
            name=name,
        )(scalar, *[pinned(value, pltpu.VMEM) for value in values])

    def cross(cut):
        return [cut, lax.ppermute(cut, axes, pairs(0, 2))]

    def pass_on(values, role):
        slots = sum(value.shape[0] for value in values[::2])
        held = kernel(pass_on_kernel, columns(slots), role, values, "pass_on")
        return [held, swap(held, 1)]

    def halves_across(cut, *earlier):
        beside = swap(cut, 1)
        half_shape = pltpu.VMEM(cut.shape[:3] + (block // 2,), jnp.bfloat16)
        picked = kernel(
            pick_half_kernel, half_shape, after(role, *earlier), [cut, beside], "pick_half"
        )
        across = swap(picked, 2)
        return [cut, beside, across, swap(across, 1)], picked

    order = ring_order(frame_axis)
    forward = [(order[i], order[(i + 1) % frame_axis]) for i in range(frame_axis)]
    backward = [(b, a) for a, b in forward]

    def hop(up, down):
        return lax.ppermute(up, "frames", forward), lax.ppermute(down, "frames", backward)

    one = hop(own, own)
    cut_one = kernel(cut_kernel, columns(3), half, [own, *one], "cut_columns")
    two = hop(after(one[0], *parts), one[1])
    in_hbm = pass_on(cross(cut_one), role)
    cut_two = kernel(cut_kernel, columns(2), half, list(two), "cut_columns")
    three = hop(*two)
    in_vmem = pass_on(cross(cut_two), role)
    half_shard = pltpu.VMEM(piece, jnp.bfloat16)
    cut_three, *halves = kernel(
        cut_last_kernel,
        (columns(2), half_shard, half_shard),
        after(half, in_hbm[0]),
        list(three),
        "cut_columns",
    )
    far = hop(*halves)
    three_halves, picked = halves_across(cut_three)
    in_vmem += three_halves
    cut_four = kernel(
        cut_far_kernel, columns(1), after(half, in_hbm[1], in_vmem[0], picked), list(far), "cut_columns"
    )
    in_vmem += halves_across(cut_four, three_halves[2])[0]
    groups = ((3, True, 2), (2, False, 2), (2, False, 4), (1, False, 4))
    rows = [own, *one, *two, *three, *far]
    covariance, projections = pl.pallas_call(
        functools.partial(
            covariance_kernel, frame_axis, atom_axis, groups, 1.0 / total_frames
        ),
        out_shape=(jax.ShapeDtypeStruct((3, 3, local_atoms, block), jnp.float32), share),
        in_specs=[SMEM]
        + [VMEM] * len(rows)
        + [HBM] * len(in_hbm)
        + [VMEM] * len(in_vmem)
        + [HBM] * len(parts),
        out_specs=(ANY, ANY),
        scratch_shapes=[
            pltpu.VMEM((2, 2 * run, total_frames), jnp.bfloat16),
            pltpu.VMEM((3, total_frames, block), jnp.bfloat16),
            pltpu.VMEM((2, 3, 2 * run, block), jnp.float32),
            pltpu.VMEM((atom_axis,) + share.shape, jnp.float32),
            pltpu.SemaphoreType.DMA((2 * frame_axis,)),
            pltpu.SemaphoreType.DMA((2, 3)),
            pltpu.SemaphoreType.DMA((atom_axis,)),
        ],
        compiler_params=params(16),
        cost_estimate=pl.CostEstimate(
            flops=18 * local_atoms * block * total_frames,
            bytes_accessed=24 * MIB,
            transcendentals=0,
        ),
        name="covariance_tile",
    )(
        role,
        *[pinned(value, pltpu.VMEM) for value in rows],
        *[pinned(value, pltpu.HBM) for value in in_hbm],
        *[pinned(value, pltpu.VMEM) for value in in_vmem],
        *[pinned(value, pltpu.HBM) for value in parts],
    )
    return jnp.transpose(covariance, (0, 2, 1, 3)), projections


def solution(mesh):
    placed = (P("frames", None, "atoms"), P(None, "atoms"), P(None, "atoms", None))
    return jax.shard_map(
        per_device,
        mesh=mesh,
        in_specs=placed,
        out_specs=(P(None, "atoms", None, "frames"), P("frames", "atoms")),
        check_vma=False,
    )
```

```python
import functools

import jax
import jax.numpy as jnp
from jax import lax
from jax.experimental import pallas as pl
from jax.experimental.pallas import tpu as pltpu
from jax.sharding import PartitionSpec as P

POLAR = 6
LANES = 128
STATS = 24
VMEM = pl.BlockSpec(memory_space=pltpu.VMEM)
SMEM = pl.BlockSpec(memory_space=pltpu.SMEM)
HBM = pl.BlockSpec(memory_space=pltpu.HBM)
ANY = pl.BlockSpec(memory_space=pl.ANY)
MIB = 1024 * 1024


def params(mib):
    return pltpu.CompilerParams(vmem_limit_bytes=mib * MIB)


def lane_mean(value):
    return jnp.sum(value, axis=1, keepdims=True) * (1.0 / value.shape[1])


def run_copies(copies):
    for copy in copies:
        copy.start()
    for copy in copies:
        copy.wait()


def stats_kernel(x_hbm, ref_hbm, out_ref, x_ref, ref_ref, sem):
    run_copies(
        [
            pltpu.make_async_copy(ref_hbm, ref_ref, sem.at[0]),
            pltpu.make_async_copy(x_hbm, x_ref, sem.at[1]),
        ]
    )
    values = []
    centred = []
    for i in range(3):
        x = x_ref[i]
        mean = lane_mean(x)
        values.append(mean)
        centred.append(x - mean)
    values.append(sum(jnp.sum(c * c, axis=1, keepdims=True) for c in centred))
    ref_mean = [lane_mean(ref_ref[j : j + 1, :]) for j in range(3)]
    ref_centred = [ref_ref[j : j + 1, :] - ref_mean[j] for j in range(3)]
    for i in range(3):
        for j in range(3):
            values.append(jnp.sum(centred[i] * ref_centred[j], axis=1, keepdims=True))
    values += ref_mean
    values.append(sum(jnp.sum(c * c, axis=1, keepdims=True) for c in ref_centred))
    shape = (x_ref.shape[1], LANES)
    lane = lax.broadcasted_iota(jnp.int32, shape, 1)
    out = jnp.zeros(shape, jnp.float32)
    for k, value in enumerate(values):
        out = jnp.where(lane == k, jnp.broadcast_to(value, shape), out)
    out_ref[...] = out.T[:STATS]


def align_kernel(parts, *refs):
    stats = refs[:parts]
    x_ref, ref_ref, piece_ref, flat_ref, turn = refs[parts:]
    local = x_ref.shape[2]
    rows = x_ref.shape[1]

    def row(at):
        return [s[at : at + 1, :] for s in stats]

    means = [row(i) for i in range(3)]
    ref_means = [row(13 + j) for j in range(3)]
    centre = [sum(m) * (1.0 / parts) for m in means]
    ref_centre = [sum(r) * (1.0 / parts) for r in ref_means]
    off = [[m - centre[i] for m in means[i]] for i in range(3)]
    ref_off = [[r - ref_centre[j] for r in ref_means[j]] for j in range(3)]
    spread = sum(row(3)) + local * sum(o * o for i in range(3) for o in off[i])
    ref_spread = sum(row(16)) + local * sum(o * o for j in range(3) for o in ref_off[j])
    scale = 1.0 / jnp.sqrt(spread * ref_spread + 1e-06)
    now = [
        [
            (sum(row(4 + 3 * i + j)) + local * sum(o * r for o, r in zip(off[i], ref_off[j])))
            * scale
            for j in range(3)
        ]
        for i in range(3)
    ]
    for _ in range(POLAR):
        gram = {}
        for i in range(3):
            for j in range(i, 3):
                gram[i, j] = sum(now[k][i] * now[k][j] for k in range(3))
                gram[j, i] = gram[i, j]
        left = [
            [(1.5 if k == j else 0.0) - 0.5 * gram[k, j] for j in range(3)] for k in range(3)
        ]
        now = [
            [sum(now[i][k] * left[k][j] for k in range(3)) for j in range(3)]
            for i in range(3)
        ]
    for k, value in enumerate(sum(now, []) + centre + ref_centre):
        turn[k : k + 1, :rows] = value
    turned = turn[...].T
    column = [turned[:rows, k : k + 1] for k in range(12)]
    centred = [x_ref[j] - column[9 + j] for j in range(3)]
    for i in range(3):
        target = ref_ref[i : i + 1, :] - turned[0:1, 12 + i : 13 + i]
        moved = sum(column[3 * j + i] * centred[j] for j in range(3)) - target
        flat_ref[i] = moved.astype(jnp.bfloat16)
        run = piece_ref.shape[2]
        for at in range(2):
            pair = [moved[:, (2 * at + k) * run : (2 * at + k + 1) * run] for k in range(2)]
            piece_ref[at, i] = jnp.concatenate(pair, axis=0).T.astype(jnp.bfloat16)


def project_kernel(me_ref, flat_ref, eig_ref, *refs):
    shares, cut = refs[:-1], refs[-1]
    total = sum(
        jnp.dot(flat_ref[c], eig_ref[c], preferred_element_type=jnp.float32) for c in range(3)
    )
    width = cut.shape[2]
    for k in range(len(shares)):
        cut[k] = total[:, k * width : (k + 1) * width]
    for k, share in enumerate(shares):
        share[...] = cut[lax.bitwise_xor(me_ref[0], k)]


def cut_columns(half_ref, halves, cols_ref):
    for half in range(2):

        @pl.when(half_ref[0] == half)
        def _(half=half):
            for k, pair in enumerate(halves):
                run, lanes = pair[half].shape[1:]
                for c in range(3):
                    turned = pair[half][c].astype(jnp.float32).T.astype(jnp.bfloat16)
                    cols_ref[k, c, :, :run] = turned[: lanes // 2]
                    cols_ref[k, c, :, run:] = turned[lanes // 2 :]


def cut_kernel(half_ref, *refs):
    cut_columns(half_ref, [(r.at[0], r.at[1]) for r in refs[:-1]], refs[-1])


def cut_last_kernel(half_ref, up_ref, down_ref, cols_ref, up_half, down_half):
    up_half[...] = up_ref[0]
    down_half[...] = down_ref[1]
    cut_columns(half_ref, [(r.at[0], r.at[1]) for r in (up_ref, down_ref)], cols_ref)


def cut_far_kernel(half_ref, up_half, down_half, cols_ref):
    cut_columns(half_ref, [(up_half, down_half)], cols_ref)


def pass_on_kernel(role_ref, *refs):
    sources, out_ref = refs[:-1], refs[-1]
    for role in range(2):

        @pl.when((role_ref[0] != 0) == bool(role))
        def _(role=role):
            to = 0
            for source in sources[role::2]:
                out_ref[to : to + source.shape[0]] = source[...]
                to += source.shape[0]


def pick_half_kernel(role_ref, own_ref, beside_ref, out_ref):
    width = out_ref.shape[3]

    @pl.when(role_ref[0] == 0)
    def _():
        out_ref[...] = own_ref[:, :, :, :width]

    @pl.when(role_ref[0] != 0)
    def _():
        out_ref[...] = beside_ref[:, :, :, width:]


def side_by_side(first, second):
    middle = first.shape[1] // 2
    left = jnp.concatenate([first[:, :middle], second[:, :middle]], axis=1)
    right = jnp.concatenate([first[:, middle:], second[:, middle:]], axis=1)
    return left, right


def covariance_kernel(slots, roles, groups, scale, role_ref, *refs):
    shards, up_half, down_half = refs[: slots - 1], refs[slots - 1], refs[slots]
    refs = refs[slots + 1 :]
    arrays = []
    for _, _, count in groups:
        arrays.append(refs[:count])
        refs = refs[count:]
    shares, refs = refs[:roles], refs[roles:]
    out_ref, proj_ref, left, right, done, held, col_sem, out_sem, share_sem = refs
    sums = [
        pltpu.make_async_copy(part, held.at[k], share_sem.at[k]) for k, part in enumerate(shares)
    ]
    for copy in sums:
        copy.start()
    depth = right.shape[1] // slots
    run = up_half.shape[1]

    def parts_of(k, role):
        if len(arrays[k]) == 2:
            return [(arrays[k][role % 2], 0)]
        own, beside, across, halves = arrays[k]
        width = across.shape[3]
        return {
            0: [(own, 0)],
            1: [(beside, 0)],
            2: [(across, 0), (halves, width)],
            3: [(halves, 0), (across, width)],
        }[role]

    def fetches(k, role, to):
        return [
            pltpu.make_async_copy(
                source.at[n],
                right.at[:, pl.ds(to + n * depth, depth), pl.ds(at, source.shape[3])],
                col_sem.at[2 * (to // depth + n) + p],
            )
            for p, (source, at) in enumerate(parts_of(k, role))
            for n in range(groups[k][0])
        ]

    def for_each_group(from_hbm, act):
        for role in range(roles):

            @pl.when(role_ref[0] == role)
            def _(role=role):
                to = 0
                for k, (count, in_hbm, _) in enumerate(groups):
                    if in_hbm == from_hbm:
                        act(k, role, to)
                    to += count * depth

    def start(k, role, to):
        for copy in fetches(k, role, to):
            copy.start()

    def wait(k, role, to):
        for copy in fetches(k, role, to):
            copy.wait()

    def load(k, role, to):
        for source, at in parts_of(k, role):
            for n in range(groups[k][0]):
                for d in range(3):
                    right[
                        d, to + n * depth : to + (n + 1) * depth, at : at + source.shape[3]
                    ] = source[n, d]

    def piece(slot, at, c):
        if slot < slots - 1:
            return shards[slot][at, c]
        return (up_half, down_half)[at][c]

    def assemble(c, at):
        for q in range(slots // 2):
            low, high = side_by_side(piece(2 * q, at, c), piece(2 * q + 1, at, c))
            left[at, :run, q * LANES : (q + 1) * LANES] = low
            left[at, run:, q * LANES : (q + 1) * LANES] = high

    for_each_group(True, start)
    for_each_group(False, load)
    assemble(0, 0)
    for_each_group(True, wait)
    def write(c, at, d):
        return pltpu.make_async_copy(
            done.at[at, d],
            out_ref.at[c, d, pl.ds(at * 2 * run, 2 * run), :],
            out_sem.at[at, d],
        )

    @pl.loop(0, 3)
    def _(c):
        for at in range(2):

            @pl.when(c > 0)
            def _():
                for d in range(3):
                    write(c - 1, at, d).wait()

            assemble(jnp.minimum(c + at, 2), 1 - at)
            for d in range(3):
                done[at, d] = scale * jnp.dot(
                    left[at], right[d], preferred_element_type=jnp.float32
                )
                write(c, at, d).start()

    for copy in sums:
        copy.wait()
    held[0] = sum(held[k] for k in range(roles))
    leave = pltpu.make_async_copy(held.at[0], proj_ref, share_sem.at[0])
    leave.start()
    for at in range(2):
        for d in range(3):
            write(2, at, d).wait()
    leave.wait()


pinned = pltpu.with_memory_space_constraint


def after(value, *others):
    return lax.optimization_barrier((value,) + others)[0] if others else value


def ring_order(count):
    return list(range(0, count, 2)) + list(range(1, count, 2))[::-1]


def long_axis_covariance(flat, half, role, block, spread_pairs, scale):
    rows = lax.all_gather(flat, "frames", axis=1, tiled=True)
    cut = lax.dynamic_slice_in_dim(rows, half * block, block, axis=2)
    cols = jnp.where(role == 0, cut, jnp.zeros_like(cut))
    for d, pairs in enumerate(spread_pairs):
        sent = lax.ppermute(cut, ("frames", "atoms"), pairs)
        cols = jnp.where(role == d + 1, sent, cols)
    return scale * jnp.einsum(
        "cfp,dfq->cpdq", rows, cols, preferred_element_type=jnp.float32
    )


def per_device(frames, mean_structure, eigvecs):
    local_frames, _, local_atoms = frames.shape
    frame_axis = lax.axis_size("frames")
    atom_axis = lax.axis_size("atoms")
    total_frames = local_frames * frame_axis
    block = local_atoms * atom_axis // frame_axis
    blocks = frame_axis // atom_axis
    me_f = lax.axis_index("frames")
    me_a = lax.axis_index("atoms")
    half = lax.rem(me_f, blocks).astype(jnp.int32).reshape(1)
    owner = lax.div(me_f, blocks)
    role = lax.bitwise_xor(me_a, owner).astype(jnp.int32).reshape(1)
    x = pinned(jnp.transpose(frames, (1, 0, 2)), pltpu.HBM)
    mean_structure = pinned(mean_structure, pltpu.HBM)
    stats, x, mean_structure = pl.pallas_call(
        stats_kernel,
        out_shape=(
            pltpu.VMEM((STATS, local_frames), jnp.float32),
            pltpu.VMEM(x.shape, jnp.float32),
            pltpu.VMEM(mean_structure.shape, jnp.float32),
        ),
        in_specs=[HBM, HBM],
        out_specs=(VMEM, VMEM, VMEM),
        scratch_shapes=[pltpu.SemaphoreType.DMA((2,))],
        compiler_params=params(8),
        name="local_moments",
    )(x, mean_structure)
    def swap(value, distance):
        return lax.ppermute(value, "atoms", [(a, a ^ distance) for a in range(atom_axis)])

    others = [swap(stats, d) for d in range(1, atom_axis)]
    run = local_atoms // 4
    piece = (3, run, 2 * local_frames)
    own, flat = pl.pallas_call(
        functools.partial(align_kernel, atom_axis),
        out_shape=(
            jax.ShapeDtypeStruct((2,) + piece, jnp.bfloat16),
            jax.ShapeDtypeStruct(x.shape, jnp.bfloat16),
        ),
        in_specs=[VMEM] * (atom_axis + 2),
        out_specs=(VMEM, VMEM),
        scratch_shapes=[pltpu.VMEM((LANES, LANES), jnp.float32)],
        compiler_params=params(8),
        name="polar_align",
    )(stats, *others, x, mean_structure)
    share = jax.ShapeDtypeStruct((local_frames, eigvecs.shape[2] // atom_axis), jnp.float32)
    shares = pl.pallas_call(
        project_kernel,
        out_shape=(share,) * atom_axis,
        in_specs=[SMEM, VMEM, VMEM],
        out_specs=(VMEM,) * atom_axis,
        scratch_shapes=[pltpu.VMEM((atom_axis,) + share.shape, jnp.float32)],
        compiler_params=params(8),
        name="project",
    )(me_a.astype(jnp.int32).reshape(1), flat, eigvecs)
    parts = [shares[0]] + [swap(shares[d], d) for d in range(1, atom_axis)]
    def pairs(source, target):
        return [
            (
                f * atom_axis + ((f // blocks) ^ source),
                f * atom_axis + ((f // blocks) ^ target),
            )
            for f in range(frame_axis)
        ]

    if blocks != 2 or frame_axis != 8:
        projections = sum(parts)
        spread_pairs = [pairs(0, d) for d in range(1, atom_axis)]
        covariance = long_axis_covariance(
            flat, half[0], role[0], block, spread_pairs, 1.0 / total_frames
        )
        return covariance, projections

    axes = ("frames", "atoms")

    def columns(slots):
        return pltpu.VMEM((slots, 3, local_frames, block), jnp.bfloat16)

    def kernel(body, out_shape, scalar, values, name):
        single = not isinstance(out_shape, tuple)
        return pl.pallas_call(
            body,
            out_shape=out_shape,
            in_specs=[SMEM] + [VMEM] * len(values),
            out_specs=VMEM if single else (VMEM,) * len(out_shape),
            compiler_params=params(4),
            name=name,
        )(scalar, *[pinned(value, pltpu.VMEM) for value in values])

    def cross(cut):
        return [cut, lax.ppermute(cut, axes, pairs(0, 2))]

    def pass_on(values, role):
        slots = sum(value.shape[0] for value in values[::2])
        held = kernel(pass_on_kernel, columns(slots), role, values, "pass_on")
        return [held, swap(held, 1)]

    def halves_across(cut, *earlier):
        beside = swap(cut, 1)
        half_shape = pltpu.VMEM(cut.shape[:3] + (block // 2,), jnp.bfloat16)
        picked = kernel(
            pick_half_kernel, half_shape, after(role, *earlier), [cut, beside], "pick_half"
        )
        across = swap(picked, 2)
        return [cut, beside, across, swap(across, 1)], picked

    order = ring_order(frame_axis)
    forward = [(order[i], order[(i + 1) % frame_axis]) for i in range(frame_axis)]
    backward = [(b, a) for a, b in forward]

    def hop(up, down):
        return lax.ppermute(up, "frames", forward), lax.ppermute(down, "frames", backward)

    one = hop(own, own)
    cut_one = kernel(cut_kernel, columns(3), half, [own, *one], "cut_columns")
    two = hop(after(one[0], *parts), one[1])
    in_hbm = pass_on(cross(cut_one), role)
    cut_two = kernel(cut_kernel, columns(2), half, list(two), "cut_columns")
    three = hop(*two)
    two_halves = halves_across(cut_two)[0]
    in_hbm += two_halves
    half_shard = pltpu.VMEM(piece, jnp.bfloat16)
    cut_three, *halves = kernel(
        cut_last_kernel,
        (columns(2), half_shard, half_shard),
        after(half, in_hbm[0], two_halves[2]),
        list(three),
        "cut_columns",
    )
    far = hop(*halves)
    in_vmem, picked = halves_across(cut_three)
    cut_four = kernel(
        cut_far_kernel, columns(1), after(half, in_hbm[1], picked), list(far), "cut_columns"
    )
    in_vmem += halves_across(cut_four, in_vmem[2], two_halves[3])[0]
    groups = ((3, True, 2), (2, True, 4), (2, False, 4), (1, False, 4))
    rows = [own, *one, *two, *three, *far]
    covariance, projections = pl.pallas_call(
        functools.partial(
            covariance_kernel, frame_axis, atom_axis, groups, 1.0 / total_frames
        ),
        out_shape=(jax.ShapeDtypeStruct((3, 3, local_atoms, block), jnp.float32), share),
        in_specs=[SMEM]
        + [VMEM] * len(rows)
        + [HBM] * len(in_hbm)
        + [VMEM] * len(in_vmem)
        + [HBM] * len(parts),
        out_specs=(ANY, ANY),
        scratch_shapes=[
            pltpu.VMEM((2, 2 * run, total_frames), jnp.bfloat16),
            pltpu.VMEM((3, total_frames, block), jnp.bfloat16),
            pltpu.VMEM((2, 3, 2 * run, block), jnp.float32),
            pltpu.VMEM((atom_axis,) + share.shape, jnp.float32),
            pltpu.SemaphoreType.DMA((2 * frame_axis,)),
            pltpu.SemaphoreType.DMA((2, 3)),
            pltpu.SemaphoreType.DMA((atom_axis,)),
        ],
        compiler_params=params(16),
        cost_estimate=pl.CostEstimate(
            flops=18 * local_atoms * block * total_frames,
            bytes_accessed=24 * MIB,
            transcendentals=0,
        ),
        name="covariance_tile",
    )(
        role,
        *[pinned(value, pltpu.VMEM) for value in rows],
        *[pinned(value, pltpu.HBM) for value in in_hbm],
        *[pinned(value, pltpu.VMEM) for value in in_vmem],
        *[pinned(value, pltpu.HBM) for value in parts],
    )
    return jnp.transpose(covariance, (0, 2, 1, 3)), projections


def solution(mesh):
    placed = (P("frames", None, "atoms"), P(None, "atoms"), P(None, "atoms", None))
    return jax.shard_map(
        per_device,
        mesh=mesh,
        in_specs=placed,
        out_specs=(P(None, "atoms", None, "frames"), P("frames", "atoms")),
        check_vma=False,
    )
```

```python
import functools

import jax
import jax.numpy as jnp
from jax import lax
from jax.experimental import pallas as pl
from jax.experimental.pallas import tpu as pltpu
from jax.sharding import PartitionSpec as P

POLAR = 6
LANES = 128
STATS = 24
VMEM = pl.BlockSpec(memory_space=pltpu.VMEM)
SMEM = pl.BlockSpec(memory_space=pltpu.SMEM)
HBM = pl.BlockSpec(memory_space=pltpu.HBM)
ANY = pl.BlockSpec(memory_space=pl.ANY)
MIB = 1024 * 1024


def params(mib):
    return pltpu.CompilerParams(vmem_limit_bytes=mib * MIB)


def lane_mean(value):
    return jnp.sum(value, axis=1, keepdims=True) * (1.0 / value.shape[1])


def run_copies(copies):
    for copy in copies:
        copy.start()
    for copy in copies:
        copy.wait()


def stats_kernel(x_hbm, ref_hbm, out_ref, x_ref, ref_ref, sem):
    run_copies(
        [
            pltpu.make_async_copy(ref_hbm, ref_ref, sem.at[0]),
            pltpu.make_async_copy(x_hbm, x_ref, sem.at[1]),
        ]
    )
    values = []
    centred = []
    for i in range(3):
        x = x_ref[i]
        mean = lane_mean(x)
        values.append(mean)
        centred.append(x - mean)
    values.append(sum(jnp.sum(c * c, axis=1, keepdims=True) for c in centred))
    ref_mean = [lane_mean(ref_ref[j : j + 1, :]) for j in range(3)]
    ref_centred = [ref_ref[j : j + 1, :] - ref_mean[j] for j in range(3)]
    for i in range(3):
        for j in range(3):
            values.append(jnp.sum(centred[i] * ref_centred[j], axis=1, keepdims=True))
    values += ref_mean
    values.append(sum(jnp.sum(c * c, axis=1, keepdims=True) for c in ref_centred))
    shape = (x_ref.shape[1], LANES)
    lane = lax.broadcasted_iota(jnp.int32, shape, 1)
    out = jnp.zeros(shape, jnp.float32)
    for k, value in enumerate(values):
        out = jnp.where(lane == k, jnp.broadcast_to(value, shape), out)
    out_ref[...] = out.T[:STATS]


def align_kernel(parts, *refs):
    stats = refs[:parts]
    x_ref, ref_ref, piece_ref, flat_ref, turn = refs[parts:]
    local = x_ref.shape[2]
    rows = x_ref.shape[1]

    def row(at):
        return [s[at : at + 1, :] for s in stats]

    means = [row(i) for i in range(3)]
    ref_means = [row(13 + j) for j in range(3)]
    centre = [sum(m) * (1.0 / parts) for m in means]
    ref_centre = [sum(r) * (1.0 / parts) for r in ref_means]
    off = [[m - centre[i] for m in means[i]] for i in range(3)]
    ref_off = [[r - ref_centre[j] for r in ref_means[j]] for j in range(3)]
    spread = sum(row(3)) + local * sum(o * o for i in range(3) for o in off[i])
    ref_spread = sum(row(16)) + local * sum(o * o for j in range(3) for o in ref_off[j])
    scale = 1.0 / jnp.sqrt(spread * ref_spread + 1e-06)
    now = [
        [
            (sum(row(4 + 3 * i + j)) + local * sum(o * r for o, r in zip(off[i], ref_off[j])))
            * scale
            for j in range(3)
        ]
        for i in range(3)
    ]
    for _ in range(POLAR):
        gram = {}
        for i in range(3):
            for j in range(i, 3):
                gram[i, j] = sum(now[k][i] * now[k][j] for k in range(3))
                gram[j, i] = gram[i, j]
        left = [
            [(1.5 if k == j else 0.0) - 0.5 * gram[k, j] for j in range(3)] for k in range(3)
        ]
        now = [
            [sum(now[i][k] * left[k][j] for k in range(3)) for j in range(3)]
            for i in range(3)
        ]
    for k, value in enumerate(sum(now, []) + centre + ref_centre):
        turn[k : k + 1, :rows] = value
    turned = turn[...].T
    column = [turned[:rows, k : k + 1] for k in range(12)]
    centred = [x_ref[j] - column[9 + j] for j in range(3)]
    for i in range(3):
        target = ref_ref[i : i + 1, :] - turned[0:1, 12 + i : 13 + i]
        moved = sum(column[3 * j + i] * centred[j] for j in range(3)) - target
        flat_ref[i] = moved.astype(jnp.bfloat16)
        run = piece_ref.shape[2]
        for at in range(2):
            pair = [moved[:, (2 * at + k) * run : (2 * at + k + 1) * run] for k in range(2)]
            piece_ref[at, i] = jnp.concatenate(pair, axis=0).T.astype(jnp.bfloat16)


def project_kernel(me_ref, flat_ref, eig_ref, *refs):
    shares, cut = refs[:-1], refs[-1]
    total = sum(
        jnp.dot(flat_ref[c], eig_ref[c], preferred_element_type=jnp.float32) for c in range(3)
    )
    width = cut.shape[2]
    for k in range(len(shares)):
        cut[k] = total[:, k * width : (k + 1) * width]
    for k, share in enumerate(shares):
        share[...] = cut[lax.bitwise_xor(me_ref[0], k)]


def cut_columns(half_ref, halves, cols_ref):
    for half in range(2):

        @pl.when(half_ref[0] == half)
        def _(half=half):
            for k, pair in enumerate(halves):
                run, lanes = pair[half].shape[1:]
                for c in range(3):
                    turned = pair[half][c].astype(jnp.float32).T.astype(jnp.bfloat16)
                    cols_ref[k, c, :, :run] = turned[: lanes // 2]
                    cols_ref[k, c, :, run:] = turned[lanes // 2 :]


def cut_kernel(half_ref, *refs):
    cut_columns(half_ref, [(r.at[0], r.at[1]) for r in refs[:-1]], refs[-1])


def cut_last_kernel(half_ref, up_ref, down_ref, cols_ref, up_half, down_half):
    up_half[...] = up_ref[0]
    down_half[...] = down_ref[1]
    cut_columns(half_ref, [(r.at[0], r.at[1]) for r in (up_ref, down_ref)], cols_ref)


def cut_far_kernel(half_ref, up_half, down_half, cols_ref):
    cut_columns(half_ref, [(up_half, down_half)], cols_ref)


def pass_on_kernel(role_ref, *refs):
    sources, out_ref = refs[:-1], refs[-1]
    for role in range(2):

        @pl.when((role_ref[0] != 0) == bool(role))
        def _(role=role):
            to = 0
            for source in sources[role::2]:
                out_ref[to : to + source.shape[0]] = source[...]
                to += source.shape[0]


def pick_half_kernel(role_ref, own_ref, beside_ref, out_ref):
    width = out_ref.shape[3]

    @pl.when(role_ref[0] == 0)
    def _():
        out_ref[...] = own_ref[:, :, :, :width]

    @pl.when(role_ref[0] != 0)
    def _():
        out_ref[...] = beside_ref[:, :, :, width:]


def side_by_side(first, second):
    middle = first.shape[1] // 2
    left = jnp.concatenate([first[:, :middle], second[:, :middle]], axis=1)
    right = jnp.concatenate([first[:, middle:], second[:, middle:]], axis=1)
    return left, right


def covariance_kernel(slots, roles, groups, scale, role_ref, *refs):
    shards, up_half, down_half = refs[: slots - 1], refs[slots - 1], refs[slots]
    refs = refs[slots + 1 :]
    arrays = []
    for _, _, count in groups:
        arrays.append(refs[:count])
        refs = refs[count:]
    shares, refs = refs[:roles], refs[roles:]
    out_ref, proj_ref, left, right, done, held, col_sem, out_sem, share_sem = refs
    sums = [
        pltpu.make_async_copy(part, held.at[k], share_sem.at[k]) for k, part in enumerate(shares)
    ]
    for copy in sums:
        copy.start()
    depth = right.shape[1] // slots
    run = up_half.shape[1]

    def parts_of(k, role):
        if len(arrays[k]) == 2:
            return [(arrays[k][role % 2], 0)]
        own, beside, across, halves = arrays[k]
        width = across.shape[3]
        return {
            0: [(own, 0)],
            1: [(beside, 0)],
            2: [(across, 0), (halves, width)],
            3: [(halves, 0), (across, width)],
        }[role]

    def fetches(k, role, to):
        return [
            pltpu.make_async_copy(
                source.at[n],
                right.at[:, pl.ds(to + n * depth, depth), pl.ds(at, source.shape[3])],
                col_sem.at[2 * (to // depth + n) + p],
            )
            for p, (source, at) in enumerate(parts_of(k, role))
            for n in range(groups[k][0])
        ]

    def for_each_group(copied, act):
        for role in range(roles):

            @pl.when(role_ref[0] == role)
            def _(role=role):
                to = 0
                for k, (count, by_copy, _) in enumerate(groups):
                    if by_copy == copied:
                        act(k, role, to)
                    to += count * depth

    def start(k, role, to):
        for copy in fetches(k, role, to):
            copy.start()

    def wait(k, role, to):
        for copy in fetches(k, role, to):
            copy.wait()

    def load(k, role, to):
        for source, at in parts_of(k, role):
            for n in range(groups[k][0]):
                for d in range(3):
                    right[
                        d, to + n * depth : to + (n + 1) * depth, at : at + source.shape[3]
                    ] = source[n, d]

    def piece(slot, at, c):
        if slot < slots - 1:
            return shards[slot][at, c]
        return (up_half, down_half)[at][c]

    def assemble(c, at):
        for q in range(slots // 2):
            low, high = side_by_side(piece(2 * q, at, c), piece(2 * q + 1, at, c))
            left[at, :run, q * LANES : (q + 1) * LANES] = low
            left[at, run:, q * LANES : (q + 1) * LANES] = high

    for_each_group(True, start)
    for_each_group(False, load)
    assemble(0, 0)
    for_each_group(True, wait)
    def write(c, at, d):
        return pltpu.make_async_copy(
            done.at[at, d],
            out_ref.at[c, d, pl.ds(at * 2 * run, 2 * run), :],
            out_sem.at[at, d],
        )

    @pl.loop(0, 3)
    def _(c):
        for at in range(2):

            @pl.when(c > 0)
            def _():
                for d in range(3):
                    write(c - 1, at, d).wait()

            assemble(jnp.minimum(c + at, 2), 1 - at)
            for d in range(3):
                done[at, d] = scale * jnp.dot(
                    left[at], right[d], preferred_element_type=jnp.float32
                )
                write(c, at, d).start()

    for copy in sums:
        copy.wait()
    held[0] = sum(held[k] for k in range(roles))
    leave = pltpu.make_async_copy(held.at[0], proj_ref, share_sem.at[0])
    leave.start()
    for at in range(2):
        for d in range(3):
            write(2, at, d).wait()
    leave.wait()


pinned = pltpu.with_memory_space_constraint


def after(value, *others):
    return lax.optimization_barrier((value,) + others)[0] if others else value


def ring_order(count):
    return list(range(0, count, 2)) + list(range(1, count, 2))[::-1]


def long_axis_covariance(flat, half, role, block, spread_pairs, scale):
    rows = lax.all_gather(flat, "frames", axis=1, tiled=True)
    cut = lax.dynamic_slice_in_dim(rows, half * block, block, axis=2)
    cols = jnp.where(role == 0, cut, jnp.zeros_like(cut))
    for d, pairs in enumerate(spread_pairs):
        sent = lax.ppermute(cut, ("frames", "atoms"), pairs)
        cols = jnp.where(role == d + 1, sent, cols)
    return scale * jnp.einsum(
        "cfp,dfq->cpdq", rows, cols, preferred_element_type=jnp.float32
    )


def per_device(frames, mean_structure, eigvecs):
    local_frames, _, local_atoms = frames.shape
    frame_axis = lax.axis_size("frames")
    atom_axis = lax.axis_size("atoms")
    total_frames = local_frames * frame_axis
    block = local_atoms * atom_axis // frame_axis
    blocks = frame_axis // atom_axis
    me_f = lax.axis_index("frames")
    me_a = lax.axis_index("atoms")
    half = lax.rem(me_f, blocks).astype(jnp.int32).reshape(1)
    owner = lax.div(me_f, blocks)
    role = lax.bitwise_xor(me_a, owner).astype(jnp.int32).reshape(1)
    x = pinned(jnp.transpose(frames, (1, 0, 2)), pltpu.HBM)
    mean_structure = pinned(mean_structure, pltpu.HBM)
    stats, x, mean_structure = pl.pallas_call(
        stats_kernel,
        out_shape=(
            pltpu.VMEM((STATS, local_frames), jnp.float32),
            pltpu.VMEM(x.shape, jnp.float32),
            pltpu.VMEM(mean_structure.shape, jnp.float32),
        ),
        in_specs=[HBM, HBM],
        out_specs=(VMEM, VMEM, VMEM),
        scratch_shapes=[pltpu.SemaphoreType.DMA((2,))],
        compiler_params=params(8),
        name="local_moments",
    )(x, mean_structure)
    def swap(value, distance):
        return lax.ppermute(value, "atoms", [(a, a ^ distance) for a in range(atom_axis)])

    others = [swap(stats, d) for d in range(1, atom_axis)]
    run = local_atoms // 4
    piece = (3, run, 2 * local_frames)
    own, flat = pl.pallas_call(
        functools.partial(align_kernel, atom_axis),
        out_shape=(
            jax.ShapeDtypeStruct((2,) + piece, jnp.bfloat16),
            jax.ShapeDtypeStruct(x.shape, jnp.bfloat16),
        ),
        in_specs=[VMEM] * (atom_axis + 2),
        out_specs=(VMEM, VMEM),
        scratch_shapes=[pltpu.VMEM((LANES, LANES), jnp.float32)],
        compiler_params=params(8),
        name="polar_align",
    )(stats, *others, x, mean_structure)
    share = jax.ShapeDtypeStruct((local_frames, eigvecs.shape[2] // atom_axis), jnp.float32)
    shares = pl.pallas_call(
        project_kernel,
        out_shape=(share,) * atom_axis,
        in_specs=[SMEM, VMEM, VMEM],
        out_specs=(VMEM,) * atom_axis,
        scratch_shapes=[pltpu.VMEM((atom_axis,) + share.shape, jnp.float32)],
        compiler_params=params(8),
        name="project",
    )(me_a.astype(jnp.int32).reshape(1), flat, eigvecs)
    parts = [shares[0]] + [swap(shares[d], d) for d in range(1, atom_axis)]
    def pairs(source, target):
        return [
            (
                f * atom_axis + ((f // blocks) ^ source),
                f * atom_axis + ((f // blocks) ^ target),
            )
            for f in range(frame_axis)
        ]

    if blocks != 2 or frame_axis != 8:
        projections = sum(parts)
        spread_pairs = [pairs(0, d) for d in range(1, atom_axis)]
        covariance = long_axis_covariance(
            flat, half[0], role[0], block, spread_pairs, 1.0 / total_frames
        )
        return covariance, projections

    axes = ("frames", "atoms")

    def columns(slots):
        return pltpu.VMEM((slots, 3, local_frames, block), jnp.bfloat16)

    def kernel(body, out_shape, scalar, values, name):
        single = not isinstance(out_shape, tuple)
        return pl.pallas_call(
            body,
            out_shape=out_shape,
            in_specs=[SMEM] + [VMEM] * len(values),
            out_specs=VMEM if single else (VMEM,) * len(out_shape),
            compiler_params=params(4),
            name=name,
        )(scalar, *[pinned(value, pltpu.VMEM) for value in values])

    def cross(cut):
        return [cut, lax.ppermute(cut, axes, pairs(0, 2))]

    def pass_on(values, role):
        slots = sum(value.shape[0] for value in values[::2])
        held = kernel(pass_on_kernel, columns(slots), role, values, "pass_on")
        return [held, swap(held, 1)]

    def halves_across(cut, *earlier):
        beside = swap(cut, 1)
        half_shape = pltpu.VMEM(cut.shape[:3] + (block // 2,), jnp.bfloat16)
        picked = kernel(
            pick_half_kernel, half_shape, after(role, *earlier), [cut, beside], "pick_half"
        )
        across = swap(picked, 2)
        return [cut, beside, across, swap(across, 1)], picked

    order = ring_order(frame_axis)
    forward = [(order[i], order[(i + 1) % frame_axis]) for i in range(frame_axis)]
    backward = [(b, a) for a, b in forward]

    def hop(up, down):
        return lax.ppermute(up, "frames", forward), lax.ppermute(down, "frames", backward)

    one = hop(own, own)
    cut_one = kernel(cut_kernel, columns(3), half, [own, *one], "cut_columns")
    two = hop(after(one[0], *parts), one[1])
    first_group = pass_on(cross(cut_one), role)
    cut_two = kernel(cut_kernel, columns(2), half, list(two), "cut_columns")
    three = hop(*two)
    in_vmem = pass_on(cross(cut_two), role)
    half_shard = pltpu.VMEM(piece, jnp.bfloat16)
    cut_three, *halves = kernel(
        cut_last_kernel,
        (columns(2), half_shard, half_shard),
        after(half, first_group[0]),
        list(three),
        "cut_columns",
    )
    far = hop(*halves)
    three_halves, picked = halves_across(cut_three)
    in_vmem += three_halves
    cut_four = kernel(
        cut_far_kernel, columns(1), after(half, first_group[1], in_vmem[0], picked), list(far), "cut_columns"
    )
    in_vmem += halves_across(cut_four, three_halves[2])[0]
    groups = ((3, True, 2), (2, False, 2), (2, False, 4), (1, False, 4))
    rows = [own, *one, *two, *three, *far]
    covariance, projections = pl.pallas_call(
        functools.partial(
            covariance_kernel, frame_axis, atom_axis, groups, 1.0 / total_frames
        ),
        out_shape=(jax.ShapeDtypeStruct((3, 3, local_atoms, block), jnp.float32), share),
        in_specs=[SMEM]
        + [VMEM] * len(rows)
        + [HBM, VMEM]
        + [VMEM] * len(in_vmem)
        + [HBM] * len(parts),
        out_specs=(ANY, ANY),
        scratch_shapes=[
            pltpu.VMEM((2, 2 * run, total_frames), jnp.bfloat16),
            pltpu.VMEM((3, total_frames, block), jnp.bfloat16),
            pltpu.VMEM((2, 3, 2 * run, block), jnp.float32),
            pltpu.VMEM((atom_axis,) + share.shape, jnp.float32),
            pltpu.SemaphoreType.DMA((2 * frame_axis,)),
            pltpu.SemaphoreType.DMA((2, 3)),
            pltpu.SemaphoreType.DMA((atom_axis,)),
        ],
        compiler_params=params(16),
        cost_estimate=pl.CostEstimate(
            flops=18 * local_atoms * block * total_frames,
            bytes_accessed=24 * MIB,
            transcendentals=0,
        ),
        name="covariance_tile",
    )(
        role,
        *[pinned(value, pltpu.VMEM) for value in rows],
        pinned(first_group[0], pltpu.HBM),
        pinned(first_group[1], pltpu.VMEM),
        *[pinned(value, pltpu.VMEM) for value in in_vmem],
        *[pinned(value, pltpu.HBM) for value in parts],
    )
    return jnp.transpose(covariance, (0, 2, 1, 3)), projections


def solution(mesh):
    placed = (P("frames", None, "atoms"), P(None, "atoms"), P(None, "atoms", None))
    return jax.shard_map(
        per_device,
        mesh=mesh,
        in_specs=placed,
        out_specs=(P(None, "atoms", None, "frames"), P("frames", "atoms")),
        check_vma=False,
    )
```

```python
import functools

import jax
import jax.numpy as jnp
from jax import lax
from jax.experimental import pallas as pl
from jax.experimental.pallas import tpu as pltpu
from jax.sharding import PartitionSpec as P

POLAR = 6
LANES = 128
STATS = 24
VMEM = pl.BlockSpec(memory_space=pltpu.VMEM)
SMEM = pl.BlockSpec(memory_space=pltpu.SMEM)
HBM = pl.BlockSpec(memory_space=pltpu.HBM)
ANY = pl.BlockSpec(memory_space=pl.ANY)
MIB = 1024 * 1024


def params(mib):
    return pltpu.CompilerParams(vmem_limit_bytes=mib * MIB)


def lane_mean(value):
    return jnp.sum(value, axis=1, keepdims=True) * (1.0 / value.shape[1])


def run_copies(copies):
    for copy in copies:
        copy.start()
    for copy in copies:
        copy.wait()


def stats_kernel(x_hbm, ref_hbm, out_ref, x_ref, ref_ref, sem):
    run_copies(
        [
            pltpu.make_async_copy(ref_hbm, ref_ref, sem.at[0]),
            pltpu.make_async_copy(x_hbm, x_ref, sem.at[1]),
        ]
    )
    values = []
    centred = []
    for i in range(3):
        x = x_ref[i]
        mean = lane_mean(x)
        values.append(mean)
        centred.append(x - mean)
    values.append(sum(jnp.sum(c * c, axis=1, keepdims=True) for c in centred))
    ref_mean = [lane_mean(ref_ref[j : j + 1, :]) for j in range(3)]
    ref_centred = [ref_ref[j : j + 1, :] - ref_mean[j] for j in range(3)]
    for i in range(3):
        for j in range(3):
            values.append(jnp.sum(centred[i] * ref_centred[j], axis=1, keepdims=True))
    values += ref_mean
    values.append(sum(jnp.sum(c * c, axis=1, keepdims=True) for c in ref_centred))
    shape = (x_ref.shape[1], LANES)
    lane = lax.broadcasted_iota(jnp.int32, shape, 1)
    out = jnp.zeros(shape, jnp.float32)
    for k, value in enumerate(values):
        out = jnp.where(lane == k, jnp.broadcast_to(value, shape), out)
    out_ref[...] = out.T[:STATS]


def align_kernel(parts, *refs):
    stats = refs[:parts]
    x_ref, ref_ref, piece_ref, flat_ref, turn = refs[parts:]
    local = x_ref.shape[2]
    rows = x_ref.shape[1]

    def row(at):
        return [s[at : at + 1, :] for s in stats]

    means = [row(i) for i in range(3)]
    ref_means = [row(13 + j) for j in range(3)]
    centre = [sum(m) * (1.0 / parts) for m in means]
    ref_centre = [sum(r) * (1.0 / parts) for r in ref_means]
    off = [[m - centre[i] for m in means[i]] for i in range(3)]
    ref_off = [[r - ref_centre[j] for r in ref_means[j]] for j in range(3)]
    spread = sum(row(3)) + local * sum(o * o for i in range(3) for o in off[i])
    ref_spread = sum(row(16)) + local * sum(o * o for j in range(3) for o in ref_off[j])
    scale = 1.0 / jnp.sqrt(spread * ref_spread + 1e-06)
    now = [
        [
            (sum(row(4 + 3 * i + j)) + local * sum(o * r for o, r in zip(off[i], ref_off[j])))
            * scale
            for j in range(3)
        ]
        for i in range(3)
    ]
    for _ in range(POLAR):
        gram = {}
        for i in range(3):
            for j in range(i, 3):
                gram[i, j] = sum(now[k][i] * now[k][j] for k in range(3))
                gram[j, i] = gram[i, j]
        left = [
            [(1.5 if k == j else 0.0) - 0.5 * gram[k, j] for j in range(3)] for k in range(3)
        ]
        now = [
            [sum(now[i][k] * left[k][j] for k in range(3)) for j in range(3)]
            for i in range(3)
        ]
    for k, value in enumerate(sum(now, []) + centre + ref_centre):
        turn[k : k + 1, :rows] = value
    turned = turn[...].T
    column = [turned[:rows, k : k + 1] for k in range(12)]
    centred = [x_ref[j] - column[9 + j] for j in range(3)]
    for i in range(3):
        target = ref_ref[i : i + 1, :] - turned[0:1, 12 + i : 13 + i]
        moved = sum(column[3 * j + i] * centred[j] for j in range(3)) - target
        flat_ref[i] = moved.astype(jnp.bfloat16)
        run = piece_ref.shape[2]
        for at in range(2):
            pair = [moved[:, (2 * at + k) * run : (2 * at + k + 1) * run] for k in range(2)]
            piece_ref[at, i] = jnp.concatenate(pair, axis=0).T.astype(jnp.bfloat16)


def project_kernel(me_ref, flat_ref, eig_ref, *refs):
    shares, cut = refs[:-1], refs[-1]
    total = sum(
        jnp.dot(flat_ref[c], eig_ref[c], preferred_element_type=jnp.float32) for c in range(3)
    )
    width = cut.shape[2]
    for k in range(len(shares)):
        cut[k] = total[:, k * width : (k + 1) * width]
    for k, share in enumerate(shares):
        share[...] = cut[lax.bitwise_xor(me_ref[0], k)]


def cut_columns(half_ref, halves, cols_ref):
    for half in range(2):

        @pl.when(half_ref[0] == half)
        def _(half=half):
            for k, pair in enumerate(halves):
                run, lanes = pair[half].shape[1:]
                for c in range(3):
                    turned = pair[half][c].astype(jnp.float32).T.astype(jnp.bfloat16)
                    cols_ref[k, c, :, :run] = turned[: lanes // 2]
                    cols_ref[k, c, :, run:] = turned[lanes // 2 :]


def cut_kernel(half_ref, *refs):
    cut_columns(half_ref, [(r.at[0], r.at[1]) for r in refs[:-1]], refs[-1])


def cut_last_kernel(half_ref, up_ref, down_ref, cols_ref, up_half, down_half):
    up_half[...] = up_ref[0]
    down_half[...] = down_ref[1]
    cut_columns(half_ref, [(r.at[0], r.at[1]) for r in (up_ref, down_ref)], cols_ref)


def cut_far_kernel(half_ref, up_half, down_half, cols_ref):
    cut_columns(half_ref, [(up_half, down_half)], cols_ref)


def pass_on_kernel(role_ref, *refs):
    sources, out_ref = refs[:-1], refs[-1]
    for role in range(2):

        @pl.when((role_ref[0] != 0) == bool(role))
        def _(role=role):
            to = 0
            for source in sources[role::2]:
                out_ref[to : to + source.shape[0]] = source[...]
                to += source.shape[0]


def pick_half_kernel(role_ref, own_ref, beside_ref, out_ref):
    width = out_ref.shape[3]

    @pl.when(role_ref[0] == 0)
    def _():
        out_ref[...] = own_ref[:, :, :, :width]

    @pl.when(role_ref[0] != 0)
    def _():
        out_ref[...] = beside_ref[:, :, :, width:]


def side_by_side(first, second):
    middle = first.shape[1] // 2
    left = jnp.concatenate([first[:, :middle], second[:, :middle]], axis=1)
    right = jnp.concatenate([first[:, middle:], second[:, middle:]], axis=1)
    return left, right


def covariance_kernel(slots, roles, groups, scale, role_ref, *refs):
    shards, up_half, down_half = refs[: slots - 1], refs[slots - 1], refs[slots]
    refs = refs[slots + 1 :]
    arrays = []
    for _, _, count in groups:
        arrays.append(refs[:count])
        refs = refs[count:]
    shares, refs = refs[:roles], refs[roles:]
    out_ref, proj_ref, left, right, done, held, kept, col_sem, out_sem, share_sem = refs
    keep = pltpu.make_async_copy(shards[0], kept, share_sem.at[roles])
    keep.start()
    shards = (kept,) + tuple(shards[1:])
    sums = [
        pltpu.make_async_copy(part, held.at[k], share_sem.at[k]) for k, part in enumerate(shares)
    ]
    for copy in sums:
        copy.start()
    depth = right.shape[1] // slots
    run = up_half.shape[1]

    def parts_of(k, role):
        if len(arrays[k]) == 2:
            return [(arrays[k][role % 2], 0)]
        own, beside, across, halves = arrays[k]
        width = across.shape[3]
        return {
            0: [(own, 0)],
            1: [(beside, 0)],
            2: [(across, 0), (halves, width)],
            3: [(halves, 0), (across, width)],
        }[role]

    def fetches(k, role, to):
        return [
            pltpu.make_async_copy(
                source.at[n],
                right.at[:, pl.ds(to + n * depth, depth), pl.ds(at, source.shape[3])],
                col_sem.at[2 * (to // depth + n) + p],
            )
            for p, (source, at) in enumerate(parts_of(k, role))
            for n in range(groups[k][0])
        ]

    def for_each_group(copied, act):
        for role in range(roles):

            @pl.when(role_ref[0] == role)
            def _(role=role):
                to = 0
                for k, (count, by_copy, _) in enumerate(groups):
                    if by_copy == copied:
                        act(k, role, to)
                    to += count * depth

    def start(k, role, to):
        for copy in fetches(k, role, to):
            copy.start()

    def wait(k, role, to):
        for copy in fetches(k, role, to):
            copy.wait()

    def load(k, role, to):
        for source, at in parts_of(k, role):
            for n in range(groups[k][0]):
                for d in range(3):
                    right[
                        d, to + n * depth : to + (n + 1) * depth, at : at + source.shape[3]
                    ] = source[n, d]

    def piece(slot, at, c):
        if slot < slots - 1:
            return shards[slot][at, c]
        return (up_half, down_half)[at][c]

    def assemble(c, at):
        for q in range(slots // 2):
            low, high = side_by_side(piece(2 * q, at, c), piece(2 * q + 1, at, c))
            left[at, :run, q * LANES : (q + 1) * LANES] = low
            left[at, run:, q * LANES : (q + 1) * LANES] = high

    for_each_group(True, start)
    for_each_group(False, load)
    keep.wait()
    assemble(0, 0)
    for_each_group(True, wait)
    def write(c, at, d):
        return pltpu.make_async_copy(
            done.at[at, d],
            out_ref.at[c, d, pl.ds(at * 2 * run, 2 * run), :],
            out_sem.at[at, d],
        )

    @pl.loop(0, 3)
    def _(c):
        for at in range(2):

            @pl.when(c > 0)
            def _():
                for d in range(3):
                    write(c - 1, at, d).wait()

            assemble(jnp.minimum(c + at, 2), 1 - at)
            for d in range(3):
                done[at, d] = scale * jnp.dot(
                    left[at], right[d], preferred_element_type=jnp.float32
                )
                write(c, at, d).start()

    for copy in sums:
        copy.wait()
    held[0] = sum(held[k] for k in range(roles))
    leave = pltpu.make_async_copy(held.at[0], proj_ref, share_sem.at[0])
    leave.start()
    for at in range(2):
        for d in range(3):
            write(2, at, d).wait()
    leave.wait()


pinned = pltpu.with_memory_space_constraint


def after(value, *others):
    return lax.optimization_barrier((value,) + others)[0] if others else value


def ring_order(count):
    return list(range(0, count, 2)) + list(range(1, count, 2))[::-1]


def long_axis_covariance(flat, half, role, block, spread_pairs, scale):
    rows = lax.all_gather(flat, "frames", axis=1, tiled=True)
    cut = lax.dynamic_slice_in_dim(rows, half * block, block, axis=2)
    cols = jnp.where(role == 0, cut, jnp.zeros_like(cut))
    for d, pairs in enumerate(spread_pairs):
        sent = lax.ppermute(cut, ("frames", "atoms"), pairs)
        cols = jnp.where(role == d + 1, sent, cols)
    return scale * jnp.einsum(
        "cfp,dfq->cpdq", rows, cols, preferred_element_type=jnp.float32
    )


def per_device(frames, mean_structure, eigvecs):
    local_frames, _, local_atoms = frames.shape
    frame_axis = lax.axis_size("frames")
    atom_axis = lax.axis_size("atoms")
    total_frames = local_frames * frame_axis
    block = local_atoms * atom_axis // frame_axis
    blocks = frame_axis // atom_axis
    me_f = lax.axis_index("frames")
    me_a = lax.axis_index("atoms")
    half = lax.rem(me_f, blocks).astype(jnp.int32).reshape(1)
    owner = lax.div(me_f, blocks)
    role = lax.bitwise_xor(me_a, owner).astype(jnp.int32).reshape(1)
    x = pinned(jnp.transpose(frames, (1, 0, 2)), pltpu.HBM)
    mean_structure = pinned(mean_structure, pltpu.HBM)
    stats, x, mean_structure = pl.pallas_call(
        stats_kernel,
        out_shape=(
            pltpu.VMEM((STATS, local_frames), jnp.float32),
            pltpu.VMEM(x.shape, jnp.float32),
            pltpu.VMEM(mean_structure.shape, jnp.float32),
        ),
        in_specs=[HBM, HBM],
        out_specs=(VMEM, VMEM, VMEM),
        scratch_shapes=[pltpu.SemaphoreType.DMA((2,))],
        compiler_params=params(8),
        name="local_moments",
    )(x, mean_structure)
    def swap(value, distance):
        return lax.ppermute(value, "atoms", [(a, a ^ distance) for a in range(atom_axis)])

    others = [swap(stats, d) for d in range(1, atom_axis)]
    run = local_atoms // 4
    piece = (3, run, 2 * local_frames)
    own, flat = pl.pallas_call(
        functools.partial(align_kernel, atom_axis),
        out_shape=(
            jax.ShapeDtypeStruct((2,) + piece, jnp.bfloat16),
            jax.ShapeDtypeStruct(x.shape, jnp.bfloat16),
        ),
        in_specs=[VMEM] * (atom_axis + 2),
        out_specs=(VMEM, VMEM),
        scratch_shapes=[pltpu.VMEM((LANES, LANES), jnp.float32)],
        compiler_params=params(8),
        name="polar_align",
    )(stats, *others, x, mean_structure)
    share = jax.ShapeDtypeStruct((local_frames, eigvecs.shape[2] // atom_axis), jnp.float32)
    shares = pl.pallas_call(
        project_kernel,
        out_shape=(share,) * atom_axis,
        in_specs=[SMEM, VMEM, VMEM],
        out_specs=(VMEM,) * atom_axis,
        scratch_shapes=[pltpu.VMEM((atom_axis,) + share.shape, jnp.float32)],
        compiler_params=params(8),
        name="project",
    )(me_a.astype(jnp.int32).reshape(1), flat, eigvecs)
    parts = [shares[0]] + [swap(shares[d], d) for d in range(1, atom_axis)]
    def pairs(source, target):
        return [
            (
                f * atom_axis + ((f // blocks) ^ source),
                f * atom_axis + ((f // blocks) ^ target),
            )
            for f in range(frame_axis)
        ]

    if blocks != 2 or frame_axis != 8:
        projections = sum(parts)
        spread_pairs = [pairs(0, d) for d in range(1, atom_axis)]
        covariance = long_axis_covariance(
            flat, half[0], role[0], block, spread_pairs, 1.0 / total_frames
        )
        return covariance, projections

    axes = ("frames", "atoms")

    def columns(slots):
        return pltpu.VMEM((slots, 3, local_frames, block), jnp.bfloat16)

    def kernel(body, out_shape, scalar, values, name):
        single = not isinstance(out_shape, tuple)
        return pl.pallas_call(
            body,
            out_shape=out_shape,
            in_specs=[SMEM] + [VMEM] * len(values),
            out_specs=VMEM if single else (VMEM,) * len(out_shape),
            compiler_params=params(4),
            name=name,
        )(scalar, *[pinned(value, pltpu.VMEM) for value in values])

    def cross(cut):
        return [cut, lax.ppermute(cut, axes, pairs(0, 2))]

    def pass_on(values, role):
        slots = sum(value.shape[0] for value in values[::2])
        held = kernel(pass_on_kernel, columns(slots), role, values, "pass_on")
        return [held, swap(held, 1)]

    def halves_across(cut, *earlier):
        beside = swap(cut, 1)
        half_shape = pltpu.VMEM(cut.shape[:3] + (block // 2,), jnp.bfloat16)
        picked = kernel(
            pick_half_kernel, half_shape, after(role, *earlier), [cut, beside], "pick_half"
        )
        across = swap(picked, 2)
        return [cut, beside, across, swap(across, 1)], picked

    order = ring_order(frame_axis)
    forward = [(order[i], order[(i + 1) % frame_axis]) for i in range(frame_axis)]
    backward = [(b, a) for a, b in forward]

    def hop(up, down):
        return lax.ppermute(up, "frames", forward), lax.ppermute(down, "frames", backward)

    one = hop(own, own)
    cut_one = kernel(cut_kernel, columns(3), half, [own, *one], "cut_columns")
    two = hop(after(one[0], *parts), one[1])
    first_group = pass_on(cross(cut_one), role)
    cut_two = kernel(cut_kernel, columns(2), half, list(two), "cut_columns")
    three = hop(*two)
    in_vmem = pass_on(cross(cut_two), role)
    half_shard = pltpu.VMEM(piece, jnp.bfloat16)
    cut_three, *halves = kernel(
        cut_last_kernel,
        (columns(2), half_shard, half_shard),
        after(half, first_group[0]),
        list(three),
        "cut_columns",
    )
    far = hop(*halves)
    three_halves, picked = halves_across(cut_three)
    in_vmem += three_halves
    cut_four = kernel(
        cut_far_kernel, columns(1), after(half, first_group[1], in_vmem[0], picked), list(far), "cut_columns"
    )
    in_vmem += halves_across(cut_four, three_halves[2])[0]
    groups = ((3, True, 2), (2, False, 2), (2, False, 4), (1, False, 4))
    rows = [own, *one, *two, *three, *far]
    covariance, projections = pl.pallas_call(
        functools.partial(
            covariance_kernel, frame_axis, atom_axis, groups, 1.0 / total_frames
        ),
        out_shape=(jax.ShapeDtypeStruct((3, 3, local_atoms, block), jnp.float32), share),
        in_specs=[SMEM, HBM]
        + [VMEM] * (len(rows) - 1)
        + [HBM, VMEM]
        + [VMEM] * len(in_vmem)
        + [HBM] * len(parts),
        out_specs=(ANY, ANY),
        scratch_shapes=[
            pltpu.VMEM((2, 2 * run, total_frames), jnp.bfloat16),
            pltpu.VMEM((3, total_frames, block), jnp.bfloat16),
            pltpu.VMEM((2, 3, 2 * run, block), jnp.float32),
            pltpu.VMEM((atom_axis,) + share.shape, jnp.float32),
            pltpu.VMEM(own.shape, jnp.bfloat16),
            pltpu.SemaphoreType.DMA((2 * frame_axis,)),
            pltpu.SemaphoreType.DMA((2, 3)),
            pltpu.SemaphoreType.DMA((atom_axis + 1,)),
        ],
        compiler_params=params(16),
        cost_estimate=pl.CostEstimate(
            flops=18 * local_atoms * block * total_frames,
            bytes_accessed=24 * MIB,
            transcendentals=0,
        ),
        name="covariance_tile",
    )(
        role,
        pinned(rows[0], pltpu.HBM),
        *[pinned(value, pltpu.VMEM) for value in rows[1:]],
        pinned(first_group[0], pltpu.HBM),
        pinned(first_group[1], pltpu.VMEM),
        *[pinned(value, pltpu.VMEM) for value in in_vmem],
        *[pinned(value, pltpu.HBM) for value in parts],
    )
    return jnp.transpose(covariance, (0, 2, 1, 3)), projections


def solution(mesh):
    placed = (P("frames", None, "atoms"), P(None, "atoms"), P(None, "atoms", None))
    return jax.shard_map(
        per_device,
        mesh=mesh,
        in_specs=placed,
        out_specs=(P(None, "atoms", None, "frames"), P("frames", "atoms")),
        check_vma=False,
    )
```
